32 devices in a mesh: dp: 8 (over z, x), inner: 4 (over y, core).
Axes of the slice: x: 2, y: 2, z: 4, core: 2. Of those that a mesh axis runs over, the one named last changes fastest.
Arguments:
- hidden: float32 [65536, 253], P(('dp', 'inner')), may hold values from -6 to 6
- codes: float32 [16, 256], replicated, may hold values from -40 to 40, as said below
- offsets: float32 [65536, 3], P(('dp', 'inner')), may hold values from -6 to 6
- shape_ids: int32 [65536], P(('dp', 'inner')), may hold values from 0 to 15, as said below
- scale_index: int32 [65536], P(('dp', 'inner')), may hold values from 0 to 2, as said below
- direction: float32 [512, 512], P(('dp', 'inner')), may hold values from -0.25 to 0.25
- gain: float32 [512], P(('dp', 'inner')), may hold values from 0.5 to 2
- bias: float32 [512], P(('dp', 'inner')), may hold values from -3 to 3
- cotangent: float32 [65536, 512], P(('dp', 'inner')), may hold values from -6 to 6
- running_mean: float32 [256], replicated, may hold values from -3 to 3
- running_var: float32 [256], replicated, may hold values from 0.5 to 2
Outputs:
- output: float32 [65536, 512], P(('dp', 'inner'))
- grad_hidden: float32 [65536, 253], P(('dp', 'inner'))
- grad_codes: float32 [16, 256], replicated
- grad_direction: float32 [512, 512], P(('dp', 'inner'))
- grad_gain: float32 [512], P(('dp', 'inner'))
- grad_bias: float32 [512], P(('dp', 'inner'))
- new_mean: float32 [256], replicated
- new_var: float32 [256], replicated
The draws below stay inside these ranges and needn't reach their ends.
Inputs may be any that keep to these rules, and one draw needn't show every extreme that they name: codes have row scales that differ between shapes. `shape_ids`: each shape has exactly 4096 points. `scale_index`: over all points exactly 32768 have index 0 and 20480 have index 1.
All inputs are finite; a program needn't handle non-finite values.
Results may differ from the reference program's by a relative error of at most 0.0067.
Values may be sent and summed in bfloat16 or wider, within the bound.
No kernel may reach another device: no remote copies, remote signals or barrier semaphores. Data moves between devices by JAX's collectives and lax.ppermute only.
A program may use at most 64 MiB of HBM per device.

```python
import jax
import jax.numpy as jnp
from jax import lax

OUT = 512
CODE = 256
HID = 253
SHAPE_PTS = 4096
POINTS = 65536
SHAPES = 16


def shape_order(key):
    return jax.random.permutation(key, SHAPES).astype(jnp.int32)


def draw_codes(key, part):
    order = shape_order(key)
    key = jax.random.fold_in(key, 7)
    scale_key, value_key = jax.random.split(key, 2)
    slot_of_shape = jnp.argsort(order).astype(jnp.int32)
    place = slot_of_shape.astype(jnp.float32) / (SHAPES - 1.0)
    rough = jax.random.uniform(scale_key, (SHAPES, 1), jnp.float32, 0.75, 1.3)
    scales = jnp.exp(jnp.log(0.4) + place * jnp.log(10.0))[:, None] * rough
    values = jnp.clip(jax.random.normal(value_key, (SHAPES, CODE), jnp.float32), -4.0, 4.0)
    return values * scales


def draw_shape_ids(key, part):
    order = shape_order(key)
    positions = jnp.arange(SHAPES * SHAPE_PTS, dtype=jnp.int32)
    spread = positions % SHAPES == 0
    rank = jnp.cumsum(jnp.where(spread, 0, 1).astype(jnp.int32)) - 1
    slot = jnp.where(spread, 0, rank // SHAPE_PTS + 1).astype(jnp.int32)
    return order[slot]


def draw_scale_index(key, part):
    key = jax.random.fold_in(key, 13)
    total = SHAPES * SHAPE_PTS
    orders = jax.random.permutation(key, total).astype(jnp.int32)
    first = (orders >= total // 2).astype(jnp.int32)
    second = (orders >= total // 2 + 5 * total // 16).astype(jnp.int32)
    return first + second


def levels(key, shape, cuts, smallest, top_value):
    def one(dim, blocks):
        heights = jax.random.uniform(jax.random.fold_in(jax.random.fold_in(key, 6), dim), (blocks,), jnp.float32, smallest / len(cuts), top_value / len(cuts))
        return jnp.repeat(jnp.exp(heights), shape[dim] // blocks).reshape((-1,) + (1,) * (len(shape) - dim - 1))

    level = one(*cuts[0])
    for cut in cuts[1:]:
        level = level * one(*cut)
    return level


def scatter_about(own_key, dims, width, limit, shards=(), held_as=jnp.bfloat16):
    drawn = jax.random.normal(own_key, dims, jnp.float32) * width
    if len(shards) > 0:
        drawn = levels(own_key, dims, shards, -0.22, 0.18) * drawn
    return jnp.clip(drawn, min=-limit, max=limit).astype(held_as)


def setup_inputs(seed: int = 0) -> dict:
    keys = jax.random.split(jax.random.key(seed), 12)
    return {
        "hidden": scatter_about(keys[0], (POINTS, HID), 1.0, 6.0, ((0, 32),), jnp.float32),
        "codes": draw_codes(jax.random.fold_in(keys[11], 71), 0),
        "offsets": scatter_about(keys[2], (POINTS, 3), 1.0, 6.0, ((0, 32),), jnp.float32),
        "shape_ids": draw_shape_ids(jax.random.fold_in(keys[11], 71), 0),
        "scale_index": draw_scale_index(jax.random.fold_in(keys[11], 71), 0),
        "direction": scatter_about(keys[5], (OUT, OUT), OUT ** -0.5, 0.25, ((0, 32),), jnp.float32),
        "gain": jnp.clip(0.5 + 1.5 * jax.random.uniform(keys[6], (OUT,), jnp.float32) ** levels(keys[6], (OUT,), ((0, 32),), -0.2, 0.2), 0.5, 2.0),
        "bias": scatter_about(keys[7], (OUT,), 0.5, 3.0, ((0, 32),), jnp.float32),
        "cotangent": scatter_about(keys[8], (POINTS, OUT), 1.0, 6.0, ((0, 32),), jnp.float32),
        "running_mean": scatter_about(keys[9], (CODE,), 0.5, 3.0, (), jnp.float32),
        "running_var": jnp.clip(jax.random.uniform(keys[10], (CODE,), jnp.float32, 0.5, 2.0), 0.5, 2.0),
    }


@jax.custom_vjp
def low(v):
    return lax.optimization_barrier(v.astype(jnp.bfloat16)).astype(jnp.float32)

@jax.custom_vjp
def low_back(v):
    return v

def low_keep(v):
    return (low(v), None)

def low_pass(kept, grad):
    return (grad,)

def back_keep(v):
    return (v, None)

def back_low(kept, grad):
    return (low(grad),)
low.defvjp(low_keep, low_pass)
low_back.defvjp(back_keep, back_low)

def jitter_of(scale_index):
    return jnp.where(scale_index == 0, 1.0, jnp.where(scale_index == 1, 0.5, 0.25)).astype(jnp.float32)

def reference(hidden, codes, offsets, shape_ids, scale_index, direction, gain, bias, cotangent, running_mean, running_var):
    xyz = offsets * jitter_of(scale_index)[:, None]

    def forward(hidden_in, codes_in, direction_in, gain_in, bias_in):
        norms = jnp.sqrt(lax.optimization_barrier(jnp.sum(direction_in * direction_in, axis=1)))
        weight = low(gain_in[:, None] * direction_in / norms[:, None])
        bias_low = low(bias_in)
        code_rows = jnp.take(codes_in, shape_ids, axis=0)
        inputs = low(jnp.concatenate([hidden_in, code_rows, xyz], axis=1))
        pre = jnp.dot(inputs, weight.T, precision=lax.Precision.HIGHEST) + bias_low[None, :]
        pre = low_back(pre)
        return jax.nn.silu(pre)
    output, pullback = jax.vjp(forward, hidden, codes, direction, gain, bias)
    grad_hidden, grad_codes, grad_direction, grad_gain, grad_bias = pullback(cotangent)
    code_rows = jnp.take(codes, shape_ids, axis=0)
    total = code_rows.shape[0]
    batch_mean = lax.optimization_barrier(jnp.mean(code_rows, axis=0))
    batch_square = lax.optimization_barrier(jnp.mean(code_rows * code_rows, axis=0))
    batch_var = (batch_square - batch_mean * batch_mean) * (total / (total - 1.0))
    new_mean = 0.9 * running_mean + 0.1 * batch_mean
    new_var = 0.9 * running_var + 0.1 * batch_var
    return (output, grad_hidden, grad_codes, grad_direction, grad_gain, grad_bias, new_mean, new_var)
```

```python
import functools

import jax
import jax.numpy as jnp
from jax import lax
from jax.experimental import pallas as pl
from jax.experimental.pallas import tpu as pltpu
from jax.sharding import PartitionSpec as P

AXES = ("dp", "inner")
LANES = 128
F32 = jnp.float32
BF16 = jnp.bfloat16
HIGHEST = lax.Precision.HIGHEST
VMEM = pltpu.VMEM
NT = (((1,), (1,)), ((), ()))
TN = (((0,), (0,)), ((), ()))


def dot(a, b, dims=(((1,), (0,)), ((), ())), precision=None):
    return lax.dot_general(a, b, dims, precision=precision, preferred_element_type=F32)


def vmem(n):
    return [pl.BlockSpec(memory_space=VMEM)] * n


def diagonal(n):
    return lax.broadcasted_iota(jnp.int32, (n, n), 0) == lax.broadcasted_iota(jnp.int32, (n, n), 1)


def to_column(row):
    n = row.shape[1]
    return jnp.sum(jnp.where(diagonal(n), row, 0.0), axis=1, keepdims=True)


def to_row(column):
    n = column.shape[0]
    return jnp.sum(jnp.where(diagonal(n), column, 0.0), axis=0, keepdims=True)


def prep_kernel(hid, direction_ref, gain_ref, bias_ref, piece_ref):
    d = direction_ref[...]
    rows, cols = d.shape
    half = cols // 2
    inverse = lax.rsqrt(jnp.sum(d * d, axis=1, keepdims=True))
    w = to_column(gain_ref[...]) * (d * inverse)
    lane = lax.broadcasted_iota(jnp.int32, (rows, half), 1)
    first = jnp.where(lane < hid, w[:, :half], w[:, half:])
    second = pltpu.roll(w, half - hid, 1)[:, half:]
    lane = lax.broadcasted_iota(jnp.int32, (rows, LANES), 1)
    last = jnp.where(lane == 0, to_column(bias_ref[...]), 0.0)
    piece_ref[:, :half] = first.astype(BF16)
    piece_ref[:, half : 2 * half] = second.astype(BF16)
    piece_ref[:, 2 * half :] = last.astype(BF16)


def main_kernel(hid, shapes, orders, split, *refs):
    n = 1 if orders is None else len(orders)
    pieces = refs[:n]
    hidden_ref, offsets_ref, ids_ref, scale_ref, cot_ref, codes_ref = refs[n : n + 6]
    out_ref, grad_hidden_ref, code_weights_ref, sums_ref = refs[n + 6 : n + 10]
    grad_refs = refs[n + 10 : -3]
    w_ref, acc_ref, turned_ref = refs[-3:]
    step = pl.program_id(0)
    tile, width = cot_ref.shape
    half = width // 2
    extra_lanes = w_ref.shape[1] - half
    me = lax.axis_index(AXES)

    @pl.when(step == 0)
    def _():
        codes = codes_ref[...].astype(BF16)
        pad = jnp.zeros((extra_lanes - 2 * shapes, codes.shape[1]), BF16)
        codes = jnp.concatenate([codes, codes, pad], axis=0)

        def place(piece, at):
            rows = piece.shape[0]
            code = piece[:, half:width]
            table = dot(code, codes, NT) + piece[:, width : width + 1].astype(F32)
            high = table.astype(BF16).astype(F32)
            lane = lax.broadcasted_iota(jnp.int32, (rows, extra_lanes), 1)
            table = jnp.where(lane < shapes, high, jnp.where(lane < 2 * shapes, table - high, 0.0))
            own = piece[:, half - LANES : half].astype(F32)
            if extra_lanes > LANES:
                own = jnp.concatenate([jnp.zeros((rows, extra_lanes - LANES), F32), own], axis=1)
            table = jnp.where(lane >= extra_lanes - (half - hid), own, table)
            w_ref[pl.ds(at, rows), :half] = piece[:, :half]
            w_ref[pl.ds(at, rows), half:] = table.astype(BF16)
            code_weights_ref[pl.ds(at, rows), :] = code

        if orders is None:
            place(pieces[0][...], 0)
        else:
            rows = pieces[0].shape[0] // len(orders[0])
            for ref, masks in zip(pieces, orders):
                for k, mask in enumerate(masks):
                    at = pl.multiple_of((me ^ mask) * rows, rows)
                    place(ref[k * rows : (k + 1) * rows, :], at)
        acc_ref[...] = jnp.zeros_like(acc_ref)

    lane = lax.broadcasted_iota(jnp.int32, (tile, half), 1)
    hidden = jnp.where(lane < hid, hidden_ref[...], 0.0)
    scale = scale_ref[...]
    jitter = jnp.where(scale == 0, 1.0, jnp.where(scale == 1, 0.5, 0.25))
    xyz = offsets_ref[...] * jitter
    row = lax.broadcasted_iota(jnp.int32, (8, tile), 0)
    last = jnp.zeros((8, tile), F32)
    for k in range(half - hid):
        last = jnp.where(row == 8 - (half - hid) + k, xyz[k : k + 1], last)
    row = lax.broadcasted_iota(jnp.int32, (extra_lanes - 8, tile), 0)
    ids = ids_ref[...]
    member = jnp.where((row == ids) | (row == ids + shapes), 1.0, 0.0)
    extra = jnp.concatenate([member, last], axis=0).T
    x = jnp.concatenate([hidden.astype(BF16), extra.astype(BF16)], axis=1)
    pre = dot(x, w_ref[...], NT)
    sigma = 0.5 * jnp.tanh(0.5 * pre) + 0.5
    out = pre * sigma
    out_ref[...] = out
    grad_pre = (cot_ref[...] * (sigma * (1.0 + (pre - out)))).astype(BF16)
    grad_hidden_ref[...] = dot(grad_pre, w_ref[:, :half])
    hidden = hidden.T
    x = jnp.concatenate([hidden[: half - 8], hidden[half - 8 :] + last, member[:shapes]], axis=0)
    acc_ref[...] += dot(x.astype(BF16), grad_pre)

    @pl.when(step == pl.num_programs(0) - 1)
    def _():
        sums_ref[...] = acc_ref[half:, :]
        for block in range(0, width, half):
            turned_ref[block : block + half, :] = acc_ref[:half, block : block + half].T
        if orders is None:
            grad_refs[0][...] = turned_ref[...].astype(BF16)
        else:
            rows = grad_refs[0].shape[0] // len(split[0])
            for ref, masks in zip(grad_refs, split):
                for k, mask in enumerate(masks):
                    at = pl.multiple_of((me ^ mask) * rows, rows)
                    ref[k * rows : (k + 1) * rows, :] = turned_ref[pl.ds(at, rows), :].astype(BF16)


def pairs(parts):
    while len(parts) > 1:
        parts = [a + b for a, b in zip(parts[::2], parts[1::2])]
    return parts[0]


def add_kernel(n, n_out, *refs):
    grads, sums, outs = refs[:n], refs[n : 2 * n], refs[2 * n :]
    total = pairs([ref[...].astype(F32) for ref in grads]).astype(BF16)
    rows = total.shape[0] // n_out
    for k in range(n_out):
        outs[k][...] = total[k * rows : (k + 1) * rows, :]
    outs[n_out][...] = pairs([ref[...] for ref in sums])


def final_kernel(hid, n, *refs):
    grads, sums = refs[:n], refs[n : 2 * n]
    direction_ref, gain_ref, codes_ref, code_weights_ref = refs[2 * n : 2 * n + 4]
    grad_codes_ref, grad_direction_ref, grad_gain_ref, grad_bias_ref, turned_ref = refs[-5:]
    me = lax.axis_index(AXES)
    d = direction_ref[...]
    rows, cols = d.shape
    half = cols // 2
    total = pairs([ref[...] for ref in sums])
    shapes = total.shape[0]
    turned_ref[...] = total.T
    grad_codes_ref[...] = dot(total, code_weights_ref[...].astype(F32), precision=HIGHEST)
    own = turned_ref[pl.ds(me * rows, rows), :]
    grad_bias_ref[...] = to_row(jnp.sum(own, axis=1, keepdims=True))
    code = dot(own, codes_ref[...].astype(BF16).astype(F32), precision=HIGHEST)
    other = pairs([ref[...].astype(F32) for ref in grads])
    packed = jnp.concatenate([other, code], axis=1)
    lane = lax.broadcasted_iota(jnp.int32, (rows, cols), 1)
    grad_weight = jnp.where(
        lane < hid,
        packed,
        jnp.where(lane < hid + half, pltpu.roll(packed, cols - (half - hid), 1), pltpu.roll(packed, half, 1)),
    )
    inverse = lax.rsqrt(jnp.sum(d * d, axis=1, keepdims=True))
    unit = d * inverse
    grad_gain = jnp.sum(grad_weight * unit, axis=1, keepdims=True)
    grad_gain_ref[...] = to_row(grad_gain)
    grad_direction_ref[...] = (to_column(gain_ref[...]) * inverse) * (grad_weight - grad_gain * unit)


def rounds_of(devices):
    bits = devices.bit_length() - 1
    groups = []
    while bits > 0:
        take = min(2, bits)
        groups.append([1 << (bits - 1 - k) for k in range(take)][::-1])
        bits -= take
    return groups


def masks_of(group):
    masks = [0]
    for bit in group:
        masks = masks + [m ^ bit for m in masks]
    return masks


def swap(x, mask, devices):
    return lax.ppermute(x, AXES, [(i, i ^ mask) for i in range(devices)])


def per_device(
    hidden,
    codes,
    offsets,
    shape_ids,
    scale_index,
    direction,
    gain,
    bias,
    cotangent,
    running_mean,
    running_var,
):
    points, hid = hidden.shape
    shapes = codes.shape[0]
    rows, cols = direction.shape
    width = cotangent.shape[1]
    half = cols // 2
    devices = lax.axis_size("dp") * lax.axis_size("inner")
    tuned = rows % 16 == 0
    gain_row = gain.reshape(1, rows)

    piece = pl.pallas_call(
        functools.partial(prep_kernel, hid),
        out_shape=jax.ShapeDtypeStruct((rows, cols + LANES), BF16),
        in_specs=vmem(3),
        out_specs=pl.BlockSpec(memory_space=VMEM),
        name="prep",
    )(direction, gain_row, bias.reshape(1, rows))

    groups = rounds_of(devices)
    if tuned:
        held, order = piece, [0]
        for group in groups[:-1]:
            masks = masks_of(group)
            held = jnp.concatenate([held] + [swap(held, m, devices) for m in masks[1:]], axis=0)
            order = [m ^ r for m in masks for r in order]
        masks = masks_of(groups[-1])
        pieces = [held] + [swap(held, m, devices) for m in masks[1:]]
        orders = split = [[m ^ r for r in order] for m in masks]
    else:
        pieces, orders = [lax.all_gather(piece, AXES, axis=0, tiled=True)], None
        split = [[0]]

    extra_lanes = -(-(2 * shapes + 8) // LANES) * LANES
    tile = min(256, points)
    results = pl.pallas_call(
        functools.partial(main_kernel, hid, shapes, orders, split),
        grid=(points // tile,),
        out_shape=[
            jax.ShapeDtypeStruct((points, width), F32),
            jax.ShapeDtypeStruct((points, hid), F32),
            jax.ShapeDtypeStruct((width, half), BF16),
            jax.ShapeDtypeStruct((shapes, width), F32),
        ]
        + [jax.ShapeDtypeStruct((width // len(split), half), BF16)] * len(split),
        in_specs=vmem(len(pieces))
        + [
            pl.BlockSpec((tile, half), lambda i: (i, 0)),
            pl.BlockSpec((half - hid, tile), lambda i: (0, i)),
            pl.BlockSpec((1, tile), lambda i: (0, i)),
            pl.BlockSpec((1, tile), lambda i: (0, i)),
            pl.BlockSpec((tile, width), lambda i: (i, 0)),
        ]
        + vmem(1),
        out_specs=[
            pl.BlockSpec((tile, width), lambda i: (i, 0)),
            pl.BlockSpec((tile, half), lambda i: (i, 0)),
        ]
        + vmem(len(split) + 2),
        scratch_shapes=[
            VMEM((width, half + extra_lanes), BF16),
            VMEM((half + shapes, width), F32),
            VMEM((width, half), F32),
        ],
        compiler_params=pltpu.CompilerParams(
            dimension_semantics=("arbitrary",), vmem_limit_bytes=32 * 1024 * 1024
        ),
        name="layer",
    )(
        *pieces,
        hidden,
        offsets.T,
        shape_ids.reshape(1, points),
        scale_index.reshape(1, points),
        cotangent,
        codes,
    )
    output, grad_hidden, code_weights, sums = results[:4]
    grads = list(results[4:])

    if tuned:
        for r, group in enumerate(groups[::-1]):
            masks = masks_of(group)
            grads = [grads[0]] + [swap(g, m, devices) for g, m in zip(grads[1:], masks[1:])]
            sums = [sums] + [swap(sums, m, devices) for m in masks[1:]]
            if r == len(groups) - 1:
                break
            n, n_out = len(masks), len(masks_of(groups[-2 - r]))
            shape = (grads[0].shape[0] // n_out, half)
            added = pl.pallas_call(
                functools.partial(add_kernel, n, n_out),
                out_shape=[jax.ShapeDtypeStruct(shape, BF16)] * n_out
                + [jax.ShapeDtypeStruct((shapes, width), F32)],
                in_specs=vmem(2 * n),
                out_specs=vmem(n_out + 1),
                name="add",
            )(*grads, *sums)
            grads, sums = list(added[:-1]), added[-1]
    else:
        grads = [lax.psum_scatter(grads[0].astype(F32), AXES, scatter_dimension=0, tiled=True)]
        sums = [lax.psum(sums, AXES)]

    n = len(grads)
    grad_codes, grad_direction, grad_gain, grad_bias = pl.pallas_call(
        functools.partial(final_kernel, hid, n),
        out_shape=[
            jax.ShapeDtypeStruct((shapes, half), F32),
            jax.ShapeDtypeStruct((rows, cols), F32),
            jax.ShapeDtypeStruct((1, rows), F32),
            jax.ShapeDtypeStruct((1, rows), F32),
        ],
        in_specs=vmem(2 * n + 4),
        out_specs=vmem(4),
        scratch_shapes=[VMEM((width, shapes), F32)],
        name="last",
    )(*grads, *sums, direction, gain_row, codes, code_weights)

    total = float(points * devices)
    batch_mean = jnp.mean(codes, axis=0)
    batch_square = jnp.mean(codes * codes, axis=0)
    batch_var = (batch_square - batch_mean * batch_mean) * (total / (total - 1.0))
    new_mean = 0.9 * running_mean + 0.1 * batch_mean
    new_var = 0.9 * running_var + 0.1 * batch_var
    return (
        output,
        grad_hidden,
        grad_codes,
        grad_direction,
        grad_gain.reshape(rows),
        grad_bias.reshape(rows),
        new_mean,
        new_var,
    )


def solution(mesh):
    return jax.shard_map(
        per_device,
        mesh=mesh,
        in_specs=(
            P(("dp", "inner"), None),
            P(),
            P(("dp", "inner"), None),
            P(("dp", "inner")),
            P(("dp", "inner")),
            P(("dp", "inner"), None),
            P(("dp", "inner")),
            P(("dp", "inner")),
            P(("dp", "inner"), None),
            P(),
            P(),
        ),
        out_specs=(
            P(("dp", "inner"), None),
            P(("dp", "inner"), None),
            P(),
            P(("dp", "inner"), None),
            P(("dp", "inner")),
            P(("dp", "inner")),
            P(),
            P(),
        ),
        check_vma=False,
    )
```

```python
import functools

import jax
import jax.numpy as jnp
from jax import lax
from jax.experimental import pallas as pl
from jax.experimental.pallas import tpu as pltpu
from jax.sharding import PartitionSpec as P

AXES = ("dp", "inner")
LANES = 128
F32 = jnp.float32
BF16 = jnp.bfloat16
HIGHEST = lax.Precision.HIGHEST
VMEM = pltpu.VMEM
NT = (((1,), (1,)), ((), ()))
TN = (((0,), (0,)), ((), ()))


def dot(a, b, dims=(((1,), (0,)), ((), ())), precision=None):
    return lax.dot_general(a, b, dims, precision=precision, preferred_element_type=F32)


def vmem(n):
    return [pl.BlockSpec(memory_space=VMEM)] * n


def diagonal(n):
    return lax.broadcasted_iota(jnp.int32, (n, n), 0) == lax.broadcasted_iota(jnp.int32, (n, n), 1)


def to_column(row):
    n = row.shape[1]
    return jnp.sum(jnp.where(diagonal(n), row, 0.0), axis=1, keepdims=True)


def to_row(column):
    n = column.shape[0]
    return jnp.sum(jnp.where(diagonal(n), column, 0.0), axis=0, keepdims=True)


def prep_kernel(hid, direction_ref, gain_ref, bias_ref, piece_ref):
    d = direction_ref[...]
    rows, cols = d.shape
    half = cols // 2
    inverse = lax.rsqrt(jnp.sum(d * d, axis=1, keepdims=True))
    w = to_column(gain_ref[...]) * (d * inverse)
    lane = lax.broadcasted_iota(jnp.int32, (rows, half), 1)
    first = jnp.where(lane < hid, w[:, :half], w[:, half:])
    second = pltpu.roll(w, half - hid, 1)[:, half:]
    lane = lax.broadcasted_iota(jnp.int32, (rows, LANES), 1)
    last = jnp.where(lane == 0, to_column(bias_ref[...]), 0.0)
    piece = jnp.concatenate([first, second, last], axis=1).astype(BF16)
    for at in range(0, piece_ref.shape[0], rows):
        piece_ref[at : at + rows, :] = piece


def main_kernel(
    hid,
    shapes,
    pieces_ref,
    hidden_ref,
    offsets_ref,
    ids_ref,
    scale_ref,
    cot_ref,
    codes_ref,
    out_ref,
    grad_hidden_ref,
    grad_ref,
    w_ref,
    acc_ref,
):
    step = pl.program_id(0)
    tile, width = cot_ref.shape
    half = width // 2
    extra_lanes = w_ref.shape[1] - half

    @pl.when(step == 0)
    def _():
        codes = codes_ref[...].astype(BF16)
        pad = jnp.zeros((extra_lanes - 2 * shapes, codes.shape[1]), BF16)
        codes = jnp.concatenate([codes, codes, pad], axis=0)
        table = dot(pieces_ref[:, half:width], codes, NT)
        table = table + pieces_ref[:, width : width + 1].astype(F32)
        high = table.astype(BF16).astype(F32)
        lane = lax.broadcasted_iota(jnp.int32, (width, extra_lanes), 1)
        table = jnp.where(lane < shapes, high, jnp.where(lane < 2 * shapes, table - high, 0.0))
        own = pieces_ref[:, half - LANES : half].astype(F32)
        if extra_lanes > LANES:
            own = jnp.concatenate([jnp.zeros((width, extra_lanes - LANES), F32), own], axis=1)
        table = jnp.where(lane >= extra_lanes - (half - hid), own, table)
        w_ref[:, :half] = pieces_ref[:, :half]
        w_ref[:, half:] = table.astype(BF16)
        acc_ref[...] = jnp.zeros_like(acc_ref)

    lane = lax.broadcasted_iota(jnp.int32, (tile, half), 1)
    hidden = jnp.where(lane < hid, hidden_ref[...], 0.0)
    scale = scale_ref[...]
    jitter = jnp.where(scale == 0, 1.0, jnp.where(scale == 1, 0.5, 0.25))
    xyz = offsets_ref[...] * jitter
    row = lax.broadcasted_iota(jnp.int32, (8, tile), 0)
    last = jnp.zeros((8, tile), F32)
    for k in range(half - hid):
        last = jnp.where(row == 8 - (half - hid) + k, xyz[k : k + 1], last)
    row = lax.broadcasted_iota(jnp.int32, (extra_lanes - 8, tile), 0)
    ids = ids_ref[...]
    member = jnp.where((row == ids) | (row == ids + shapes), 1.0, 0.0)
    extra = jnp.concatenate([member, last], axis=0).T
    x = jnp.concatenate([hidden.astype(BF16), extra.astype(BF16)], axis=1)
    pre = dot(x, w_ref[...], NT)
    sigma = 0.5 * jnp.tanh(0.5 * pre) + 0.5
    out = pre * sigma
    out_ref[...] = out
    grad_pre = (cot_ref[...] * (sigma * (1.0 + (pre - out)))).astype(BF16)
    grad_hidden_ref[...] = dot(grad_pre, w_ref[:, :half])
    hidden = hidden.T
    x = jnp.concatenate([hidden[: half - 8], hidden[half - 8 :] + last, member[:shapes]], axis=0)
    acc_ref[...] += dot(x.astype(BF16), grad_pre)

    @pl.when(step == pl.num_programs(0) - 1)
    def _():
        sums = acc_ref[half:, :]
        high = sums.astype(BF16).astype(F32)
        pad = jnp.zeros((grad_ref.shape[1] - half - 2 * shapes, width), F32)
        sums = jnp.concatenate([high, sums - high, pad], axis=0)
        for at in range(0, width, half):
            grad_ref[at : at + half, :half] = acc_ref[:half, at : at + half].T.astype(BF16)
            grad_ref[at : at + half, half:] = sums[:, at : at + half].T.astype(BF16)


def sum_kernel(
    hid,
    shapes,
    grad_ref,
    direction_ref,
    gain_ref,
    codes_ref,
    sums_ref,
    grad_direction_ref,
    grad_gain_ref,
    grad_bias_ref,
):
    d = direction_ref[...]
    rows, cols = d.shape
    half = cols // 2
    n = grad_ref.shape[0]
    take = lax.broadcasted_iota(jnp.int32, (rows, n), 1) % rows
    take = jnp.where(take == lax.broadcasted_iota(jnp.int32, (rows, n), 0), 1.0, 0.0).astype(BF16)
    total = dot(take, grad_ref[...])
    sums = total[:, half:]
    sums = sums + pltpu.roll(sums, sums.shape[1] - shapes, 1)
    lane = lax.broadcasted_iota(jnp.int32, sums.shape, 1)
    sums = jnp.where(lane < shapes, sums, 0.0)
    high = sums.astype(BF16).astype(F32)
    sent = jnp.where(lane < shapes, high, pltpu.roll(sums - high, shapes, 1)).astype(BF16)
    for at in range(0, n, rows):
        sums_ref[at : at + rows, :] = sent
    grad_bias_ref[...] = to_row(jnp.sum(sums, axis=1, keepdims=True))
    codes = codes_ref[...].astype(BF16).astype(F32)
    pad = jnp.zeros((sums.shape[1] - shapes, codes.shape[1]), F32)
    code = dot(sums, jnp.concatenate([codes, pad], axis=0), precision=HIGHEST)
    packed = jnp.concatenate([total[:, :half], code], axis=1)
    lane = lax.broadcasted_iota(jnp.int32, (rows, cols), 1)
    grad_weight = jnp.where(
        lane < hid,
        packed,
        jnp.where(lane < hid + half, pltpu.roll(packed, cols - (half - hid), 1), pltpu.roll(packed, half, 1)),
    )
    inverse = lax.rsqrt(jnp.sum(d * d, axis=1, keepdims=True))
    unit = d * inverse
    grad_gain = jnp.sum(grad_weight * unit, axis=1, keepdims=True)
    grad_gain_ref[...] = to_row(grad_gain)
    grad_direction_ref[...] = (to_column(gain_ref[...]) * inverse) * (grad_weight - grad_gain * unit)


def codes_kernel(shapes, sums_ref, pieces_ref, grad_codes_ref):
    half = grad_codes_ref.shape[1]
    terms = dot(sums_ref[...], pieces_ref[:, half : 2 * half], TN)
    grad_codes_ref[...] = terms[:shapes] + terms[shapes : 2 * shapes]


def per_device(
    hidden,
    codes,
    offsets,
    shape_ids,
    scale_index,
    direction,
    gain,
    bias,
    cotangent,
    running_mean,
    running_var,
):
    points, hid = hidden.shape
    shapes = codes.shape[0]
    rows, cols = direction.shape
    width = cotangent.shape[1]
    half = cols // 2
    devices = lax.axis_size("dp") * lax.axis_size("inner")
    tuned = rows % 16 == 0
    gain_row = gain.reshape(1, rows)

    pieces = pl.pallas_call(
        functools.partial(prep_kernel, hid),
        out_shape=jax.ShapeDtypeStruct((devices * rows, cols + LANES), BF16),
        in_specs=vmem(3),
        out_specs=pl.BlockSpec(memory_space=VMEM),
        name="prep",
    )(direction, gain_row, bias.reshape(1, rows))
    pieces = lax.all_to_all(pieces, AXES, 0, 0, tiled=True)

    extra_lanes = -(-(2 * shapes + 8) // LANES) * LANES
    tile = min(256, points)
    output, grad_hidden, grad = pl.pallas_call(
        functools.partial(main_kernel, hid, shapes),
        grid=(points // tile,),
        out_shape=[
            jax.ShapeDtypeStruct((points, width), F32),
            jax.ShapeDtypeStruct((points, hid), F32),
            jax.ShapeDtypeStruct((width, half + extra_lanes), BF16),
        ],
        in_specs=vmem(1)
        + [
            pl.BlockSpec((tile, half), lambda i: (i, 0)),
            pl.BlockSpec((half - hid, tile), lambda i: (0, i)),
            pl.BlockSpec((1, tile), lambda i: (0, i)),
            pl.BlockSpec((1, tile), lambda i: (0, i)),
            pl.BlockSpec((tile, width), lambda i: (i, 0)),
        ]
        + vmem(1),
        out_specs=[
            pl.BlockSpec((tile, width), lambda i: (i, 0)),
            pl.BlockSpec((tile, half), lambda i: (i, 0)),
        ]
        + vmem(1),
        scratch_shapes=[
            VMEM((width, half + extra_lanes), BF16),
            VMEM((half + shapes, width), F32),
        ],
        compiler_params=pltpu.CompilerParams(
            dimension_semantics=("arbitrary",), vmem_limit_bytes=56 * 1024 * 1024
        ),
        name="layer",
    )(
        pieces,
        hidden,
        offsets.T,
        shape_ids.reshape(1, points),
        scale_index.reshape(1, points),
        cotangent,
        codes,
    )

    grad = lax.all_to_all(grad, AXES, 0, 0, tiled=True)
    sums, grad_direction, grad_gain, grad_bias = pl.pallas_call(
        functools.partial(sum_kernel, hid, shapes),
        out_shape=[
            jax.ShapeDtypeStruct((devices * rows, extra_lanes), BF16),
            jax.ShapeDtypeStruct((rows, cols), F32),
            jax.ShapeDtypeStruct((1, rows), F32),
            jax.ShapeDtypeStruct((1, rows), F32),
        ],
        in_specs=vmem(4),
        out_specs=vmem(4),
        name="sum",
    )(grad, direction, gain_row, codes)
    sums = lax.all_to_all(sums, AXES, 0, 0, tiled=True)
    grad_codes = pl.pallas_call(
        functools.partial(codes_kernel, shapes),
        out_shape=jax.ShapeDtypeStruct((shapes, half), F32),
        in_specs=vmem(2),
        out_specs=pl.BlockSpec(memory_space=VMEM),
        name="codes",
    )(sums, pieces)

    total = float(points * devices)
    batch_mean = jnp.mean(codes, axis=0)
    batch_square = jnp.mean(codes * codes, axis=0)
    batch_var = (batch_square - batch_mean * batch_mean) * (total / (total - 1.0))
    new_mean = 0.9 * running_mean + 0.1 * batch_mean
    new_var = 0.9 * running_var + 0.1 * batch_var
    return (
        output,
        grad_hidden,
        grad_codes,
        grad_direction,
        grad_gain.reshape(rows),
        grad_bias.reshape(rows),
        new_mean,
        new_var,
    )


def solution(mesh):
    return jax.shard_map(
        per_device,
        mesh=mesh,
        in_specs=(
            P(("dp", "inner"), None),
            P(),
            P(("dp", "inner"), None),
            P(("dp", "inner")),
            P(("dp", "inner")),
            P(("dp", "inner"), None),
            P(("dp", "inner")),
            P(("dp", "inner")),
            P(("dp", "inner"), None),
            P(),
            P(),
        ),
        out_specs=(
            P(("dp", "inner"), None),
            P(("dp", "inner"), None),
            P(),
            P(("dp", "inner"), None),
            P(("dp", "inner")),
            P(("dp", "inner")),
            P(),
            P(),
        ),
        check_vma=False,
    )
```

```python
import functools

import jax
import jax.numpy as jnp
from jax import lax
from jax.experimental import pallas as pl
from jax.experimental.pallas import tpu as pltpu
from jax.sharding import PartitionSpec as P

AXES = ("dp", "inner")
LANES = 128
F32 = jnp.float32
BF16 = jnp.bfloat16
VMEM = pltpu.VMEM
NT = (((1,), (1,)), ((), ()))


def dot(a, b, dims=(((1,), (0,)), ((), ()))):
    return lax.dot_general(a, b, dims, preferred_element_type=F32)


def vmem(n):
    return [pl.BlockSpec(memory_space=VMEM)] * n


def diagonal(n):
    return lax.broadcasted_iota(jnp.int32, (n, n), 0) == lax.broadcasted_iota(jnp.int32, (n, n), 1)


def to_column(row):
    n = row.shape[1]
    return jnp.sum(jnp.where(diagonal(n), row, 0.0), axis=1, keepdims=True)


def to_row(column):
    n = column.shape[0]
    return jnp.sum(jnp.where(diagonal(n), column, 0.0), axis=0, keepdims=True)


def stacked_codes(codes_ref, count):
    codes = codes_ref[...].astype(BF16)
    parts = [codes, codes]
    if count > 2 * codes.shape[0]:
        parts.append(jnp.zeros((count - 2 * codes.shape[0], codes.shape[1]), BF16))
    return jnp.concatenate(parts, axis=0)


def split(x):
    high = x.astype(BF16).astype(F32)
    return high, x - high


def prep_kernel(hid, direction_ref, gain_ref, bias_ref, codes_ref, piece_ref):
    d = direction_ref[...]
    shapes = codes_ref.shape[0]
    rows, cols = d.shape
    half = cols // 2
    extra_lanes = piece_ref.shape[2] - cols
    inverse = lax.rsqrt(jnp.sum(d * d, axis=1, keepdims=True))
    w = to_column(gain_ref[...]) * (d * inverse)
    lane = lax.broadcasted_iota(jnp.int32, (rows, half), 1)
    first = jnp.where(lane < hid, w[:, :half], w[:, half:])
    code = pltpu.roll(w, half - hid, 1)[:, half:].astype(BF16)
    bias = to_column(bias_ref[...]).astype(BF16).astype(F32)
    high, low = split(dot(code, stacked_codes(codes_ref, extra_lanes), NT) + bias)
    own = first[:, half - LANES :]
    if extra_lanes > LANES:
        own = jnp.concatenate([jnp.zeros((rows, extra_lanes - LANES), F32), own], axis=1)
    lane = lax.broadcasted_iota(jnp.int32, (rows, extra_lanes), 1)
    table = jnp.where(lane < shapes, high, jnp.where(lane < 2 * shapes, low, 0.0))
    table = jnp.where(lane >= extra_lanes - (half - hid), own, table)
    for k in range(piece_ref.shape[0]):
        piece_ref[k, :, :half] = first.astype(BF16)
        piece_ref[k, :, half : half + extra_lanes] = table.astype(BF16)
        piece_ref[k, :, half + extra_lanes :] = code


def spread_kernel(piece_ref, weight_ref, code_ref):
    lanes = weight_ref.shape[3]
    for k in range(weight_ref.shape[0]):
        weight_ref[k] = piece_ref[:, :, :lanes]
        code_ref[k] = piece_ref[:, :, lanes:]


def natural(ref, store):
    local, outer, rows = ref.shape[:3]
    for k in range(outer):
        for j in range(local):
            store((k * local + j) * rows, rows, ref[j, k])


def main_kernel(
    hid,
    shapes,
    weight_ref,
    hidden_ref,
    offsets_ref,
    ids_ref,
    scale_ref,
    cot_ref,
    out_ref,
    grad_hidden_ref,
    grad_ref,
    w_ref,
    acc_ref,
    turned_ref,
):
    step = pl.program_id(0)
    tile, width = cot_ref.shape
    half = width // 2
    extra_lanes = w_ref.shape[1] - half

    @pl.when(step == 0)
    def _():
        def store(at, rows, value):
            w_ref[at : at + rows, :] = value

        natural(weight_ref, store)
        acc_ref[...] = jnp.zeros_like(acc_ref)

    lane = lax.broadcasted_iota(jnp.int32, (tile, half), 1)
    hidden = jnp.where(lane < hid, hidden_ref[...], 0.0)
    scale = scale_ref[...]
    jitter = jnp.where(scale == 0, 1.0, jnp.where(scale == 1, 0.5, 0.25))
    xyz = offsets_ref[...] * jitter
    row = lax.broadcasted_iota(jnp.int32, (8, tile), 0)
    last = jnp.zeros((8, tile), F32)
    for k in range(half - hid):
        last = jnp.where(row == 8 - (half - hid) + k, xyz[k : k + 1], last)
    row = lax.broadcasted_iota(jnp.int32, (extra_lanes - 8, tile), 0)
    ids = ids_ref[...]
    member = jnp.where((row == ids) | (row == ids + shapes), 1.0, 0.0)
    extra = jnp.concatenate([member, last], axis=0).T
    x = jnp.concatenate([hidden.astype(BF16), extra.astype(BF16)], axis=1)
    pre = dot(x, w_ref[...], NT)
    sigma = 0.5 * jnp.tanh(0.5 * pre) + 0.5
    out = pre * sigma
    out_ref[...] = out
    grad_pre = (cot_ref[...] * (sigma * (1.0 + (pre - out)))).astype(BF16)
    grad_hidden_ref[...] = dot(grad_pre, w_ref[:, :half])
    hidden = hidden.T
    x = jnp.concatenate([hidden[: half - 8], hidden[half - 8 :] + last, member[:shapes]], axis=0)
    acc_ref[...] += dot(x.astype(BF16), grad_pre)

    @pl.when(step == pl.num_programs(0) - 1)
    def _():
        sums = jnp.concatenate(split(acc_ref[half:, :]), axis=0).astype(BF16)
        for at in range(0, width, half):
            turned_ref[at : at + half, :] = acc_ref[:half, at : at + half].T
        local, outer, rows = weight_ref.shape[:3]
        for j in range(local):
            grad_ref[j, : 2 * shapes, :] = sums[:, :half]
            grad_ref[j, 2 * shapes : 4 * shapes, :] = sums[:, half:]
            for k in range(outer):
                at = (k * local + j) * rows
                to = 4 * shapes + k * rows
                grad_ref[j, to : to + rows, :] = turned_ref[at : at + rows, :].astype(BF16)


def sum_of(ref):
    total = ref[0].astype(F32)
    for k in range(1, ref.shape[0]):
        total = total + ref[k].astype(F32)
    return total


def shape_sums(total, shapes):
    left = total[:shapes] + total[shapes : 2 * shapes]
    right = total[2 * shapes : 3 * shapes] + total[3 * shapes : 4 * shapes]
    return left, right


def add_kernel(shapes, grad_ref, out_ref):
    total = sum_of(grad_ref)
    left, right = shape_sums(total, shapes)
    sums = jnp.concatenate(split(left) + split(right), axis=0).astype(BF16)
    outer = out_ref.shape[0]
    rows = out_ref.shape[1] - 4 * shapes
    for k in range(outer):
        at = 4 * shapes + k * rows
        out_ref[k, : 4 * shapes, :] = sums
        out_ref[k, 4 * shapes :, :] = total[at : at + rows].astype(BF16)


def last_kernel(
    hid,
    shapes,
    grad_ref,
    direction_ref,
    gain_ref,
    codes_ref,
    code_weight_ref,
    grad_codes_ref,
    grad_direction_ref,
    grad_gain_ref,
    grad_bias_ref,
    code_scratch,
):
    d = direction_ref[...]
    rows, cols = d.shape
    half = cols // 2
    me = lax.axis_index(AXES)

    def store(at, rows, value):
        code_scratch[at : at + rows, :] = value

    natural(code_weight_ref, store)
    total = sum_of(grad_ref)
    sums = jnp.concatenate(shape_sums(total, shapes), axis=1)
    sums = jnp.concatenate(split(sums), axis=0).astype(BF16)
    terms = dot(sums, code_scratch[...])
    grad_codes_ref[...] = terms[:shapes] + terms[shapes:]
    width = sums.shape[1]
    mine = lax.broadcasted_iota(jnp.int32, (rows, width), 0) + me * rows
    mine = jnp.where(mine == lax.broadcasted_iota(jnp.int32, (rows, width), 1), 1.0, 0.0).astype(BF16)
    own = dot(mine, sums, NT)
    grad_bias_ref[...] = to_row(jnp.sum(own, axis=1, keepdims=True))
    code = dot(own.astype(BF16), stacked_codes(codes_ref, 2 * shapes))
    packed = jnp.concatenate([total[4 * shapes :], code], axis=1)
    lane = lax.broadcasted_iota(jnp.int32, (rows, cols), 1)
    grad_weight = jnp.where(
        lane < hid,
        packed,
        jnp.where(lane < hid + half, pltpu.roll(packed, cols - (half - hid), 1), pltpu.roll(packed, half, 1)),
    )
    inverse = lax.rsqrt(jnp.sum(d * d, axis=1, keepdims=True))
    unit = d * inverse
    grad_gain = jnp.sum(grad_weight * unit, axis=1, keepdims=True)
    grad_gain_ref[...] = to_row(grad_gain)
    grad_direction_ref[...] = (to_column(gain_ref[...]) * inverse) * (grad_weight - grad_gain * unit)


def exchange(x, groups):
    return lax.all_to_all(x, AXES, 0, 0, axis_index_groups=groups, tiled=True)


def per_device(
    hidden,
    codes,
    offsets,
    shape_ids,
    scale_index,
    direction,
    gain,
    bias,
    cotangent,
    running_mean,
    running_var,
):
    points, hid = hidden.shape
    shapes = codes.shape[0]
    rows, cols = direction.shape
    width = cotangent.shape[1]
    half = cols // 2
    devices = lax.axis_size("dp") * lax.axis_size("inner")
    tuned = rows % 16 == 0
    local = min(8, devices)
    outer = devices // local
    near = [[k * local + j for j in range(local)] for k in range(outer)]
    far = [[k * local + j for k in range(outer)] for j in range(local)]
    extra_lanes = -(-(2 * shapes + 8) // LANES) * LANES
    lanes = half + extra_lanes
    gain_row = gain.reshape(1, rows)

    pieces = pl.pallas_call(
        functools.partial(prep_kernel, hid),
        out_shape=jax.ShapeDtypeStruct((outer, rows, lanes + half), BF16),
        in_specs=vmem(4),
        out_specs=pl.BlockSpec(memory_space=VMEM),
        name="prep",
    )(direction, gain_row, bias.reshape(1, rows), codes)
    pieces = exchange(pieces, far)
    weight, code_weight = pl.pallas_call(
        spread_kernel,
        out_shape=[
            jax.ShapeDtypeStruct((local, outer, rows, lanes), BF16),
            jax.ShapeDtypeStruct((local, outer, rows, half), BF16),
        ],
        in_specs=vmem(1),
        out_specs=vmem(2),
        name="spread",
    )(pieces)
    weight = exchange(weight, near)
    code_weight = exchange(code_weight, near)

    tile = min(256, points)
    output, grad_hidden, grad = pl.pallas_call(
        functools.partial(main_kernel, hid, shapes),
        grid=(points // tile,),
        out_shape=[
            jax.ShapeDtypeStruct((points, width), F32),
            jax.ShapeDtypeStruct((points, hid), F32),
            jax.ShapeDtypeStruct((local, 4 * shapes + outer * rows, half), BF16),
        ],
        in_specs=vmem(1)
        + [
            pl.BlockSpec((tile, half), lambda i: (i, 0)),
            pl.BlockSpec((half - hid, tile), lambda i: (0, i)),
            pl.BlockSpec((1, tile), lambda i: (0, i)),
            pl.BlockSpec((1, tile), lambda i: (0, i)),
            pl.BlockSpec((tile, width), lambda i: (i, 0)),
        ],
        out_specs=[
            pl.BlockSpec((tile, width), lambda i: (i, 0)),
            pl.BlockSpec((tile, half), lambda i: (i, 0)),
        ]
        + vmem(1),
        scratch_shapes=[
            VMEM((width, lanes), BF16),
            VMEM((half + shapes, width), F32),
            VMEM((width, half), F32),
        ],
        compiler_params=pltpu.CompilerParams(
            dimension_semantics=("arbitrary",), vmem_limit_bytes=56 * 1024 * 1024
        ),
        cost_estimate=pl.CostEstimate(
            flops=6 * points * width * cols,
            bytes_accessed=8 * points * (width + half),
            transcendentals=points * width,
        ),
        name="layer",
    )(
        weight,
        hidden,
        offsets.T,
        shape_ids.reshape(1, points),
        scale_index.reshape(1, points),
        cotangent,
    )

    grad = exchange(grad, near)
    grad = pl.pallas_call(
        functools.partial(add_kernel, shapes),
        out_shape=jax.ShapeDtypeStruct((outer, 4 * shapes + rows, half), BF16),
        in_specs=vmem(1),
        out_specs=pl.BlockSpec(memory_space=VMEM),
        name="add",
    )(grad)
    grad = exchange(grad, far)
    grad_codes, grad_direction, grad_gain, grad_bias = pl.pallas_call(
        functools.partial(last_kernel, hid, shapes),
        out_shape=[
            jax.ShapeDtypeStruct((shapes, half), F32),
            jax.ShapeDtypeStruct((rows, cols), F32),
            jax.ShapeDtypeStruct((1, rows), F32),
            jax.ShapeDtypeStruct((1, rows), F32),
        ],
        in_specs=vmem(5),
        out_specs=vmem(4),
        scratch_shapes=[VMEM((width, half), BF16)],
        name="last",
    )(grad, direction, gain_row, codes, code_weight)

    total = float(points * devices)
    batch_mean = jnp.mean(codes, axis=0)
    batch_square = jnp.mean(codes * codes, axis=0)
    batch_var = (batch_square - batch_mean * batch_mean) * (total / (total - 1.0))
    new_mean = 0.9 * running_mean + 0.1 * batch_mean
    new_var = 0.9 * running_var + 0.1 * batch_var
    return (
        output,
        grad_hidden,
        grad_codes,
        grad_direction,
        grad_gain.reshape(rows),
        grad_bias.reshape(rows),
        new_mean,
        new_var,
    )


def solution(mesh):
    return jax.shard_map(
        per_device,
        mesh=mesh,
        in_specs=(
            P(("dp", "inner"), None),
            P(),
            P(("dp", "inner"), None),
            P(("dp", "inner")),
            P(("dp", "inner")),
            P(("dp", "inner"), None),
            P(("dp", "inner")),
            P(("dp", "inner")),
            P(("dp", "inner"), None),
            P(),
            P(),
        ),
        out_specs=(
            P(("dp", "inner"), None),
            P(("dp", "inner"), None),
            P(),
            P(("dp", "inner"), None),
            P(("dp", "inner")),
            P(("dp", "inner")),
            P(),
            P(),
        ),
        check_vma=False,
    )
```

```python
import functools

import jax
import jax.numpy as jnp
from jax import lax
from jax.experimental import pallas as pl
from jax.experimental.pallas import tpu as pltpu
from jax.sharding import PartitionSpec as P

AXES = ("dp", "inner")
LANES = 128
MIB = 1024 * 1024
F32 = jnp.float32
BF16 = jnp.bfloat16
VMEM = pltpu.VMEM
NT = (((1,), (1,)), ((), ()))


def dot(a, b, dims=(((1,), (0,)), ((), ()))):
    return lax.dot_general(a, b, dims, preferred_element_type=F32)


def vmem(n):
    return [pl.BlockSpec(memory_space=VMEM)] * n


def small_kernel(name, body, out_shape, *args, scratch=()):
    many = isinstance(out_shape, list)
    return pl.pallas_call(
        body,
        out_shape=out_shape,
        in_specs=vmem(len(args)),
        out_specs=vmem(len(out_shape)) if many else vmem(1)[0],
        scratch_shapes=list(scratch),
        compiler_params=pltpu.CompilerParams(vmem_limit_bytes=8 * MIB),
        cost_estimate=pl.CostEstimate(
            flops=4000 * MIB, bytes_accessed=8 * MIB, transcendentals=4 * MIB
        ),
        name=name,
    )(*args)


def diagonal(n):
    return lax.broadcasted_iota(jnp.int32, (n, n), 0) == lax.broadcasted_iota(jnp.int32, (n, n), 1)


def to_column(row):
    n = row.shape[1]
    return jnp.sum(jnp.where(diagonal(n), row, 0.0), axis=1, keepdims=True)


def to_row(column):
    n = column.shape[0]
    return jnp.sum(jnp.where(diagonal(n), column, 0.0), axis=0, keepdims=True)


def stacked_codes(codes_ref, count):
    codes = codes_ref[...].astype(BF16)
    parts = [codes, codes]
    if count > 2 * codes.shape[0]:
        parts.append(jnp.zeros((count - 2 * codes.shape[0], codes.shape[1]), BF16))
    return jnp.concatenate(parts, axis=0)


def split(x):
    high = x.astype(BF16).astype(F32)
    return high, x - high


def prep_kernel(hid, direction_ref, gain_ref, bias_ref, codes_ref, piece_ref):
    d = direction_ref[...]
    shapes = codes_ref.shape[0]
    rows, cols = d.shape
    half = cols // 2
    extra_lanes = piece_ref.shape[1] - cols
    inverse = lax.rsqrt(jnp.sum(d * d, axis=1, keepdims=True))
    w = to_column(gain_ref[...]) * (d * inverse)
    lane = lax.broadcasted_iota(jnp.int32, (rows, half), 1)
    first = jnp.where(lane < hid, w[:, :half], w[:, half:])
    code = pltpu.roll(w, half - hid, 1)[:, half:].astype(BF16)
    bias = to_column(bias_ref[...]).astype(BF16).astype(F32)
    high, low = split(dot(code, stacked_codes(codes_ref, extra_lanes), NT) + bias)
    own = first[:, half - LANES :]
    if extra_lanes > LANES:
        own = jnp.concatenate([jnp.zeros((rows, extra_lanes - LANES), F32), own], axis=1)
    lane = lax.broadcasted_iota(jnp.int32, (rows, extra_lanes), 1)
    table = jnp.where(lane < shapes, high, jnp.where(lane < 2 * shapes, low, 0.0))
    table = jnp.where(lane >= extra_lanes - (half - hid), own, table)
    piece_ref[:, :half] = first.astype(BF16)
    piece_ref[:, half : half + extra_lanes] = table.astype(BF16)
    piece_ref[:, half + extra_lanes :] = code


def join_kernel(*refs):
    rows = refs[0].shape[0]
    for k, ref in enumerate(refs[:-1]):
        refs[-1][k * rows : (k + 1) * rows, :] = ref[...]


def place(refs, orders, me, lane, out_ref):
    lanes = out_ref.shape[1]
    if orders is None:
        out_ref[...] = refs[0][:, lane : lane + lanes]
        return
    rows = refs[0].shape[0] // len(orders[0])
    for ref, order in zip(refs, orders):
        for k, mask in enumerate(order):
            at = pl.multiple_of((me ^ mask) * rows, rows)
            out_ref[pl.ds(at, rows), :] = ref[k * rows : (k + 1) * rows, lane : lane + lanes]


def main_kernel(hid, shapes, orders, parts, *refs):
    n = 1 if orders is None else len(orders)
    pieces = refs[:n]
    hidden_ref, offsets_ref, ids_ref, scale_ref, cot_ref, out_ref, grad_hidden_ref = refs[n : n + 7]
    grad_refs = refs[n + 7 : -3]
    w_ref, acc_ref, turned_ref = refs[-3:]
    me = lax.axis_index(AXES)
    step = pl.program_id(0)
    tile, width = cot_ref.shape
    half = width // 2
    extra_lanes = w_ref.shape[1] - half

    @pl.when(step == 0)
    def _():
        place(pieces, orders, me, 0, w_ref)
        acc_ref[...] = jnp.zeros_like(acc_ref)

    lane = lax.broadcasted_iota(jnp.int32, (tile, half), 1)
    hidden = jnp.where(lane < hid, hidden_ref[...], 0.0)
    scale = scale_ref[...]
    jitter = jnp.where(scale == 0, 1.0, jnp.where(scale == 1, 0.5, 0.25))
    xyz = offsets_ref[...] * jitter
    row = lax.broadcasted_iota(jnp.int32, (8, tile), 0)
    last = jnp.zeros((8, tile), F32)
    for k in range(half - hid):
        last = jnp.where(row == 8 - (half - hid) + k, xyz[k : k + 1], last)
    row = lax.broadcasted_iota(jnp.int32, (extra_lanes - 8, tile), 0)
    ids = ids_ref[...]
    member = jnp.where((row == ids) | (row == ids + shapes), 1.0, 0.0)
    extra = jnp.concatenate([member, last], axis=0).T
    x = jnp.concatenate([hidden.astype(BF16), extra.astype(BF16)], axis=1)
    pre = dot(x, w_ref[...], NT)
    sigma = 0.5 * jnp.tanh(0.5 * pre) + 0.5
    out = pre * sigma
    out_ref[...] = out
    grad_pre = (cot_ref[...] * (sigma * (1.0 + (pre - out)))).astype(BF16)
    grad_hidden_ref[...] = dot(grad_pre, w_ref[:, :half])
    hidden = hidden.T
    x = jnp.concatenate([hidden[: half - 8], hidden[half - 8 :] + last, member[:shapes]], axis=0)
    acc_ref[...] += dot(x.astype(BF16), grad_pre)

    @pl.when(step == pl.num_programs(0) - 1)
    def _():
        sums = jnp.concatenate(split(acc_ref[half:, :]), axis=0).astype(BF16)
        for at in range(0, width, half):
            turned_ref[at : at + half, :] = acc_ref[:half, at : at + half].T
        for ref, order in zip(grad_refs, parts):
            ref[: 2 * shapes, :] = sums[:, :half]
            ref[2 * shapes : 4 * shapes, :] = sums[:, half:]
            if orders is None:
                ref[4 * shapes :, :] = turned_ref[...].astype(BF16)
                continue
            rows = (ref.shape[0] - 4 * shapes) // len(order)
            for k, mask in enumerate(order):
                at = pl.multiple_of((me ^ mask) * rows, rows)
                to = 4 * shapes + k * rows
                ref[to : to + rows, :] = turned_ref[pl.ds(at, rows), :].astype(BF16)


def sum_of(refs):
    terms = [ref[...].astype(F32) for ref in refs]
    while len(terms) > 1:
        terms = [a + b for a, b in zip(terms[::2], terms[1::2])]
    return terms[0]


def shape_sums(total, shapes):
    left = total[:shapes] + total[shapes : 2 * shapes]
    right = total[2 * shapes : 3 * shapes] + total[3 * shapes : 4 * shapes]
    return left, right


def add_kernel(shapes, n, *refs):
    total = sum_of(refs[:n])
    left, right = shape_sums(total, shapes)
    sums = jnp.concatenate(split(left) + split(right), axis=0).astype(BF16)
    for k, ref in enumerate(refs[n:]):
        rows = ref.shape[0] - 4 * shapes
        at = 4 * shapes + k * rows
        ref[: 4 * shapes, :] = sums
        ref[4 * shapes :, :] = total[at : at + rows].astype(BF16)


def last_kernel(hid, shapes, orders, n, *refs):
    direction_ref, gain_ref, codes_ref = refs[n : n + 3]
    pieces = refs[n + 3 : -5]
    grad_codes_ref, grad_direction_ref, grad_gain_ref, grad_bias_ref, code_scratch = refs[-5:]
    d = direction_ref[...]
    rows, cols = d.shape
    half = cols // 2
    me = lax.axis_index(AXES)
    place(pieces, orders, me, pieces[0].shape[1] - half, code_scratch)
    total = sum_of(refs[:n])
    sums = jnp.concatenate(shape_sums(total, shapes), axis=1)
    sums = jnp.concatenate(split(sums), axis=0).astype(BF16)
    terms = dot(sums, code_scratch[...])
    grad_codes_ref[...] = terms[:shapes] + terms[shapes:]
    width = sums.shape[1]
    mine = lax.broadcasted_iota(jnp.int32, (rows, width), 0) + me * rows
    mine = jnp.where(mine == lax.broadcasted_iota(jnp.int32, (rows, width), 1), 1.0, 0.0).astype(BF16)
    own = dot(mine, sums, NT)
    grad_bias_ref[...] = to_row(jnp.sum(own, axis=1, keepdims=True))
    code = dot(own.astype(BF16), stacked_codes(codes_ref, 2 * shapes))
    packed = jnp.concatenate([total[4 * shapes :], code], axis=1)
    lane = lax.broadcasted_iota(jnp.int32, (rows, cols), 1)
    grad_weight = jnp.where(
        lane < hid,
        packed,
        jnp.where(lane < hid + half, pltpu.roll(packed, cols - (half - hid), 1), pltpu.roll(packed, half, 1)),
    )
    inverse = lax.rsqrt(jnp.sum(d * d, axis=1, keepdims=True))
    unit = d * inverse
    grad_gain = jnp.sum(grad_weight * unit, axis=1, keepdims=True)
    grad_gain_ref[...] = to_row(grad_gain)
    grad_direction_ref[...] = (to_column(gain_ref[...]) * inverse) * (grad_weight - grad_gain * unit)


def masks_of(group):
    masks = [0]
    for bit in group:
        masks = masks + [m ^ bit for m in masks]
    return masks


def order_of(groups):
    order = [0]
    for group in groups:
        order = [m ^ r for m in masks_of(group) for r in order]
    return order


def swap(x, mask, devices):
    return lax.ppermute(x, AXES, [(i, i ^ mask) for i in range(devices)])


def per_device(
    hidden,
    codes,
    offsets,
    shape_ids,
    scale_index,
    direction,
    gain,
    bias,
    cotangent,
    running_mean,
    running_var,
):
    points, hid = hidden.shape
    shapes = codes.shape[0]
    rows, cols = direction.shape
    width = cotangent.shape[1]
    half = cols // 2
    devices = lax.axis_size("dp") * lax.axis_size("inner")
    tuned = rows % 16 == 0
    groups = [[1 << k] for k in range(devices.bit_length() - 1)][::-1]
    tuned = rows % 16 == 0
    extra_lanes = -(-(2 * shapes + 8) // LANES) * LANES
    lanes = half + extra_lanes
    gain_row = gain.reshape(1, rows)

    def shape_of(rows, lanes, dtype):
        return jax.ShapeDtypeStruct((rows, lanes), dtype)

    held = small_kernel(
        "prep",
        functools.partial(prep_kernel, hid),
        shape_of(rows, lanes + half, BF16),
        direction,
        gain_row,
        bias.reshape(1, rows),
        codes,
    )
    if tuned:
        for group in groups[:-1]:
            arrays = [held] + [swap(held, m, devices) for m in masks_of(group)[1:]]
            held = small_kernel(
                "join",
                join_kernel,
                shape_of(held.shape[0] * len(arrays), lanes + half, BF16),
                *arrays,
            )
        last_masks = masks_of(groups[-1])
        pieces = [held] + [swap(held, m, devices) for m in last_masks[1:]]
        orders = [[m ^ r for r in order_of(groups[:-1])] for m in last_masks]
        parts = orders
    else:
        pieces, orders, parts = [lax.all_gather(held, AXES, axis=0, tiled=True)], None, [[0]]

    tile = min(256, points)
    output, grad_hidden, *grads = pl.pallas_call(
        functools.partial(main_kernel, hid, shapes, orders, parts),
        grid=(points // tile,),
        out_shape=[shape_of(points, width, F32), shape_of(points, hid, F32)]
        + [shape_of(4 * shapes + width // len(parts), half, BF16)] * len(parts),
        in_specs=vmem(len(pieces))
        + [
            pl.BlockSpec((tile, half), lambda i: (i, 0)),
            pl.BlockSpec((half - hid, tile), lambda i: (0, i)),
            pl.BlockSpec((1, tile), lambda i: (0, i)),
            pl.BlockSpec((1, tile), lambda i: (0, i)),
            pl.BlockSpec((tile, width), lambda i: (i, 0)),
        ],
        out_specs=[
            pl.BlockSpec((tile, width), lambda i: (i, 0)),
            pl.BlockSpec((tile, half), lambda i: (i, 0)),
        ]
        + vmem(len(parts)),
        scratch_shapes=[
            VMEM((width, lanes), BF16),
            VMEM((half + shapes, width), F32),
            VMEM((width, half), F32),
        ],
        compiler_params=pltpu.CompilerParams(
            dimension_semantics=("arbitrary",), vmem_limit_bytes=24 * MIB
        ),
        cost_estimate=pl.CostEstimate(
            flops=6 * points * width * cols,
            bytes_accessed=8 * points * (width + half),
            transcendentals=points * width,
        ),
        name="layer",
    )(
        *pieces,
        hidden,
        offsets.T,
        shape_ids.reshape(1, points),
        scale_index.reshape(1, points),
        cotangent,
    )

    if tuned:
        for r, group in enumerate(groups[::-1]):
            masks = masks_of(group)
            grads = [grads[0]] + [swap(g, m, devices) for g, m in zip(grads[1:], masks[1:])]
            if r == len(groups) - 1:
                break
            n_out = len(masks_of(groups[-2 - r]))
            left = (grads[0].shape[0] - 4 * shapes) // n_out
            grads = small_kernel(
                "add",
                functools.partial(add_kernel, shapes, len(grads)),
                [shape_of(4 * shapes + left, half, BF16)] * n_out,
                *grads,
            )
    else:
        sums = lax.psum(grads[0][: 4 * shapes].astype(F32), AXES)
        high = sums.astype(BF16)
        own = lax.psum_scatter(grads[0][4 * shapes :].astype(F32), AXES, scatter_dimension=0, tiled=True)
        low = jnp.zeros((4 * shapes + rows, half), BF16).at[: 4 * shapes].set((sums - high).astype(BF16))
        grads = [jnp.concatenate([high, own.astype(BF16)], axis=0), low]
    grad_codes, grad_direction, grad_gain, grad_bias = small_kernel(
        "last",
        functools.partial(last_kernel, hid, shapes, orders, len(grads)),
        [
            shape_of(shapes, half, F32),
            shape_of(rows, cols, F32),
            shape_of(1, rows, F32),
            shape_of(1, rows, F32),
        ],
        *grads,
        direction,
        gain_row,
        codes,
        *pieces,
        scratch=[VMEM((width, half), BF16)],
    )

    total = float(points * devices)
    batch_mean = jnp.mean(codes, axis=0)
    batch_square = jnp.mean(codes * codes, axis=0)
    batch_var = (batch_square - batch_mean * batch_mean) * (total / (total - 1.0))
    new_mean = 0.9 * running_mean + 0.1 * batch_mean
    new_var = 0.9 * running_var + 0.1 * batch_var
    return (
        output,
        grad_hidden,
        grad_codes,
        grad_direction,
        grad_gain.reshape(rows),
        grad_bias.reshape(rows),
        new_mean,
        new_var,
    )


def solution(mesh):
    return jax.shard_map(
        per_device,
        mesh=mesh,
        in_specs=(
            P(("dp", "inner"), None),
            P(),
            P(("dp", "inner"), None),
            P(("dp", "inner")),
            P(("dp", "inner")),
            P(("dp", "inner"), None),
            P(("dp", "inner")),
            P(("dp", "inner")),
            P(("dp", "inner"), None),
            P(),
            P(),
        ),
        out_specs=(
            P(("dp", "inner"), None),
            P(("dp", "inner"), None),
            P(),
            P(("dp", "inner"), None),
            P(("dp", "inner")),
            P(("dp", "inner")),
            P(),
            P(),
        ),
        check_vma=False,
    )
```

```python
import functools

import jax
import jax.numpy as jnp
from jax import lax
from jax.experimental import pallas as pl
from jax.experimental.pallas import tpu as pltpu
from jax.sharding import PartitionSpec as P

AXES = ("dp", "inner")
LANES = 128
MIB = 1024 * 1024
F32 = jnp.float32
BF16 = jnp.bfloat16
VMEM = pltpu.VMEM
NT = (((1,), (1,)), ((), ()))


def dot(a, b, dims=(((1,), (0,)), ((), ()))):
    return lax.dot_general(a, b, dims, preferred_element_type=F32)


def vmem(n):
    return [pl.BlockSpec(memory_space=VMEM)] * n


def small_kernel(name, body, out_shape, *args, scratch=(), space=VMEM, limit=8):
    many = isinstance(out_shape, list)
    return pl.pallas_call(
        body,
        out_shape=out_shape,
        in_specs=[pl.BlockSpec(memory_space=space)] * len(args),
        out_specs=vmem(len(out_shape)) if many else vmem(1)[0],
        scratch_shapes=list(scratch),
        compiler_params=pltpu.CompilerParams(vmem_limit_bytes=limit * MIB),
        cost_estimate=pl.CostEstimate(
            flops=4000 * MIB, bytes_accessed=8 * MIB, transcendentals=4 * MIB
        ),
        name=name,
    )(*args)


def diagonal(n):
    return lax.broadcasted_iota(jnp.int32, (n, n), 0) == lax.broadcasted_iota(jnp.int32, (n, n), 1)


def to_column(row):
    n = row.shape[1]
    return jnp.sum(jnp.where(diagonal(n), row, 0.0), axis=1, keepdims=True)


def to_row(column):
    n = column.shape[0]
    return jnp.sum(jnp.where(diagonal(n), column, 0.0), axis=0, keepdims=True)


def stacked_codes(codes_ref, count):
    codes = codes_ref[...].astype(BF16)
    parts = [codes, codes]
    if count > 2 * codes.shape[0]:
        parts.append(jnp.zeros((count - 2 * codes.shape[0], codes.shape[1]), BF16))
    return jnp.concatenate(parts, axis=0)


def split(x):
    high = x.astype(BF16).astype(F32)
    return high, x - high


def prep_kernel(hid, *refs):
    piece_ref, direction_ref, gain_ref, bias_ref, codes_ref, sems = refs[4:]
    copies = [
        pltpu.make_async_copy(source, target, sems.at[k])
        for k, (source, target) in enumerate(zip(refs[:4], refs[5:9]))
    ]
    for copy in copies:
        copy.start()
    for copy in copies:
        copy.wait()
    d = direction_ref[...]
    shapes = codes_ref.shape[0]
    rows, cols = d.shape
    half = cols // 2
    extra_lanes = piece_ref.shape[1] - cols
    inverse = lax.rsqrt(jnp.sum(d * d, axis=1, keepdims=True))
    w = to_column(gain_ref[...]) * (d * inverse)
    lane = lax.broadcasted_iota(jnp.int32, (rows, half), 1)
    first = jnp.where(lane < hid, w[:, :half], w[:, half:])
    code = pltpu.roll(w, half - hid, 1)[:, half:].astype(BF16)
    bias = to_column(bias_ref[...]).astype(BF16).astype(F32)
    high, low = split(dot(code, stacked_codes(codes_ref, extra_lanes), NT) + bias)
    own = first[:, half - LANES :]
    if extra_lanes > LANES:
        own = jnp.concatenate([jnp.zeros((rows, extra_lanes - LANES), F32), own], axis=1)
    lane = lax.broadcasted_iota(jnp.int32, (rows, extra_lanes), 1)
    table = jnp.where(lane < shapes, high, jnp.where(lane < 2 * shapes, low, 0.0))
    table = jnp.where(lane >= extra_lanes - (half - hid), own, table)
    piece_ref[:, :half] = first.astype(BF16)
    piece_ref[:, half : half + extra_lanes] = table.astype(BF16)
    piece_ref[:, half + extra_lanes :] = code


def join_kernel(*refs):
    rows = refs[0].shape[0]
    for k, ref in enumerate(refs[:-1]):
        refs[-1][k * rows : (k + 1) * rows, :] = ref[...]


def place(refs, orders, me, lane, out_ref):
    lanes = out_ref.shape[1]
    if orders is None:
        out_ref[...] = refs[0][:, lane : lane + lanes]
        return
    rows = refs[0].shape[0] // len(orders[0])
    for ref, order in zip(refs, orders):
        for k, mask in enumerate(order):
            at = pl.multiple_of((me ^ mask) * rows, rows)
            out_ref[pl.ds(at, rows), :] = ref[k * rows : (k + 1) * rows, lane : lane + lanes]


def main_kernel(hid, shapes, orders, parts, *refs):
    n = 1 if orders is None else len(orders)
    pieces = refs[:n]
    hidden_ref, offsets_ref, ids_ref, scale_ref, cot_ref, out_ref, grad_hidden_ref = refs[n : n + 7]
    grad_refs = refs[n + 7 : -3]
    w_ref, acc_ref, turned_ref = refs[-3:]
    me = lax.axis_index(AXES)
    step = pl.program_id(0)
    tile, width = cot_ref.shape
    half = width // 2
    extra_lanes = w_ref.shape[1] - half

    @pl.when(step == 0)
    def _():
        place(pieces, orders, me, 0, w_ref)
        acc_ref[...] = jnp.zeros_like(acc_ref)

    lane = lax.broadcasted_iota(jnp.int32, (tile, half), 1)
    hidden = jnp.where(lane < hid, hidden_ref[...], 0.0)
    scale = scale_ref[...]
    jitter = jnp.where(scale == 0, 1.0, jnp.where(scale == 1, 0.5, 0.25))
    xyz = offsets_ref[...] * jitter
    row = lax.broadcasted_iota(jnp.int32, (8, tile), 0)
    last = jnp.zeros((8, tile), F32)
    for k in range(half - hid):
        last = jnp.where(row == 8 - (half - hid) + k, xyz[k : k + 1], last)
    row = lax.broadcasted_iota(jnp.int32, (extra_lanes - 8, tile), 0)
    ids = ids_ref[...]
    member = jnp.where((row == ids) | (row == ids + shapes), 1.0, 0.0)
    extra = jnp.concatenate([member, last], axis=0).T
    x = jnp.concatenate([hidden.astype(BF16), extra.astype(BF16)], axis=1)
    pre = dot(x, w_ref[...], NT)
    sigma = 0.5 * jnp.tanh(0.5 * pre) + 0.5
    out = pre * sigma
    out_ref[...] = out
    grad_pre = (cot_ref[...] * (sigma * (1.0 + (pre - out)))).astype(BF16)
    grad_hidden_ref[...] = dot(grad_pre, w_ref[:, :half])
    hidden = hidden.T
    x = jnp.concatenate([hidden[: half - 8], hidden[half - 8 :] + last, member[:shapes]], axis=0)
    acc_ref[...] += dot(x.astype(BF16), grad_pre)

    @pl.when(step == pl.num_programs(0) - 1)
    def _():
        sums = jnp.concatenate(split(acc_ref[half:, :]), axis=0).astype(BF16)
        for at in range(0, width, half):
            turned_ref[at : at + half, :] = acc_ref[:half, at : at + half].T
        for ref, order in zip(grad_refs, parts):
            ref[: 2 * shapes, :] = sums[:, :half]
            ref[2 * shapes : 4 * shapes, :] = sums[:, half:]
            if orders is None:
                ref[4 * shapes :, :] = turned_ref[...].astype(BF16)
                continue
            rows = (ref.shape[0] - 4 * shapes) // len(order)
            for k, mask in enumerate(order):
                at = pl.multiple_of((me ^ mask) * rows, rows)
                to = 4 * shapes + k * rows
                ref[to : to + rows, :] = turned_ref[pl.ds(at, rows), :].astype(BF16)


def sum_of(refs):
    terms = [ref[...].astype(F32) for ref in refs]
    while len(terms) > 1:
        terms = [a + b for a, b in zip(terms[::2], terms[1::2])]
    return terms[0]


def shape_sums(total, shapes):
    left = total[:shapes] + total[shapes : 2 * shapes]
    right = total[2 * shapes : 3 * shapes] + total[3 * shapes : 4 * shapes]
    return left, right


def add_kernel(shapes, n, *refs):
    total = sum_of(refs[:n])
    left, right = shape_sums(total, shapes)
    sums = jnp.concatenate(split(left) + split(right), axis=0).astype(BF16)
    for k, ref in enumerate(refs[n:]):
        rows = ref.shape[0] - 4 * shapes
        at = 4 * shapes + k * rows
        ref[: 4 * shapes, :] = sums
        ref[4 * shapes :, :] = total[at : at + rows].astype(BF16)


def last_kernel(hid, shapes, orders, n, *refs):
    direction_ref, gain_ref, codes_ref = refs[n : n + 3]
    pieces = refs[n + 3 : -5]
    grad_codes_ref, grad_direction_ref, grad_gain_ref, grad_bias_ref, code_scratch = refs[-5:]
    d = direction_ref[...]
    rows, cols = d.shape
    half = cols // 2
    me = lax.axis_index(AXES)
    place(pieces, orders, me, pieces[0].shape[1] - half, code_scratch)
    total = sum_of(refs[:n])
    sums = jnp.concatenate(shape_sums(total, shapes), axis=1)
    sums = jnp.concatenate(split(sums), axis=0).astype(BF16)
    terms = dot(sums, code_scratch[...])
    grad_codes_ref[...] = terms[:shapes] + terms[shapes:]
    width = sums.shape[1]
    mine = lax.broadcasted_iota(jnp.int32, (rows, width), 0) + me * rows
    mine = jnp.where(mine == lax.broadcasted_iota(jnp.int32, (rows, width), 1), 1.0, 0.0).astype(BF16)
    own = dot(mine, sums, NT)
    grad_bias_ref[...] = to_row(jnp.sum(own, axis=1, keepdims=True))
    code = dot(own.astype(BF16), stacked_codes(codes_ref, 2 * shapes))
    packed = jnp.concatenate([total[4 * shapes :], code], axis=1)
    lane = lax.broadcasted_iota(jnp.int32, (rows, cols), 1)
    grad_weight = jnp.where(
        lane < hid,
        packed,
        jnp.where(lane < hid + half, pltpu.roll(packed, cols - (half - hid), 1), pltpu.roll(packed, half, 1)),
    )
    inverse = lax.rsqrt(jnp.sum(d * d, axis=1, keepdims=True))
    unit = d * inverse
    grad_gain = jnp.sum(grad_weight * unit, axis=1, keepdims=True)
    grad_gain_ref[...] = to_row(grad_gain)
    grad_direction_ref[...] = (to_column(gain_ref[...]) * inverse) * (grad_weight - grad_gain * unit)


def masks_of(group):
    masks = [0]
    for bit in group:
        masks = masks + [m ^ bit for m in masks]
    return masks


def order_of(groups):
    order = [0]
    for group in groups:
        order = [m ^ r for m in masks_of(group) for r in order]
    return order


def swap(x, mask, devices):
    return lax.ppermute(x, AXES, [(i, i ^ mask) for i in range(devices)])


def per_device(
    hidden,
    codes,
    offsets,
    shape_ids,
    scale_index,
    direction,
    gain,
    bias,
    cotangent,
    running_mean,
    running_var,
):
    points, hid = hidden.shape
    shapes = codes.shape[0]
    rows, cols = direction.shape
    width = cotangent.shape[1]
    half = cols // 2
    devices = lax.axis_size("dp") * lax.axis_size("inner")
    tuned = rows % 16 == 0
    bits = [1 << k for k in range(devices.bit_length() - 1)]
    groups = [bits[k - 2 : k] for k in range(len(bits), 1, -2)]
    groups = groups + [bits[:1]] * (len(bits) % 2)
    tuned = rows % 16 == 0
    extra_lanes = -(-(2 * shapes + 8) // LANES) * LANES
    lanes = half + extra_lanes
    gain_row = gain.reshape(1, rows)

    def shape_of(rows, lanes, dtype):
        return jax.ShapeDtypeStruct((rows, lanes), dtype)

    held = small_kernel(
        "prep",
        functools.partial(prep_kernel, hid),
        shape_of(rows, lanes + half, BF16),
        direction,
        gain_row,
        bias.reshape(1, rows),
        codes,
        scratch=[
            VMEM((rows, cols), F32),
            VMEM((1, rows), F32),
            VMEM((1, rows), F32),
            VMEM((shapes, half), F32),
            pltpu.SemaphoreType.DMA((4,)),
        ],
        space=pl.ANY,
        limit=62,
    )
    if tuned:
        for r, group in enumerate(groups[:-1]):
            moved = [swap(held, m, devices) for m in masks_of(group)[1:]]
            if r == 0:
                held = small_kernel("lift", join_kernel, shape_of(rows, lanes + half, BF16), held)
            arrays = [held] + moved
            held = small_kernel(
                "join",
                join_kernel,
                shape_of(held.shape[0] * len(arrays), lanes + half, BF16),
                *arrays,
            )
        last_masks = masks_of(groups[-1])
        pieces = [held] + [swap(held, m, devices) for m in last_masks[1:]]
        orders = [[m ^ r for r in order_of(groups[:-1])] for m in last_masks]
        parts = orders
    else:
        pieces, orders, parts = [lax.all_gather(held, AXES, axis=0, tiled=True)], None, [[0]]

    tile = min(256, points)
    output, grad_hidden, *grads = pl.pallas_call(
        functools.partial(main_kernel, hid, shapes, orders, parts),
        grid=(points // tile,),
        out_shape=[shape_of(points, width, F32), shape_of(points, hid, F32)]
        + [shape_of(4 * shapes + width // len(parts), half, BF16)] * len(parts),
        in_specs=vmem(len(pieces))
        + [
            pl.BlockSpec((tile, half), lambda i: (i, 0)),
            pl.BlockSpec((half - hid, tile), lambda i: (0, i)),
            pl.BlockSpec((1, tile), lambda i: (0, i)),
            pl.BlockSpec((1, tile), lambda i: (0, i)),
            pl.BlockSpec((tile, width), lambda i: (i, 0)),
        ],
        out_specs=[
            pl.BlockSpec((tile, width), lambda i: (i, 0)),
            pl.BlockSpec((tile, half), lambda i: (i, 0)),
        ]
        + vmem(len(parts)),
        scratch_shapes=[
            VMEM((width, lanes), BF16),
            VMEM((half + shapes, width), F32),
            VMEM((width, half), F32),
        ],
        compiler_params=pltpu.CompilerParams(
            dimension_semantics=("arbitrary",), vmem_limit_bytes=24 * MIB
        ),
        cost_estimate=pl.CostEstimate(
            flops=6 * points * width * cols,
            bytes_accessed=8 * points * (width + half),
            transcendentals=points * width,
        ),
        name="layer",
    )(
        *pieces,
        hidden,
        offsets.T,
        shape_ids.reshape(1, points),
        scale_index.reshape(1, points),
        cotangent,
    )

    if tuned:
        for r, group in enumerate(groups[::-1]):
            masks = masks_of(group)
            grads = [grads[0]] + [swap(g, m, devices) for g, m in zip(grads[1:], masks[1:])]
            if r == len(groups) - 1:
                break
            n_out = len(masks_of(groups[-2 - r]))
            left = (grads[0].shape[0] - 4 * shapes) // n_out
            grads = small_kernel(
                "add",
                functools.partial(add_kernel, shapes, len(grads)),
                [shape_of(4 * shapes + left, half, BF16)] * n_out,
                *grads,
            )
    else:
        sums = lax.psum(grads[0][: 4 * shapes].astype(F32), AXES)
        high = sums.astype(BF16)
        own = lax.psum_scatter(grads[0][4 * shapes :].astype(F32), AXES, scatter_dimension=0, tiled=True)
        low = jnp.zeros((4 * shapes + rows, half), BF16).at[: 4 * shapes].set((sums - high).astype(BF16))
        grads = [jnp.concatenate([high, own.astype(BF16)], axis=0), low]
    grad_codes, grad_direction, grad_gain, grad_bias = small_kernel(
        "last",
        functools.partial(last_kernel, hid, shapes, orders, len(grads)),
        [
            shape_of(shapes, half, F32),
            shape_of(rows, cols, F32),
            shape_of(1, rows, F32),
            shape_of(1, rows, F32),
        ],
        *grads,
        direction,
        gain_row,
        codes,
        *pieces,
        scratch=[VMEM((width, half), BF16)],
    )

    total = float(points * devices)
    batch_mean = jnp.mean(codes, axis=0)
    batch_square = jnp.mean(codes * codes, axis=0)
    batch_var = (batch_square - batch_mean * batch_mean) * (total / (total - 1.0))
    new_mean = 0.9 * running_mean + 0.1 * batch_mean
    new_var = 0.9 * running_var + 0.1 * batch_var
    return (
        output,
        grad_hidden,
        grad_codes,
        grad_direction,
        grad_gain.reshape(rows),
        grad_bias.reshape(rows),
        new_mean,
        new_var,
    )


def solution(mesh):
    return jax.shard_map(
        per_device,
        mesh=mesh,
        in_specs=(
            P(("dp", "inner"), None),
            P(),
            P(("dp", "inner"), None),
            P(("dp", "inner")),
            P(("dp", "inner")),
            P(("dp", "inner"), None),
            P(("dp", "inner")),
            P(("dp", "inner")),
            P(("dp", "inner"), None),
            P(),
            P(),
        ),
        out_specs=(
            P(("dp", "inner"), None),
            P(("dp", "inner"), None),
            P(),
            P(("dp", "inner"), None),
            P(("dp", "inner")),
            P(("dp", "inner")),
            P(),
            P(),
        ),
        check_vma=False,
    )
```

```python
import functools

import jax
import jax.numpy as jnp
from jax import lax
from jax.experimental import pallas as pl
from jax.experimental.pallas import tpu as pltpu
from jax.sharding import PartitionSpec as P

AXES = ("dp", "inner")
LANES = 128
MIB = 1024 * 1024
F32 = jnp.float32
BF16 = jnp.bfloat16
VMEM = pltpu.VMEM
NT = (((1,), (1,)), ((), ()))


def dot(a, b, dims=(((1,), (0,)), ((), ()))):
    return lax.dot_general(a, b, dims, preferred_element_type=F32)


def vmem(n):
    return [pl.BlockSpec(memory_space=VMEM)] * n


def small_kernel(name, body, out_shape, *args, scratch=(), space=VMEM, limit=8):
    many = isinstance(out_shape, list)
    return pl.pallas_call(
        body,
        out_shape=out_shape,
        in_specs=[pl.BlockSpec(memory_space=space)] * len(args),
        out_specs=vmem(len(out_shape)) if many else vmem(1)[0],
        scratch_shapes=list(scratch),
        compiler_params=pltpu.CompilerParams(vmem_limit_bytes=limit * MIB),
        cost_estimate=pl.CostEstimate(
            flops=4000 * MIB, bytes_accessed=8 * MIB, transcendentals=4 * MIB
        ),
        name=name,
    )(*args)


def diagonal(n):
    return lax.broadcasted_iota(jnp.int32, (n, n), 0) == lax.broadcasted_iota(jnp.int32, (n, n), 1)


def to_column(row):
    n = row.shape[1]
    return jnp.sum(jnp.where(diagonal(n), row, 0.0), axis=1, keepdims=True)


def to_row(column):
    n = column.shape[0]
    return jnp.sum(jnp.where(diagonal(n), column, 0.0), axis=0, keepdims=True)


def stacked_codes(codes_ref, count):
    codes = codes_ref[...].astype(BF16)
    parts = [codes, codes]
    if count > 2 * codes.shape[0]:
        parts.append(jnp.zeros((count - 2 * codes.shape[0], codes.shape[1]), BF16))
    return jnp.concatenate(parts, axis=0)


def split(x):
    high = x.astype(BF16).astype(F32)
    return high, x - high


def prep_kernel(hid, *refs):
    piece_ref, direction_ref, gain_ref, bias_ref, codes_ref, sems = refs[4:]
    copies = [
        pltpu.make_async_copy(source, target, sems.at[k])
        for k, (source, target) in enumerate(zip(refs[:4], refs[5:9]))
    ]
    for copy in copies:
        copy.start()
    for copy in copies:
        copy.wait()
    d = direction_ref[...]
    shapes = codes_ref.shape[0]
    rows, cols = d.shape
    half = cols // 2
    extra_lanes = piece_ref.shape[1] - cols
    inverse = lax.rsqrt(jnp.sum(d * d, axis=1, keepdims=True))
    w = to_column(gain_ref[...]) * (d * inverse)
    lane = lax.broadcasted_iota(jnp.int32, (rows, half), 1)
    first = jnp.where(lane < hid, w[:, :half], w[:, half:])
    code = pltpu.roll(w, half - hid, 1)[:, half:].astype(BF16)
    bias = to_column(bias_ref[...]).astype(BF16).astype(F32)
    high, low = split(dot(code, stacked_codes(codes_ref, extra_lanes), NT) + bias)
    own = first[:, half - LANES :]
    if extra_lanes > LANES:
        own = jnp.concatenate([jnp.zeros((rows, extra_lanes - LANES), F32), own], axis=1)
    lane = lax.broadcasted_iota(jnp.int32, (rows, extra_lanes), 1)
    table = jnp.where(lane < shapes, high, jnp.where(lane < 2 * shapes, low, 0.0))
    table = jnp.where(lane >= extra_lanes - (half - hid), own, table)
    piece_ref[:, :half] = first.astype(BF16)
    piece_ref[:, half : half + extra_lanes] = table.astype(BF16)
    piece_ref[:, half + extra_lanes :] = code


def join_kernel(*refs):
    rows = refs[0].shape[0]
    for k, ref in enumerate(refs[:-1]):
        refs[-1][k * rows : (k + 1) * rows, :] = ref[...]


def place(refs, orders, me, lane, out_ref):
    lanes = out_ref.shape[1]
    if orders is None:
        out_ref[...] = refs[0][:, lane : lane + lanes]
        return
    rows = refs[0].shape[0] // len(orders[0])
    for ref, order in zip(refs, orders):
        for k, mask in enumerate(order):
            at = pl.multiple_of((me ^ mask) * rows, rows)
            out_ref[pl.ds(at, rows), :] = ref[k * rows : (k + 1) * rows, lane : lane + lanes]


def inputs_kernel(hid, shapes, hidden_ref, offsets_ref, ids_ref, scale_ref, x_ref, x_t_ref):
    step = pl.program_id(0)
    tile, half = hidden_ref.shape
    extra_lanes = x_ref.shape[1] - half
    here = pl.ds(pl.multiple_of(step * tile, tile), tile)
    lane = lax.broadcasted_iota(jnp.int32, (tile, half), 1)
    hidden = jnp.where(lane < hid, hidden_ref[...], 0.0)
    scale = scale_ref[...]
    jitter = jnp.where(scale == 0, 1.0, jnp.where(scale == 1, 0.5, 0.25))
    xyz = offsets_ref[...] * jitter
    row = lax.broadcasted_iota(jnp.int32, (8, tile), 0)
    last = jnp.zeros((8, tile), F32)
    for k in range(half - hid):
        last = jnp.where(row == 8 - (half - hid) + k, xyz[k : k + 1], last)
    row = lax.broadcasted_iota(jnp.int32, (extra_lanes - 8, tile), 0)
    ids = ids_ref[...]
    member = jnp.where((row == ids) | (row == ids + shapes), 1.0, 0.0)
    extra = jnp.concatenate([member, last], axis=0).T
    x_ref[here, :half] = hidden.astype(BF16)
    x_ref[here, half:] = extra.astype(BF16)
    hidden = hidden.T
    x = jnp.concatenate([hidden[: half - 8], hidden[half - 8 :] + last, member[:shapes]], axis=0)
    x_t_ref[:, here] = x.astype(BF16)


def layer_kernel(hid, shapes, tile, orders, parts, *refs):
    n = 1 if orders is None else len(orders)
    pieces = refs[:n]
    x_ref, x_t_ref, cot_ref, out_hbm, grad_hidden_hbm = refs[n : n + 5]
    grad_refs = refs[n + 5 : -6]
    w_ref, acc_ref, turned_ref, out_ref, grad_hidden_ref, sems = refs[-6:]
    points, width = cot_ref.shape
    half = width // 2
    me = lax.axis_index(AXES)
    place(pieces, orders, me, 0, w_ref)
    acc_ref[...] = jnp.zeros_like(acc_ref)

    def stores(step):
        here = pl.ds(pl.multiple_of(step * tile, tile), tile)
        return [
            pltpu.make_async_copy(source.at[here, :], target.at[here, :], sems.at[k, step])
            for k, (source, target) in enumerate(
                [(out_ref, out_hbm), (grad_hidden_ref, grad_hidden_hbm)]
            )
        ]

    def body(step, carry):
        here = pl.ds(pl.multiple_of(step * tile, tile), tile)
        pre = dot(x_ref[here, :], w_ref[...], NT)
        sigma = 0.5 * jnp.tanh(0.5 * pre) + 0.5
        out = pre * sigma
        out_ref[here, :] = out
        grad_pre = (cot_ref[here, :] * (sigma * (1.0 + (pre - out)))).astype(BF16)
        grad_hidden_ref[here, :] = dot(grad_pre, w_ref[:, :half])[:, :hid]
        for copy in stores(step):
            copy.start()
        acc_ref[...] += dot(x_t_ref[:, here], grad_pre)
        return carry

    lax.fori_loop(0, points // tile, body, 0)
    sums = jnp.concatenate(split(acc_ref[half:, :]), axis=0).astype(BF16)
    for at in range(0, width, half):
        turned_ref[at : at + half, :] = acc_ref[:half, at : at + half].T
    for ref, order in zip(grad_refs, parts):
        ref[: 2 * shapes, :] = sums[:, :half]
        ref[2 * shapes : 4 * shapes, :] = sums[:, half:]
        if orders is None:
            ref[4 * shapes :, :] = turned_ref[...].astype(BF16)
            continue
        rows = (ref.shape[0] - 4 * shapes) // len(order)
        for k, mask in enumerate(order):
            at = pl.multiple_of((me ^ mask) * rows, rows)
            to = 4 * shapes + k * rows
            ref[to : to + rows, :] = turned_ref[pl.ds(at, rows), :].astype(BF16)

    def finish(step, carry):
        for copy in stores(step):
            copy.wait()
        return carry

    lax.fori_loop(0, points // tile, finish, 0)


def sum_of(refs):
    terms = [ref[...].astype(F32) for ref in refs]
    while len(terms) > 1:
        terms = [a + b for a, b in zip(terms[::2], terms[1::2])]
    return terms[0]


def shape_sums(total, shapes):
    left = total[:shapes] + total[shapes : 2 * shapes]
    right = total[2 * shapes : 3 * shapes] + total[3 * shapes : 4 * shapes]
    return left, right


def add_kernel(shapes, n, *refs):
    total = sum_of(refs[:n])
    left, right = shape_sums(total, shapes)
    sums = jnp.concatenate(split(left) + split(right), axis=0).astype(BF16)
    for k, ref in enumerate(refs[n:]):
        rows = ref.shape[0] - 4 * shapes
        at = 4 * shapes + k * rows
        ref[: 4 * shapes, :] = sums
        ref[4 * shapes :, :] = total[at : at + rows].astype(BF16)


def last_kernel(hid, shapes, orders, n, *refs):
    direction_ref, gain_ref, codes_ref = refs[n : n + 3]
    pieces = refs[n + 3 : -5]
    grad_codes_ref, grad_direction_ref, grad_gain_ref, grad_bias_ref, code_scratch = refs[-5:]
    d = direction_ref[...]
    rows, cols = d.shape
    half = cols // 2
    me = lax.axis_index(AXES)
    place(pieces, orders, me, pieces[0].shape[1] - half, code_scratch)
    total = sum_of(refs[:n])
    sums = jnp.concatenate(shape_sums(total, shapes), axis=1)
    sums = jnp.concatenate(split(sums), axis=0).astype(BF16)
    terms = dot(sums, code_scratch[...])
    grad_codes_ref[...] = terms[:shapes] + terms[shapes:]
    width = sums.shape[1]
    mine = lax.broadcasted_iota(jnp.int32, (rows, width), 0) + me * rows
    mine = jnp.where(mine == lax.broadcasted_iota(jnp.int32, (rows, width), 1), 1.0, 0.0).astype(BF16)
    own = dot(mine, sums, NT)
    grad_bias_ref[...] = to_row(jnp.sum(own, axis=1, keepdims=True))
    code = dot(own.astype(BF16), stacked_codes(codes_ref, 2 * shapes))
    packed = jnp.concatenate([total[4 * shapes :], code], axis=1)
    lane = lax.broadcasted_iota(jnp.int32, (rows, cols), 1)
    grad_weight = jnp.where(
        lane < hid,
        packed,
        jnp.where(lane < hid + half, pltpu.roll(packed, cols - (half - hid), 1), pltpu.roll(packed, half, 1)),
    )
    inverse = lax.rsqrt(jnp.sum(d * d, axis=1, keepdims=True))
    unit = d * inverse
    grad_gain = jnp.sum(grad_weight * unit, axis=1, keepdims=True)
    grad_gain_ref[...] = to_row(grad_gain)
    grad_direction_ref[...] = (to_column(gain_ref[...]) * inverse) * (grad_weight - grad_gain * unit)


def masks_of(group):
    masks = [0]
    for bit in group:
        masks = masks + [m ^ bit for m in masks]
    return masks


def order_of(groups):
    order = [0]
    for group in groups:
        order = [m ^ r for m in masks_of(group) for r in order]
    return order


def swap(x, mask, devices):
    return lax.ppermute(x, AXES, [(i, i ^ mask) for i in range(devices)])


def per_device(
    hidden,
    codes,
    offsets,
    shape_ids,
    scale_index,
    direction,
    gain,
    bias,
    cotangent,
    running_mean,
    running_var,
):
    points, hid = hidden.shape
    shapes = codes.shape[0]
    rows, cols = direction.shape
    width = cotangent.shape[1]
    half = cols // 2
    devices = lax.axis_size("dp") * lax.axis_size("inner")
    tuned = rows % 16 == 0
    bits = [1 << k for k in range(devices.bit_length() - 1)]
    groups = [bits[k - 2 : k] for k in range(len(bits), 1, -2)]
    groups = groups + [bits[:1]] * (len(bits) % 2)
    tuned = rows % 16 == 0
    extra_lanes = -(-(2 * shapes + 8) // LANES) * LANES
    lanes = half + extra_lanes
    gain_row = gain.reshape(1, rows)

    def shape_of(rows, lanes, dtype):
        return jax.ShapeDtypeStruct((rows, lanes), dtype)

    held = small_kernel(
        "prep",
        functools.partial(prep_kernel, hid),
        shape_of(rows, lanes + half, BF16),
        *[
            pltpu.with_memory_space_constraint(x, pltpu.HBM)
            for x in (direction, gain_row, bias.reshape(1, rows), codes)
        ],
        scratch=[
            VMEM((rows, cols), F32),
            VMEM((1, rows), F32),
            VMEM((1, rows), F32),
            VMEM((shapes, half), F32),
            pltpu.SemaphoreType.DMA((4,)),
        ],
        space=pl.ANY,
    )
    tile = min(512, points)
    x, x_t = pl.pallas_call(
        functools.partial(inputs_kernel, hid, shapes),
        grid=(points // tile,),
        out_shape=[shape_of(points, lanes, BF16), shape_of(half + shapes, points, BF16)],
        in_specs=[
            pl.BlockSpec((tile, half), lambda i: (i, 0)),
            pl.BlockSpec((half - hid, tile), lambda i: (0, i)),
            pl.BlockSpec((1, tile), lambda i: (0, i)),
            pl.BlockSpec((1, tile), lambda i: (0, i)),
        ],
        out_specs=vmem(2),
        compiler_params=pltpu.CompilerParams(
            dimension_semantics=("arbitrary",), vmem_limit_bytes=12 * MIB
        ),
        cost_estimate=pl.CostEstimate(
            flops=4000 * MIB, bytes_accessed=8 * points * half, transcendentals=0
        ),
        name="inputs",
    )(
        *[
            pltpu.with_memory_space_constraint(a, pltpu.HBM)
            for a in (
                hidden,
                offsets.T,
                shape_ids.reshape(1, points),
                scale_index.reshape(1, points),
            )
        ]
    )
    if tuned:
        for group in groups[:-1]:
            arrays = [held] + [swap(held, m, devices) for m in masks_of(group)[1:]]
            held = small_kernel(
                "join",
                join_kernel,
                shape_of(held.shape[0] * len(arrays), lanes + half, BF16),
                *arrays,
            )
        held, x, x_t = lax.optimization_barrier((held, x, x_t))
        last_masks = masks_of(groups[-1])
        pieces = [held] + [swap(held, m, devices) for m in last_masks[1:]]
        orders = [[m ^ r for r in order_of(groups[:-1])] for m in last_masks]
        parts = orders
    else:
        pieces, orders, parts = [lax.all_gather(held, AXES, axis=0, tiled=True)], None, [[0]]

    output, grad_hidden, *grads = pl.pallas_call(
        functools.partial(layer_kernel, hid, shapes, tile, orders, parts),
        out_shape=[pltpu.HBM((points, width), F32), pltpu.HBM((points, hid), F32)]
        + [shape_of(4 * shapes + width // len(parts), half, BF16)] * len(parts),
        in_specs=vmem(len(pieces) + 3),
        out_specs=[pl.BlockSpec(memory_space=pltpu.HBM)] * 2 + vmem(len(parts)),
        scratch_shapes=[
            VMEM((width, lanes), BF16),
            VMEM((half + shapes, width), F32),
            VMEM((width, half), F32),
            VMEM((points, width), F32),
            VMEM((points, hid), F32),
            pltpu.SemaphoreType.DMA((2, points // tile)),
        ],
        compiler_params=pltpu.CompilerParams(vmem_limit_bytes=20 * MIB),
        cost_estimate=pl.CostEstimate(
            flops=6 * points * width * cols,
            bytes_accessed=8 * points * (width + half),
            transcendentals=points * width,
        ),
        name="layer",
    )(*pieces, x, x_t, cotangent)

    if tuned:
        for r, group in enumerate(groups[::-1]):
            masks = masks_of(group)
            grads = [grads[0]] + [swap(g, m, devices) for g, m in zip(grads[1:], masks[1:])]
            if r == len(groups) - 1:
                break
            n_out = len(masks_of(groups[-2 - r]))
            left = (grads[0].shape[0] - 4 * shapes) // n_out
            grads = small_kernel(
                "add",
                functools.partial(add_kernel, shapes, len(grads)),
                [shape_of(4 * shapes + left, half, BF16)] * n_out,
                *grads,
            )
    else:
        sums = lax.psum(grads[0][: 4 * shapes].astype(F32), AXES)
        high = sums.astype(BF16)
        own = lax.psum_scatter(grads[0][4 * shapes :].astype(F32), AXES, scatter_dimension=0, tiled=True)
        low = jnp.zeros((4 * shapes + rows, half), BF16).at[: 4 * shapes].set((sums - high).astype(BF16))
        grads = [jnp.concatenate([high, own.astype(BF16)], axis=0), low]
    grad_codes, grad_direction, grad_gain, grad_bias = small_kernel(
        "last",
        functools.partial(last_kernel, hid, shapes, orders, len(grads)),
        [
            shape_of(shapes, half, F32),
            shape_of(rows, cols, F32),
            shape_of(1, rows, F32),
            shape_of(1, rows, F32),
        ],
        *grads,
        direction,
        gain_row,
        codes,
        *pieces,
        scratch=[VMEM((width, half), BF16)],
    )

    total = float(points * devices)
    batch_mean = jnp.mean(codes, axis=0)
    batch_square = jnp.mean(codes * codes, axis=0)
    batch_var = (batch_square - batch_mean * batch_mean) * (total / (total - 1.0))
    new_mean = 0.9 * running_mean + 0.1 * batch_mean
    new_var = 0.9 * running_var + 0.1 * batch_var
    return (
        output,
        grad_hidden,
        grad_codes,
        grad_direction,
        grad_gain.reshape(rows),
        grad_bias.reshape(rows),
        new_mean,
        new_var,
    )


def solution(mesh):
    return jax.shard_map(
        per_device,
        mesh=mesh,
        in_specs=(
            P(("dp", "inner"), None),
            P(),
            P(("dp", "inner"), None),
            P(("dp", "inner")),
            P(("dp", "inner")),
            P(("dp", "inner"), None),
            P(("dp", "inner")),
            P(("dp", "inner")),
            P(("dp", "inner"), None),
            P(),
            P(),
        ),
        out_specs=(
            P(("dp", "inner"), None),
            P(("dp", "inner"), None),
            P(),
            P(("dp", "inner"), None),
            P(("dp", "inner")),
            P(("dp", "inner")),
            P(),
            P(),
        ),
        check_vma=False,
    )
```

```python
import functools

import jax
import jax.numpy as jnp
from jax import lax
from jax.experimental import pallas as pl
from jax.experimental.pallas import tpu as pltpu
from jax.sharding import PartitionSpec as P

AXES = ("dp", "inner")
LANES = 128
MIB = 1024 * 1024
F32 = jnp.float32
BF16 = jnp.bfloat16
VMEM = pltpu.VMEM
NT = (((1,), (1,)), ((), ()))


def dot(a, b, dims=(((1,), (0,)), ((), ()))):
    return lax.dot_general(a, b, dims, preferred_element_type=F32)


def vmem(n):
    return [pl.BlockSpec(memory_space=VMEM)] * n


def small_kernel(name, body, out_shape, *args, scratch=(), space=VMEM, limit=8):
    many = isinstance(out_shape, list)
    return pl.pallas_call(
        body,
        out_shape=out_shape,
        in_specs=[pl.BlockSpec(memory_space=space)] * len(args),
        out_specs=vmem(len(out_shape)) if many else vmem(1)[0],
        scratch_shapes=list(scratch),
        compiler_params=pltpu.CompilerParams(vmem_limit_bytes=limit * MIB),
        cost_estimate=pl.CostEstimate(
            flops=4000 * MIB, bytes_accessed=8 * MIB, transcendentals=4 * MIB
        ),
        name=name,
    )(*args)


def diagonal(n):
    return lax.broadcasted_iota(jnp.int32, (n, n), 0) == lax.broadcasted_iota(jnp.int32, (n, n), 1)


def to_column(row):
    n = row.shape[1]
    return jnp.sum(jnp.where(diagonal(n), row, 0.0), axis=1, keepdims=True)


def to_row(column):
    n = column.shape[0]
    return jnp.sum(jnp.where(diagonal(n), column, 0.0), axis=0, keepdims=True)


def stacked_codes(codes_ref, count):
    codes = codes_ref[...].astype(BF16)
    parts = [codes, codes]
    if count > 2 * codes.shape[0]:
        parts.append(jnp.zeros((count - 2 * codes.shape[0], codes.shape[1]), BF16))
    return jnp.concatenate(parts, axis=0)


def split(x):
    high = x.astype(BF16).astype(F32)
    return high, x - high


def prep_kernel(hid, *refs):
    piece_ref, direction_ref, gain_ref, bias_ref, codes_ref, sems = refs[4:]
    copies = [
        pltpu.make_async_copy(source, target, sems.at[k])
        for k, (source, target) in enumerate(zip(refs[:4], refs[5:9]))
    ]
    for copy in copies:
        copy.start()
    for copy in copies:
        copy.wait()
    d = direction_ref[...]
    shapes = codes_ref.shape[0]
    rows, cols = d.shape
    half = cols // 2
    extra_lanes = piece_ref.shape[1] - cols
    inverse = lax.rsqrt(jnp.sum(d * d, axis=1, keepdims=True))
    w = to_column(gain_ref[...]) * (d * inverse)
    lane = lax.broadcasted_iota(jnp.int32, (rows, half), 1)
    first = jnp.where(lane < hid, w[:, :half], w[:, half:])
    code = pltpu.roll(w, half - hid, 1)[:, half:].astype(BF16)
    bias = to_column(bias_ref[...]).astype(BF16).astype(F32)
    high, low = split(dot(code, stacked_codes(codes_ref, extra_lanes), NT) + bias)
    own = first[:, half - LANES :]
    if extra_lanes > LANES:
        own = jnp.concatenate([jnp.zeros((rows, extra_lanes - LANES), F32), own], axis=1)
    lane = lax.broadcasted_iota(jnp.int32, (rows, extra_lanes), 1)
    table = jnp.where(lane < shapes, high, jnp.where(lane < 2 * shapes, low, 0.0))
    table = jnp.where(lane >= extra_lanes - (half - hid), own, table)
    piece_ref[:, :half] = first.astype(BF16)
    piece_ref[:, half : half + extra_lanes] = table.astype(BF16)
    piece_ref[:, half + extra_lanes :] = code


def join_kernel(*refs):
    rows = refs[0].shape[0]
    for k, ref in enumerate(refs[:-1]):
        refs[-1][k * rows : (k + 1) * rows, :] = ref[...]


def place(refs, orders, me, lane, out_ref):
    lanes = out_ref.shape[1]
    if orders is None:
        out_ref[...] = refs[0][:, lane : lane + lanes]
        return
    rows = refs[0].shape[0] // len(orders[0])
    for ref, order in zip(refs, orders):
        for k, mask in enumerate(order):
            at = pl.multiple_of((me ^ mask) * rows, rows)
            out_ref[pl.ds(at, rows), :] = ref[k * rows : (k + 1) * rows, lane : lane + lanes]


def inputs_kernel(hid, shapes, hidden_ref, offsets_ref, ids_ref, scale_ref, x_ref, x_t_ref):
    step = pl.program_id(0)
    tile = hidden_ref.shape[0]
    half = x_t_ref.shape[0] - shapes
    extra_lanes = x_ref.shape[1] - half
    here = pl.ds(pl.multiple_of(step * tile, tile), tile)
    scale = scale_ref[...]
    jitter = jnp.where(scale == 0, 1.0, jnp.where(scale == 1, 0.5, 0.25))
    xyz = offsets_ref[...] * jitter
    row = lax.broadcasted_iota(jnp.int32, (8, tile), 0)
    last = jnp.zeros((8, tile), F32)
    for k in range(half - hid):
        last = jnp.where(row == 8 - (half - hid) + k, xyz[k : k + 1], last)
    row = lax.broadcasted_iota(jnp.int32, (extra_lanes - 8, tile), 0)
    ids = ids_ref[...]
    member = jnp.where((row == ids) | (row == ids + shapes), 1.0, 0.0)
    extra = jnp.concatenate([member, last], axis=0).T
    x_ref[here, half - LANES : half] = jnp.zeros((tile, LANES), BF16)
    x_ref[here, :hid] = hidden_ref[...].astype(BF16)
    x_ref[here, half:] = extra.astype(BF16)
    hidden = x_ref[here, :half].astype(F32).T
    x = jnp.concatenate([hidden[: half - 8], hidden[half - 8 :] + last, member[:shapes]], axis=0)
    x_t_ref[:, here] = x.astype(BF16)


def layer_kernel(hid, shapes, tile, orders, parts, *refs):
    n = 1 if orders is None else len(orders)
    pieces = refs[:n]
    x_ref, x_t_ref, cot_ref, out_hbm, grad_hidden_hbm = refs[n : n + 5]
    grad_refs = refs[n + 5 : -6]
    w_ref, acc_ref, turned_ref, out_ref, grad_hidden_ref, sems = refs[-6:]
    points, width = cot_ref.shape
    half = width // 2
    me = lax.axis_index(AXES)
    place(pieces, orders, me, 0, w_ref)
    acc_ref[...] = jnp.zeros_like(acc_ref)

    def stores(step):
        here = pl.ds(pl.multiple_of(step * tile, tile), tile)
        return [
            pltpu.make_async_copy(source.at[here, :], target.at[here, :], sems.at[k, step])
            for k, (source, target) in enumerate(
                [(out_ref, out_hbm), (grad_hidden_ref, grad_hidden_hbm)]
            )
        ]

    def body(step, carry):
        here = pl.ds(pl.multiple_of(step * tile, tile), tile)
        pre = dot(x_ref[here, :], w_ref[...], NT)
        sigma = 0.5 * jnp.tanh(0.5 * pre) + 0.5
        out = pre * sigma
        out_ref[here, :] = out
        grad_pre = (cot_ref[here, :] * (sigma * (1.0 + (pre - out)))).astype(BF16)
        grad_hidden_ref[here, :] = dot(grad_pre, w_ref[:, :half])[:, :hid]
        for copy in stores(step):
            copy.start()
        acc_ref[...] += dot(x_t_ref[:, here], grad_pre)
        return carry

    lax.fori_loop(0, points // tile, body, 0)
    sums = jnp.concatenate(split(acc_ref[half:, :]), axis=0).astype(BF16)
    for at in range(0, width, half):
        turned_ref[at : at + half, :] = acc_ref[:half, at : at + half].T
    for ref, order in zip(grad_refs, parts):
        ref[: 2 * shapes, :] = sums[:, :half]
        ref[2 * shapes : 4 * shapes, :] = sums[:, half:]
        if orders is None:
            ref[4 * shapes :, :] = turned_ref[...].astype(BF16)
            continue
        rows = (ref.shape[0] - 4 * shapes) // len(order)
        for k, mask in enumerate(order):
            at = pl.multiple_of((me ^ mask) * rows, rows)
            to = 4 * shapes + k * rows
            ref[to : to + rows, :] = turned_ref[pl.ds(at, rows), :].astype(BF16)

    def finish(step, carry):
        for copy in stores(step):
            copy.wait()
        return carry

    lax.fori_loop(0, points // tile, finish, 0)


def sum_of(refs):
    terms = [ref[...].astype(F32) for ref in refs]
    while len(terms) > 1:
        terms = [a + b for a, b in zip(terms[::2], terms[1::2])]
    return terms[0]


def shape_sums(total, shapes):
    left = total[:shapes] + total[shapes : 2 * shapes]
    right = total[2 * shapes : 3 * shapes] + total[3 * shapes : 4 * shapes]
    return left, right


def add_kernel(shapes, n, *refs):
    total = sum_of(refs[:n])
    left, right = shape_sums(total, shapes)
    sums = jnp.concatenate(split(left) + split(right), axis=0).astype(BF16)
    for k, ref in enumerate(refs[n:]):
        rows = ref.shape[0] - 4 * shapes
        at = 4 * shapes + k * rows
        ref[: 4 * shapes, :] = sums
        ref[4 * shapes :, :] = total[at : at + rows].astype(BF16)


def last_kernel(hid, shapes, orders, n, *refs):
    direction_ref, gain_ref, codes_ref = refs[n : n + 3]
    pieces = refs[n + 3 : -5]
    grad_codes_ref, grad_direction_ref, grad_gain_ref, grad_bias_ref, code_scratch = refs[-5:]
    d = direction_ref[...]
    rows, cols = d.shape
    half = cols // 2
    me = lax.axis_index(AXES)
    place(pieces, orders, me, pieces[0].shape[1] - half, code_scratch)
    total = sum_of(refs[:n])
    sums = jnp.concatenate(shape_sums(total, shapes), axis=1)
    sums = jnp.concatenate(split(sums), axis=0).astype(BF16)
    terms = dot(sums, code_scratch[...])
    grad_codes_ref[...] = terms[:shapes] + terms[shapes:]
    width = sums.shape[1]
    mine = lax.broadcasted_iota(jnp.int32, (rows, width), 0) + me * rows
    mine = jnp.where(mine == lax.broadcasted_iota(jnp.int32, (rows, width), 1), 1.0, 0.0).astype(BF16)
    own = dot(mine, sums, NT)
    grad_bias_ref[...] = to_row(jnp.sum(own, axis=1, keepdims=True))
    code = dot(own.astype(BF16), stacked_codes(codes_ref, 2 * shapes))
    packed = jnp.concatenate([total[4 * shapes :], code], axis=1)
    lane = lax.broadcasted_iota(jnp.int32, (rows, cols), 1)
    grad_weight = jnp.where(
        lane < hid,
        packed,
        jnp.where(lane < hid + half, pltpu.roll(packed, cols - (half - hid), 1), pltpu.roll(packed, half, 1)),
    )
    inverse = lax.rsqrt(jnp.sum(d * d, axis=1, keepdims=True))
    unit = d * inverse
    grad_gain = jnp.sum(grad_weight * unit, axis=1, keepdims=True)
    grad_gain_ref[...] = to_row(grad_gain)
    grad_direction_ref[...] = (to_column(gain_ref[...]) * inverse) * (grad_weight - grad_gain * unit)


def masks_of(group):
    masks = [0]
    for bit in group:
        masks = masks + [m ^ bit for m in masks]
    return masks


def order_of(groups):
    order = [0]
    for group in groups:
        order = [m ^ r for m in masks_of(group) for r in order]
    return order


def swaps(arrays, masks, devices):
    moved = [
        lax.ppermute(x, AXES, [(i, i ^ mask) for i in range(devices)])
        for x, mask in list(zip(arrays, masks))[::-1]
    ]
    return moved[::-1]


def per_device(
    hidden,
    codes,
    offsets,
    shape_ids,
    scale_index,
    direction,
    gain,
    bias,
    cotangent,
    running_mean,
    running_var,
):
    points, hid = hidden.shape
    shapes = codes.shape[0]
    rows, cols = direction.shape
    width = cotangent.shape[1]
    half = cols // 2
    devices = lax.axis_size("dp") * lax.axis_size("inner")
    tuned = rows % 16 == 0
    bits = [1 << k for k in range(devices.bit_length() - 1)]
    groups = [bits[k - 2 : k] for k in range(len(bits), 1, -2)]
    groups = groups + [bits[:1]] * (len(bits) % 2)
    tuned = rows % 16 == 0
    extra_lanes = -(-(2 * shapes + 8) // LANES) * LANES
    lanes = half + extra_lanes
    gain_row = gain.reshape(1, rows)

    def shape_of(rows, lanes, dtype):
        return jax.ShapeDtypeStruct((rows, lanes), dtype)

    held = small_kernel(
        "prep",
        functools.partial(prep_kernel, hid),
        shape_of(rows, lanes + half, BF16),
        *[
            pltpu.with_memory_space_constraint(x, pltpu.HBM)
            for x in (direction, gain_row, bias.reshape(1, rows), codes)
        ],
        scratch=[
            VMEM((rows, cols), F32),
            VMEM((1, rows), F32),
            VMEM((1, rows), F32),
            VMEM((shapes, half), F32),
            pltpu.SemaphoreType.DMA((4,)),
        ],
        space=pl.ANY,
    )
    tile = min(512, points)
    x, x_t = pl.pallas_call(
        functools.partial(inputs_kernel, hid, shapes),
        grid=(points // tile,),
        out_shape=[shape_of(points, lanes, BF16), shape_of(half + shapes, points, BF16)],
        in_specs=[
            pl.BlockSpec((tile, hid), lambda i: (i, 0)),
            pl.BlockSpec((half - hid, tile), lambda i: (0, i)),
            pl.BlockSpec((1, tile), lambda i: (0, i)),
            pl.BlockSpec((1, tile), lambda i: (0, i)),
        ],
        out_specs=vmem(2),
        compiler_params=pltpu.CompilerParams(
            dimension_semantics=("arbitrary",), vmem_limit_bytes=12 * MIB
        ),
        cost_estimate=pl.CostEstimate(
            flops=4000 * MIB, bytes_accessed=8 * points * half, transcendentals=0
        ),
        name="inputs",
    )(
        *[
            pltpu.with_memory_space_constraint(a, pltpu.HBM)
            for a in (
                hidden,
                offsets.T,
                shape_ids.reshape(1, points),
                scale_index.reshape(1, points),
            )
        ]
    )
    if tuned:
        for group in groups[:-1]:
            arrays = [held] + swaps([held] * (2 ** len(group) - 1), masks_of(group)[1:], devices)
            held = small_kernel(
                "join",
                join_kernel,
                shape_of(held.shape[0] * len(arrays), lanes + half, BF16),
                *arrays,
            )
        held, x, x_t = lax.optimization_barrier((held, x, x_t))
        last_masks = masks_of(groups[-1])
        pieces = [held] + swaps([held] * (len(last_masks) - 1), last_masks[1:], devices)
        orders = [[m ^ r for r in order_of(groups[:-1])] for m in last_masks]
        parts = orders
    else:
        pieces, orders, parts = [lax.all_gather(held, AXES, axis=0, tiled=True)], None, [[0]]

    output, grad_hidden, *grads = pl.pallas_call(
        functools.partial(layer_kernel, hid, shapes, tile, orders, parts),
        out_shape=[pltpu.HBM((points, width), F32), pltpu.HBM((points, hid), F32)]
        + [shape_of(4 * shapes + width // len(parts), half, BF16)] * len(parts),
        in_specs=vmem(len(pieces) + 3),
        out_specs=[pl.BlockSpec(memory_space=pltpu.HBM)] * 2 + vmem(len(parts)),
        scratch_shapes=[
            VMEM((width, lanes), BF16),
            VMEM((half + shapes, width), F32),
            VMEM((width, half), F32),
            VMEM((points, width), F32),
            VMEM((points, hid), F32),
            pltpu.SemaphoreType.DMA((2, points // tile)),
        ],
        compiler_params=pltpu.CompilerParams(vmem_limit_bytes=20 * MIB),
        cost_estimate=pl.CostEstimate(
            flops=6 * points * width * cols,
            bytes_accessed=8 * points * (width + half),
            transcendentals=points * width,
        ),
        name="layer",
    )(*pieces, x, x_t, cotangent)

    if tuned:
        for r, group in enumerate(groups[::-1]):
            masks = masks_of(group)
            grads = [grads[0]] + swaps(grads[1:], masks[1:], devices)
            if r == len(groups) - 1:
                break
            n_out = len(masks_of(groups[-2 - r]))
            left = (grads[0].shape[0] - 4 * shapes) // n_out
            grads = small_kernel(
                "add",
                functools.partial(add_kernel, shapes, len(grads)),
                [shape_of(4 * shapes + left, half, BF16)] * n_out,
                *grads,
            )
    else:
        sums = lax.psum(grads[0][: 4 * shapes].astype(F32), AXES)
        high = sums.astype(BF16)
        own = lax.psum_scatter(grads[0][4 * shapes :].astype(F32), AXES, scatter_dimension=0, tiled=True)
        low = jnp.zeros((4 * shapes + rows, half), BF16).at[: 4 * shapes].set((sums - high).astype(BF16))
        grads = [jnp.concatenate([high, own.astype(BF16)], axis=0), low]
    grad_codes, grad_direction, grad_gain, grad_bias = small_kernel(
        "last",
        functools.partial(last_kernel, hid, shapes, orders, len(grads)),
        [
            shape_of(shapes, half, F32),
            shape_of(rows, cols, F32),
            shape_of(1, rows, F32),
            shape_of(1, rows, F32),
        ],
        *grads,
        direction,
        gain_row,
        codes,
        *pieces,
        scratch=[VMEM((width, half), BF16)],
    )

    total = float(points * devices)
    batch_mean = jnp.mean(codes, axis=0)
    batch_square = jnp.mean(codes * codes, axis=0)
    batch_var = (batch_square - batch_mean * batch_mean) * (total / (total - 1.0))
    new_mean = 0.9 * running_mean + 0.1 * batch_mean
    new_var = 0.9 * running_var + 0.1 * batch_var
    return (
        output,
        grad_hidden,
        grad_codes,
        grad_direction,
        grad_gain.reshape(rows),
        grad_bias.reshape(rows),
        new_mean,
        new_var,
    )


def solution(mesh):
    return jax.shard_map(
        per_device,
        mesh=mesh,
        in_specs=(
            P(("dp", "inner"), None),
            P(),
            P(("dp", "inner"), None),
            P(("dp", "inner")),
            P(("dp", "inner")),
            P(("dp", "inner"), None),
            P(("dp", "inner")),
            P(("dp", "inner")),
            P(("dp", "inner"), None),
            P(),
            P(),
        ),
        out_specs=(
            P(("dp", "inner"), None),
            P(("dp", "inner"), None),
            P(),
            P(("dp", "inner"), None),
            P(("dp", "inner")),
            P(("dp", "inner")),
            P(),
            P(),
        ),
        check_vma=False,
    )
```

```python
import functools

import jax
import jax.numpy as jnp
from jax import lax
from jax.experimental import pallas as pl
from jax.experimental.pallas import tpu as pltpu
from jax.sharding import PartitionSpec as P

AXES = ("dp", "inner")
LANES = 128
MIB = 1024 * 1024
F32 = jnp.float32
BF16 = jnp.bfloat16
VMEM = pltpu.VMEM
NT = (((1,), (1,)), ((), ()))


def dot(a, b, dims=(((1,), (0,)), ((), ()))):
    return lax.dot_general(a, b, dims, preferred_element_type=F32)


def vmem(n):
    return [pl.BlockSpec(memory_space=VMEM)] * n


def small_kernel(name, body, out_shape, *args, scratch=(), space=VMEM, limit=8):
    many = isinstance(out_shape, list)
    return pl.pallas_call(
        body,
        out_shape=out_shape,
        in_specs=[pl.BlockSpec(memory_space=space)] * len(args),
        out_specs=vmem(len(out_shape)) if many else vmem(1)[0],
        scratch_shapes=list(scratch),
        compiler_params=pltpu.CompilerParams(vmem_limit_bytes=limit * MIB),
        cost_estimate=pl.CostEstimate(
            flops=4000 * MIB, bytes_accessed=8 * MIB, transcendentals=4 * MIB
        ),
        name=name,
    )(*args)


def diagonal(n):
    return lax.broadcasted_iota(jnp.int32, (n, n), 0) == lax.broadcasted_iota(jnp.int32, (n, n), 1)


def to_column(row):
    n = row.shape[1]
    return jnp.sum(jnp.where(diagonal(n), row, 0.0), axis=1, keepdims=True)


def to_row(column):
    n = column.shape[0]
    return jnp.sum(jnp.where(diagonal(n), column, 0.0), axis=0, keepdims=True)


def stacked_codes(codes_ref, count):
    codes = codes_ref[...].astype(BF16)
    parts = [codes, codes]
    if count > 2 * codes.shape[0]:
        parts.append(jnp.zeros((count - 2 * codes.shape[0], codes.shape[1]), BF16))
    return jnp.concatenate(parts, axis=0)


def split(x):
    high = x.astype(BF16).astype(F32)
    return high, x - high


def prep_kernel(hid, *refs):
    piece_ref, direction_ref, gain_ref, bias_ref, codes_ref, sems = refs[4:]
    copies = [
        pltpu.make_async_copy(source, target, sems.at[k])
        for k, (source, target) in enumerate(zip(refs[:4], refs[5:9]))
    ]
    for copy in copies:
        copy.start()
    for copy in copies:
        copy.wait()
    d = direction_ref[...]
    shapes = codes_ref.shape[0]
    rows, cols = d.shape
    half = cols // 2
    extra_lanes = piece_ref.shape[1] - cols
    inverse = lax.rsqrt(jnp.sum(d * d, axis=1, keepdims=True))
    w = to_column(gain_ref[...]) * (d * inverse)
    lane = lax.broadcasted_iota(jnp.int32, (rows, half), 1)
    first = jnp.where(lane < hid, w[:, :half], w[:, half:])
    code = pltpu.roll(w, half - hid, 1)[:, half:].astype(BF16)
    bias = to_column(bias_ref[...]).astype(BF16).astype(F32)
    high, low = split(dot(code, stacked_codes(codes_ref, extra_lanes), NT) + bias)
    own = first[:, half - LANES :]
    if extra_lanes > LANES:
        own = jnp.concatenate([jnp.zeros((rows, extra_lanes - LANES), F32), own], axis=1)
    lane = lax.broadcasted_iota(jnp.int32, (rows, extra_lanes), 1)
    table = jnp.where(lane < shapes, high, jnp.where(lane < 2 * shapes, low, 0.0))
    table = jnp.where(lane >= extra_lanes - (half - hid), own, table)
    piece_ref[:, :half] = first.astype(BF16)
    piece_ref[:, half : half + extra_lanes] = table.astype(BF16)
    piece_ref[:, half + extra_lanes :] = code


def join_kernel(*refs):
    rows = refs[0].shape[0]
    for k, ref in enumerate(refs[-2::-1]):
        refs[-1][k * rows : (k + 1) * rows, :] = ref[...]


def place(refs, orders, me, lane, out_ref):
    lanes = out_ref.shape[1]
    if orders is None:
        out_ref[...] = refs[0][:, lane : lane + lanes]
        return
    rows = refs[0].shape[0] // len(orders[0])
    for ref, order in zip(refs, orders):
        for k, mask in enumerate(order):
            at = pl.multiple_of((me ^ mask) * rows, rows)
            out_ref[pl.ds(at, rows), :] = ref[k * rows : (k + 1) * rows, lane : lane + lanes]


def inputs_kernel(hid, shapes, hidden_ref, offsets_ref, ids_ref, scale_ref, x_ref, x_t_ref):
    step = pl.program_id(0)
    tile = hidden_ref.shape[0]
    half = x_t_ref.shape[0] - shapes
    extra_lanes = x_ref.shape[1] - half
    here = pl.ds(pl.multiple_of(step * tile, tile), tile)
    scale = scale_ref[...]
    jitter = jnp.where(scale == 0, 1.0, jnp.where(scale == 1, 0.5, 0.25))
    xyz = offsets_ref[...] * jitter
    row = lax.broadcasted_iota(jnp.int32, (8, tile), 0)
    last = jnp.zeros((8, tile), F32)
    for k in range(half - hid):
        last = jnp.where(row == 8 - (half - hid) + k, xyz[k : k + 1], last)
    row = lax.broadcasted_iota(jnp.int32, (extra_lanes - 8, tile), 0)
    ids = ids_ref[...]
    member = jnp.where((row == ids) | (row == ids + shapes), 1.0, 0.0)
    extra = jnp.concatenate([member, last], axis=0).T
    x_ref[here, half - LANES : half] = jnp.zeros((tile, LANES), BF16)
    x_ref[here, :hid] = hidden_ref[...].astype(BF16)
    x_ref[here, half:] = extra.astype(BF16)
    hidden = x_ref[here, :half].astype(F32).T
    x = jnp.concatenate([hidden[: half - 8], hidden[half - 8 :] + last, member[:shapes]], axis=0)
    x_t_ref[:, here] = x.astype(BF16)


def layer_kernel(hid, shapes, tile, orders, parts, *refs):
    n = 1 if orders is None else len(orders)
    pieces = refs[:n]
    x_ref, x_t_ref, cot_ref, out_hbm, grad_hidden_hbm = refs[n : n + 5]
    grad_refs = refs[n + 5 : -6]
    w_ref, acc_ref, turned_ref, out_ref, grad_hidden_ref, sems = refs[-6:]
    points, width = cot_ref.shape
    half = width // 2
    me = lax.axis_index(AXES)
    place(pieces, orders, me, 0, w_ref)
    acc_ref[...] = jnp.zeros_like(acc_ref)

    def stores(step):
        here = pl.ds(pl.multiple_of(step * tile, tile), tile)
        return [
            pltpu.make_async_copy(source.at[here, :], target.at[here, :], sems.at[k, step])
            for k, (source, target) in enumerate(
                [(out_ref, out_hbm), (grad_hidden_ref, grad_hidden_hbm)]
            )
        ]

    def body(step, carry):
        here = pl.ds(pl.multiple_of(step * tile, tile), tile)
        pre = dot(x_ref[here, :], w_ref[...], NT)
        sigma = 0.5 * jnp.tanh(0.5 * pre) + 0.5
        out = pre * sigma
        out_ref[here, :] = out
        grad_pre = (cot_ref[here, :] * (sigma * (1.0 + (pre - out)))).astype(BF16)
        grad_hidden_ref[here, :] = dot(grad_pre, w_ref[:, :half])[:, :hid]
        for copy in stores(step):
            copy.start()
        acc_ref[...] += dot(x_t_ref[:, here], grad_pre)
        return carry

    lax.fori_loop(0, points // tile, body, 0)
    sums = jnp.concatenate(split(acc_ref[half:, :]), axis=0).astype(BF16)
    for at in range(0, width, half):
        turned_ref[at : at + half, :] = acc_ref[:half, at : at + half].T
    for ref, order in zip(grad_refs, parts):
        ref[: 2 * shapes, :] = sums[:, :half]
        ref[2 * shapes : 4 * shapes, :] = sums[:, half:]
        if orders is None:
            ref[4 * shapes :, :] = turned_ref[...].astype(BF16)
            continue
        rows = (ref.shape[0] - 4 * shapes) // len(order)
        for k, mask in enumerate(order):
            at = pl.multiple_of((me ^ mask) * rows, rows)
            to = 4 * shapes + k * rows
            ref[to : to + rows, :] = turned_ref[pl.ds(at, rows), :].astype(BF16)

    def finish(step, carry):
        for copy in stores(step):
            copy.wait()
        return carry

    lax.fori_loop(0, points // tile, finish, 0)


def sum_of(refs):
    terms = [ref[...].astype(F32) for ref in refs]
    while len(terms) > 1:
        terms = [a + b for a, b in zip(terms[::2], terms[1::2])]
    return terms[0]


def shape_sums(total, shapes):
    left = total[:shapes] + total[shapes : 2 * shapes]
    right = total[2 * shapes : 3 * shapes] + total[3 * shapes : 4 * shapes]
    return left, right


def add_kernel(shapes, n, *refs):
    total = sum_of(refs[:n])
    left, right = shape_sums(total, shapes)
    sums = jnp.concatenate(split(left) + split(right), axis=0).astype(BF16)
    for k, ref in enumerate(refs[n:]):
        rows = ref.shape[0] - 4 * shapes
        at = 4 * shapes + k * rows
        ref[: 4 * shapes, :] = sums
        ref[4 * shapes :, :] = total[at : at + rows].astype(BF16)


def last_kernel(hid, shapes, orders, n, *refs):
    direction_ref, gain_ref, codes_ref = refs[n : n + 3]
    pieces = refs[n + 3 : -5]
    grad_codes_ref, grad_direction_ref, grad_gain_ref, grad_bias_ref, code_scratch = refs[-5:]
    d = direction_ref[...]
    rows, cols = d.shape
    half = cols // 2
    me = lax.axis_index(AXES)
    place(pieces, orders, me, pieces[0].shape[1] - half, code_scratch)
    total = sum_of(refs[:n])
    sums = jnp.concatenate(shape_sums(total, shapes), axis=1)
    sums = jnp.concatenate(split(sums), axis=0).astype(BF16)
    terms = dot(sums, code_scratch[...])
    grad_codes_ref[...] = terms[:shapes] + terms[shapes:]
    width = sums.shape[1]
    mine = lax.broadcasted_iota(jnp.int32, (rows, width), 0) + me * rows
    mine = jnp.where(mine == lax.broadcasted_iota(jnp.int32, (rows, width), 1), 1.0, 0.0).astype(BF16)
    own = dot(mine, sums, NT)
    grad_bias_ref[...] = to_row(jnp.sum(own, axis=1, keepdims=True))
    code = dot(own.astype(BF16), stacked_codes(codes_ref, 2 * shapes))
    packed = jnp.concatenate([total[4 * shapes :], code], axis=1)
    lane = lax.broadcasted_iota(jnp.int32, (rows, cols), 1)
    grad_weight = jnp.where(
        lane < hid,
        packed,
        jnp.where(lane < hid + half, pltpu.roll(packed, cols - (half - hid), 1), pltpu.roll(packed, half, 1)),
    )
    inverse = lax.rsqrt(jnp.sum(d * d, axis=1, keepdims=True))
    unit = d * inverse
    grad_gain = jnp.sum(grad_weight * unit, axis=1, keepdims=True)
    grad_gain_ref[...] = to_row(grad_gain)
    grad_direction_ref[...] = (to_column(gain_ref[...]) * inverse) * (grad_weight - grad_gain * unit)


def masks_of(group):
    masks = [0]
    for bit in group:
        masks = masks + [m ^ bit for m in masks]
    return masks


def order_of(groups):
    order = [0]
    for group in groups:
        order = [m ^ r for m in masks_of(group) for r in order]
    return order


def swaps(arrays, masks, devices):
    moved = [
        lax.ppermute(x, AXES, [(i, i ^ mask) for i in range(devices)])
        for x, mask in list(zip(arrays, masks))[::-1]
    ]
    return moved[::-1]


def per_device(
    hidden,
    codes,
    offsets,
    shape_ids,
    scale_index,
    direction,
    gain,
    bias,
    cotangent,
    running_mean,
    running_var,
):
    points, hid = hidden.shape
    shapes = codes.shape[0]
    rows, cols = direction.shape
    width = cotangent.shape[1]
    half = cols // 2
    devices = lax.axis_size("dp") * lax.axis_size("inner")
    tuned = rows % 16 == 0
    bits = [1 << k for k in range(devices.bit_length() - 1)]
    groups = [bits[k - 2 : k] for k in range(len(bits), 1, -2)]
    groups = groups + [bits[:1]] * (len(bits) % 2)
    tuned = rows % 16 == 0
    extra_lanes = -(-(2 * shapes + 8) // LANES) * LANES
    lanes = half + extra_lanes
    gain_row = gain.reshape(1, rows)

    def shape_of(rows, lanes, dtype):
        return jax.ShapeDtypeStruct((rows, lanes), dtype)

    held = small_kernel(
        "prep",
        functools.partial(prep_kernel, hid),
        shape_of(rows, lanes + half, BF16),
        *[
            pltpu.with_memory_space_constraint(x, pltpu.HBM)
            for x in (direction, gain_row, bias.reshape(1, rows), codes)
        ],
        scratch=[
            VMEM((rows, cols), F32),
            VMEM((1, rows), F32),
            VMEM((1, rows), F32),
            VMEM((shapes, half), F32),
            pltpu.SemaphoreType.DMA((4,)),
        ],
        space=pl.ANY,
    )
    tile = min(512, points)
    x, x_t = pl.pallas_call(
        functools.partial(inputs_kernel, hid, shapes),
        grid=(points // tile,),
        out_shape=[shape_of(points, lanes, BF16), shape_of(half + shapes, points, BF16)],
        in_specs=[
            pl.BlockSpec((tile, hid), lambda i: (i, 0)),
            pl.BlockSpec((half - hid, tile), lambda i: (0, i)),
            pl.BlockSpec((1, tile), lambda i: (0, i)),
            pl.BlockSpec((1, tile), lambda i: (0, i)),
        ],
        out_specs=vmem(2),
        compiler_params=pltpu.CompilerParams(
            dimension_semantics=("arbitrary",), vmem_limit_bytes=12 * MIB
        ),
        cost_estimate=pl.CostEstimate(
            flops=4000 * MIB, bytes_accessed=8 * points * half, transcendentals=0
        ),
        name="inputs",
    )(
        *[
            pltpu.with_memory_space_constraint(a, pltpu.HBM)
            for a in (
                hidden,
                offsets.T,
                shape_ids.reshape(1, points),
                scale_index.reshape(1, points),
            )
        ]
    )
    if tuned:
        for group in groups[:-1]:
            arrays = [held] + swaps([held] * (2 ** len(group) - 1), masks_of(group)[1:], devices)
            held = small_kernel(
                "join",
                join_kernel,
                shape_of(held.shape[0] * len(arrays), lanes + half, BF16),
                *arrays[::-1],
            )
        held, x, x_t = lax.optimization_barrier((held, x, x_t))
        last_masks = masks_of(groups[-1])
        pieces = [held] + swaps([held] * (len(last_masks) - 1), last_masks[1:], devices)
        orders = [[m ^ r for r in order_of(groups[:-1])] for m in last_masks]
        parts = orders
    else:
        pieces, orders, parts = [lax.all_gather(held, AXES, axis=0, tiled=True)], None, [[0]]

    output, grad_hidden, *grads = pl.pallas_call(
        functools.partial(layer_kernel, hid, shapes, tile, orders, parts),
        out_shape=[pltpu.HBM((points, width), F32), pltpu.HBM((points, hid), F32)]
        + [shape_of(4 * shapes + width // len(parts), half, BF16)] * len(parts),
        in_specs=vmem(len(pieces) + 3),
        out_specs=[pl.BlockSpec(memory_space=pltpu.HBM)] * 2 + vmem(len(parts)),
        scratch_shapes=[
            VMEM((width, lanes), BF16),
            VMEM((half + shapes, width), F32),
            VMEM((width, half), F32),
            VMEM((points, width), F32),
            VMEM((points, hid), F32),
            pltpu.SemaphoreType.DMA((2, points // tile)),
        ],
        compiler_params=pltpu.CompilerParams(vmem_limit_bytes=20 * MIB),
        cost_estimate=pl.CostEstimate(
            flops=6 * points * width * cols,
            bytes_accessed=8 * points * (width + half),
            transcendentals=points * width,
        ),
        name="layer",
    )(*pieces, x, x_t, cotangent)

    if tuned:
        for r, group in enumerate(groups[::-1]):
            masks = masks_of(group)
            grads = [grads[0]] + swaps(grads[1:], masks[1:], devices)
            if r == len(groups) - 1:
                break
            n_out = len(masks_of(groups[-2 - r]))
            left = (grads[0].shape[0] - 4 * shapes) // n_out
            grads = small_kernel(
                "add",
                functools.partial(add_kernel, shapes, len(grads)),
                [shape_of(4 * shapes + left, half, BF16)] * n_out,
                *grads,
            )
    else:
        sums = lax.psum(grads[0][: 4 * shapes].astype(F32), AXES)
        high = sums.astype(BF16)
        own = lax.psum_scatter(grads[0][4 * shapes :].astype(F32), AXES, scatter_dimension=0, tiled=True)
        low = jnp.zeros((4 * shapes + rows, half), BF16).at[: 4 * shapes].set((sums - high).astype(BF16))
        grads = [jnp.concatenate([high, own.astype(BF16)], axis=0), low]
    grad_codes, grad_direction, grad_gain, grad_bias = small_kernel(
        "last",
        functools.partial(last_kernel, hid, shapes, orders, len(grads)),
        [
            shape_of(shapes, half, F32),
            shape_of(rows, cols, F32),
            shape_of(1, rows, F32),
            shape_of(1, rows, F32),
        ],
        *grads[::-1],
        direction,
        gain_row,
        codes,
        *pieces,
        scratch=[VMEM((width, half), BF16)],
    )

    total = float(points * devices)
    batch_mean = jnp.mean(codes, axis=0)
    batch_square = jnp.mean(codes * codes, axis=0)
    batch_var = (batch_square - batch_mean * batch_mean) * (total / (total - 1.0))
    new_mean = 0.9 * running_mean + 0.1 * batch_mean
    new_var = 0.9 * running_var + 0.1 * batch_var
    return (
        output,
        grad_hidden,
        grad_codes,
        grad_direction,
        grad_gain.reshape(rows),
        grad_bias.reshape(rows),
        new_mean,
        new_var,
    )


def solution(mesh):
    return jax.shard_map(
        per_device,
        mesh=mesh,
        in_specs=(
            P(("dp", "inner"), None),
            P(),
            P(("dp", "inner"), None),
            P(("dp", "inner")),
            P(("dp", "inner")),
            P(("dp", "inner"), None),
            P(("dp", "inner")),
            P(("dp", "inner")),
            P(("dp", "inner"), None),
            P(),
            P(),
        ),
        out_specs=(
            P(("dp", "inner"), None),
            P(("dp", "inner"), None),
            P(),
            P(("dp", "inner"), None),
            P(("dp", "inner")),
            P(("dp", "inner")),
            P(),
            P(),
        ),
        check_vma=False,
    )
```

```python
import functools

import jax
import jax.numpy as jnp
from jax import lax
from jax.experimental import pallas as pl
from jax.experimental.pallas import tpu as pltpu
from jax.sharding import PartitionSpec as P

AXES = ("dp", "inner")
LANES = 128
MIB = 1024 * 1024
F32 = jnp.float32
BF16 = jnp.bfloat16
VMEM = pltpu.VMEM
NT = (((1,), (1,)), ((), ()))


def dot(a, b, dims=(((1,), (0,)), ((), ()))):
    return lax.dot_general(a, b, dims, preferred_element_type=F32)


def vmem(n):
    return [pl.BlockSpec(memory_space=VMEM)] * n


def small_kernel(name, body, out_shape, *args, scratch=(), space=VMEM, limit=8):
    many = isinstance(out_shape, list)
    return pl.pallas_call(
        body,
        out_shape=out_shape,
        in_specs=[pl.BlockSpec(memory_space=space)] * len(args),
        out_specs=vmem(len(out_shape)) if many else vmem(1)[0],
        scratch_shapes=list(scratch),
        compiler_params=pltpu.CompilerParams(vmem_limit_bytes=limit * MIB),
        cost_estimate=pl.CostEstimate(
            flops=4000 * MIB, bytes_accessed=8 * MIB, transcendentals=4 * MIB
        ),
        name=name,
    )(*args)


def diagonal(n):
    return lax.broadcasted_iota(jnp.int32, (n, n), 0) == lax.broadcasted_iota(jnp.int32, (n, n), 1)


def to_column(row):
    n = row.shape[1]
    return jnp.sum(jnp.where(diagonal(n), row, 0.0), axis=1, keepdims=True)


def to_row(column):
    n = column.shape[0]
    return jnp.sum(jnp.where(diagonal(n), column, 0.0), axis=0, keepdims=True)


def stacked_codes(codes_ref, count):
    codes = codes_ref[...].astype(BF16)
    parts = [codes, codes]
    if count > 2 * codes.shape[0]:
        parts.append(jnp.zeros((count - 2 * codes.shape[0], codes.shape[1]), BF16))
    return jnp.concatenate(parts, axis=0)


def split(x):
    high = x.astype(BF16).astype(F32)
    return high, x - high


def prep_kernel(hid, *refs):
    piece_ref, direction_ref, gain_ref, bias_ref, codes_ref, sems = refs[4:]
    copies = [
        pltpu.make_async_copy(source, target, sems.at[k])
        for k, (source, target) in enumerate(zip(refs[:4], refs[5:9]))
    ]
    for copy in copies:
        copy.start()
    for copy in copies:
        copy.wait()
    d = direction_ref[...]
    shapes = codes_ref.shape[0]
    rows, cols = d.shape
    half = cols // 2
    extra_lanes = piece_ref.shape[1] - cols
    inverse = lax.rsqrt(jnp.sum(d * d, axis=1, keepdims=True))
    w = to_column(gain_ref[...]) * (d * inverse)
    lane = lax.broadcasted_iota(jnp.int32, (rows, half), 1)
    first = jnp.where(lane < hid, w[:, :half], w[:, half:])
    code = pltpu.roll(w, half - hid, 1)[:, half:].astype(BF16)
    bias = to_column(bias_ref[...]).astype(BF16).astype(F32)
    high, low = split(dot(code, stacked_codes(codes_ref, extra_lanes), NT) + bias)
    own = first[:, half - LANES :]
    if extra_lanes > LANES:
        own = jnp.concatenate([jnp.zeros((rows, extra_lanes - LANES), F32), own], axis=1)
    lane = lax.broadcasted_iota(jnp.int32, (rows, extra_lanes), 1)
    table = jnp.where(lane < shapes, high, jnp.where(lane < 2 * shapes, low, 0.0))
    table = jnp.where(lane >= extra_lanes - (half - hid), own, table)
    piece_ref[:, :half] = first.astype(BF16)
    piece_ref[:, half : half + extra_lanes] = table.astype(BF16)
    piece_ref[:, half + extra_lanes :] = code


def join_kernel(*refs):
    rows = refs[0].shape[0]
    for k, ref in enumerate(refs[-2::-1]):
        refs[-1][k * rows : (k + 1) * rows, :] = ref[...]


def place(refs, orders, me, lane, out_ref):
    lanes = out_ref.shape[1]
    if orders is None:
        out_ref[...] = refs[0][:, lane : lane + lanes]
        return
    rows = refs[0].shape[0] // len(orders[0])
    for ref, order in zip(refs, orders):
        for k, mask in enumerate(order):
            at = pl.multiple_of((me ^ mask) * rows, rows)
            out_ref[pl.ds(at, rows), :] = ref[k * rows : (k + 1) * rows, lane : lane + lanes]


def inputs_kernel(hid, shapes, hidden_ref, offsets_ref, ids_ref, scale_ref, x_ref, x_t_ref):
    step = pl.program_id(0)
    tile = hidden_ref.shape[0]
    half = x_t_ref.shape[0] - shapes
    extra_lanes = x_ref.shape[1] - half
    here = pl.ds(pl.multiple_of(step * tile, tile), tile)
    scale = scale_ref[...]
    jitter = jnp.where(scale == 0, 1.0, jnp.where(scale == 1, 0.5, 0.25))
    xyz = offsets_ref[...] * jitter
    row = lax.broadcasted_iota(jnp.int32, (16, tile), 0)
    last = jnp.zeros((16, tile), F32)
    for k in range(half - hid):
        last = jnp.where(row == 16 - (half - hid) + k, xyz[k : k + 1], last)
    last = last.astype(BF16)
    row = lax.broadcasted_iota(jnp.int32, (extra_lanes - 16, tile), 0)
    ids = ids_ref[...]
    member = jnp.where((row == ids) | (row == ids + shapes), 1.0, 0.0).astype(BF16)
    x_ref[here, half - LANES : half] = jnp.zeros((tile, LANES), BF16)
    x_ref[here, :hid] = hidden_ref[...].astype(BF16)
    x_ref[here, half:] = jnp.concatenate([member, last], axis=0).T
    hidden = x_ref[here, :half].T
    x_t_ref[: half - 16, here] = hidden[: half - 16]
    x_t_ref[half - 16 : half, here] = hidden[half - 16 :] + last
    x_t_ref[half:, here] = member[:shapes]


def layer_kernel(hid, shapes, tile, orders, parts, *refs):
    n = 1 if orders is None else len(orders)
    pieces = refs[:n]
    x_ref, x_t_ref, cot_ref, out_hbm, grad_hidden_hbm = refs[n : n + 5]
    grad_refs = refs[n + 5 : -6]
    w_ref, acc_ref, turned_ref, out_ref, grad_hidden_ref, sems = refs[-6:]
    points, width = cot_ref.shape
    half = width // 2
    me = lax.axis_index(AXES)
    place(pieces, orders, me, 0, w_ref)
    acc_ref[...] = jnp.zeros_like(acc_ref)

    def stores(step):
        here = pl.ds(pl.multiple_of(step * tile, tile), tile)
        return [
            pltpu.make_async_copy(source.at[here, :], target.at[here, :], sems.at[k, step])
            for k, (source, target) in enumerate(
                [(out_ref, out_hbm), (grad_hidden_ref, grad_hidden_hbm)]
            )
        ]

    def body(step, carry):
        here = pl.ds(pl.multiple_of(step * tile, tile), tile)
        pre = dot(x_ref[here, :], w_ref[...], NT)
        sigma = 0.5 * jnp.tanh(0.5 * pre) + 0.5
        out = pre * sigma
        out_ref[here, :] = out
        grad_pre = (cot_ref[here, :] * (sigma * (1.0 + (pre - out)))).astype(BF16)
        grad_hidden_ref[here, :] = dot(grad_pre, w_ref[:, :half])[:, :hid]
        for copy in stores(step):
            copy.start()
        acc_ref[...] += dot(x_t_ref[:, here], grad_pre)
        return carry

    lax.fori_loop(0, points // tile, body, 0)
    sums = jnp.concatenate(split(acc_ref[half:, :]), axis=0).astype(BF16)
    for at in range(0, width, half):
        turned_ref[at : at + half, :] = acc_ref[:half, at : at + half].T
    for ref, order in zip(grad_refs, parts):
        ref[: 2 * shapes, :] = sums[:, :half]
        ref[2 * shapes : 4 * shapes, :] = sums[:, half:]
        if orders is None:
            ref[4 * shapes :, :] = turned_ref[...].astype(BF16)
            continue
        rows = (ref.shape[0] - 4 * shapes) // len(order)
        for k, mask in enumerate(order):
            at = pl.multiple_of((me ^ mask) * rows, rows)
            to = 4 * shapes + k * rows
            ref[to : to + rows, :] = turned_ref[pl.ds(at, rows), :].astype(BF16)

    def finish(step, carry):
        for copy in stores(step):
            copy.wait()
        return carry

    lax.fori_loop(0, points // tile, finish, 0)


def sum_of(refs):
    terms = [ref[...].astype(F32) for ref in refs]
    while len(terms) > 1:
        terms = [a + b for a, b in zip(terms[::2], terms[1::2])]
    return terms[0]


def shape_sums(total, shapes):
    left = total[:shapes] + total[shapes : 2 * shapes]
    right = total[2 * shapes : 3 * shapes] + total[3 * shapes : 4 * shapes]
    return left, right


def add_kernel(shapes, n, *refs):
    total = sum_of(refs[:n])
    left, right = shape_sums(total, shapes)
    sums = jnp.concatenate(split(left) + split(right), axis=0).astype(BF16)
    for k, ref in enumerate(refs[n:]):
        rows = ref.shape[0] - 4 * shapes
        at = 4 * shapes + k * rows
        ref[: 4 * shapes, :] = sums
        ref[4 * shapes :, :] = total[at : at + rows].astype(BF16)


def last_kernel(hid, shapes, orders, n, *refs):
    direction_ref, gain_ref, codes_ref = refs[n : n + 3]
    pieces = refs[n + 3 : -5]
    grad_codes_ref, grad_direction_ref, grad_gain_ref, grad_bias_ref, code_scratch = refs[-5:]
    d = direction_ref[...]
    rows, cols = d.shape
    half = cols // 2
    me = lax.axis_index(AXES)
    place(pieces, orders, me, pieces[0].shape[1] - half, code_scratch)
    total = sum_of(refs[:n])
    sums = jnp.concatenate(shape_sums(total, shapes), axis=1)
    sums = jnp.concatenate(split(sums), axis=0).astype(BF16)
    terms = dot(sums, code_scratch[...])
    grad_codes_ref[...] = terms[:shapes] + terms[shapes:]
    width = sums.shape[1]
    mine = lax.broadcasted_iota(jnp.int32, (rows, width), 0) + me * rows
    mine = jnp.where(mine == lax.broadcasted_iota(jnp.int32, (rows, width), 1), 1.0, 0.0).astype(BF16)
    own = dot(mine, sums, NT)
    grad_bias_ref[...] = to_row(jnp.sum(own, axis=1, keepdims=True))
    code = dot(own.astype(BF16), stacked_codes(codes_ref, 2 * shapes))
    packed = jnp.concatenate([total[4 * shapes :], code], axis=1)
    lane = lax.broadcasted_iota(jnp.int32, (rows, cols), 1)
    grad_weight = jnp.where(
        lane < hid,
        packed,
        jnp.where(lane < hid + half, pltpu.roll(packed, cols - (half - hid), 1), pltpu.roll(packed, half, 1)),
    )
    inverse = lax.rsqrt(jnp.sum(d * d, axis=1, keepdims=True))
    unit = d * inverse
    grad_gain = jnp.sum(grad_weight * unit, axis=1, keepdims=True)
    grad_gain_ref[...] = to_row(grad_gain)
    grad_direction_ref[...] = (to_column(gain_ref[...]) * inverse) * (grad_weight - grad_gain * unit)


def masks_of(group):
    masks = [0]
    for bit in group:
        masks = masks + [m ^ bit for m in masks]
    return masks


def order_of(groups):
    order = [0]
    for group in groups:
        order = [m ^ r for m in masks_of(group) for r in order]
    return order


def swaps(arrays, masks, devices):
    moved = [
        lax.ppermute(x, AXES, [(i, i ^ mask) for i in range(devices)])
        for x, mask in list(zip(arrays, masks))[::-1]
    ]
    return moved[::-1]


def per_device(
    hidden,
    codes,
    offsets,
    shape_ids,
    scale_index,
    direction,
    gain,
    bias,
    cotangent,
    running_mean,
    running_var,
):
    points, hid = hidden.shape
    shapes = codes.shape[0]
    rows, cols = direction.shape
    width = cotangent.shape[1]
    half = cols // 2
    devices = lax.axis_size("dp") * lax.axis_size("inner")
    tuned = rows % 16 == 0
    bits = [1 << k | 1 for k in range(devices.bit_length() - 1)]
    groups = [bits[k - 2 : k] for k in range(len(bits), 1, -2)]
    groups = groups + [bits[:1]] * (len(bits) % 2)
    tuned = rows % 16 == 0
    extra_lanes = -(-(2 * shapes + 16) // LANES) * LANES
    lanes = half + extra_lanes
    gain_row = gain.reshape(1, rows)

    def shape_of(rows, lanes, dtype):
        return jax.ShapeDtypeStruct((rows, lanes), dtype)

    held = small_kernel(
        "prep",
        functools.partial(prep_kernel, hid),
        shape_of(rows, lanes + half, BF16),
        *[
            pltpu.with_memory_space_constraint(x, pltpu.HBM)
            for x in (direction, gain_row, bias.reshape(1, rows), codes)
        ],
        scratch=[
            VMEM((rows, cols), F32),
            VMEM((1, rows), F32),
            VMEM((1, rows), F32),
            VMEM((shapes, half), F32),
            pltpu.SemaphoreType.DMA((4,)),
        ],
        space=pl.ANY,
    )
    tile = min(512, points)
    x, x_t = pl.pallas_call(
        functools.partial(inputs_kernel, hid, shapes),
        grid=(points // tile,),
        out_shape=[shape_of(points, lanes, BF16), shape_of(half + shapes, points, BF16)],
        in_specs=[
            pl.BlockSpec((tile, hid), lambda i: (i, 0)),
            pl.BlockSpec((half - hid, tile), lambda i: (0, i)),
            pl.BlockSpec((1, tile), lambda i: (0, i)),
            pl.BlockSpec((1, tile), lambda i: (0, i)),
        ],
        out_specs=vmem(2),
        compiler_params=pltpu.CompilerParams(
            dimension_semantics=("arbitrary",), vmem_limit_bytes=12 * MIB
        ),
        cost_estimate=pl.CostEstimate(
            flops=4000 * MIB, bytes_accessed=8 * points * half, transcendentals=0
        ),
        name="inputs",
    )(
        *[
            pltpu.with_memory_space_constraint(a, pltpu.HBM)
            for a in (
                hidden,
                offsets.T,
                shape_ids.reshape(1, points),
                scale_index.reshape(1, points),
            )
        ]
    )
    if tuned:
        for group in groups[:-1]:
            arrays = [held] + swaps([held] * (2 ** len(group) - 1), masks_of(group)[1:], devices)
            held = small_kernel(
                "join",
                join_kernel,
                shape_of(held.shape[0] * len(arrays), lanes + half, BF16),
                *arrays[::-1],
            )
        held, x, x_t = lax.optimization_barrier((held, x, x_t))
        last_masks = masks_of(groups[-1])
        pieces = [held] + swaps([held] * (len(last_masks) - 1), last_masks[1:], devices)
        orders = [[m ^ r for r in order_of(groups[:-1])] for m in last_masks]
        parts = orders
    else:
        pieces, orders, parts = [lax.all_gather(held, AXES, axis=0, tiled=True)], None, [[0]]

    output, grad_hidden, *grads = pl.pallas_call(
        functools.partial(layer_kernel, hid, shapes, tile, orders, parts),
        out_shape=[pltpu.HBM((points, width), F32), pltpu.HBM((points, hid), F32)]
        + [shape_of(4 * shapes + width // len(parts), half, BF16)] * len(parts),
        in_specs=vmem(len(pieces) + 3),
        out_specs=[pl.BlockSpec(memory_space=pltpu.HBM)] * 2 + vmem(len(parts)),
        scratch_shapes=[
            VMEM((width, lanes), BF16),
            VMEM((half + shapes, width), F32),
            VMEM((width, half), F32),
            VMEM((points, width), F32),
            VMEM((points, hid), F32),
            pltpu.SemaphoreType.DMA((2, points // tile)),
        ],
        compiler_params=pltpu.CompilerParams(vmem_limit_bytes=20 * MIB),
        cost_estimate=pl.CostEstimate(
            flops=6 * points * width * cols,
            bytes_accessed=8 * points * (width + half),
            transcendentals=points * width,
        ),
        name="layer",
    )(*pieces, x, x_t, cotangent)

    if tuned:
        for r, group in enumerate(groups[::-1]):
            masks = masks_of(group)
            grads = [grads[0]] + swaps(grads[1:], masks[1:], devices)
            if r == len(groups) - 1:
                break
            n_out = len(masks_of(groups[-2 - r]))
            left = (grads[0].shape[0] - 4 * shapes) // n_out
            grads = small_kernel(
                "add",
                functools.partial(add_kernel, shapes, len(grads)),
                [shape_of(4 * shapes + left, half, BF16)] * n_out,
                *grads,
            )
    else:
        sums = lax.psum(grads[0][: 4 * shapes].astype(F32), AXES)
        high = sums.astype(BF16)
        own = lax.psum_scatter(grads[0][4 * shapes :].astype(F32), AXES, scatter_dimension=0, tiled=True)
        low = jnp.zeros((4 * shapes + rows, half), BF16).at[: 4 * shapes].set((sums - high).astype(BF16))
        grads = [jnp.concatenate([high, own.astype(BF16)], axis=0), low]
    grad_codes, grad_direction, grad_gain, grad_bias = small_kernel(
        "last",
        functools.partial(last_kernel, hid, shapes, orders, len(grads)),
        [
            shape_of(shapes, half, F32),
            shape_of(rows, cols, F32),
            shape_of(1, rows, F32),
            shape_of(1, rows, F32),
        ],
        *grads[::-1],
        direction,
        gain_row,
        codes,
        *pieces,
        scratch=[VMEM((width, half), BF16)],
    )

    total = float(points * devices)
    batch_mean = jnp.mean(codes, axis=0)
    batch_square = jnp.mean(codes * codes, axis=0)
    batch_var = (batch_square - batch_mean * batch_mean) * (total / (total - 1.0))
    new_mean = 0.9 * running_mean + 0.1 * batch_mean
    new_var = 0.9 * running_var + 0.1 * batch_var
    return (
        output,
        grad_hidden,
        grad_codes,
        grad_direction,
        grad_gain.reshape(rows),
        grad_bias.reshape(rows),
        new_mean,
        new_var,
    )


def solution(mesh):
    return jax.shard_map(
        per_device,
        mesh=mesh,
        in_specs=(
            P(("dp", "inner"), None),
            P(),
            P(("dp", "inner"), None),
            P(("dp", "inner")),
            P(("dp", "inner")),
            P(("dp", "inner"), None),
            P(("dp", "inner")),
            P(("dp", "inner")),
            P(("dp", "inner"), None),
            P(),
            P(),
        ),
        out_specs=(
            P(("dp", "inner"), None),
            P(("dp", "inner"), None),
            P(),
            P(("dp", "inner"), None),
            P(("dp", "inner")),
            P(("dp", "inner")),
            P(),
            P(),
        ),
        check_vma=False,
    )
```

```python
import functools

import jax
import jax.numpy as jnp
from jax import lax
from jax.experimental import pallas as pl
from jax.experimental.pallas import tpu as pltpu
from jax.sharding import PartitionSpec as P

AXES = ("dp", "inner")
LANES = 128
MIB = 1024 * 1024
F32 = jnp.float32
BF16 = jnp.bfloat16
VMEM = pltpu.VMEM
NT = (((1,), (1,)), ((), ()))


def dot(a, b, dims=(((1,), (0,)), ((), ()))):
    return lax.dot_general(a, b, dims, preferred_element_type=F32)


def vmem(n):
    return [pl.BlockSpec(memory_space=VMEM)] * n


def small_kernel(name, body, out_shape, *args, scratch=(), space=VMEM, limit=8):
    many = isinstance(out_shape, list)
    return pl.pallas_call(
        body,
        out_shape=out_shape,
        in_specs=[pl.BlockSpec(memory_space=space)] * len(args),
        out_specs=vmem(len(out_shape)) if many else vmem(1)[0],
        scratch_shapes=list(scratch),
        compiler_params=pltpu.CompilerParams(vmem_limit_bytes=limit * MIB),
        cost_estimate=pl.CostEstimate(
            flops=4000 * MIB, bytes_accessed=8 * MIB, transcendentals=4 * MIB
        ),
        name=name,
    )(*args)


def diagonal(n):
    return lax.broadcasted_iota(jnp.int32, (n, n), 0) == lax.broadcasted_iota(jnp.int32, (n, n), 1)


def to_column(row):
    n = row.shape[1]
    return jnp.sum(jnp.where(diagonal(n), row, 0.0), axis=1, keepdims=True)


def to_row(column):
    n = column.shape[0]
    return jnp.sum(jnp.where(diagonal(n), column, 0.0), axis=0, keepdims=True)


def stacked_codes(codes_ref, count):
    codes = codes_ref[...].astype(BF16)
    parts = [codes, codes]
    if count > 2 * codes.shape[0]:
        parts.append(jnp.zeros((count - 2 * codes.shape[0], codes.shape[1]), BF16))
    return jnp.concatenate(parts, axis=0)


def split(x):
    high = x.astype(BF16).astype(F32)
    return high, x - high


def prep_kernel(hid, *refs):
    piece_ref, direction_ref, gain_ref, bias_ref, codes_ref, sems = refs[4:]
    copies = [
        pltpu.make_async_copy(source, target, sems.at[k])
        for k, (source, target) in enumerate(zip(refs[:4], refs[5:9]))
    ]
    for copy in copies:
        copy.start()
    for copy in copies:
        copy.wait()
    d = direction_ref[...]
    shapes = codes_ref.shape[0]
    rows, cols = d.shape
    half = cols // 2
    extra_lanes = piece_ref.shape[1] - cols
    inverse = lax.rsqrt(jnp.sum(d * d, axis=1, keepdims=True))
    w = to_column(gain_ref[...]) * (d * inverse)
    lane = lax.broadcasted_iota(jnp.int32, (rows, half), 1)
    first = jnp.where(lane < hid, w[:, :half], w[:, half:])
    code = pltpu.roll(w, half - hid, 1)[:, half:].astype(BF16)
    bias = to_column(bias_ref[...]).astype(BF16).astype(F32)
    high, low = split(dot(code, stacked_codes(codes_ref, extra_lanes), NT) + bias)
    own = first[:, half - LANES :]
    if extra_lanes > LANES:
        own = jnp.concatenate([jnp.zeros((rows, extra_lanes - LANES), F32), own], axis=1)
    lane = lax.broadcasted_iota(jnp.int32, (rows, extra_lanes), 1)
    table = jnp.where(lane < shapes, high, jnp.where(lane < 2 * shapes, low, 0.0))
    table = jnp.where(lane >= extra_lanes - (half - hid), own, table)
    piece_ref[:, :half] = first.astype(BF16)
    piece_ref[:, half : half + extra_lanes] = table.astype(BF16)
    piece_ref[:, half + extra_lanes :] = code


def join_kernel(*refs):
    rows = refs[0].shape[0]
    for k, ref in enumerate(refs[-2::-1]):
        refs[-1][k * rows : (k + 1) * rows, :] = ref[...]


def place(refs, orders, me, lane, out_ref):
    lanes = out_ref.shape[1]
    if orders is None:
        out_ref[...] = refs[0][:, lane : lane + lanes]
        return
    rows = refs[0].shape[0] // len(orders[0])
    for ref, order in zip(refs, orders):
        for k, mask in enumerate(order):
            at = pl.multiple_of((me ^ mask) * rows, rows)
            out_ref[pl.ds(at, rows), :] = ref[k * rows : (k + 1) * rows, lane : lane + lanes]


def inputs_kernel(hid, tile, *refs):
    x_ref, x_t_ref, hidden_ref, offsets_ref, ids_ref, scale_ref, sems = refs[4:]
    points = x_ref.shape[0]
    half = (hid + LANES - 1) // LANES * LANES
    shapes = x_t_ref.shape[0] - half
    extra_lanes = x_ref.shape[1] - half
    steps = points // tile
    small = [
        pltpu.make_async_copy(source, target, sems.at[steps + k])
        for k, (source, target) in enumerate(zip(refs[1:4], (offsets_ref, ids_ref, scale_ref)))
    ]
    large = [
        pltpu.make_async_copy(
            refs[0].at[pl.ds(k * tile, tile), :], hidden_ref.at[pl.ds(k * tile, tile), :], sems.at[k]
        )
        for k in range(steps)
    ]
    for copy in small + large:
        copy.start()
    for copy in small:
        copy.wait()
    for step, copy in enumerate(large):
        here = slice(step * tile, (step + 1) * tile)
        scale = scale_ref[:, here]
        jitter = jnp.where(scale == 0, 1.0, jnp.where(scale == 1, 0.5, 0.25))
        xyz = offsets_ref[:, here] * jitter
        row = lax.broadcasted_iota(jnp.int32, (16, tile), 0)
        last = jnp.zeros((16, tile), F32)
        for k in range(half - hid):
            last = jnp.where(row == 16 - (half - hid) + k, xyz[k : k + 1], last)
        last = last.astype(BF16)
        row = lax.broadcasted_iota(jnp.int32, (extra_lanes - 16, tile), 0)
        ids = ids_ref[:, here]
        member = jnp.where((row == ids) | (row == ids + shapes), 1.0, 0.0).astype(BF16)
        x_ref[here, half:] = jnp.concatenate([member, last], axis=0).T
        x_t_ref[half:, here] = member[:shapes]
        copy.wait()
        x_ref[here, half - LANES : half] = jnp.zeros((tile, LANES), BF16)
        x_ref[here, :hid] = hidden_ref[here, :].astype(BF16)
        hidden = x_ref[here, :half].T
        x_t_ref[: half - 16, here] = hidden[: half - 16]
        x_t_ref[half - 16 : half, here] = hidden[half - 16 :] + last


def layer_kernel(hid, shapes, tile, orders, parts, *refs):
    n = 1 if orders is None else len(orders)
    pieces = refs[:n]
    x_ref, x_t_ref, cot_ref, out_hbm, grad_hidden_hbm = refs[n : n + 5]
    grad_refs = refs[n + 5 : -6]
    w_ref, acc_ref, turned_ref, out_ref, grad_hidden_ref, sems = refs[-6:]
    points, width = cot_ref.shape
    half = width // 2
    me = lax.axis_index(AXES)
    place(pieces, orders, me, 0, w_ref)
    acc_ref[...] = jnp.zeros_like(acc_ref)

    def stores(step):
        here = pl.ds(pl.multiple_of(step * tile, tile), tile)
        return [
            pltpu.make_async_copy(source.at[here, :], target.at[here, :], sems.at[k, step])
            for k, (source, target) in enumerate(
                [(out_ref, out_hbm), (grad_hidden_ref, grad_hidden_hbm)]
            )
        ]

    def body(step, carry):
        here = pl.ds(pl.multiple_of(step * tile, tile), tile)
        pre = dot(x_ref[here, :], w_ref[...], NT)
        sigma = 0.5 * jnp.tanh(0.5 * pre) + 0.5
        out = pre * sigma
        out_ref[here, :] = out
        grad_pre = (cot_ref[here, :] * (sigma * (1.0 + (pre - out)))).astype(BF16)
        grad_hidden_ref[here, :] = dot(grad_pre, w_ref[:, :half])[:, :hid]
        for copy in stores(step):
            copy.start()
        acc_ref[...] += dot(x_t_ref[:, here], grad_pre)
        return carry

    lax.fori_loop(0, points // tile, body, 0)
    sums = acc_ref[half:, :].astype(BF16)
    for at in range(0, width, half):
        turned_ref[at : at + half, :] = acc_ref[:half, at : at + half].T
    for ref, order in zip(grad_refs, parts):
        ref[:shapes, :] = sums[:, :half]
        ref[shapes : 2 * shapes, :] = sums[:, half:]
        if orders is None:
            ref[2 * shapes :, :] = turned_ref[...].astype(BF16)
            continue
        rows = (ref.shape[0] - 2 * shapes) // len(order)
        for k, mask in enumerate(order):
            at = pl.multiple_of((me ^ mask) * rows, rows)
            to = 2 * shapes + k * rows
            ref[to : to + rows, :] = turned_ref[pl.ds(at, rows), :].astype(BF16)

    def finish(step, carry):
        for copy in stores(step):
            copy.wait()
        return carry

    lax.fori_loop(0, points // tile, finish, 0)


def sum_of(refs):
    terms = [ref[...].astype(F32) for ref in refs]
    while len(terms) > 1:
        terms = [a + b for a, b in zip(terms[::2], terms[1::2])]
    return terms[0]


def add_kernel(shapes, n, *refs):
    total = sum_of(refs[:n]).astype(BF16)
    for k, ref in enumerate(refs[n:]):
        rows = ref.shape[0] - 2 * shapes
        at = 2 * shapes + k * rows
        ref[: 2 * shapes, :] = total[: 2 * shapes]
        ref[2 * shapes :, :] = total[at : at + rows]


def last_kernel(hid, shapes, orders, n, *refs):
    direction_ref, gain_ref, codes_ref = refs[n : n + 3]
    pieces = refs[n + 3 : -5]
    grad_codes_ref, grad_direction_ref, grad_gain_ref, grad_bias_ref, code_scratch = refs[-5:]
    d = direction_ref[...]
    rows, cols = d.shape
    half = cols // 2
    me = lax.axis_index(AXES)
    place(pieces, orders, me, pieces[0].shape[1] - half, code_scratch)
    total = sum_of(refs[:n])
    sums = jnp.concatenate([total[:shapes], total[shapes : 2 * shapes]], axis=1)
    sums = jnp.concatenate(split(sums), axis=0).astype(BF16)
    terms = dot(sums, code_scratch[...])
    grad_codes_ref[...] = terms[:shapes] + terms[shapes:]
    width = sums.shape[1]
    mine = lax.broadcasted_iota(jnp.int32, (rows, width), 0) + me * rows
    mine = jnp.where(mine == lax.broadcasted_iota(jnp.int32, (rows, width), 1), 1.0, 0.0).astype(BF16)
    own = dot(mine, sums, NT)
    grad_bias_ref[...] = to_row(jnp.sum(own, axis=1, keepdims=True))
    code = dot(own.astype(BF16), stacked_codes(codes_ref, 2 * shapes))
    packed = jnp.concatenate([total[2 * shapes :], code], axis=1)
    lane = lax.broadcasted_iota(jnp.int32, (rows, cols), 1)
    grad_weight = jnp.where(
        lane < hid,
        packed,
        jnp.where(lane < hid + half, pltpu.roll(packed, cols - (half - hid), 1), pltpu.roll(packed, half, 1)),
    )
    inverse = lax.rsqrt(jnp.sum(d * d, axis=1, keepdims=True))
    unit = d * inverse
    grad_gain = jnp.sum(grad_weight * unit, axis=1, keepdims=True)
    grad_gain_ref[...] = to_row(grad_gain)
    grad_direction_ref[...] = (to_column(gain_ref[...]) * inverse) * (grad_weight - grad_gain * unit)


def masks_of(group):
    masks = [0]
    for bit in group:
        masks = masks + [m ^ bit for m in masks]
    return masks


def order_of(groups):
    order = [0]
    for group in groups:
        order = [m ^ r for m in masks_of(group) for r in order]
    return order


def swaps(arrays, masks, devices):
    moved = [
        lax.ppermute(x, AXES, [(i, i ^ mask) for i in range(devices)])
        for x, mask in list(zip(arrays, masks))[::-1]
    ]
    return moved[::-1]


def per_device(
    hidden,
    codes,
    offsets,
    shape_ids,
    scale_index,
    direction,
    gain,
    bias,
    cotangent,
    running_mean,
    running_var,
):
    points, hid = hidden.shape
    shapes = codes.shape[0]
    rows, cols = direction.shape
    width = cotangent.shape[1]
    half = cols // 2
    devices = lax.axis_size("dp") * lax.axis_size("inner")
    tuned = rows % 16 == 0
    bits = [1 << k | 1 for k in range(devices.bit_length() - 1)]
    groups = [bits[k - 2 : k] for k in range(len(bits), 1, -2)]
    groups = groups + [bits[:1]] * (len(bits) % 2)
    tuned = rows % 16 == 0
    extra_lanes = -(-(2 * shapes + 16) // LANES) * LANES
    lanes = half + extra_lanes
    gain_row = gain.reshape(1, rows)

    def shape_of(rows, lanes, dtype):
        return jax.ShapeDtypeStruct((rows, lanes), dtype)

    held = small_kernel(
        "prep",
        functools.partial(prep_kernel, hid),
        shape_of(rows, lanes + half, BF16),
        *[
            pltpu.with_memory_space_constraint(x, pltpu.HBM)
            for x in (direction, gain_row, bias.reshape(1, rows), codes)
        ],
        scratch=[
            VMEM((rows, cols), F32),
            VMEM((1, rows), F32),
            VMEM((1, rows), F32),
            VMEM((shapes, half), F32),
            pltpu.SemaphoreType.DMA((4,)),
        ],
        space=pl.ANY,
    )
    tile = min(512, points)
    x, x_t = pl.pallas_call(
        functools.partial(inputs_kernel, hid, tile),
        out_shape=[shape_of(points, lanes, BF16), shape_of(half + shapes, points, BF16)],
        in_specs=[pl.BlockSpec(memory_space=pl.ANY)] * 4,
        out_specs=vmem(2),
        scratch_shapes=[
            VMEM((points, hid), F32),
            VMEM((half - hid, points), F32),
            VMEM((1, points), jnp.int32),
            VMEM((1, points), jnp.int32),
            pltpu.SemaphoreType.DMA((points // tile + 3,)),
        ],
        compiler_params=pltpu.CompilerParams(vmem_limit_bytes=12 * MIB),
        cost_estimate=pl.CostEstimate(
            flops=4000 * MIB, bytes_accessed=8 * points * half, transcendentals=0
        ),
        name="inputs",
    )(
        *[
            pltpu.with_memory_space_constraint(a, pltpu.HBM)
            for a in (
                hidden,
                offsets.T,
                shape_ids.reshape(1, points),
                scale_index.reshape(1, points),
            )
        ]
    )
    if tuned:
        for group in groups[:-1]:
            arrays = [held] + swaps([held] * (2 ** len(group) - 1), masks_of(group)[1:], devices)
            held = small_kernel(
                "join",
                join_kernel,
                shape_of(held.shape[0] * len(arrays), lanes + half, BF16),
                *arrays[::-1],
            )
        held, x, x_t = lax.optimization_barrier((held, x, x_t))
        last_masks = masks_of(groups[-1])
        pieces = [held] + swaps([held] * (len(last_masks) - 1), last_masks[1:], devices)
        orders = [[m ^ r for r in order_of(groups[:-1])] for m in last_masks]
        parts = orders
    else:
        pieces, orders, parts = [lax.all_gather(held, AXES, axis=0, tiled=True)], None, [[0]]

    output, grad_hidden, *grads = pl.pallas_call(
        functools.partial(layer_kernel, hid, shapes, tile, orders, parts),
        out_shape=[pltpu.HBM((points, width), F32), pltpu.HBM((points, hid), F32)]
        + [shape_of(2 * shapes + width // len(parts), half, BF16)] * len(parts),
        in_specs=vmem(len(pieces) + 3),
        out_specs=[pl.BlockSpec(memory_space=pltpu.HBM)] * 2 + vmem(len(parts)),
        scratch_shapes=[
            VMEM((width, lanes), BF16),
            VMEM((half + shapes, width), F32),
            VMEM((width, half), F32),
            VMEM((points, width), F32),
            VMEM((points, hid), F32),
            pltpu.SemaphoreType.DMA((2, points // tile)),
        ],
        compiler_params=pltpu.CompilerParams(vmem_limit_bytes=20 * MIB),
        cost_estimate=pl.CostEstimate(
            flops=6 * points * width * cols,
            bytes_accessed=8 * points * (width + half),
            transcendentals=points * width,
        ),
        name="layer",
    )(*pieces, x, x_t, cotangent)

    if tuned:
        for r, group in enumerate(groups[::-1]):
            masks = masks_of(group)
            grads = [grads[0]] + swaps(grads[1:], masks[1:], devices)
            if r == len(groups) - 1:
                break
            n_out = len(masks_of(groups[-2 - r]))
            left = (grads[0].shape[0] - 2 * shapes) // n_out
            grads = small_kernel(
                "add",
                functools.partial(add_kernel, shapes, len(grads)),
                [shape_of(2 * shapes + left, half, BF16)] * n_out,
                *grads,
            )
    else:
        sums = lax.psum(grads[0][: 2 * shapes].astype(F32), AXES)
        high = sums.astype(BF16)
        own = lax.psum_scatter(grads[0][2 * shapes :].astype(F32), AXES, scatter_dimension=0, tiled=True)
        low = jnp.zeros((2 * shapes + rows, half), BF16).at[: 2 * shapes].set((sums - high).astype(BF16))
        grads = [jnp.concatenate([high, own.astype(BF16)], axis=0), low]
    grad_codes, grad_direction, grad_gain, grad_bias = small_kernel(
        "last",
        functools.partial(last_kernel, hid, shapes, orders, len(grads)),
        [
            shape_of(shapes, half, F32),
            shape_of(rows, cols, F32),
            shape_of(1, rows, F32),
            shape_of(1, rows, F32),
        ],
        *grads[::-1],
        direction,
        gain_row,
        codes,
        *pieces,
        scratch=[VMEM((width, half), BF16)],
    )

    total = float(points * devices)
    batch_mean = jnp.mean(codes, axis=0)
    batch_square = jnp.mean(codes * codes, axis=0)
    batch_var = (batch_square - batch_mean * batch_mean) * (total / (total - 1.0))
    new_mean = 0.9 * running_mean + 0.1 * batch_mean
    new_var = 0.9 * running_var + 0.1 * batch_var
    return (
        output,
        grad_hidden,
        grad_codes,
        grad_direction,
        grad_gain.reshape(rows),
        grad_bias.reshape(rows),
        new_mean,
        new_var,
    )


def solution(mesh):
    return jax.shard_map(
        per_device,
        mesh=mesh,
        in_specs=(
            P(("dp", "inner"), None),
            P(),
            P(("dp", "inner"), None),
            P(("dp", "inner")),
            P(("dp", "inner")),
            P(("dp", "inner"), None),
            P(("dp", "inner")),
            P(("dp", "inner")),
            P(("dp", "inner"), None),
            P(),
            P(),
        ),
        out_specs=(
            P(("dp", "inner"), None),
            P(("dp", "inner"), None),
            P(),
            P(("dp", "inner"), None),
            P(("dp", "inner")),
            P(("dp", "inner")),
            P(),
            P(),
        ),
        check_vma=False,
    )
```

```python
import functools

import jax
import jax.numpy as jnp
from jax import lax
from jax.experimental import pallas as pl
from jax.experimental.pallas import tpu as pltpu
from jax.sharding import PartitionSpec as P

AXES = ("dp", "inner")
LANES = 128
MIB = 1024 * 1024
F32 = jnp.float32
BF16 = jnp.bfloat16
VMEM = pltpu.VMEM
NT = (((1,), (1,)), ((), ()))


def dot(a, b, dims=(((1,), (0,)), ((), ()))):
    return lax.dot_general(a, b, dims, preferred_element_type=F32)


def vmem(n):
    return [pl.BlockSpec(memory_space=VMEM)] * n


def small_kernel(name, body, out_shape, *args, scratch=(), space=VMEM, limit=8):
    many = isinstance(out_shape, list)
    return pl.pallas_call(
        body,
        out_shape=out_shape,
        in_specs=[pl.BlockSpec(memory_space=space)] * len(args),
        out_specs=vmem(len(out_shape)) if many else vmem(1)[0],
        scratch_shapes=list(scratch),
        compiler_params=pltpu.CompilerParams(vmem_limit_bytes=limit * MIB),
        cost_estimate=pl.CostEstimate(
            flops=4000 * MIB, bytes_accessed=8 * MIB, transcendentals=4 * MIB
        ),
        name=name,
    )(*args)


def diagonal(n):
    return lax.broadcasted_iota(jnp.int32, (n, n), 0) == lax.broadcasted_iota(jnp.int32, (n, n), 1)


def to_column(row):
    n = row.shape[1]
    return jnp.sum(jnp.where(diagonal(n), row, 0.0), axis=1, keepdims=True)


def to_row(column):
    n = column.shape[0]
    return jnp.sum(jnp.where(diagonal(n), column, 0.0), axis=0, keepdims=True)


def stacked_codes(codes_ref, count):
    codes = codes_ref[...].astype(BF16)
    parts = [codes, codes]
    if count > 2 * codes.shape[0]:
        parts.append(jnp.zeros((count - 2 * codes.shape[0], codes.shape[1]), BF16))
    return jnp.concatenate(parts, axis=0)


def split(x):
    high = x.astype(BF16).astype(F32)
    return high, x - high


def prep_kernel(hid, *refs):
    piece_ref, direction_ref, gain_ref, bias_ref, codes_ref, sems = refs[4:]
    copies = [
        pltpu.make_async_copy(source, target, sems.at[k])
        for k, (source, target) in enumerate(zip(refs[:4], refs[5:9]))
    ]
    for copy in copies:
        copy.start()
    for copy in copies:
        copy.wait()
    d = direction_ref[...]
    shapes = codes_ref.shape[0]
    rows, cols = d.shape
    half = cols // 2
    extra_lanes = piece_ref.shape[1] - cols
    inverse = lax.rsqrt(jnp.sum(d * d, axis=1, keepdims=True))
    w = to_column(gain_ref[...]) * (d * inverse)
    lane = lax.broadcasted_iota(jnp.int32, (rows, half), 1)
    first = jnp.where(lane < hid, w[:, :half], w[:, half:])
    code = pltpu.roll(w, half - hid, 1)[:, half:].astype(BF16)
    bias = to_column(bias_ref[...]).astype(BF16).astype(F32)
    high, low = split(dot(code, stacked_codes(codes_ref, extra_lanes), NT) + bias)
    own = first[:, half - LANES :]
    if extra_lanes > LANES:
        own = jnp.concatenate([jnp.zeros((rows, extra_lanes - LANES), F32), own], axis=1)
    lane = lax.broadcasted_iota(jnp.int32, (rows, extra_lanes), 1)
    table = jnp.where(lane < shapes, high, jnp.where(lane < 2 * shapes, low, 0.0))
    table = jnp.where(lane >= extra_lanes - (half - hid), own, table)
    piece_ref[:, :half] = first.astype(BF16)
    piece_ref[:, half : half + extra_lanes] = table.astype(BF16)
    piece_ref[:, half + extra_lanes :] = code


def join_kernel(*refs):
    rows = refs[0].shape[0]
    for k, ref in enumerate(refs[-2::-1]):
        refs[-1][k * rows : (k + 1) * rows, :] = ref[...]


def place(refs, orders, me, lane, out_ref):
    lanes = out_ref.shape[1]
    if orders is None:
        out_ref[...] = refs[0][:, lane : lane + lanes]
        return
    rows = refs[0].shape[0] // len(orders[0])
    for ref, order in zip(refs, orders):
        for k, mask in enumerate(order):
            at = pl.multiple_of((me ^ mask) * rows, rows)
            out_ref[pl.ds(at, rows), :] = ref[k * rows : (k + 1) * rows, lane : lane + lanes]


def inputs_kernel(hid, tile, *refs):
    x_ref, x_t_ref, hidden_ref, offsets_ref, ids_ref, scale_ref, sems = refs[4:]
    points = x_ref.shape[0]
    half = (hid + LANES - 1) // LANES * LANES
    shapes = x_t_ref.shape[0] - half
    extra_lanes = x_ref.shape[1] - half
    steps = points // tile
    small = [
        pltpu.make_async_copy(source, target, sems.at[steps + k])
        for k, (source, target) in enumerate(zip(refs[1:4], (offsets_ref, ids_ref, scale_ref)))
    ]
    large = [
        pltpu.make_async_copy(
            refs[0].at[pl.ds(k * tile, tile), :], hidden_ref.at[pl.ds(k * tile, tile), :], sems.at[k]
        )
        for k in range(steps)
    ]
    for copy in small + large:
        copy.start()
    for copy in small:
        copy.wait()
    for step, copy in enumerate(large):
        here = slice(step * tile, (step + 1) * tile)
        scale = scale_ref[:, here]
        jitter = jnp.where(scale == 0, 1.0, jnp.where(scale == 1, 0.5, 0.25))
        xyz = offsets_ref[:, here] * jitter
        row = lax.broadcasted_iota(jnp.int32, (16, tile), 0)
        last = jnp.zeros((16, tile), F32)
        for k in range(half - hid):
            last = jnp.where(row == 16 - (half - hid) + k, xyz[k : k + 1], last)
        last = last.astype(BF16)
        row = lax.broadcasted_iota(jnp.int32, (extra_lanes - 16, tile), 0)
        ids = ids_ref[:, here]
        member = jnp.where((row == ids) | (row == ids + shapes), 1.0, 0.0).astype(BF16)
        x_ref[here, half:] = jnp.concatenate([member, last], axis=0).T
        x_t_ref[half:, here] = member[:shapes]
        copy.wait()
        x_ref[here, half - LANES : half] = jnp.zeros((tile, LANES), BF16)
        x_ref[here, :hid] = hidden_ref[here, :].astype(BF16)
        hidden = x_ref[here, :half].T
        x_t_ref[: half - 16, here] = hidden[: half - 16]
        x_t_ref[half - 16 : half, here] = hidden[half - 16 :] + last


def layer_kernel(hid, shapes, tile, orders, parts, *refs):
    n = 1 if orders is None else len(orders)
    pieces = refs[:n]
    x_ref, x_t_ref, cot_ref, out_hbm, grad_hidden_hbm = refs[n : n + 5]
    grad_refs = refs[n + 5 : -6]
    w_ref, turned_ref, out_ref, grad_hidden_ref, grad_pre_ref, pre_ref, sems = refs[-7:]
    points, width = cot_ref.shape
    half = width // 2
    steps = points // tile
    me = lax.axis_index(AXES)
    place(pieces, orders, me, 0, w_ref)
    copies = []

    def rows_of(step):
        return slice(step * tile, (step + 1) * tile)

    def forward(step):
        pre_ref[step % 2] = dot(x_ref[rows_of(step), :], w_ref[...], NT)

    def middle(step):
        here = rows_of(step)
        pre = pre_ref[step % 2]
        sigma = 0.5 * jnp.tanh(0.5 * pre) + 0.5
        out = pre * sigma
        out_ref[here, :] = out
        grad_pre_ref[here, :] = (cot_ref[here, :] * (sigma * (1.0 + (pre - out)))).astype(BF16)

    def backward(step):
        here = rows_of(step)
        grad_hidden_ref[here, :] = dot(grad_pre_ref[here, :], w_ref[:, :half])[:, :hid]

    def store(step, k, source, target):
        here = pl.ds(step * tile, tile)
        copy = pltpu.make_async_copy(source.at[here, :], target.at[here, :], sems.at[k, step])
        copy.start()
        copies.append(copy)

    forward(0)
    for step in range(steps):
        if step + 1 < steps:
            forward(step + 1)
        middle(step)
        store(step, 0, out_ref, out_hbm)
        if step > 0:
            backward(step - 1)
            store(step - 1, 1, grad_hidden_ref, grad_hidden_hbm)
    backward(steps - 1)
    store(steps - 1, 1, grad_hidden_ref, grad_hidden_hbm)
    grad = dot(x_t_ref[...], grad_pre_ref[...])
    sums = grad[half:].astype(BF16)
    for at in range(0, width, half):
        turned_ref[at : at + half, :] = grad[:half, at : at + half].T
    for ref, order in zip(grad_refs, parts):
        ref[:shapes, :] = sums[:, :half]
        ref[shapes : 2 * shapes, :] = sums[:, half:]
        if orders is None:
            ref[2 * shapes :, :] = turned_ref[...].astype(BF16)
            continue
        rows = (ref.shape[0] - 2 * shapes) // len(order)
        for k, mask in enumerate(order):
            at = pl.multiple_of((me ^ mask) * rows, rows)
            to = 2 * shapes + k * rows
            ref[to : to + rows, :] = turned_ref[pl.ds(at, rows), :].astype(BF16)

    for copy in copies:
        copy.wait()


def sum_of(refs):
    terms = [ref[...].astype(F32) for ref in refs]
    while len(terms) > 1:
        terms = [a + b for a, b in zip(terms[::2], terms[1::2])]
    return terms[0]


def add_kernel(shapes, n, *refs):
    total = sum_of(refs[:n]).astype(BF16)
    for k, ref in enumerate(refs[n:]):
        rows = ref.shape[0] - 2 * shapes
        at = 2 * shapes + k * rows
        ref[: 2 * shapes, :] = total[: 2 * shapes]
        ref[2 * shapes :, :] = total[at : at + rows]


def last_kernel(hid, shapes, orders, n, *refs):
    direction_ref, gain_ref, codes_ref = refs[n : n + 3]
    pieces = refs[n + 3 : -5]
    grad_codes_ref, grad_direction_ref, grad_gain_ref, grad_bias_ref, code_scratch = refs[-5:]
    d = direction_ref[...]
    rows, cols = d.shape
    half = cols // 2
    me = lax.axis_index(AXES)
    place(pieces, orders, me, pieces[0].shape[1] - half, code_scratch)
    total = sum_of(refs[:n])
    sums = jnp.concatenate([total[:shapes], total[shapes : 2 * shapes]], axis=1)
    sums = jnp.concatenate(split(sums), axis=0).astype(BF16)
    terms = dot(sums, code_scratch[...])
    grad_codes_ref[...] = terms[:shapes] + terms[shapes:]
    width = sums.shape[1]
    mine = lax.broadcasted_iota(jnp.int32, (rows, width), 0) + me * rows
    mine = jnp.where(mine == lax.broadcasted_iota(jnp.int32, (rows, width), 1), 1.0, 0.0).astype(BF16)
    own = dot(mine, sums, NT)
    grad_bias_ref[...] = to_row(jnp.sum(own, axis=1, keepdims=True))
    code = dot(own.astype(BF16), stacked_codes(codes_ref, 2 * shapes))
    packed = jnp.concatenate([total[2 * shapes :], code], axis=1)
    lane = lax.broadcasted_iota(jnp.int32, (rows, cols), 1)
    grad_weight = jnp.where(
        lane < hid,
        packed,
        jnp.where(lane < hid + half, pltpu.roll(packed, cols - (half - hid), 1), pltpu.roll(packed, half, 1)),
    )
    inverse = lax.rsqrt(jnp.sum(d * d, axis=1, keepdims=True))
    unit = d * inverse
    grad_gain = jnp.sum(grad_weight * unit, axis=1, keepdims=True)
    grad_gain_ref[...] = to_row(grad_gain)
    grad_direction_ref[...] = (to_column(gain_ref[...]) * inverse) * (grad_weight - grad_gain * unit)


def masks_of(group):
    masks = [0]
    for bit in group:
        masks = masks + [m ^ bit for m in masks]
    return masks


def order_of(groups):
    order = [0]
    for group in groups:
        order = [m ^ r for m in masks_of(group) for r in order]
    return order


def swaps(arrays, masks, devices):
    moved = [
        lax.ppermute(x, AXES, [(i, i ^ mask) for i in range(devices)])
        for x, mask in list(zip(arrays, masks))[::-1]
    ]
    return moved[::-1]


def per_device(
    hidden,
    codes,
    offsets,
    shape_ids,
    scale_index,
    direction,
    gain,
    bias,
    cotangent,
    running_mean,
    running_var,
):
    points, hid = hidden.shape
    shapes = codes.shape[0]
    rows, cols = direction.shape
    width = cotangent.shape[1]
    half = cols // 2
    devices = lax.axis_size("dp") * lax.axis_size("inner")
    tuned = rows % 16 == 0
    bits = [1 << k | 1 for k in range(devices.bit_length() - 1)]
    groups = [bits[k - 2 : k] for k in range(len(bits), 1, -2)]
    groups = groups + [bits[:1]] * (len(bits) % 2)
    tuned = rows % 16 == 0
    extra_lanes = -(-(2 * shapes + 16) // LANES) * LANES
    lanes = half + extra_lanes
    gain_row = gain.reshape(1, rows)

    def shape_of(rows, lanes, dtype):
        return jax.ShapeDtypeStruct((rows, lanes), dtype)

    held = small_kernel(
        "prep",
        functools.partial(prep_kernel, hid),
        shape_of(rows, lanes + half, BF16),
        *[
            pltpu.with_memory_space_constraint(x, pltpu.HBM)
            for x in (direction, gain_row, bias.reshape(1, rows), codes)
        ],
        scratch=[
            VMEM((rows, cols), F32),
            VMEM((1, rows), F32),
            VMEM((1, rows), F32),
            VMEM((shapes, half), F32),
            pltpu.SemaphoreType.DMA((4,)),
        ],
        space=pl.ANY,
    )
    tile, layer_tile = min(512, points), min(256, points)
    x, x_t = pl.pallas_call(
        functools.partial(inputs_kernel, hid, tile),
        out_shape=[shape_of(points, lanes, BF16), shape_of(half + shapes, points, BF16)],
        in_specs=[pl.BlockSpec(memory_space=pl.ANY)] * 4,
        out_specs=vmem(2),
        scratch_shapes=[
            VMEM((points, hid), F32),
            VMEM((half - hid, points), F32),
            VMEM((1, points), jnp.int32),
            VMEM((1, points), jnp.int32),
            pltpu.SemaphoreType.DMA((points // tile + 3,)),
        ],
        compiler_params=pltpu.CompilerParams(vmem_limit_bytes=12 * MIB),
        cost_estimate=pl.CostEstimate(
            flops=4000 * MIB, bytes_accessed=8 * points * half, transcendentals=0
        ),
        name="inputs",
    )(
        *[
            pltpu.with_memory_space_constraint(a, pltpu.HBM)
            for a in (
                hidden,
                offsets.T,
                shape_ids.reshape(1, points),
                scale_index.reshape(1, points),
            )
        ]
    )
    if tuned:
        for group in groups[:-1]:
            arrays = [held] + swaps([held] * (2 ** len(group) - 1), masks_of(group)[1:], devices)
            held = small_kernel(
                "join",
                join_kernel,
                shape_of(held.shape[0] * len(arrays), lanes + half, BF16),
                *arrays[::-1],
            )
        held, x, x_t = lax.optimization_barrier((held, x, x_t))
        last_masks = masks_of(groups[-1])
        pieces = [held] + swaps([held] * (len(last_masks) - 1), last_masks[1:], devices)
        orders = [[m ^ r for r in order_of(groups[:-1])] for m in last_masks]
        parts = orders
    else:
        pieces, orders, parts = [lax.all_gather(held, AXES, axis=0, tiled=True)], None, [[0]]

    output, grad_hidden, *grads = pl.pallas_call(
        functools.partial(layer_kernel, hid, shapes, layer_tile, orders, parts),
        out_shape=[pltpu.HBM((points, width), F32), pltpu.HBM((points, hid), F32)]
        + [shape_of(2 * shapes + width // len(parts), half, BF16)] * len(parts),
        in_specs=vmem(len(pieces) + 3),
        out_specs=[pl.BlockSpec(memory_space=pltpu.HBM)] * 2 + vmem(len(parts)),
        scratch_shapes=[
            VMEM((width, lanes), BF16),
            VMEM((width, half), F32),
            VMEM((points, width), F32),
            VMEM((points, hid), F32),
            VMEM((points, width), BF16),
            VMEM((2, layer_tile, width), F32),
            pltpu.SemaphoreType.DMA((2, points // layer_tile)),
        ],
        compiler_params=pltpu.CompilerParams(vmem_limit_bytes=20 * MIB),
        cost_estimate=pl.CostEstimate(
            flops=6 * points * width * cols,
            bytes_accessed=8 * points * (width + half),
            transcendentals=points * width,
        ),
        name="layer",
    )(*pieces, x, x_t, cotangent)

    if tuned:
        for r, group in enumerate(groups[::-1]):
            masks = masks_of(group)
            grads = [grads[0]] + swaps(grads[1:], masks[1:], devices)
            if r == len(groups) - 1:
                break
            n_out = len(masks_of(groups[-2 - r]))
            left = (grads[0].shape[0] - 2 * shapes) // n_out
            grads = small_kernel(
                "add",
                functools.partial(add_kernel, shapes, len(grads)),
                [shape_of(2 * shapes + left, half, BF16)] * n_out,
                *grads,
            )
    else:
        sums = lax.psum(grads[0][: 2 * shapes].astype(F32), AXES)
        high = sums.astype(BF16)
        own = lax.psum_scatter(grads[0][2 * shapes :].astype(F32), AXES, scatter_dimension=0, tiled=True)
        low = jnp.zeros((2 * shapes + rows, half), BF16).at[: 2 * shapes].set((sums - high).astype(BF16))
        grads = [jnp.concatenate([high, own.astype(BF16)], axis=0), low]
    grad_codes, grad_direction, grad_gain, grad_bias = small_kernel(
        "last",
        functools.partial(last_kernel, hid, shapes, orders, len(grads)),
        [
            shape_of(shapes, half, F32),
            shape_of(rows, cols, F32),
            shape_of(1, rows, F32),
            shape_of(1, rows, F32),
        ],
        *grads[::-1],
        direction,
        gain_row,
        codes,
        *pieces,
        scratch=[VMEM((width, half), BF16)],
    )

    total = float(points * devices)
    batch_mean = jnp.mean(codes, axis=0)
    batch_square = jnp.mean(codes * codes, axis=0)
    batch_var = (batch_square - batch_mean * batch_mean) * (total / (total - 1.0))
    new_mean = 0.9 * running_mean + 0.1 * batch_mean
    new_var = 0.9 * running_var + 0.1 * batch_var
    return (
        output,
        grad_hidden,
        grad_codes,
        grad_direction,
        grad_gain.reshape(rows),
        grad_bias.reshape(rows),
        new_mean,
        new_var,
    )


def solution(mesh):
    return jax.shard_map(
        per_device,
        mesh=mesh,
        in_specs=(
            P(("dp", "inner"), None),
            P(),
            P(("dp", "inner"), None),
            P(("dp", "inner")),
            P(("dp", "inner")),
            P(("dp", "inner"), None),
            P(("dp", "inner")),
            P(("dp", "inner")),
            P(("dp", "inner"), None),
            P(),
            P(),
        ),
        out_specs=(
            P(("dp", "inner"), None),
            P(("dp", "inner"), None),
            P(),
            P(("dp", "inner"), None),
            P(("dp", "inner")),
            P(("dp", "inner")),
            P(),
            P(),
        ),
        check_vma=False,
    )
```

```python
import functools

import jax
import jax.numpy as jnp
from jax import lax
from jax.experimental import pallas as pl
from jax.experimental.pallas import tpu as pltpu
from jax.sharding import PartitionSpec as P

AXES = ("dp", "inner")
LANES = 128
MIB = 1024 * 1024
F32 = jnp.float32
BF16 = jnp.bfloat16
VMEM = pltpu.VMEM
NT = (((1,), (1,)), ((), ()))


def dot(a, b, dims=(((1,), (0,)), ((), ()))):
    return lax.dot_general(a, b, dims, preferred_element_type=F32)


def vmem(n):
    return [pl.BlockSpec(memory_space=VMEM)] * n


def small_kernel(name, body, out_shape, *args, scratch=(), space=VMEM, limit=8):
    many = isinstance(out_shape, list)
    return pl.pallas_call(
        body,
        out_shape=out_shape,
        in_specs=[pl.BlockSpec(memory_space=space)] * len(args),
        out_specs=vmem(len(out_shape)) if many else vmem(1)[0],
        scratch_shapes=list(scratch),
        compiler_params=pltpu.CompilerParams(vmem_limit_bytes=limit * MIB),
        cost_estimate=pl.CostEstimate(
            flops=4000 * MIB, bytes_accessed=8 * MIB, transcendentals=4 * MIB
        ),
        name=name,
    )(*args)


def diagonal(n):
    return lax.broadcasted_iota(jnp.int32, (n, n), 0) == lax.broadcasted_iota(jnp.int32, (n, n), 1)


def to_column(row):
    n = row.shape[1]
    return jnp.sum(jnp.where(diagonal(n), row, 0.0), axis=1, keepdims=True)


def to_row(column):
    n = column.shape[0]
    return jnp.sum(jnp.where(diagonal(n), column, 0.0), axis=0, keepdims=True)


def stacked_codes(codes_ref, count):
    codes = codes_ref[...].astype(BF16)
    parts = [codes, codes]
    if count > 2 * codes.shape[0]:
        parts.append(jnp.zeros((count - 2 * codes.shape[0], codes.shape[1]), BF16))
    return jnp.concatenate(parts, axis=0)


def split(x):
    high = x.astype(BF16).astype(F32)
    return high, x - high


def prep_kernel(hid, *refs):
    piece_ref, direction_ref, gain_ref, bias_ref, codes_ref, sems = refs[4:]
    copies = [
        pltpu.make_async_copy(source, target, sems.at[k])
        for k, (source, target) in enumerate(zip(refs[:4], refs[5:9]))
    ]
    for copy in copies:
        copy.start()
    for copy in copies:
        copy.wait()
    d = direction_ref[...]
    shapes = codes_ref.shape[0]
    rows, cols = d.shape
    half = cols // 2
    extra_lanes = piece_ref.shape[1] - cols
    inverse = lax.rsqrt(jnp.sum(d * d, axis=1, keepdims=True))
    w = to_column(gain_ref[...]) * (d * inverse)
    lane = lax.broadcasted_iota(jnp.int32, (rows, half), 1)
    first = jnp.where(lane < hid, w[:, :half], w[:, half:])
    code = pltpu.roll(w, half - hid, 1)[:, half:].astype(BF16)
    bias = to_column(bias_ref[...]).astype(BF16).astype(F32)
    high, low = split(dot(code, stacked_codes(codes_ref, extra_lanes), NT) + bias)
    own = first[:, half - LANES :]
    if extra_lanes > LANES:
        own = jnp.concatenate([jnp.zeros((rows, extra_lanes - LANES), F32), own], axis=1)
    lane = lax.broadcasted_iota(jnp.int32, (rows, extra_lanes), 1)
    table = jnp.where(lane < shapes, high, jnp.where(lane < 2 * shapes, low, 0.0))
    table = jnp.where(lane >= extra_lanes - (half - hid), own, table)
    piece_ref[:, :half] = first.astype(BF16)
    piece_ref[:, half : half + extra_lanes] = table.astype(BF16)
    piece_ref[:, half + extra_lanes :] = code


def join_kernel(n, *refs):
    rows = refs[0].shape[0]
    for k, ref in enumerate(refs[n - 1 :: -1]):
        lane = 0
        for out_ref in refs[n:]:
            lanes = out_ref.shape[1]
            out_ref[k * rows : (k + 1) * rows, :] = ref[:, lane : lane + lanes]
            lane += lanes


def place(refs, orders, me, out_ref):
    if orders is None:
        out_ref[...] = refs[0][...]
        return
    rows = refs[0].shape[0] // len(orders[0])
    for ref, order in zip(refs, orders):
        for k, mask in enumerate(order):
            at = pl.multiple_of((me ^ mask) * rows, rows)
            out_ref[pl.ds(at, rows), :] = ref[k * rows : (k + 1) * rows, :]


def inputs_kernel(hid, tile, *refs):
    x_ref, x_t_ref, hidden_ref, offsets_ref, ids_ref, scale_ref, sems = refs[4:]
    points = x_ref.shape[0]
    half = (hid + LANES - 1) // LANES * LANES
    shapes = x_t_ref.shape[0] - half
    extra_lanes = x_ref.shape[1] - half
    steps = points // tile
    small = [
        pltpu.make_async_copy(source, target, sems.at[steps + k])
        for k, (source, target) in enumerate(zip(refs[1:4], (offsets_ref, ids_ref, scale_ref)))
    ]
    large = [
        pltpu.make_async_copy(
            refs[0].at[pl.ds(k * tile, tile), :], hidden_ref.at[pl.ds(k * tile, tile), :], sems.at[k]
        )
        for k in range(steps)
    ]
    for copy in small + large:
        copy.start()
    for copy in small:
        copy.wait()
    for step, copy in enumerate(large):
        here = slice(step * tile, (step + 1) * tile)
        scale = scale_ref[:, here]
        jitter = jnp.where(scale == 0, 1.0, jnp.where(scale == 1, 0.5, 0.25))
        xyz = offsets_ref[:, here] * jitter
        row = lax.broadcasted_iota(jnp.int32, (16, tile), 0)
        last = jnp.zeros((16, tile), F32)
        for k in range(half - hid):
            last = jnp.where(row == 16 - (half - hid) + k, xyz[k : k + 1], last)
        last = last.astype(BF16)
        row = lax.broadcasted_iota(jnp.int32, (extra_lanes - 16, tile), 0)
        ids = ids_ref[:, here]
        member = jnp.where((row == ids) | (row == ids + shapes), 1.0, 0.0).astype(BF16)
        x_ref[here, half:] = jnp.concatenate([member, last], axis=0).T
        x_t_ref[half:, here] = member[:shapes]
        copy.wait()
        x_ref[here, half - LANES : half] = jnp.zeros((tile, LANES), BF16)
        x_ref[here, :hid] = hidden_ref[here, :].astype(BF16)
        hidden = x_ref[here, :half].T
        x_t_ref[: half - 16, here] = hidden[: half - 16]
        x_t_ref[half - 16 : half, here] = hidden[half - 16 :] + last


def layer_kernel(hid, shapes, tile, orders, parts, *refs):
    n = 1 if orders is None else len(orders)
    pieces = refs[:n]
    x_ref, x_t_ref, cot_ref, out_hbm, grad_hidden_hbm = refs[n : n + 5]
    grad_refs = refs[n + 5 : -6]
    w_ref, turned_ref, out_ref, grad_hidden_ref, grad_pre_ref, pre_ref, sems = refs[-7:]
    points, width = cot_ref.shape
    half = width // 2
    steps = points // tile
    me = lax.axis_index(AXES)
    place(pieces, orders, me, w_ref)
    copies = []

    def rows_of(step):
        return slice(step * tile, (step + 1) * tile)

    def forward(step):
        pre_ref[step % 2] = dot(x_ref[rows_of(step), :], w_ref[...], NT)

    def middle(step):
        here = rows_of(step)
        pre = pre_ref[step % 2]
        sigma = 0.5 * jnp.tanh(0.5 * pre) + 0.5
        out = pre * sigma
        out_ref[here, :] = out
        grad_pre_ref[here, :] = (cot_ref[here, :] * (sigma * (1.0 + (pre - out)))).astype(BF16)

    def backward(step):
        here = rows_of(step)
        grad_hidden_ref[here, :] = dot(grad_pre_ref[here, :], w_ref[:, :half])[:, :hid]

    def store(step, k, source, target):
        here = pl.ds(step * tile, tile)
        copy = pltpu.make_async_copy(source.at[here, :], target.at[here, :], sems.at[k, step])
        copy.start()
        copies.append(copy)

    forward(0)
    for step in range(steps):
        if step + 1 < steps:
            forward(step + 1)
        middle(step)
        store(step, 0, out_ref, out_hbm)
        if step > 0:
            backward(step - 1)
            store(step - 1, 1, grad_hidden_ref, grad_hidden_hbm)
    backward(steps - 1)
    store(steps - 1, 1, grad_hidden_ref, grad_hidden_hbm)
    grad = dot(x_t_ref[...], grad_pre_ref[...])
    sums = grad[half:].astype(BF16)
    for at in range(0, width, half):
        turned_ref[at : at + half, :] = grad[:half, at : at + half].T
    for ref, order in zip(grad_refs, parts):
        ref[:shapes, :] = sums[:, :half]
        ref[shapes : 2 * shapes, :] = sums[:, half:]
        if orders is None:
            ref[2 * shapes :, :] = turned_ref[...].astype(BF16)
            continue
        rows = (ref.shape[0] - 2 * shapes) // len(order)
        for k, mask in enumerate(order):
            at = pl.multiple_of((me ^ mask) * rows, rows)
            to = 2 * shapes + k * rows
            ref[to : to + rows, :] = turned_ref[pl.ds(at, rows), :].astype(BF16)

    for copy in copies:
        copy.wait()


def sum_of(refs):
    terms = [ref[...].astype(F32) for ref in refs]
    while len(terms) > 1:
        terms = [a + b for a, b in zip(terms[::2], terms[1::2])]
    return terms[0]


def add_kernel(shapes, n, *refs):
    total = sum_of(refs[:n]).astype(BF16)
    for k, ref in enumerate(refs[n:]):
        rows = ref.shape[0] - 2 * shapes
        at = 2 * shapes + k * rows
        ref[: 2 * shapes, :] = total[: 2 * shapes]
        ref[2 * shapes :, :] = total[at : at + rows]


def last_kernel(hid, shapes, orders, n, *refs):
    direction_ref, gain_ref, codes_ref = refs[n : n + 3]
    pieces = refs[n + 3 : -5]
    grad_codes_ref, grad_direction_ref, grad_gain_ref, grad_bias_ref, code_scratch = refs[-5:]
    d = direction_ref[...]
    rows, cols = d.shape
    half = cols // 2
    me = lax.axis_index(AXES)
    place(pieces, orders, me, code_scratch)
    total = sum_of(refs[:n])
    sums = jnp.concatenate([total[:shapes], total[shapes : 2 * shapes]], axis=1)
    sums = jnp.concatenate(split(sums), axis=0).astype(BF16)
    terms = dot(sums, code_scratch[...])
    grad_codes_ref[...] = terms[:shapes] + terms[shapes:]
    width = sums.shape[1]
    mine = lax.broadcasted_iota(jnp.int32, (rows, width), 0) + me * rows
    mine = jnp.where(mine == lax.broadcasted_iota(jnp.int32, (rows, width), 1), 1.0, 0.0).astype(BF16)
    own = dot(mine, sums, NT)
    grad_bias_ref[...] = to_row(jnp.sum(own, axis=1, keepdims=True))
    code = dot(own.astype(BF16), stacked_codes(codes_ref, 2 * shapes))
    packed = jnp.concatenate([total[2 * shapes :], code], axis=1)
    lane = lax.broadcasted_iota(jnp.int32, (rows, cols), 1)
    grad_weight = jnp.where(
        lane < hid,
        packed,
        jnp.where(lane < hid + half, pltpu.roll(packed, cols - (half - hid), 1), pltpu.roll(packed, half, 1)),
    )
    inverse = lax.rsqrt(jnp.sum(d * d, axis=1, keepdims=True))
    unit = d * inverse
    grad_gain = jnp.sum(grad_weight * unit, axis=1, keepdims=True)
    grad_gain_ref[...] = to_row(grad_gain)
    grad_direction_ref[...] = (to_column(gain_ref[...]) * inverse) * (grad_weight - grad_gain * unit)


def masks_of(group):
    masks = [0]
    for bit in group:
        masks = masks + [m ^ bit for m in masks]
    return masks


def order_of(groups):
    order = [0]
    for group in groups:
        order = [m ^ r for m in masks_of(group) for r in order]
    return order


def swaps(arrays, masks, devices):
    moved = [
        lax.ppermute(x, AXES, [(i, i ^ mask) for i in range(devices)])
        for x, mask in list(zip(arrays, masks))[::-1]
    ]
    return moved[::-1]


def per_device(
    hidden,
    codes,
    offsets,
    shape_ids,
    scale_index,
    direction,
    gain,
    bias,
    cotangent,
    running_mean,
    running_var,
):
    points, hid = hidden.shape
    shapes = codes.shape[0]
    rows, cols = direction.shape
    width = cotangent.shape[1]
    half = cols // 2
    devices = lax.axis_size("dp") * lax.axis_size("inner")
    tuned = rows % 16 == 0
    bits = [1 << k | 1 for k in range(devices.bit_length() - 1)]
    groups = [bits[k - 2 : k] for k in range(len(bits), 1, -2)]
    groups = groups + [bits[:1]] * (len(bits) % 2)
    tuned = rows % 16 == 0
    extra_lanes = -(-(2 * shapes + 16) // LANES) * LANES
    lanes = half + extra_lanes
    gain_row = gain.reshape(1, rows)

    def shape_of(rows, lanes, dtype):
        return jax.ShapeDtypeStruct((rows, lanes), dtype)

    held = small_kernel(
        "prep",
        functools.partial(prep_kernel, hid),
        shape_of(rows, lanes + half, BF16),
        *[
            pltpu.with_memory_space_constraint(x, pltpu.HBM)
            for x in (direction, gain_row, bias.reshape(1, rows), codes)
        ],
        scratch=[
            VMEM((rows, cols), F32),
            VMEM((1, rows), F32),
            VMEM((1, rows), F32),
            VMEM((shapes, half), F32),
            pltpu.SemaphoreType.DMA((4,)),
        ],
        space=pl.ANY,
    )
    tile, layer_tile = min(512, points), min(256, points)
    x, x_t = pl.pallas_call(
        functools.partial(inputs_kernel, hid, tile),
        out_shape=[shape_of(points, lanes, BF16), shape_of(half + shapes, points, BF16)],
        in_specs=[pl.BlockSpec(memory_space=pl.ANY)] * 4,
        out_specs=vmem(2),
        scratch_shapes=[
            VMEM((points, hid), F32),
            VMEM((half - hid, points), F32),
            VMEM((1, points), jnp.int32),
            VMEM((1, points), jnp.int32),
            pltpu.SemaphoreType.DMA((points // tile + 3,)),
        ],
        compiler_params=pltpu.CompilerParams(vmem_limit_bytes=12 * MIB),
        cost_estimate=pl.CostEstimate(
            flops=4000 * MIB, bytes_accessed=8 * points * half, transcendentals=0
        ),
        name="inputs",
    )(
        *[
            pltpu.with_memory_space_constraint(a, pltpu.HBM)
            for a in (
                hidden,
                offsets.T,
                shape_ids.reshape(1, points),
                scale_index.reshape(1, points),
            )
        ]
    )
    def gather(array, group):
        masks = masks_of(group)[1:]
        return [array] + swaps([array] * len(masks), masks, devices)

    def join(arrays, *widths):
        height = sum(a.shape[0] for a in arrays)
        return small_kernel(
            "join",
            functools.partial(join_kernel, len(arrays)),
            [shape_of(height, width, BF16) for width in widths],
            *arrays[::-1],
        )

    if tuned:
        weight, code_weight = join(gather(held, groups[0]), lanes, half)
        weight, code_weight, x, x_t = lax.optimization_barrier((weight, code_weight, x, x_t))
        for group in groups[1:-1]:
            weights, code_weights = gather(weight, group), gather(code_weight, group)
            (weight,) = join(weights, lanes)
            (code_weight,) = join(code_weights, half)
        weights = gather(weight, groups[-1])
        *weights, code_weight = lax.optimization_barrier((*weights, code_weight))
        code_weights = gather(code_weight, groups[-1])
        orders = [[m ^ r for r in order_of(groups[:-1])] for m in masks_of(groups[-1])]
        parts = orders
    else:
        held = lax.all_gather(held, AXES, axis=0, tiled=True)
        weights, code_weights, orders, parts = [held[:, :lanes]], [held[:, lanes:]], None, [[0]]

    output, grad_hidden, *grads = pl.pallas_call(
        functools.partial(layer_kernel, hid, shapes, layer_tile, orders, parts),
        out_shape=[pltpu.HBM((points, width), F32), pltpu.HBM((points, hid), F32)]
        + [shape_of(2 * shapes + width // len(parts), half, BF16)] * len(parts),
        in_specs=vmem(len(weights) + 3),
        out_specs=[pl.BlockSpec(memory_space=pltpu.HBM)] * 2 + vmem(len(parts)),
        scratch_shapes=[
            VMEM((width, lanes), BF16),
            VMEM((width, half), F32),
            VMEM((points, width), F32),
            VMEM((points, hid), F32),
            VMEM((points, width), BF16),
            VMEM((2, layer_tile, width), F32),
            pltpu.SemaphoreType.DMA((2, points // layer_tile)),
        ],
        compiler_params=pltpu.CompilerParams(vmem_limit_bytes=20 * MIB),
        cost_estimate=pl.CostEstimate(
            flops=6 * points * width * cols,
            bytes_accessed=8 * points * (width + half),
            transcendentals=points * width,
        ),
        name="layer",
    )(*weights, x, x_t, cotangent)

    if tuned:
        for r, group in enumerate(groups[::-1]):
            masks = masks_of(group)
            grads = [grads[0]] + swaps(grads[1:], masks[1:], devices)
            if r == len(groups) - 1:
                break
            n_out = len(masks_of(groups[-2 - r]))
            left = (grads[0].shape[0] - 2 * shapes) // n_out
            grads = small_kernel(
                "add",
                functools.partial(add_kernel, shapes, len(grads)),
                [shape_of(2 * shapes + left, half, BF16)] * n_out,
                *grads[::-1],
            )
    else:
        sums = lax.psum(grads[0][: 2 * shapes].astype(F32), AXES)
        high = sums.astype(BF16)
        own = lax.psum_scatter(grads[0][2 * shapes :].astype(F32), AXES, scatter_dimension=0, tiled=True)
        low = jnp.zeros((2 * shapes + rows, half), BF16).at[: 2 * shapes].set((sums - high).astype(BF16))
        grads = [jnp.concatenate([high, own.astype(BF16)], axis=0), low]
    grad_codes, grad_direction, grad_gain, grad_bias = small_kernel(
        "last",
        functools.partial(last_kernel, hid, shapes, orders, len(grads)),
        [
            shape_of(shapes, half, F32),
            shape_of(rows, cols, F32),
            shape_of(1, rows, F32),
            shape_of(1, rows, F32),
        ],
        *grads[::-1],
        direction,
        gain_row,
        codes,
        *code_weights,
        scratch=[VMEM((width, half), BF16)],
    )

    total = float(points * devices)
    batch_mean = jnp.mean(codes, axis=0)
    batch_square = jnp.mean(codes * codes, axis=0)
    batch_var = (batch_square - batch_mean * batch_mean) * (total / (total - 1.0))
    new_mean = 0.9 * running_mean + 0.1 * batch_mean
    new_var = 0.9 * running_var + 0.1 * batch_var
    return (
        output,
        grad_hidden,
        grad_codes,
        grad_direction,
        grad_gain.reshape(rows),
        grad_bias.reshape(rows),
        new_mean,
        new_var,
    )


def solution(mesh):
    return jax.shard_map(
        per_device,
        mesh=mesh,
        in_specs=(
            P(("dp", "inner"), None),
            P(),
            P(("dp", "inner"), None),
            P(("dp", "inner")),
            P(("dp", "inner")),
            P(("dp", "inner"), None),
            P(("dp", "inner")),
            P(("dp", "inner")),
            P(("dp", "inner"), None),
            P(),
            P(),
        ),
        out_specs=(
            P(("dp", "inner"), None),
            P(("dp", "inner"), None),
            P(),
            P(("dp", "inner"), None),
            P(("dp", "inner")),
            P(("dp", "inner")),
            P(),
            P(),
        ),
        check_vma=False,
    )
```

```python
import functools

import jax
import jax.numpy as jnp
from jax import lax
from jax.experimental import pallas as pl
from jax.experimental.pallas import tpu as pltpu
from jax.sharding import PartitionSpec as P

AXES = ("dp", "inner")
LANES = 128
MIB = 1024 * 1024
F32 = jnp.float32
BF16 = jnp.bfloat16
VMEM = pltpu.VMEM
NT = (((1,), (1,)), ((), ()))


def dot(a, b, dims=(((1,), (0,)), ((), ()))):
    return lax.dot_general(a, b, dims, preferred_element_type=F32)


def vmem(n):
    return [pl.BlockSpec(memory_space=VMEM)] * n


def small_kernel(name, body, out_shape, *args, scratch=(), space=VMEM, limit=8):
    many = isinstance(out_shape, list)
    return pl.pallas_call(
        body,
        out_shape=out_shape,
        in_specs=[pl.BlockSpec(memory_space=space)] * len(args),
        out_specs=vmem(len(out_shape)) if many else vmem(1)[0],
        scratch_shapes=list(scratch),
        compiler_params=pltpu.CompilerParams(vmem_limit_bytes=limit * MIB),
        cost_estimate=pl.CostEstimate(
            flops=4000 * MIB, bytes_accessed=8 * MIB, transcendentals=4 * MIB
        ),
        name=name,
    )(*args)


def diagonal(n):
    return lax.broadcasted_iota(jnp.int32, (n, n), 0) == lax.broadcasted_iota(jnp.int32, (n, n), 1)


def to_column(row):
    n = row.shape[1]
    return jnp.sum(jnp.where(diagonal(n), row, 0.0), axis=1, keepdims=True)


def to_row(column):
    n = column.shape[0]
    return jnp.sum(jnp.where(diagonal(n), column, 0.0), axis=0, keepdims=True)


def stacked_codes(codes_ref, count):
    codes = codes_ref[...].astype(BF16)
    parts = [codes, codes]
    if count > 2 * codes.shape[0]:
        parts.append(jnp.zeros((count - 2 * codes.shape[0], codes.shape[1]), BF16))
    return jnp.concatenate(parts, axis=0)


def split(x):
    high = x.astype(BF16).astype(F32)
    return high, x - high


def prep_kernel(hid, *refs):
    piece_ref, direction_ref, gain_ref, bias_ref, codes_ref, sems = refs[4:]
    copies = [
        pltpu.make_async_copy(source, target, sems.at[k])
        for k, (source, target) in enumerate(zip(refs[:4], refs[5:9]))
    ]
    for copy in copies:
        copy.start()
    for copy in copies:
        copy.wait()
    d = direction_ref[...]
    shapes = codes_ref.shape[0]
    rows, cols = d.shape
    half = cols // 2
    extra_lanes = piece_ref.shape[1] - cols
    inverse = lax.rsqrt(jnp.sum(d * d, axis=1, keepdims=True))
    w = to_column(gain_ref[...]) * (d * inverse)
    lane = lax.broadcasted_iota(jnp.int32, (rows, half), 1)
    first = jnp.where(lane < hid, w[:, :half], w[:, half:])
    code = pltpu.roll(w, half - hid, 1)[:, half:].astype(BF16)
    bias = to_column(bias_ref[...]).astype(BF16).astype(F32)
    high, low = split(dot(code, stacked_codes(codes_ref, extra_lanes), NT) + bias)
    own = first[:, half - LANES :]
    if extra_lanes > LANES:
        own = jnp.concatenate([jnp.zeros((rows, extra_lanes - LANES), F32), own], axis=1)
    lane = lax.broadcasted_iota(jnp.int32, (rows, extra_lanes), 1)
    table = jnp.where(lane < shapes, high, jnp.where(lane < 2 * shapes, low, 0.0))
    table = jnp.where(lane >= extra_lanes - (half - hid), own, table)
    piece_ref[:, :half] = first.astype(BF16)
    piece_ref[:, half : half + extra_lanes] = table.astype(BF16)
    piece_ref[:, half + extra_lanes :] = code


def arrivals(refs, me):
    n = len(refs) // 2
    odd = me % 2 == 1
    return [jnp.where(odd, a[...], b[...]) for a, b in zip(refs[:n], refs[n:])]


def join_kernel(*refs):
    own, out_ref = refs[-2:]
    rows = own.shape[0]
    values = [own[...]] + arrivals(refs[:-2], lax.axis_index(AXES))
    for k, value in enumerate(values):
        out_ref[k * rows : (k + 1) * rows, :] = value


def place(refs, orders, me, lane, out_ref):
    lanes = out_ref.shape[1]
    if orders is None:
        out_ref[...] = refs[0][:, lane : lane + lanes]
        return
    rows = refs[0].shape[0] // len(orders[0])
    for ref, order in zip(refs, orders):
        for k, mask in enumerate(order):
            at = pl.multiple_of((me ^ mask) * rows, rows)
            out_ref[pl.ds(at, rows), :] = ref[k * rows : (k + 1) * rows, lane : lane + lanes]


def inputs_kernel(hid, tile, *refs):
    x_ref, x_t_ref, hidden_ref, offsets_ref, ids_ref, scale_ref, sems = refs[4:]
    points = x_ref.shape[0]
    half = (hid + LANES - 1) // LANES * LANES
    shapes = x_t_ref.shape[0] - half
    extra_lanes = x_ref.shape[1] - half
    steps = points // tile
    small = [
        pltpu.make_async_copy(source, target, sems.at[steps + k])
        for k, (source, target) in enumerate(zip(refs[1:4], (offsets_ref, ids_ref, scale_ref)))
    ]
    large = [
        pltpu.make_async_copy(
            refs[0].at[pl.ds(k * tile, tile), :], hidden_ref.at[pl.ds(k * tile, tile), :], sems.at[k]
        )
        for k in range(steps)
    ]
    for copy in small + large:
        copy.start()
    for copy in small:
        copy.wait()
    for step, copy in enumerate(large):
        here = slice(step * tile, (step + 1) * tile)
        scale = scale_ref[:, here]
        jitter = jnp.where(scale == 0, 1.0, jnp.where(scale == 1, 0.5, 0.25))
        xyz = offsets_ref[:, here] * jitter
        row = lax.broadcasted_iota(jnp.int32, (16, tile), 0)
        last = jnp.zeros((16, tile), F32)
        for k in range(half - hid):
            last = jnp.where(row == 16 - (half - hid) + k, xyz[k : k + 1], last)
        last = last.astype(BF16)
        row = lax.broadcasted_iota(jnp.int32, (extra_lanes - 16, tile), 0)
        ids = ids_ref[:, here]
        member = jnp.where((row == ids) | (row == ids + shapes), 1.0, 0.0).astype(BF16)
        x_ref[here, half:] = jnp.concatenate([member, last], axis=0).T
        x_t_ref[half:, here] = member[:shapes]
        copy.wait()
        x_ref[here, half - LANES : half] = jnp.zeros((tile, LANES), BF16)
        x_ref[here, :hid] = hidden_ref[here, :].astype(BF16)
        hidden = x_ref[here, :half].T
        x_t_ref[: half - 16, here] = hidden[: half - 16]
        x_t_ref[half - 16 : half, here] = hidden[half - 16 :] + last


def layer_kernel(hid, shapes, tile, orders, parts, *refs):
    n = 1 if orders is None else len(orders)
    pieces = refs[:n]
    x_ref, x_t_ref, cot_ref, out_hbm, grad_hidden_hbm = refs[n : n + 5]
    grad_refs = refs[n + 5 : -6]
    w_ref, turned_ref, out_ref, grad_hidden_ref, grad_pre_ref, pre_ref, sems = refs[-7:]
    points, width = cot_ref.shape
    half = width // 2
    steps = points // tile
    me = lax.axis_index(AXES)
    place(pieces, orders, me, 0, w_ref)
    copies = []

    def rows_of(step):
        return slice(step * tile, (step + 1) * tile)

    def forward(step):
        pre_ref[step % 2] = dot(x_ref[rows_of(step), :], w_ref[...], NT)

    def middle(step):
        here = rows_of(step)
        pre = pre_ref[step % 2]
        sigma = 0.5 * jnp.tanh(0.5 * pre) + 0.5
        out = pre * sigma
        out_ref[here, :] = out
        grad_pre_ref[here, :] = (cot_ref[here, :] * (sigma * (1.0 + (pre - out)))).astype(BF16)

    def backward(step):
        here = rows_of(step)
        grad_hidden_ref[here, :] = dot(grad_pre_ref[here, :], w_ref[:, :half])[:, :hid]

    def store(step, k, source, target):
        here = pl.ds(step * tile, tile)
        copy = pltpu.make_async_copy(source.at[here, :], target.at[here, :], sems.at[k, step])
        copy.start()
        copies.append(copy)

    forward(0)
    for step in range(steps):
        if step + 1 < steps:
            forward(step + 1)
        middle(step)
        store(step, 0, out_ref, out_hbm)
        if step > 0:
            backward(step - 1)
            store(step - 1, 1, grad_hidden_ref, grad_hidden_hbm)
    backward(steps - 1)
    store(steps - 1, 1, grad_hidden_ref, grad_hidden_hbm)
    grad = dot(x_t_ref[...], grad_pre_ref[...])
    sums = grad[half:].astype(BF16)
    for at in range(0, width, half):
        turned_ref[at : at + half, :] = grad[:half, at : at + half].T
    for ref, order in zip(grad_refs, parts):
        ref[:shapes, :] = sums[:, :half]
        ref[shapes : 2 * shapes, :] = sums[:, half:]
        if orders is None:
            ref[2 * shapes :, :] = turned_ref[...].astype(BF16)
            continue
        rows = (ref.shape[0] - 2 * shapes) // len(order)
        for k, mask in enumerate(order):
            at = pl.multiple_of((me ^ mask) * rows, rows)
            to = 2 * shapes + k * rows
            ref[to : to + rows, :] = turned_ref[pl.ds(at, rows), :].astype(BF16)

    for copy in copies:
        copy.wait()


def sum_of(refs):
    own = refs[-1][...]
    if len(refs) == 2:
        terms = [own, refs[0][...]]
    else:
        terms = [own] + arrivals(refs[:-1], lax.axis_index(AXES))
    terms = [term.astype(F32) for term in terms]
    while len(terms) > 1:
        terms = [a + b for a, b in zip(terms[::2], terms[1::2])]
    return terms[0]


def add_kernel(shapes, n, *refs):
    total = sum_of(refs[:n]).astype(BF16)
    for k, ref in enumerate(refs[n:]):
        rows = ref.shape[0] - 2 * shapes
        at = 2 * shapes + k * rows
        ref[: 2 * shapes, :] = total[: 2 * shapes]
        ref[2 * shapes :, :] = total[at : at + rows]


def last_kernel(hid, shapes, orders, n, *refs):
    direction_ref, gain_ref, codes_ref = refs[n : n + 3]
    pieces = refs[n + 3 : -5]
    grad_codes_ref, grad_direction_ref, grad_gain_ref, grad_bias_ref, code_scratch = refs[-5:]
    d = direction_ref[...]
    rows, cols = d.shape
    half = cols // 2
    me = lax.axis_index(AXES)
    place(pieces, orders, me, pieces[0].shape[1] - half, code_scratch)
    total = sum_of(refs[:n])
    sums = jnp.concatenate([total[:shapes], total[shapes : 2 * shapes]], axis=1)
    sums = jnp.concatenate(split(sums), axis=0).astype(BF16)
    terms = dot(sums, code_scratch[...])
    grad_codes_ref[...] = terms[:shapes] + terms[shapes:]
    width = sums.shape[1]
    mine = lax.broadcasted_iota(jnp.int32, (rows, width), 0) + me * rows
    mine = jnp.where(mine == lax.broadcasted_iota(jnp.int32, (rows, width), 1), 1.0, 0.0).astype(BF16)
    own = dot(mine, sums, NT)
    grad_bias_ref[...] = to_row(jnp.sum(own, axis=1, keepdims=True))
    code = dot(own.astype(BF16), stacked_codes(codes_ref, 2 * shapes))
    packed = jnp.concatenate([total[2 * shapes :], code], axis=1)
    lane = lax.broadcasted_iota(jnp.int32, (rows, cols), 1)
    grad_weight = jnp.where(
        lane < hid,
        packed,
        jnp.where(lane < hid + half, pltpu.roll(packed, cols - (half - hid), 1), pltpu.roll(packed, half, 1)),
    )
    inverse = lax.rsqrt(jnp.sum(d * d, axis=1, keepdims=True))
    unit = d * inverse
    grad_gain = jnp.sum(grad_weight * unit, axis=1, keepdims=True)
    grad_gain_ref[...] = to_row(grad_gain)
    grad_direction_ref[...] = (to_column(gain_ref[...]) * inverse) * (grad_weight - grad_gain * unit)


def rounds_of(devices):
    bits = [1 << k for k in range(1, devices.bit_length() - 1)][::-1]
    rounds = []
    while bits:
        masks = [0]
        for bit in bits[:2][::-1]:
            masks = masks + [m ^ bit for m in masks]
        rounds.append([0] + [m | 1 for m in masks[1:]])
        bits = bits[2:]
    return rounds + [[0, 1]]


def order_of(rounds):
    order = [0]
    for masks in rounds:
        order = [m ^ r for m in masks for r in order]
    return order


def swaps(arrays, masks, devices):
    def send(sources):
        return [
            lax.ppermute(x, AXES, [(i, i ^ mask) for i in sources])
            for x, mask in zip(arrays, masks)
        ]

    if masks == [1]:
        return send(range(devices))
    return send(range(0, devices, 2)) + send(range(1, devices, 2))


def per_device(
    hidden,
    codes,
    offsets,
    shape_ids,
    scale_index,
    direction,
    gain,
    bias,
    cotangent,
    running_mean,
    running_var,
):
    points, hid = hidden.shape
    shapes = codes.shape[0]
    rows, cols = direction.shape
    width = cotangent.shape[1]
    half = cols // 2
    devices = lax.axis_size("dp") * lax.axis_size("inner")
    tuned = rows % 16 == 0
    rounds = rounds_of(devices)
    tuned = rows % 16 == 0
    bits = [1 << k | 1 for k in range(devices.bit_length() - 1)]
    groups = [bits[k - 2 : k] for k in range(len(bits), 1, -2)]
    groups = groups + [bits[:1]] * (len(bits) % 2)
    tuned = rows % 16 == 0
    extra_lanes = -(-(2 * shapes + 16) // LANES) * LANES
    lanes = half + extra_lanes
    gain_row = gain.reshape(1, rows)

    def shape_of(rows, lanes, dtype):
        return jax.ShapeDtypeStruct((rows, lanes), dtype)

    held = small_kernel(
        "prep",
        functools.partial(prep_kernel, hid),
        shape_of(rows, lanes + half, BF16),
        *[
            pltpu.with_memory_space_constraint(x, pltpu.HBM)
            for x in (direction, gain_row, bias.reshape(1, rows), codes)
        ],
        scratch=[
            VMEM((rows, cols), F32),
            VMEM((1, rows), F32),
            VMEM((1, rows), F32),
            VMEM((shapes, half), F32),
            pltpu.SemaphoreType.DMA((4,)),
        ],
        space=pl.ANY,
    )
    tile, layer_tile = min(512, points), min(256, points)
    x, x_t = pl.pallas_call(
        functools.partial(inputs_kernel, hid, tile),
        out_shape=[shape_of(points, lanes, BF16), shape_of(half + shapes, points, BF16)],
        in_specs=[pl.BlockSpec(memory_space=pl.ANY)] * 4,
        out_specs=vmem(2),
        scratch_shapes=[
            VMEM((points, hid), F32),
            VMEM((half - hid, points), F32),
            VMEM((1, points), jnp.int32),
            VMEM((1, points), jnp.int32),
            pltpu.SemaphoreType.DMA((points // tile + 3,)),
        ],
        compiler_params=pltpu.CompilerParams(vmem_limit_bytes=12 * MIB),
        cost_estimate=pl.CostEstimate(
            flops=4000 * MIB, bytes_accessed=8 * points * half, transcendentals=0
        ),
        name="inputs",
    )(
        *[
            pltpu.with_memory_space_constraint(a, pltpu.HBM)
            for a in (
                hidden,
                offsets.T,
                shape_ids.reshape(1, points),
                scale_index.reshape(1, points),
            )
        ]
    )
    if tuned:
        for masks in rounds[:-1]:
            held = small_kernel(
                "join",
                join_kernel,
                shape_of(held.shape[0] * len(masks), lanes + half, BF16),
                *swaps([held] * (len(masks) - 1), masks[1:], devices),
                held,
            )
        held, x, x_t = lax.optimization_barrier((held, x, x_t))
        pieces = [held] + swaps([held], [1], devices)
        orders = [[m ^ r for r in order_of(rounds[:-1])] for m in rounds[-1]]
        parts = orders
    else:
        pieces, orders, parts = [lax.all_gather(held, AXES, axis=0, tiled=True)], None, [[0]]

    output, grad_hidden, *grads = pl.pallas_call(
        functools.partial(layer_kernel, hid, shapes, layer_tile, orders, parts),
        out_shape=[pltpu.HBM((points, width), F32), pltpu.HBM((points, hid), F32)]
        + [shape_of(2 * shapes + width // len(parts), half, BF16)] * len(parts),
        in_specs=vmem(len(pieces) + 3),
        out_specs=[pl.BlockSpec(memory_space=pltpu.HBM)] * 2 + vmem(len(parts)),
        scratch_shapes=[
            VMEM((width, lanes), BF16),
            VMEM((width, half), F32),
            VMEM((points, width), F32),
            VMEM((points, hid), F32),
            VMEM((points, width), BF16),
            VMEM((2, layer_tile, width), F32),
            pltpu.SemaphoreType.DMA((2, points // layer_tile)),
        ],
        compiler_params=pltpu.CompilerParams(vmem_limit_bytes=20 * MIB),
        cost_estimate=pl.CostEstimate(
            flops=6 * points * width * cols,
            bytes_accessed=8 * points * (width + half),
            transcendentals=points * width,
        ),
        name="layer",
    )(*pieces, x, x_t, cotangent)

    if tuned:
        for masks, later in zip(rounds[::-1], rounds[-2::-1] + [None]):
            grads = swaps(grads[1:], masks[1:], devices) + [grads[0]]
            if later is None:
                break
            left = (grads[0].shape[0] - 2 * shapes) // len(later)
            grads = small_kernel(
                "add",
                functools.partial(add_kernel, shapes, len(grads)),
                [shape_of(2 * shapes + left, half, BF16)] * len(later),
                *grads,
            )
    else:
        sums = lax.psum(grads[0][: 2 * shapes].astype(F32), AXES)
        high = sums.astype(BF16)
        own = lax.psum_scatter(grads[0][2 * shapes :].astype(F32), AXES, scatter_dimension=0, tiled=True)
        low = jnp.zeros((2 * shapes + rows, half), BF16).at[: 2 * shapes].set((sums - high).astype(BF16))
        grads = [jnp.concatenate([high, own.astype(BF16)], axis=0), low]
    grad_codes, grad_direction, grad_gain, grad_bias = small_kernel(
        "last",
        functools.partial(last_kernel, hid, shapes, orders, len(grads)),
        [
            shape_of(shapes, half, F32),
            shape_of(rows, cols, F32),
            shape_of(1, rows, F32),
            shape_of(1, rows, F32),
        ],
        *grads,
        direction,
        gain_row,
        codes,
        *pieces,
        scratch=[VMEM((width, half), BF16)],
    )

    total = float(points * devices)
    batch_mean = jnp.mean(codes, axis=0)
    batch_square = jnp.mean(codes * codes, axis=0)
    batch_var = (batch_square - batch_mean * batch_mean) * (total / (total - 1.0))
    new_mean = 0.9 * running_mean + 0.1 * batch_mean
    new_var = 0.9 * running_var + 0.1 * batch_var
    return (
        output,
        grad_hidden,
        grad_codes,
        grad_direction,
        grad_gain.reshape(rows),
        grad_bias.reshape(rows),
        new_mean,
        new_var,
    )


def solution(mesh):
    return jax.shard_map(
        per_device,
        mesh=mesh,
        in_specs=(
            P(("dp", "inner"), None),
            P(),
            P(("dp", "inner"), None),
            P(("dp", "inner")),
            P(("dp", "inner")),
            P(("dp", "inner"), None),
            P(("dp", "inner")),
            P(("dp", "inner")),
            P(("dp", "inner"), None),
            P(),
            P(),
        ),
        out_specs=(
            P(("dp", "inner"), None),
            P(("dp", "inner"), None),
            P(),
            P(("dp", "inner"), None),
            P(("dp", "inner")),
            P(("dp", "inner")),
            P(),
            P(),
        ),
        check_vma=False,
    )
```

```python
import functools

import jax
import jax.numpy as jnp
from jax import lax
from jax.experimental import pallas as pl
from jax.experimental.pallas import tpu as pltpu
from jax.sharding import PartitionSpec as P

AXES = ("dp", "inner")
LANES = 128
MIB = 1024 * 1024
F32 = jnp.float32
BF16 = jnp.bfloat16
VMEM = pltpu.VMEM
NT = (((1,), (1,)), ((), ()))


def dot(a, b, dims=(((1,), (0,)), ((), ()))):
    return lax.dot_general(a, b, dims, preferred_element_type=F32)


def vmem(n):
    return [pl.BlockSpec(memory_space=VMEM)] * n


def small_kernel(name, body, out_shape, *args, scratch=(), space=VMEM, limit=8):
    many = isinstance(out_shape, list)
    return pl.pallas_call(
        body,
        out_shape=out_shape,
        in_specs=[pl.BlockSpec(memory_space=space)] * len(args),
        out_specs=vmem(len(out_shape)) if many else vmem(1)[0],
        scratch_shapes=list(scratch),
        compiler_params=pltpu.CompilerParams(vmem_limit_bytes=limit * MIB),
        cost_estimate=pl.CostEstimate(
            flops=4000 * MIB, bytes_accessed=8 * MIB, transcendentals=4 * MIB
        ),
        name=name,
    )(*args)


def diagonal(n):
    return lax.broadcasted_iota(jnp.int32, (n, n), 0) == lax.broadcasted_iota(jnp.int32, (n, n), 1)


def to_column(row):
    n = row.shape[1]
    return jnp.sum(jnp.where(diagonal(n), row, 0.0), axis=1, keepdims=True)


def to_row(column):
    n = column.shape[0]
    return jnp.sum(jnp.where(diagonal(n), column, 0.0), axis=0, keepdims=True)


def stacked_codes(codes_ref, count):
    codes = codes_ref[...].astype(BF16)
    parts = [codes, codes]
    if count > 2 * codes.shape[0]:
        parts.append(jnp.zeros((count - 2 * codes.shape[0], codes.shape[1]), BF16))
    return jnp.concatenate(parts, axis=0)


def split(x):
    high = x.astype(BF16).astype(F32)
    return high, x - high


def prep_kernel(hid, *refs):
    piece_ref, direction_ref, gain_ref, bias_ref, codes_ref, sems = refs[4:]
    copies = [
        pltpu.make_async_copy(source, target, sems.at[k])
        for k, (source, target) in enumerate(zip(refs[:4], refs[5:9]))
    ]
    for copy in copies:
        copy.start()
    for copy in copies:
        copy.wait()
    d = direction_ref[...]
    shapes = codes_ref.shape[0]
    rows, cols = d.shape
    half = cols // 2
    extra_lanes = piece_ref.shape[1] - cols
    inverse = lax.rsqrt(jnp.sum(d * d, axis=1, keepdims=True))
    w = to_column(gain_ref[...]) * (d * inverse)
    lane = lax.broadcasted_iota(jnp.int32, (rows, half), 1)
    first = jnp.where(lane < hid, w[:, :half], w[:, half:])
    code = pltpu.roll(w, half - hid, 1)[:, half:].astype(BF16)
    bias = to_column(bias_ref[...]).astype(BF16).astype(F32)
    high, low = split(dot(code, stacked_codes(codes_ref, extra_lanes), NT) + bias)
    own = first[:, half - LANES :]
    if extra_lanes > LANES:
        own = jnp.concatenate([jnp.zeros((rows, extra_lanes - LANES), F32), own], axis=1)
    lane = lax.broadcasted_iota(jnp.int32, (rows, extra_lanes), 1)
    table = jnp.where(lane < shapes, high, jnp.where(lane < 2 * shapes, low, 0.0))
    table = jnp.where(lane >= extra_lanes - (half - hid), own, table)
    piece_ref[:, :half] = first.astype(BF16)
    piece_ref[:, half : half + extra_lanes] = table.astype(BF16)
    piece_ref[:, half + extra_lanes :] = code


def join_kernel(n, *refs):
    rows = refs[0].shape[0]
    for k, ref in enumerate(refs[n - 1 :: -1]):
        lane = 0
        for out_ref in refs[n:]:
            lanes = out_ref.shape[1]
            out_ref[k * rows : (k + 1) * rows, :] = ref[:, lane : lane + lanes]
            lane += lanes


def place(refs, orders, me, out_ref):
    if orders is None:
        out_ref[...] = refs[0][...]
        return
    rows = refs[0].shape[0] // len(orders[0])
    for ref, order in zip(refs, orders):
        for k, mask in enumerate(order):
            at = pl.multiple_of((me ^ mask) * rows, rows)
            out_ref[pl.ds(at, rows), :] = ref[k * rows : (k + 1) * rows, :]


def inputs_kernel(hid, tile, *refs):
    x_ref, x_t_ref, hidden_ref, offsets_ref, ids_ref, scale_ref, sems = refs[4:]
    points = x_ref.shape[0]
    half = (hid + LANES - 1) // LANES * LANES
    shapes = x_t_ref.shape[0] - half
    extra_lanes = x_ref.shape[1] - half
    steps = points // tile
    small = [
        pltpu.make_async_copy(source, target, sems.at[steps + k])
        for k, (source, target) in enumerate(zip(refs[1:4], (offsets_ref, ids_ref, scale_ref)))
    ]
    large = [
        pltpu.make_async_copy(
            refs[0].at[pl.ds(k * tile, tile), :], hidden_ref.at[pl.ds(k * tile, tile), :], sems.at[k]
        )
        for k in range(steps)
    ]
    for copy in small + large:
        copy.start()
    for copy in small:
        copy.wait()
    for step, copy in enumerate(large):
        here = slice(step * tile, (step + 1) * tile)
        scale = scale_ref[:, here]
        jitter = jnp.where(scale == 0, 1.0, jnp.where(scale == 1, 0.5, 0.25))
        xyz = offsets_ref[:, here] * jitter
        row = lax.broadcasted_iota(jnp.int32, (16, tile), 0)
        last = jnp.zeros((16, tile), F32)
        for k in range(half - hid):
            last = jnp.where(row == 16 - (half - hid) + k, xyz[k : k + 1], last)
        last = last.astype(BF16)
        row = lax.broadcasted_iota(jnp.int32, (extra_lanes - 16, tile), 0)
        ids = ids_ref[:, here]
        member = jnp.where((row == ids) | (row == ids + shapes), 1.0, 0.0).astype(BF16)
        x_ref[here, half:] = jnp.concatenate([member, last], axis=0).T
        x_t_ref[half:, here] = member[:shapes]
        copy.wait()
        x_ref[here, half - LANES : half] = jnp.zeros((tile, LANES), BF16)
        x_ref[here, :hid] = hidden_ref[here, :].astype(BF16)
        hidden = x_ref[here, :half].T
        x_t_ref[: half - 16, here] = hidden[: half - 16]
        x_t_ref[half - 16 : half, here] = hidden[half - 16 :] + last


def layer_kernel(hid, shapes, tile, orders, parts, *refs):
    n = 1 if orders is None else len(orders)
    pieces = refs[:n]
    x_ref, x_t_ref, cot_ref, out_hbm, grad_hidden_hbm = refs[n : n + 5]
    grad_refs = refs[n + 5 : -6]
    w_ref, turned_ref, out_ref, grad_hidden_ref, grad_pre_ref, pre_ref, sems = refs[-7:]
    points, width = cot_ref.shape
    half = width // 2
    steps = points // tile
    me = lax.axis_index(AXES)
    place(pieces, orders, me, w_ref)
    copies = []

    def rows_of(step):
        return slice(step * tile, (step + 1) * tile)

    def forward(step):
        pre_ref[step % 2] = dot(x_ref[rows_of(step), :], w_ref[...], NT)

    def middle(step):
        here = rows_of(step)
        pre = pre_ref[step % 2]
        sigma = 0.5 * jnp.tanh(0.5 * pre) + 0.5
        out = pre * sigma
        out_ref[here, :] = out
        grad_pre_ref[here, :] = (cot_ref[here, :] * (sigma * (1.0 + (pre - out)))).astype(BF16)

    def backward(step):
        here = rows_of(step)
        grad_hidden_ref[here, :] = dot(grad_pre_ref[here, :], w_ref[:, :half])[:, :hid]

    def store(step, k, source, target):
        here = pl.ds(step * tile, tile)
        copy = pltpu.make_async_copy(source.at[here, :], target.at[here, :], sems.at[k, step])
        copy.start()
        copies.append(copy)

    forward(0)
    for step in range(steps):
        if step + 1 < steps:
            forward(step + 1)
        middle(step)
        store(step, 0, out_ref, out_hbm)
        if step > 0:
            backward(step - 1)
            store(step - 1, 1, grad_hidden_ref, grad_hidden_hbm)
    backward(steps - 1)
    store(steps - 1, 1, grad_hidden_ref, grad_hidden_hbm)
    grad = dot(x_t_ref[...], grad_pre_ref[...])
    sums = grad[half:].astype(BF16)
    for at in range(0, width, half):
        turned_ref[at : at + half, :] = grad[:half, at : at + half].T
    for ref, order in zip(grad_refs, parts):
        ref[:shapes, :] = sums[:, :half]
        ref[shapes : 2 * shapes, :] = sums[:, half:]
        if orders is None:
            ref[2 * shapes :, :] = turned_ref[...].astype(BF16)
            continue
        rows = (ref.shape[0] - 2 * shapes) // len(order)
        for k, mask in enumerate(order):
            at = pl.multiple_of((me ^ mask) * rows, rows)
            to = 2 * shapes + k * rows
            ref[to : to + rows, :] = turned_ref[pl.ds(at, rows), :].astype(BF16)

    for copy in copies:
        copy.wait()


def sum_of(refs):
    terms = [ref[...].astype(F32) for ref in refs]
    while len(terms) > 1:
        terms = [a + b for a, b in zip(terms[::2], terms[1::2])]
    return terms[0]


def add_kernel(shapes, n, *refs):
    total = sum_of(refs[:n]).astype(BF16)
    for k, ref in enumerate(refs[n:]):
        rows = ref.shape[0] - 2 * shapes
        at = 2 * shapes + k * rows
        ref[: 2 * shapes, :] = total[: 2 * shapes]
        ref[2 * shapes :, :] = total[at : at + rows]


def last_kernel(hid, shapes, orders, n, *refs):
    direction_ref, gain_ref, codes_ref = refs[n : n + 3]
    pieces = refs[n + 3 : -5]
    grad_codes_ref, grad_direction_ref, grad_gain_ref, grad_bias_ref, code_scratch = refs[-5:]
    d = direction_ref[...]
    rows, cols = d.shape
    half = cols // 2
    me = lax.axis_index(AXES)
    place(pieces, orders, me, code_scratch)
    total = sum_of(refs[:n])
    sums = jnp.concatenate([total[:shapes], total[shapes : 2 * shapes]], axis=1)
    sums = jnp.concatenate(split(sums), axis=0).astype(BF16)
    terms = dot(sums, code_scratch[...])
    grad_codes_ref[...] = terms[:shapes] + terms[shapes:]
    width = sums.shape[1]
    mine = lax.broadcasted_iota(jnp.int32, (rows, width), 0) + me * rows
    mine = jnp.where(mine == lax.broadcasted_iota(jnp.int32, (rows, width), 1), 1.0, 0.0).astype(BF16)
    own = dot(mine, sums, NT)
    grad_bias_ref[...] = to_row(jnp.sum(own, axis=1, keepdims=True))
    code = dot(own.astype(BF16), stacked_codes(codes_ref, 2 * shapes))
    packed = jnp.concatenate([total[2 * shapes :], code], axis=1)
    lane = lax.broadcasted_iota(jnp.int32, (rows, cols), 1)
    grad_weight = jnp.where(
        lane < hid,
        packed,
        jnp.where(lane < hid + half, pltpu.roll(packed, cols - (half - hid), 1), pltpu.roll(packed, half, 1)),
    )
    inverse = lax.rsqrt(jnp.sum(d * d, axis=1, keepdims=True))
    unit = d * inverse
    grad_gain = jnp.sum(grad_weight * unit, axis=1, keepdims=True)
    grad_gain_ref[...] = to_row(grad_gain)
    grad_direction_ref[...] = (to_column(gain_ref[...]) * inverse) * (grad_weight - grad_gain * unit)


def masks_of(group):
    masks = [0]
    for bit in group:
        masks = masks + [m ^ bit for m in masks]
    return masks


def order_of(groups):
    order = [0]
    for group in groups:
        order = [m ^ r for m in masks_of(group) for r in order]
    return order


def swaps(arrays, masks, devices):
    moved = [
        lax.ppermute(x, AXES, [(i, i ^ mask) for i in range(devices)])
        for x, mask in list(zip(arrays, masks))[::-1]
    ]
    return moved[::-1]


def per_device(
    hidden,
    codes,
    offsets,
    shape_ids,
    scale_index,
    direction,
    gain,
    bias,
    cotangent,
    running_mean,
    running_var,
):
    points, hid = hidden.shape
    shapes = codes.shape[0]
    rows, cols = direction.shape
    width = cotangent.shape[1]
    half = cols // 2
    devices = lax.axis_size("dp") * lax.axis_size("inner")
    tuned = rows % 16 == 0
    bits = [1 << k | 1 for k in range(devices.bit_length() - 1)]
    groups = [bits[k - 2 : k] for k in range(len(bits), 1, -2)]
    groups = groups + [bits[:1]] * (len(bits) % 2)
    tuned = rows % 16 == 0
    extra_lanes = -(-(2 * shapes + 16) // LANES) * LANES
    lanes = half + extra_lanes
    gain_row = gain.reshape(1, rows)

    def shape_of(rows, lanes, dtype):
        return jax.ShapeDtypeStruct((rows, lanes), dtype)

    held = small_kernel(
        "prep",
        functools.partial(prep_kernel, hid),
        shape_of(rows, lanes + half, BF16),
        *[
            pltpu.with_memory_space_constraint(x, pltpu.HBM)
            for x in (direction, gain_row, bias.reshape(1, rows), codes)
        ],
        scratch=[
            VMEM((rows, cols), F32),
            VMEM((1, rows), F32),
            VMEM((1, rows), F32),
            VMEM((shapes, half), F32),
            pltpu.SemaphoreType.DMA((4,)),
        ],
        space=pl.ANY,
    )
    tile, layer_tile = min(512, points), min(256, points)
    x, x_t = pl.pallas_call(
        functools.partial(inputs_kernel, hid, tile),
        out_shape=[shape_of(points, lanes, BF16), shape_of(half + shapes, points, BF16)],
        in_specs=[pl.BlockSpec(memory_space=pl.ANY)] * 4,
        out_specs=vmem(2),
        scratch_shapes=[
            VMEM((points, hid), F32),
            VMEM((half - hid, points), F32),
            VMEM((1, points), jnp.int32),
            VMEM((1, points), jnp.int32),
            pltpu.SemaphoreType.DMA((points // tile + 3,)),
        ],
        compiler_params=pltpu.CompilerParams(vmem_limit_bytes=12 * MIB),
        cost_estimate=pl.CostEstimate(
            flops=4000 * MIB, bytes_accessed=8 * points * half, transcendentals=0
        ),
        name="inputs",
    )(
        *[
            pltpu.with_memory_space_constraint(a, pltpu.HBM)
            for a in (
                hidden,
                offsets.T,
                shape_ids.reshape(1, points),
                scale_index.reshape(1, points),
            )
        ]
    )
    def gather(array, group):
        masks = masks_of(group)[1:]
        return [array] + swaps([array] * len(masks), masks, devices)

    def join(arrays, *widths):
        height = sum(a.shape[0] for a in arrays)
        return small_kernel(
            "join",
            functools.partial(join_kernel, len(arrays)),
            [shape_of(height, width, BF16) for width in widths],
            *arrays[::-1],
        )

    if tuned:
        weight, code_weight = join(gather(held, groups[0]), lanes, half)
        weight, code_weight, x, x_t = lax.optimization_barrier((weight, code_weight, x, x_t))
        steps = [[bit] for group in groups[1:-1] for bit in group[::-1]]
        code_order = order_of(groups[:1] + steps)
        for group in groups[1:-1]:
            weights, code_weights = gather(weight, group), gather(code_weight, steps[0])
            (weight,) = join(weights, lanes)
            (code_weight,) = join(code_weights, half)
        weights = gather(weight, groups[-1])
        code_weights = gather(code_weight, steps[1])
        orders = [[m ^ r for r in order_of(groups[:-1])] for m in masks_of(groups[-1])]
        code_orders = [[m ^ r for r in code_order] for m in masks_of(groups[-1])]
        parts = orders
    else:
        held = lax.all_gather(held, AXES, axis=0, tiled=True)
        weights, code_weights, orders, code_orders, parts = [held[:, :lanes]], [held[:, lanes:]], None, None, [[0]]

    output, grad_hidden, *grads = pl.pallas_call(
        functools.partial(layer_kernel, hid, shapes, layer_tile, orders, parts),
        out_shape=[pltpu.HBM((points, width), F32), pltpu.HBM((points, hid), F32)]
        + [shape_of(2 * shapes + width // len(parts), half, BF16)] * len(parts),
        in_specs=vmem(len(weights) + 3),
        out_specs=[pl.BlockSpec(memory_space=pltpu.HBM)] * 2 + vmem(len(parts)),
        scratch_shapes=[
            VMEM((width, lanes), BF16),
            VMEM((width, half), F32),
            VMEM((points, width), F32),
            VMEM((points, hid), F32),
            VMEM((points, width), BF16),
            VMEM((2, layer_tile, width), F32),
            pltpu.SemaphoreType.DMA((2, points // layer_tile)),
        ],
        compiler_params=pltpu.CompilerParams(vmem_limit_bytes=20 * MIB),
        cost_estimate=pl.CostEstimate(
            flops=6 * points * width * cols,
            bytes_accessed=8 * points * (width + half),
            transcendentals=points * width,
        ),
        name="layer",
    )(*weights, x, x_t, cotangent)

    if tuned:
        *grads, code_weight = lax.optimization_barrier((*grads, code_weights[1]))
        (code_weight,) = join([code_weights[0], code_weight], half)
        code_weights = gather(code_weight, groups[-1])
        for r, group in enumerate(groups[::-1]):
            masks = masks_of(group)
            grads = [grads[0]] + swaps(grads[1:], masks[1:], devices)
            if r == len(groups) - 1:
                break
            n_out = len(masks_of(groups[-2 - r]))
            left = (grads[0].shape[0] - 2 * shapes) // n_out
            grads = small_kernel(
                "add",
                functools.partial(add_kernel, shapes, len(grads)),
                [shape_of(2 * shapes + left, half, BF16)] * n_out,
                *grads[::-1],
            )
    else:
        sums = lax.psum(grads[0][: 2 * shapes].astype(F32), AXES)
        high = sums.astype(BF16)
        own = lax.psum_scatter(grads[0][2 * shapes :].astype(F32), AXES, scatter_dimension=0, tiled=True)
        low = jnp.zeros((2 * shapes + rows, half), BF16).at[: 2 * shapes].set((sums - high).astype(BF16))
        grads = [jnp.concatenate([high, own.astype(BF16)], axis=0), low]
    grad_codes, grad_direction, grad_gain, grad_bias = small_kernel(
        "last",
        functools.partial(last_kernel, hid, shapes, code_orders, len(grads)),
        [
            shape_of(shapes, half, F32),
            shape_of(rows, cols, F32),
            shape_of(1, rows, F32),
            shape_of(1, rows, F32),
        ],
        *grads[::-1],
        direction,
        gain_row,
        codes,
        *code_weights,
        scratch=[VMEM((width, half), BF16)],
    )

    total = float(points * devices)
    batch_mean = jnp.mean(codes, axis=0)
    batch_square = jnp.mean(codes * codes, axis=0)
    batch_var = (batch_square - batch_mean * batch_mean) * (total / (total - 1.0))
    new_mean = 0.9 * running_mean + 0.1 * batch_mean
    new_var = 0.9 * running_var + 0.1 * batch_var
    return (
        output,
        grad_hidden,
        grad_codes,
        grad_direction,
        grad_gain.reshape(rows),
        grad_bias.reshape(rows),
        new_mean,
        new_var,
    )


def solution(mesh):
    return jax.shard_map(
        per_device,
        mesh=mesh,
        in_specs=(
            P(("dp", "inner"), None),
            P(),
            P(("dp", "inner"), None),
            P(("dp", "inner")),
            P(("dp", "inner")),
            P(("dp", "inner"), None),
            P(("dp", "inner")),
            P(("dp", "inner")),
            P(("dp", "inner"), None),
            P(),
            P(),
        ),
        out_specs=(
            P(("dp", "inner"), None),
            P(("dp", "inner"), None),
            P(),
            P(("dp", "inner"), None),
            P(("dp", "inner")),
            P(("dp", "inner")),
            P(),
            P(),
        ),
        check_vma=False,
    )
```

```python
import functools

import jax
import jax.numpy as jnp
from jax import lax
from jax.experimental import pallas as pl
from jax.experimental.pallas import tpu as pltpu
from jax.sharding import PartitionSpec as P

AXES = ("dp", "inner")
LANES = 128
MIB = 1024 * 1024
F32 = jnp.float32
BF16 = jnp.bfloat16
VMEM = pltpu.VMEM
NT = (((1,), (1,)), ((), ()))


def dot(a, b, dims=(((1,), (0,)), ((), ()))):
    return lax.dot_general(a, b, dims, preferred_element_type=F32)


def vmem(n):
    return [pl.BlockSpec(memory_space=VMEM)] * n


def small_kernel(name, body, out_shape, *args, scratch=(), space=VMEM, limit=8):
    many = isinstance(out_shape, list)
    return pl.pallas_call(
        body,
        out_shape=out_shape,
        in_specs=[pl.BlockSpec(memory_space=space)] * len(args),
        out_specs=vmem(len(out_shape)) if many else vmem(1)[0],
        scratch_shapes=list(scratch),
        compiler_params=pltpu.CompilerParams(vmem_limit_bytes=limit * MIB),
        cost_estimate=pl.CostEstimate(
            flops=600 * MIB, bytes_accessed=8 * MIB, transcendentals=0
        ),
        name=name,
    )(*args)


def diagonal(n):
    return lax.broadcasted_iota(jnp.int32, (n, n), 0) == lax.broadcasted_iota(jnp.int32, (n, n), 1)


def to_column(row):
    n = row.shape[1]
    return jnp.sum(jnp.where(diagonal(n), row, 0.0), axis=1, keepdims=True)


def to_row(column):
    n = column.shape[0]
    return jnp.sum(jnp.where(diagonal(n), column, 0.0), axis=0, keepdims=True)


def stacked_codes(codes_ref, count):
    codes = codes_ref[...].astype(BF16)
    parts = [codes, codes]
    if count > 2 * codes.shape[0]:
        parts.append(jnp.zeros((count - 2 * codes.shape[0], codes.shape[1]), BF16))
    return jnp.concatenate(parts, axis=0)


def split(x):
    high = x.astype(BF16).astype(F32)
    return high, x - high


def prep_kernel(hid, *refs):
    piece_ref, direction_ref, gain_ref, bias_ref, codes_ref, sems = refs[4:]
    copies = [
        pltpu.make_async_copy(source, target, sems.at[k])
        for k, (source, target) in enumerate(zip(refs[:4], refs[5:9]))
    ]
    for copy in copies:
        copy.start()
    for copy in copies:
        copy.wait()
    d = direction_ref[...]
    shapes = codes_ref.shape[0]
    rows, cols = d.shape
    half = cols // 2
    extra_lanes = piece_ref.shape[1] - cols
    inverse = lax.rsqrt(jnp.sum(d * d, axis=1, keepdims=True))
    w = to_column(gain_ref[...]) * (d * inverse)
    lane = lax.broadcasted_iota(jnp.int32, (rows, half), 1)
    first = 0.5 * jnp.where(lane < hid, w[:, :half], w[:, half:])
    code = pltpu.roll(w, half - hid, 1)[:, half:].astype(BF16)
    bias = to_column(bias_ref[...]).astype(BF16).astype(F32)
    high, low = split(0.5 * (dot(code, stacked_codes(codes_ref, extra_lanes), NT) + bias))
    own = first[:, half - LANES :]
    if extra_lanes > LANES:
        own = jnp.concatenate([jnp.zeros((rows, extra_lanes - LANES), F32), own], axis=1)
    lane = lax.broadcasted_iota(jnp.int32, (rows, extra_lanes), 1)
    table = jnp.where(lane < shapes, high, jnp.where(lane < 2 * shapes, low, 0.0))
    table = jnp.where(lane >= extra_lanes - (half - hid), own, table)
    piece_ref[:, :half] = first.astype(BF16)
    piece_ref[:, half : half + extra_lanes] = table.astype(BF16)
    piece_ref[:, half + extra_lanes :] = code


def join_kernel(n, *refs):
    rows = refs[0].shape[0]
    for k, ref in enumerate(refs[n - 1 :: -1]):
        lane = 0
        for out_ref in refs[n:]:
            lanes = out_ref.shape[1]
            out_ref[k * rows : (k + 1) * rows, :] = ref[:, lane : lane + lanes]
            lane += lanes


def place(refs, orders, me, out_ref):
    if orders is None:
        out_ref[...] = refs[0][...]
        return
    rows = refs[0].shape[0] // len(orders[0])
    for ref, order in zip(refs, orders):
        for k, mask in enumerate(order):
            at = pl.multiple_of((me ^ mask) * rows, rows)
            out_ref[pl.ds(at, rows), :] = ref[k * rows : (k + 1) * rows, :]


def inputs_kernel(hid, tile, *refs):
    x_ref, x_t_ref, hidden_ref, offsets_ref, ids_ref, scale_ref, sems = refs[4:]
    points = x_ref.shape[0]
    half = (hid + LANES - 1) // LANES * LANES
    shapes = x_t_ref.shape[0] - half
    extra_lanes = x_ref.shape[1] - half
    steps = points // tile
    small = [
        pltpu.make_async_copy(source, target, sems.at[steps + k])
        for k, (source, target) in enumerate(zip(refs[1:4], (offsets_ref, ids_ref, scale_ref)))
    ]
    large = [
        pltpu.make_async_copy(
            refs[0].at[pl.ds(k * tile, tile), :], hidden_ref.at[pl.ds(k * tile, tile), :], sems.at[k]
        )
        for k in range(steps)
    ]
    for copy in small + large:
        copy.start()
    for copy in small:
        copy.wait()
    for step, copy in enumerate(large):
        here = slice(step * tile, (step + 1) * tile)
        scale = scale_ref[:, here]
        jitter = jnp.where(scale == 0, 1.0, jnp.where(scale == 1, 0.5, 0.25))
        xyz = offsets_ref[:, here] * jitter
        row = lax.broadcasted_iota(jnp.int32, (16, tile), 0)
        last = jnp.zeros((16, tile), F32)
        for k in range(half - hid):
            last = jnp.where(row == 16 - (half - hid) + k, xyz[k : k + 1], last)
        last = last.astype(BF16)
        row = lax.broadcasted_iota(jnp.int32, (extra_lanes - 16, tile), 0)
        ids = ids_ref[:, here]
        member = jnp.where((row == ids) | (row == ids + shapes), 1.0, 0.0).astype(BF16)
        x_ref[here, half:] = jnp.concatenate([member, last], axis=0).T
        x_t_ref[half:, here] = member[:shapes]
        copy.wait()
        x_ref[here, half - LANES : half] = jnp.zeros((tile, LANES), BF16)
        x_ref[here, :hid] = hidden_ref[here, :].astype(BF16)
        hidden = x_ref[here, :half].T
        x_t_ref[: half - 16, here] = hidden[: half - 16]
        x_t_ref[half - 16 : half, here] = hidden[half - 16 :] + last


def layer_kernel(hid, shapes, tile, orders, parts, *refs):
    n = 1 if orders is None else len(orders)
    pieces = refs[:n]
    x_ref, x_t_ref, cot_ref, out_hbm, grad_hidden_hbm = refs[n : n + 5]
    grad_refs = refs[n + 5 : -6]
    w_ref, turned_ref, out_ref, grad_hidden_ref, grad_pre_ref, pre_ref, sems = refs[-7:]
    points, width = cot_ref.shape
    half = width // 2
    steps = points // tile
    me = lax.axis_index(AXES)
    place(pieces, orders, me, w_ref)
    copies = []

    def rows_of(step):
        return slice(step * tile, (step + 1) * tile)

    def forward(step):
        pre_ref[step % 2] = dot(x_ref[rows_of(step), :], w_ref[...], NT)

    def middle(step):
        here = rows_of(step)
        h = pre_ref[step % 2]
        u = jnp.tanh(h) + 1.0
        out = h * u
        out_ref[here, :] = out
        grad_pre_ref[here, :] = (cot_ref[here, :] * (u * ((h + h) + 1.0 - out))).astype(BF16)

    def backward(step):
        here = rows_of(step)
        grad_hidden_ref[here, :] = dot(grad_pre_ref[here, :], w_ref[:, :half])[:, :hid]

    def store(step, k, source, target):
        here = pl.ds(step * tile, tile)
        copy = pltpu.make_async_copy(source.at[here, :], target.at[here, :], sems.at[k, step])
        copy.start()
        copies.append(copy)

    forward(0)
    for step in range(steps):
        if step + 1 < steps:
            forward(step + 1)
        middle(step)
        store(step, 0, out_ref, out_hbm)
        if step > 0:
            backward(step - 1)
            store(step - 1, 1, grad_hidden_ref, grad_hidden_hbm)
    backward(steps - 1)
    store(steps - 1, 1, grad_hidden_ref, grad_hidden_hbm)
    grad = (0.5 * dot(x_t_ref[...], grad_pre_ref[...])).astype(BF16)
    sums = grad[half:]
    for at in range(0, width, half):
        turned_ref[at : at + half, :] = grad[:half, at : at + half].T
    for ref, order in zip(grad_refs, parts):
        ref[:shapes, :] = sums[:, :half]
        ref[shapes : 2 * shapes, :] = sums[:, half:]
        if orders is None:
            ref[2 * shapes :, :] = turned_ref[...]
            continue
        rows = (ref.shape[0] - 2 * shapes) // len(order)
        for k, mask in enumerate(order):
            at = pl.multiple_of((me ^ mask) * rows, rows)
            to = 2 * shapes + k * rows
            ref[to : to + rows, :] = turned_ref[pl.ds(at, rows), :]

    for copy in copies:
        copy.wait()


def sum_of(refs):
    terms = [ref[...].astype(F32) for ref in refs]
    while len(terms) > 1:
        terms = [a + b for a, b in zip(terms[::2], terms[1::2])]
    return terms[0]


def add_kernel(shapes, n, *refs):
    total = sum_of(refs[:n]).astype(BF16)
    for k, ref in enumerate(refs[n:]):
        rows = ref.shape[0] - 2 * shapes
        at = 2 * shapes + k * rows
        ref[: 2 * shapes, :] = total[: 2 * shapes]
        ref[2 * shapes :, :] = total[at : at + rows]


def last_kernel(hid, shapes, orders, n, *refs):
    direction_ref, gain_ref, codes_ref = refs[n : n + 3]
    pieces = refs[n + 3 : -5]
    grad_codes_ref, grad_direction_ref, grad_gain_ref, grad_bias_ref, code_scratch = refs[-5:]
    d = direction_ref[...]
    rows, cols = d.shape
    half = cols // 2
    me = lax.axis_index(AXES)
    place(pieces, orders, me, code_scratch)
    total = sum_of(refs[:n])
    sums = jnp.concatenate([total[:shapes], total[shapes : 2 * shapes]], axis=1)
    sums = jnp.concatenate(split(sums), axis=0).astype(BF16)
    terms = dot(sums, code_scratch[...])
    grad_codes_ref[...] = terms[:shapes] + terms[shapes:]
    width = sums.shape[1]
    mine = lax.broadcasted_iota(jnp.int32, (rows, width), 0) + me * rows
    mine = jnp.where(mine == lax.broadcasted_iota(jnp.int32, (rows, width), 1), 1.0, 0.0).astype(BF16)
    own = dot(mine, sums, NT)
    grad_bias_ref[...] = to_row(jnp.sum(own, axis=1, keepdims=True))
    code = dot(own.astype(BF16), stacked_codes(codes_ref, 2 * shapes))
    packed = jnp.concatenate([total[2 * shapes :], code], axis=1)
    lane = lax.broadcasted_iota(jnp.int32, (rows, cols), 1)
    grad_weight = jnp.where(
        lane < hid,
        packed,
        jnp.where(lane < hid + half, pltpu.roll(packed, cols - (half - hid), 1), pltpu.roll(packed, half, 1)),
    )
    inverse = lax.rsqrt(jnp.sum(d * d, axis=1, keepdims=True))
    unit = d * inverse
    grad_gain = jnp.sum(grad_weight * unit, axis=1, keepdims=True)
    grad_gain_ref[...] = to_row(grad_gain)
    grad_direction_ref[...] = (to_column(gain_ref[...]) * inverse) * (grad_weight - grad_gain * unit)


def masks_of(group):
    masks = [0]
    for bit in group:
        masks = masks + [m ^ bit for m in masks]
    return masks


def order_of(groups):
    order = [0]
    for group in groups:
        order = [m ^ r for m in masks_of(group) for r in order]
    return order


def swaps(arrays, masks, devices):
    moved = [
        lax.ppermute(x, AXES, [(i, i ^ mask) for i in range(devices)])
        for x, mask in list(zip(arrays, masks))[::-1]
    ]
    return moved[::-1]


def per_device(
    hidden,
    codes,
    offsets,
    shape_ids,
    scale_index,
    direction,
    gain,
    bias,
    cotangent,
    running_mean,
    running_var,
):
    points, hid = hidden.shape
    shapes = codes.shape[0]
    rows, cols = direction.shape
    width = cotangent.shape[1]
    half = cols // 2
    devices = lax.axis_size("dp") * lax.axis_size("inner")
    tuned = rows % 16 == 0
    bits = [1 << k | 1 for k in range(devices.bit_length() - 1)]
    groups = [bits[k - 2 : k] for k in range(len(bits), 1, -2)]
    groups = groups + [bits[:1]] * (len(bits) % 2)
    tuned = rows % 16 == 0
    extra_lanes = -(-(2 * shapes + 16) // LANES) * LANES
    lanes = half + extra_lanes
    gain_row = gain.reshape(1, rows)

    def shape_of(rows, lanes, dtype):
        return jax.ShapeDtypeStruct((rows, lanes), dtype)

    held = small_kernel(
        "prep",
        functools.partial(prep_kernel, hid),
        shape_of(rows, lanes + half, BF16),
        *[
            pltpu.with_memory_space_constraint(x, pltpu.HBM)
            for x in (direction, gain_row, bias.reshape(1, rows), codes)
        ],
        scratch=[
            VMEM((rows, cols), F32),
            VMEM((1, rows), F32),
            VMEM((1, rows), F32),
            VMEM((shapes, half), F32),
            pltpu.SemaphoreType.DMA((4,)),
        ],
        space=pl.ANY,
    )
    tile, layer_tile = min(512, points), min(256, points)
    x, x_t = pl.pallas_call(
        functools.partial(inputs_kernel, hid, tile),
        out_shape=[shape_of(points, lanes, BF16), shape_of(half + shapes, points, BF16)],
        in_specs=[pl.BlockSpec(memory_space=pl.ANY)] * 4,
        out_specs=vmem(2),
        scratch_shapes=[
            VMEM((points, hid), F32),
            VMEM((half - hid, points), F32),
            VMEM((1, points), jnp.int32),
            VMEM((1, points), jnp.int32),
            pltpu.SemaphoreType.DMA((points // tile + 3,)),
        ],
        compiler_params=pltpu.CompilerParams(vmem_limit_bytes=12 * MIB),
        cost_estimate=pl.CostEstimate(
            flops=4000 * MIB, bytes_accessed=8 * points * half, transcendentals=0
        ),
        name="inputs",
    )(
        *[
            pltpu.with_memory_space_constraint(a, pltpu.HBM)
            for a in (
                hidden,
                offsets.T,
                shape_ids.reshape(1, points),
                scale_index.reshape(1, points),
            )
        ]
    )
    def gather(array, group):
        masks = masks_of(group)[1:]
        return [array] + swaps([array] * len(masks), masks, devices)

    def join(arrays, *widths):
        height = sum(a.shape[0] for a in arrays)
        return small_kernel(
            "join",
            functools.partial(join_kernel, len(arrays)),
            [shape_of(height, width, BF16) for width in widths],
            *arrays[::-1],
        )

    if tuned:
        weight, code_weight = join(gather(held, groups[0]), lanes, half)
        weight, code_weight, x, x_t = lax.optimization_barrier((weight, code_weight, x, x_t))
        steps = [[bit] for group in groups[1:-1] for bit in group[::-1]]
        code_order = order_of(groups[:1] + steps)
        for group in groups[1:-1]:
            weights, code_weights = gather(weight, group), gather(code_weight, steps[0])
            (weight,) = join(weights, lanes)
            (code_weight,) = join(code_weights, half)
        weights = gather(weight, groups[-1])
        code_weights = gather(code_weight, steps[1])
        orders = [[m ^ r for r in order_of(groups[:-1])] for m in masks_of(groups[-1])]
        code_orders = [[m ^ r for r in code_order] for m in masks_of(groups[-1])]
        parts = orders
    else:
        held = lax.all_gather(held, AXES, axis=0, tiled=True)
        weights, code_weights, orders, code_orders, parts = [held[:, :lanes]], [held[:, lanes:]], None, None, [[0]]

    output, grad_hidden, *grads = pl.pallas_call(
        functools.partial(layer_kernel, hid, shapes, layer_tile, orders, parts),
        out_shape=[pltpu.HBM((points, width), F32), pltpu.HBM((points, hid), F32)]
        + [shape_of(2 * shapes + width // len(parts), half, BF16)] * len(parts),
        in_specs=vmem(len(weights) + 3),
        out_specs=[pl.BlockSpec(memory_space=pltpu.HBM)] * 2 + vmem(len(parts)),
        scratch_shapes=[
            VMEM((width, lanes), BF16),
            VMEM((width, half), BF16),
            VMEM((points, width), F32),
            VMEM((points, hid), F32),
            VMEM((points, width), BF16),
            VMEM((2, layer_tile, width), F32),
            pltpu.SemaphoreType.DMA((2, points // layer_tile)),
        ],
        compiler_params=pltpu.CompilerParams(vmem_limit_bytes=20 * MIB),
        cost_estimate=pl.CostEstimate(
            flops=6 * points * width * cols,
            bytes_accessed=8 * points * (width + half),
            transcendentals=points * width,
        ),
        name="layer",
    )(*weights, x, x_t, cotangent)

    if tuned:
        *grads, code_weight = lax.optimization_barrier((*grads, code_weights[1]))
        (code_weight,) = join([code_weights[0], code_weight], half)
        code_weights = gather(code_weight, groups[-1])
        for r, group in enumerate(groups[::-1]):
            masks = masks_of(group)
            grads = [grads[0]] + swaps(grads[1:], masks[1:], devices)
            if r == len(groups) - 1:
                break
            n_out = len(masks_of(groups[-2 - r]))
            left = (grads[0].shape[0] - 2 * shapes) // n_out
            grads = small_kernel(
                "add",
                functools.partial(add_kernel, shapes, len(grads)),
                [shape_of(2 * shapes + left, half, BF16)] * n_out,
                *grads[::-1],
            )
    else:
        sums = lax.psum(grads[0][: 2 * shapes].astype(F32), AXES)
        high = sums.astype(BF16)
        own = lax.psum_scatter(grads[0][2 * shapes :].astype(F32), AXES, scatter_dimension=0, tiled=True)
        low = jnp.zeros((2 * shapes + rows, half), BF16).at[: 2 * shapes].set((sums - high).astype(BF16))
        grads = [jnp.concatenate([high, own.astype(BF16)], axis=0), low]
    grad_codes, grad_direction, grad_gain, grad_bias = small_kernel(
        "last",
        functools.partial(last_kernel, hid, shapes, code_orders, len(grads)),
        [
            shape_of(shapes, half, F32),
            shape_of(rows, cols, F32),
            shape_of(1, rows, F32),
            shape_of(1, rows, F32),
        ],
        *grads[::-1],
        direction,
        gain_row,
        codes,
        *code_weights,
        scratch=[VMEM((width, half), BF16)],
    )

    total = float(points * devices)
    batch_mean = jnp.mean(codes, axis=0)
    batch_square = jnp.mean(codes * codes, axis=0)
    batch_var = (batch_square - batch_mean * batch_mean) * (total / (total - 1.0))
    new_mean = 0.9 * running_mean + 0.1 * batch_mean
    new_var = 0.9 * running_var + 0.1 * batch_var
    return (
        output,
        grad_hidden,
        grad_codes,
        grad_direction,
        grad_gain.reshape(rows),
        grad_bias.reshape(rows),
        new_mean,
        new_var,
    )


def solution(mesh):
    return jax.shard_map(
        per_device,
        mesh=mesh,
        in_specs=(
            P(("dp", "inner"), None),
            P(),
            P(("dp", "inner"), None),
            P(("dp", "inner")),
            P(("dp", "inner")),
            P(("dp", "inner"), None),
            P(("dp", "inner")),
            P(("dp", "inner")),
            P(("dp", "inner"), None),
            P(),
            P(),
        ),
        out_specs=(
            P(("dp", "inner"), None),
            P(("dp", "inner"), None),
            P(),
            P(("dp", "inner"), None),
            P(("dp", "inner")),
            P(("dp", "inner")),
            P(),
            P(),
        ),
        check_vma=False,
    )
```

```python
import functools

import jax
import jax.numpy as jnp
from jax import lax
from jax.experimental import pallas as pl
from jax.experimental.pallas import tpu as pltpu
from jax.sharding import PartitionSpec as P

AXES = ("dp", "inner")
LANES = 128
MIB = 1024 * 1024
F32 = jnp.float32
BF16 = jnp.bfloat16
VMEM = pltpu.VMEM
NT = (((1,), (1,)), ((), ()))


def dot(a, b, dims=(((1,), (0,)), ((), ()))):
    return lax.dot_general(a, b, dims, preferred_element_type=F32)


def vmem(n):
    return [pl.BlockSpec(memory_space=VMEM)] * n


def small_kernel(name, body, out_shape, *args, scratch=(), space=VMEM, limit=8):
    many = isinstance(out_shape, list)
    return pl.pallas_call(
        body,
        out_shape=out_shape,
        in_specs=[pl.BlockSpec(memory_space=space)] * len(args),
        out_specs=vmem(len(out_shape)) if many else vmem(1)[0],
        scratch_shapes=list(scratch),
        compiler_params=pltpu.CompilerParams(vmem_limit_bytes=limit * MIB),
        cost_estimate=pl.CostEstimate(
            flops=4000 * MIB, bytes_accessed=8 * MIB, transcendentals=4 * MIB
        ),
        name=name,
    )(*args)


def diagonal(n):
    return lax.broadcasted_iota(jnp.int32, (n, n), 0) == lax.broadcasted_iota(jnp.int32, (n, n), 1)


def to_column(row):
    n = row.shape[1]
    return jnp.sum(jnp.where(diagonal(n), row, 0.0), axis=1, keepdims=True)


def to_row(column):
    n = column.shape[0]
    return jnp.sum(jnp.where(diagonal(n), column, 0.0), axis=0, keepdims=True)


def stacked_codes(codes_ref, count):
    codes = codes_ref[...].astype(BF16)
    parts = [codes, codes]
    if count > 2 * codes.shape[0]:
        parts.append(jnp.zeros((count - 2 * codes.shape[0], codes.shape[1]), BF16))
    return jnp.concatenate(parts, axis=0)


def split(x):
    high = x.astype(BF16).astype(F32)
    return high, x - high


def prep_kernel(hid, *refs):
    piece_ref, direction_ref, gain_ref, bias_ref, codes_ref, sems = refs[4:]
    copies = [
        pltpu.make_async_copy(source, target, sems.at[k])
        for k, (source, target) in enumerate(zip(refs[:4], refs[5:9]))
    ]
    for copy in copies:
        copy.start()
    for copy in copies:
        copy.wait()
    d = direction_ref[...]
    shapes = codes_ref.shape[0]
    rows, cols = d.shape
    half = cols // 2
    extra_lanes = piece_ref.shape[1] - cols
    inverse = lax.rsqrt(jnp.sum(d * d, axis=1, keepdims=True))
    w = to_column(gain_ref[...]) * (d * inverse)
    lane = lax.broadcasted_iota(jnp.int32, (rows, half), 1)
    first = jnp.where(lane < hid, w[:, :half], w[:, half:])
    code = pltpu.roll(w, half - hid, 1)[:, half:].astype(BF16)
    bias = to_column(bias_ref[...]).astype(BF16).astype(F32)
    high, low = split(dot(code, stacked_codes(codes_ref, extra_lanes), NT) + bias)
    own = first[:, half - LANES :]
    if extra_lanes > LANES:
        own = jnp.concatenate([jnp.zeros((rows, extra_lanes - LANES), F32), own], axis=1)
    lane = lax.broadcasted_iota(jnp.int32, (rows, extra_lanes), 1)
    table = jnp.where(lane < shapes, high, jnp.where(lane < 2 * shapes, low, 0.0))
    table = jnp.where(lane >= extra_lanes - (half - hid), own, table)
    piece_ref[:, :half] = first.astype(BF16)
    piece_ref[:, half : half + extra_lanes] = table.astype(BF16)
    piece_ref[:, half + extra_lanes :] = code


def join_kernel(n, *refs):
    rows = refs[0].shape[0]
    for k, ref in enumerate(refs[n - 1 :: -1]):
        lane = 0
        for out_ref in refs[n:]:
            lanes = out_ref.shape[1]
            out_ref[k * rows : (k + 1) * rows, :] = ref[:, lane : lane + lanes]
            lane += lanes


def place(refs, orders, me, out_ref):
    if orders is None:
        out_ref[...] = refs[0][...]
        return
    rows = refs[0].shape[0] // len(orders[0])
    for ref, order in zip(refs, orders):
        for k, mask in enumerate(order):
            at = pl.multiple_of((me ^ mask) * rows, rows)
            out_ref[pl.ds(at, rows), :] = ref[k * rows : (k + 1) * rows, :]


def inputs_kernel(hid, tile, *refs):
    x_ref, x_t_ref, hidden_ref, offsets_ref, ids_ref, scale_ref, sems = refs[4:]
    points = x_ref.shape[0]
    half = (hid + LANES - 1) // LANES * LANES
    shapes = x_t_ref.shape[0] - half
    extra_lanes = x_ref.shape[1] - half
    steps = points // tile
    small = [
        pltpu.make_async_copy(source, target, sems.at[steps + k])
        for k, (source, target) in enumerate(zip(refs[1:4], (offsets_ref, ids_ref, scale_ref)))
    ]
    large = [
        pltpu.make_async_copy(
            refs[0].at[pl.ds(k * tile, tile), :], hidden_ref.at[pl.ds(k * tile, tile), :], sems.at[k]
        )
        for k in range(steps)
    ]
    for copy in small + large:
        copy.start()
    for copy in small:
        copy.wait()
    for step, copy in enumerate(large):
        here = slice(step * tile, (step + 1) * tile)
        scale = scale_ref[:, here]
        jitter = jnp.where(scale == 0, 1.0, jnp.where(scale == 1, 0.5, 0.25))
        xyz = offsets_ref[:, here] * jitter
        row = lax.broadcasted_iota(jnp.int32, (16, tile), 0)
        last = jnp.zeros((16, tile), F32)
        for k in range(half - hid):
            last = jnp.where(row == 16 - (half - hid) + k, xyz[k : k + 1], last)
        last = last.astype(BF16)
        row = lax.broadcasted_iota(jnp.int32, (extra_lanes - 16, tile), 0)
        ids = ids_ref[:, here]
        member = jnp.where((row == ids) | (row == ids + shapes), 1.0, 0.0).astype(BF16)
        x_ref[here, half:] = jnp.concatenate([member, last], axis=0).T
        x_t_ref[half:, here] = member[:shapes]
        copy.wait()
        x_ref[here, half - LANES : half] = jnp.zeros((tile, LANES), BF16)
        x_ref[here, :hid] = hidden_ref[here, :].astype(BF16)
        hidden = x_ref[here, :half].T
        x_t_ref[: half - 16, here] = hidden[: half - 16]
        x_t_ref[half - 16 : half, here] = hidden[half - 16 :] + last


def layer_kernel(hid, shapes, tile, orders, parts, *refs):
    n = 1 if orders is None else len(orders)
    pieces = refs[:n]
    x_ref, x_t_ref, cot_hbm, out_hbm, grad_hidden_hbm = refs[n : n + 5]
    grad_refs = refs[n + 5 : -8]
    w_ref, turned_ref, out_ref, grad_hidden_ref, grad_pre_ref, pre_ref, cot_ref, sems = refs[-8:]
    points, width = cot_ref.shape
    half = width // 2
    steps = points // tile
    me = lax.axis_index(AXES)
    copies = []

    def rows_of(step):
        return slice(step * tile, (step + 1) * tile)

    def move(step, k, source, target):
        here = pl.ds(step * tile, tile)
        copy = pltpu.make_async_copy(source.at[here, :], target.at[here, :], sems.at[k, step])
        copy.start()
        return copy

    fetched = [move(step, 2, cot_hbm, cot_ref) for step in range(steps)]
    place(pieces, orders, me, w_ref)

    def forward(step):
        pre_ref[step % 2] = dot(x_ref[rows_of(step), :], w_ref[...], NT)

    def middle(step):
        here = rows_of(step)
        pre = pre_ref[step % 2]
        sigma = 0.5 * jnp.tanh(0.5 * pre) + 0.5
        out = pre * sigma
        out_ref[here, :] = out
        grad_pre_ref[here, :] = (cot_ref[here, :] * (sigma * (1.0 + (pre - out)))).astype(BF16)

    def backward(step):
        here = rows_of(step)
        grad_hidden_ref[here, :] = dot(grad_pre_ref[here, :], w_ref[:, :half])[:, :hid]

    forward(0)
    for step in range(steps):
        if step + 1 < steps:
            forward(step + 1)
        fetched[step].wait()
        middle(step)
        copies.append(move(step, 0, out_ref, out_hbm))
        if step > 0:
            backward(step - 1)
            copies.append(move(step - 1, 1, grad_hidden_ref, grad_hidden_hbm))
    backward(steps - 1)
    copies.append(move(steps - 1, 1, grad_hidden_ref, grad_hidden_hbm))
    grad = dot(x_t_ref[...], grad_pre_ref[...])
    sums = grad[half:].astype(BF16)
    for at in range(0, width, half):
        turned_ref[at : at + half, :] = grad[:half, at : at + half].T
    for ref, order in zip(grad_refs, parts):
        ref[:shapes, :] = sums[:, :half]
        ref[shapes : 2 * shapes, :] = sums[:, half:]
        if orders is None:
            ref[2 * shapes :, :] = turned_ref[...].astype(BF16)
            continue
        rows = (ref.shape[0] - 2 * shapes) // len(order)
        for k, mask in enumerate(order):
            at = pl.multiple_of((me ^ mask) * rows, rows)
            to = 2 * shapes + k * rows
            ref[to : to + rows, :] = turned_ref[pl.ds(at, rows), :].astype(BF16)

    for copy in copies:
        copy.wait()


def sum_of(refs):
    terms = [ref[...].astype(F32) for ref in refs]
    while len(terms) > 1:
        terms = [a + b for a, b in zip(terms[::2], terms[1::2])]
    return terms[0]


def add_kernel(shapes, n, *refs):
    total = sum_of(refs[:n]).astype(BF16)
    for k, ref in enumerate(refs[n:]):
        rows = ref.shape[0] - 2 * shapes
        at = 2 * shapes + k * rows
        ref[: 2 * shapes, :] = total[: 2 * shapes]
        ref[2 * shapes :, :] = total[at : at + rows]


def last_kernel(hid, shapes, orders, n, *refs):
    direction_ref, gain_ref, codes_ref = refs[n : n + 3]
    pieces = refs[n + 3 : -5]
    grad_codes_ref, grad_direction_ref, grad_gain_ref, grad_bias_ref, code_scratch = refs[-5:]
    d = direction_ref[...]
    rows, cols = d.shape
    half = cols // 2
    me = lax.axis_index(AXES)
    place(pieces, orders, me, code_scratch)
    total = sum_of(refs[:n])
    sums = jnp.concatenate([total[:shapes], total[shapes : 2 * shapes]], axis=1)
    sums = jnp.concatenate(split(sums), axis=0).astype(BF16)
    terms = dot(sums, code_scratch[...])
    grad_codes_ref[...] = terms[:shapes] + terms[shapes:]
    width = sums.shape[1]
    mine = lax.broadcasted_iota(jnp.int32, (rows, width), 0) + me * rows
    mine = jnp.where(mine == lax.broadcasted_iota(jnp.int32, (rows, width), 1), 1.0, 0.0).astype(BF16)
    own = dot(mine, sums, NT)
    grad_bias_ref[...] = to_row(jnp.sum(own, axis=1, keepdims=True))
    code = dot(own.astype(BF16), stacked_codes(codes_ref, 2 * shapes))
    packed = jnp.concatenate([total[2 * shapes :], code], axis=1)
    lane = lax.broadcasted_iota(jnp.int32, (rows, cols), 1)
    grad_weight = jnp.where(
        lane < hid,
        packed,
        jnp.where(lane < hid + half, pltpu.roll(packed, cols - (half - hid), 1), pltpu.roll(packed, half, 1)),
    )
    inverse = lax.rsqrt(jnp.sum(d * d, axis=1, keepdims=True))
    unit = d * inverse
    grad_gain = jnp.sum(grad_weight * unit, axis=1, keepdims=True)
    grad_gain_ref[...] = to_row(grad_gain)
    grad_direction_ref[...] = (to_column(gain_ref[...]) * inverse) * (grad_weight - grad_gain * unit)


def masks_of(group):
    masks = [0]
    for bit in group:
        masks = masks + [m ^ bit for m in masks]
    return masks


def order_of(groups):
    order = [0]
    for group in groups:
        order = [m ^ r for m in masks_of(group) for r in order]
    return order


def swaps(arrays, masks, devices):
    moved = [
        lax.ppermute(x, AXES, [(i, i ^ mask) for i in range(devices)])
        for x, mask in list(zip(arrays, masks))[::-1]
    ]
    return moved[::-1]


def per_device(
    hidden,
    codes,
    offsets,
    shape_ids,
    scale_index,
    direction,
    gain,
    bias,
    cotangent,
    running_mean,
    running_var,
):
    points, hid = hidden.shape
    shapes = codes.shape[0]
    rows, cols = direction.shape
    width = cotangent.shape[1]
    half = cols // 2
    devices = lax.axis_size("dp") * lax.axis_size("inner")
    tuned = rows % 16 == 0
    bits = [1 << k | 1 for k in range(devices.bit_length() - 1)]
    groups = [bits[k - 2 : k] for k in range(len(bits), 1, -2)]
    groups = groups + [bits[:1]] * (len(bits) % 2)
    tuned = rows % 16 == 0
    extra_lanes = -(-(2 * shapes + 16) // LANES) * LANES
    lanes = half + extra_lanes
    gain_row = gain.reshape(1, rows)

    def shape_of(rows, lanes, dtype):
        return jax.ShapeDtypeStruct((rows, lanes), dtype)

    held = small_kernel(
        "prep",
        functools.partial(prep_kernel, hid),
        shape_of(rows, lanes + half, BF16),
        *[
            pltpu.with_memory_space_constraint(x, pltpu.HBM)
            for x in (direction, gain_row, bias.reshape(1, rows), codes)
        ],
        scratch=[
            VMEM((rows, cols), F32),
            VMEM((1, rows), F32),
            VMEM((1, rows), F32),
            VMEM((shapes, half), F32),
            pltpu.SemaphoreType.DMA((4,)),
        ],
        space=pl.ANY,
    )
    tile, layer_tile = min(512, points), min(256, points)
    x, x_t = pl.pallas_call(
        functools.partial(inputs_kernel, hid, tile),
        out_shape=[shape_of(points, lanes, BF16), shape_of(half + shapes, points, BF16)],
        in_specs=[pl.BlockSpec(memory_space=pl.ANY)] * 4,
        out_specs=vmem(2),
        scratch_shapes=[
            VMEM((points, hid), F32),
            VMEM((half - hid, points), F32),
            VMEM((1, points), jnp.int32),
            VMEM((1, points), jnp.int32),
            pltpu.SemaphoreType.DMA((points // tile + 3,)),
        ],
        compiler_params=pltpu.CompilerParams(vmem_limit_bytes=12 * MIB),
        cost_estimate=pl.CostEstimate(
            flops=4000 * MIB, bytes_accessed=8 * points * half, transcendentals=0
        ),
        name="inputs",
    )(
        *[
            pltpu.with_memory_space_constraint(a, pltpu.HBM)
            for a in (
                hidden,
                offsets.T,
                shape_ids.reshape(1, points),
                scale_index.reshape(1, points),
            )
        ]
    )
    def gather(array, group):
        masks = masks_of(group)[1:]
        return [array] + swaps([array] * len(masks), masks, devices)

    def join(arrays, *widths):
        height = sum(a.shape[0] for a in arrays)
        return small_kernel(
            "join",
            functools.partial(join_kernel, len(arrays)),
            [shape_of(height, width, BF16) for width in widths],
            *arrays[::-1],
        )

    if tuned:
        weight, code_weight = join(gather(held, groups[0]), lanes, half)
        weight, code_weight, x, x_t = lax.optimization_barrier((weight, code_weight, x, x_t))
        steps = [[bit] for group in groups[1:-1] for bit in group[::-1]]
        code_order = order_of(groups[:1] + steps)
        for group in groups[1:-1]:
            weights, code_weights = gather(weight, group), gather(code_weight, steps[0])
            (weight,) = join(weights, lanes)
            (code_weight,) = join(code_weights, half)
        weights = gather(weight, groups[-1])
        code_weights = gather(code_weight, steps[1])
        orders = [[m ^ r for r in order_of(groups[:-1])] for m in masks_of(groups[-1])]
        code_orders = [[m ^ r for r in code_order] for m in masks_of(groups[-1])]
        parts = orders
    else:
        held = lax.all_gather(held, AXES, axis=0, tiled=True)
        weights, code_weights, orders, code_orders, parts = [held[:, :lanes]], [held[:, lanes:]], None, None, [[0]]

    output, grad_hidden, *grads = pl.pallas_call(
        functools.partial(layer_kernel, hid, shapes, layer_tile, orders, parts),
        out_shape=[pltpu.HBM((points, width), F32), pltpu.HBM((points, hid), F32)]
        + [shape_of(2 * shapes + width // len(parts), half, BF16)] * len(parts),
        in_specs=vmem(len(weights) + 2) + [pl.BlockSpec(memory_space=pltpu.HBM)],
        out_specs=[pl.BlockSpec(memory_space=pltpu.HBM)] * 2 + vmem(len(parts)),
        scratch_shapes=[
            VMEM((width, lanes), BF16),
            VMEM((width, half), F32),
            VMEM((points, width), F32),
            VMEM((points, hid), F32),
            VMEM((points, width), BF16),
            VMEM((2, layer_tile, width), F32),
            VMEM((points, width), F32),
            pltpu.SemaphoreType.DMA((3, points // layer_tile)),
        ],
        compiler_params=pltpu.CompilerParams(vmem_limit_bytes=24 * MIB),
        cost_estimate=pl.CostEstimate(
            flops=6 * points * width * cols,
            bytes_accessed=8 * points * (width + half),
            transcendentals=points * width,
        ),
        name="layer",
    )(*weights, x, x_t, pltpu.with_memory_space_constraint(cotangent, pltpu.HBM))

    if tuned:
        *grads, code_weight = lax.optimization_barrier((*grads, code_weights[1]))
        (code_weight,) = join([code_weights[0], code_weight], half)
        code_weights = gather(code_weight, groups[-1])
        for r, group in enumerate(groups[::-1]):
            masks = masks_of(group)
            grads = [grads[0]] + swaps(grads[1:], masks[1:], devices)
            if r == len(groups) - 1:
                break
            n_out = len(masks_of(groups[-2 - r]))
            left = (grads[0].shape[0] - 2 * shapes) // n_out
            grads = small_kernel(
                "add",
                functools.partial(add_kernel, shapes, len(grads)),
                [shape_of(2 * shapes + left, half, BF16)] * n_out,
                *grads[::-1],
            )
    else:
        sums = lax.psum(grads[0][: 2 * shapes].astype(F32), AXES)
        high = sums.astype(BF16)
        own = lax.psum_scatter(grads[0][2 * shapes :].astype(F32), AXES, scatter_dimension=0, tiled=True)
        low = jnp.zeros((2 * shapes + rows, half), BF16).at[: 2 * shapes].set((sums - high).astype(BF16))
        grads = [jnp.concatenate([high, own.astype(BF16)], axis=0), low]
    grad_codes, grad_direction, grad_gain, grad_bias = small_kernel(
        "last",
        functools.partial(last_kernel, hid, shapes, code_orders, len(grads)),
        [
            shape_of(shapes, half, F32),
            shape_of(rows, cols, F32),
            shape_of(1, rows, F32),
            shape_of(1, rows, F32),
        ],
        *grads[::-1],
        direction,
        gain_row,
        codes,
        *code_weights,
        scratch=[VMEM((width, half), BF16)],
    )

    total = float(points * devices)
    batch_mean = jnp.mean(codes, axis=0)
    batch_square = jnp.mean(codes * codes, axis=0)
    batch_var = (batch_square - batch_mean * batch_mean) * (total / (total - 1.0))
    new_mean = 0.9 * running_mean + 0.1 * batch_mean
    new_var = 0.9 * running_var + 0.1 * batch_var
    return (
        output,
        grad_hidden,
        grad_codes,
        grad_direction,
        grad_gain.reshape(rows),
        grad_bias.reshape(rows),
        new_mean,
        new_var,
    )


def solution(mesh):
    return jax.shard_map(
        per_device,
        mesh=mesh,
        in_specs=(
            P(("dp", "inner"), None),
            P(),
            P(("dp", "inner"), None),
            P(("dp", "inner")),
            P(("dp", "inner")),
            P(("dp", "inner"), None),
            P(("dp", "inner")),
            P(("dp", "inner")),
            P(("dp", "inner"), None),
            P(),
            P(),
        ),
        out_specs=(
            P(("dp", "inner"), None),
            P(("dp", "inner"), None),
            P(),
            P(("dp", "inner"), None),
            P(("dp", "inner")),
            P(("dp", "inner")),
            P(),
            P(),
        ),
        check_vma=False,
    )
```

```python
import functools

import jax
import jax.numpy as jnp
from jax import lax
from jax.experimental import pallas as pl
from jax.experimental.pallas import tpu as pltpu
from jax.sharding import PartitionSpec as P

AXES = ("dp", "inner")
LANES = 128
MIB = 1024 * 1024
F32 = jnp.float32
BF16 = jnp.bfloat16
VMEM = pltpu.VMEM
NT = (((1,), (1,)), ((), ()))


def dot(a, b, dims=(((1,), (0,)), ((), ()))):
    return lax.dot_general(a, b, dims, preferred_element_type=F32)


def vmem(n):
    return [pl.BlockSpec(memory_space=VMEM)] * n


def small_kernel(name, body, out_shape, *args, scratch=(), space=VMEM, limit=8):
    many = isinstance(out_shape, list)
    return pl.pallas_call(
        body,
        out_shape=out_shape,
        in_specs=[pl.BlockSpec(memory_space=space)] * len(args),
        out_specs=vmem(len(out_shape)) if many else vmem(1)[0],
        scratch_shapes=list(scratch),
        compiler_params=pltpu.CompilerParams(vmem_limit_bytes=limit * MIB),
        cost_estimate=pl.CostEstimate(
            flops=4000 * MIB, bytes_accessed=8 * MIB, transcendentals=4 * MIB
        ),
        name=name,
    )(*args)


def diagonal(n):
    return lax.broadcasted_iota(jnp.int32, (n, n), 0) == lax.broadcasted_iota(jnp.int32, (n, n), 1)


def to_column(row):
    n = row.shape[1]
    return jnp.sum(jnp.where(diagonal(n), row, 0.0), axis=1, keepdims=True)


def to_row(column):
    n = column.shape[0]
    return jnp.sum(jnp.where(diagonal(n), column, 0.0), axis=0, keepdims=True)


def stacked_codes(codes_ref, count):
    codes = codes_ref[...].astype(BF16)
    parts = [codes, codes]
    if count > 2 * codes.shape[0]:
        parts.append(jnp.zeros((count - 2 * codes.shape[0], codes.shape[1]), BF16))
    return jnp.concatenate(parts, axis=0)


def split(x):
    high = x.astype(BF16).astype(F32)
    return high, x - high


def prep_kernel(hid, *refs):
    piece_ref, direction_ref, gain_ref, bias_ref, codes_ref, sems = refs[4:]
    copies = [
        pltpu.make_async_copy(source, target, sems.at[k])
        for k, (source, target) in enumerate(zip(refs[:4], refs[5:9]))
    ]
    for copy in copies:
        copy.start()
    for copy in copies:
        copy.wait()
    d = direction_ref[...]
    shapes = codes_ref.shape[0]
    rows, cols = d.shape
    half = cols // 2
    extra_lanes = piece_ref.shape[1] - cols
    inverse = lax.rsqrt(jnp.sum(d * d, axis=1, keepdims=True))
    w = to_column(gain_ref[...]) * (d * inverse)
    lane = lax.broadcasted_iota(jnp.int32, (rows, half), 1)
    first = jnp.where(lane < hid, w[:, :half], w[:, half:])
    code = pltpu.roll(w, half - hid, 1)[:, half:].astype(BF16)
    bias = to_column(bias_ref[...]).astype(BF16).astype(F32)
    high, low = split(dot(code, stacked_codes(codes_ref, extra_lanes), NT) + bias)
    own = first[:, half - LANES :]
    if extra_lanes > LANES:
        own = jnp.concatenate([jnp.zeros((rows, extra_lanes - LANES), F32), own], axis=1)
    lane = lax.broadcasted_iota(jnp.int32, (rows, extra_lanes), 1)
    table = jnp.where(lane < shapes, high, jnp.where(lane < 2 * shapes, low, 0.0))
    table = jnp.where(lane >= extra_lanes - (half - hid), own, table)
    piece_ref[:, :half] = first.astype(BF16)
    piece_ref[:, half : half + extra_lanes] = table.astype(BF16)
    piece_ref[:, half + extra_lanes :] = code


def join_kernel(n, *refs):
    rows = refs[0].shape[0]
    for k, ref in enumerate(refs[n - 1 :: -1]):
        lane = 0
        for out_ref in refs[n:]:
            lanes = out_ref.shape[1]
            out_ref[k * rows : (k + 1) * rows, :] = ref[:, lane : lane + lanes]
            lane += lanes


def place(refs, orders, me, out_ref):
    if orders is None:
        out_ref[...] = refs[0][...]
        return
    rows = refs[0].shape[0] // len(orders[0])
    for ref, order in zip(refs, orders):
        for k, mask in enumerate(order):
            at = pl.multiple_of((me ^ mask) * rows, rows)
            out_ref[pl.ds(at, rows), :] = ref[k * rows : (k + 1) * rows, :]


def inputs_kernel(hid, tile, *refs):
    x_ref, x_t_ref, cot_ref, hidden_ref, offsets_ref, ids_ref, scale_ref, sems = refs[5:]
    points = x_ref.shape[0]
    half = (hid + LANES - 1) // LANES * LANES
    shapes = x_t_ref.shape[0] - half
    extra_lanes = x_ref.shape[1] - half
    steps = points // tile
    small = [
        pltpu.make_async_copy(source, target, sems.at[steps + k])
        for k, (source, target) in enumerate(zip(refs[1:4], (offsets_ref, ids_ref, scale_ref)))
    ]
    large = [
        pltpu.make_async_copy(
            refs[0].at[pl.ds(k * tile, tile), :], hidden_ref.at[pl.ds(k * tile, tile), :], sems.at[k]
        )
        for k in range(steps)
    ]
    cotangent = pltpu.make_async_copy(refs[4], cot_ref, sems.at[steps + 3])
    for copy in small + large + [cotangent]:
        copy.start()
    for copy in small:
        copy.wait()
    for step, copy in enumerate(large):
        here = slice(step * tile, (step + 1) * tile)
        scale = scale_ref[:, here]
        jitter = jnp.where(scale == 0, 1.0, jnp.where(scale == 1, 0.5, 0.25))
        xyz = offsets_ref[:, here] * jitter
        row = lax.broadcasted_iota(jnp.int32, (16, tile), 0)
        last = jnp.zeros((16, tile), F32)
        for k in range(half - hid):
            last = jnp.where(row == 16 - (half - hid) + k, xyz[k : k + 1], last)
        last = last.astype(BF16)
        row = lax.broadcasted_iota(jnp.int32, (extra_lanes - 16, tile), 0)
        ids = ids_ref[:, here]
        member = jnp.where((row == ids) | (row == ids + shapes), 1.0, 0.0).astype(BF16)
        x_ref[here, half:] = jnp.concatenate([member, last], axis=0).T
        x_t_ref[half:, here] = member[:shapes]
        copy.wait()
        x_ref[here, half - LANES : half] = jnp.zeros((tile, LANES), BF16)
        x_ref[here, :hid] = hidden_ref[here, :].astype(BF16)
        hidden = x_ref[here, :half].T
        x_t_ref[: half - 16, here] = hidden[: half - 16]
        x_t_ref[half - 16 : half, here] = hidden[half - 16 :] + last
    cotangent.wait()


def layer_kernel(hid, shapes, tile, orders, parts, *refs):
    n = 1 if orders is None else len(orders)
    pieces = refs[:n]
    x_ref, x_t_ref, cot_ref, out_hbm, grad_hidden_hbm = refs[n : n + 5]
    grad_refs = refs[n + 5 : -6]
    w_ref, turned_ref, out_ref, grad_hidden_ref, grad_pre_ref, pre_ref, sems = refs[-7:]
    points, width = cot_ref.shape
    half = width // 2
    steps = points // tile
    me = lax.axis_index(AXES)
    place(pieces, orders, me, w_ref)
    copies = []

    def rows_of(step):
        return slice(step * tile, (step + 1) * tile)

    def forward(step):
        pre_ref[step % 2] = dot(x_ref[rows_of(step), :], w_ref[...], NT)

    def middle(step):
        here = rows_of(step)
        pre = pre_ref[step % 2]
        sigma = 0.5 * jnp.tanh(0.5 * pre) + 0.5
        out = pre * sigma
        out_ref[here, :] = out
        grad_pre_ref[here, :] = (cot_ref[here, :] * (sigma * (1.0 + (pre - out)))).astype(BF16)

    def backward(step):
        here = rows_of(step)
        grad_hidden_ref[here, :] = dot(grad_pre_ref[here, :], w_ref[:, :half])[:, :hid]

    def store(step, k, source, target):
        here = pl.ds(step * tile, tile)
        copy = pltpu.make_async_copy(source.at[here, :], target.at[here, :], sems.at[k, step])
        copy.start()
        copies.append(copy)

    forward(0)
    for step in range(steps):
        if step + 1 < steps:
            forward(step + 1)
        middle(step)
        store(step, 0, out_ref, out_hbm)
        if step > 0:
            backward(step - 1)
            store(step - 1, 1, grad_hidden_ref, grad_hidden_hbm)
    backward(steps - 1)
    store(steps - 1, 1, grad_hidden_ref, grad_hidden_hbm)
    grad = dot(x_t_ref[...], grad_pre_ref[...])
    sums = grad[half:].astype(BF16)
    for at in range(0, width, half):
        turned_ref[at : at + half, :] = grad[:half, at : at + half].T
    for ref, order in zip(grad_refs, parts):
        ref[:shapes, :] = sums[:, :half]
        ref[shapes : 2 * shapes, :] = sums[:, half:]
        if orders is None:
            ref[2 * shapes :, :] = turned_ref[...].astype(BF16)
            continue
        rows = (ref.shape[0] - 2 * shapes) // len(order)
        for k, mask in enumerate(order):
            at = pl.multiple_of((me ^ mask) * rows, rows)
            to = 2 * shapes + k * rows
            ref[to : to + rows, :] = turned_ref[pl.ds(at, rows), :].astype(BF16)

    for copy in copies:
        copy.wait()


def sum_of(refs):
    terms = [ref[...].astype(F32) for ref in refs]
    while len(terms) > 1:
        terms = [a + b for a, b in zip(terms[::2], terms[1::2])]
    return terms[0]


def add_kernel(shapes, n, *refs):
    total = sum_of(refs[:n]).astype(BF16)
    for k, ref in enumerate(refs[n:]):
        rows = ref.shape[0] - 2 * shapes
        at = 2 * shapes + k * rows
        ref[: 2 * shapes, :] = total[: 2 * shapes]
        ref[2 * shapes :, :] = total[at : at + rows]


def last_kernel(hid, shapes, orders, n, *refs):
    direction_ref, gain_ref, codes_ref = refs[n : n + 3]
    pieces = refs[n + 3 : -5]
    grad_codes_ref, grad_direction_ref, grad_gain_ref, grad_bias_ref, code_scratch = refs[-5:]
    d = direction_ref[...]
    rows, cols = d.shape
    half = cols // 2
    me = lax.axis_index(AXES)
    place(pieces, orders, me, code_scratch)
    total = sum_of(refs[:n])
    sums = jnp.concatenate([total[:shapes], total[shapes : 2 * shapes]], axis=1)
    sums = jnp.concatenate(split(sums), axis=0).astype(BF16)
    terms = dot(sums, code_scratch[...])
    grad_codes_ref[...] = terms[:shapes] + terms[shapes:]
    width = sums.shape[1]
    mine = lax.broadcasted_iota(jnp.int32, (rows, width), 0) + me * rows
    mine = jnp.where(mine == lax.broadcasted_iota(jnp.int32, (rows, width), 1), 1.0, 0.0).astype(BF16)
    own = dot(mine, sums, NT)
    grad_bias_ref[...] = to_row(jnp.sum(own, axis=1, keepdims=True))
    code = dot(own.astype(BF16), stacked_codes(codes_ref, 2 * shapes))
    packed = jnp.concatenate([total[2 * shapes :], code], axis=1)
    lane = lax.broadcasted_iota(jnp.int32, (rows, cols), 1)
    grad_weight = jnp.where(
        lane < hid,
        packed,
        jnp.where(lane < hid + half, pltpu.roll(packed, cols - (half - hid), 1), pltpu.roll(packed, half, 1)),
    )
    inverse = lax.rsqrt(jnp.sum(d * d, axis=1, keepdims=True))
    unit = d * inverse
    grad_gain = jnp.sum(grad_weight * unit, axis=1, keepdims=True)
    grad_gain_ref[...] = to_row(grad_gain)
    grad_direction_ref[...] = (to_column(gain_ref[...]) * inverse) * (grad_weight - grad_gain * unit)


def masks_of(group):
    masks = [0]
    for bit in group:
        masks = masks + [m ^ bit for m in masks]
    return masks


def order_of(groups):
    order = [0]
    for group in groups:
        order = [m ^ r for m in masks_of(group) for r in order]
    return order


def swaps(arrays, masks, devices):
    moved = [
        lax.ppermute(x, AXES, [(i, i ^ mask) for i in range(devices)])
        for x, mask in list(zip(arrays, masks))[::-1]
    ]
    return moved[::-1]


def per_device(
    hidden,
    codes,
    offsets,
    shape_ids,
    scale_index,
    direction,
    gain,
    bias,
    cotangent,
    running_mean,
    running_var,
):
    points, hid = hidden.shape
    shapes = codes.shape[0]
    rows, cols = direction.shape
    width = cotangent.shape[1]
    half = cols // 2
    devices = lax.axis_size("dp") * lax.axis_size("inner")
    tuned = rows % 16 == 0
    bits = [1 << k | 1 for k in range(devices.bit_length() - 1)]
    groups = [bits[k - 2 : k] for k in range(len(bits), 1, -2)]
    groups = groups + [bits[:1]] * (len(bits) % 2)
    tuned = rows % 16 == 0
    extra_lanes = -(-(2 * shapes + 16) // LANES) * LANES
    lanes = half + extra_lanes
    gain_row = gain.reshape(1, rows)

    def shape_of(rows, lanes, dtype):
        return jax.ShapeDtypeStruct((rows, lanes), dtype)

    held = small_kernel(
        "prep",
        functools.partial(prep_kernel, hid),
        shape_of(rows, lanes + half, BF16),
        *[
            pltpu.with_memory_space_constraint(x, pltpu.HBM)
            for x in (direction, gain_row, bias.reshape(1, rows), codes)
        ],
        scratch=[
            VMEM((rows, cols), F32),
            VMEM((1, rows), F32),
            VMEM((1, rows), F32),
            VMEM((shapes, half), F32),
            pltpu.SemaphoreType.DMA((4,)),
        ],
        space=pl.ANY,
    )
    tile, layer_tile = min(512, points), min(256, points)
    x, x_t, cotangent = pl.pallas_call(
        functools.partial(inputs_kernel, hid, tile),
        out_shape=[
            shape_of(points, lanes, BF16),
            shape_of(half + shapes, points, BF16),
            pltpu.VMEM((points, width), F32),
        ],
        in_specs=[pl.BlockSpec(memory_space=pl.ANY)] * 5,
        out_specs=vmem(3),
        scratch_shapes=[
            VMEM((points, hid), F32),
            VMEM((half - hid, points), F32),
            VMEM((1, points), jnp.int32),
            VMEM((1, points), jnp.int32),
            pltpu.SemaphoreType.DMA((points // tile + 4,)),
        ],
        compiler_params=pltpu.CompilerParams(vmem_limit_bytes=12 * MIB),
        cost_estimate=pl.CostEstimate(
            flops=4000 * MIB, bytes_accessed=8 * points * half, transcendentals=0
        ),
        name="inputs",
    )(
        *[
            pltpu.with_memory_space_constraint(a, pltpu.HBM)
            for a in (
                hidden,
                offsets.T,
                shape_ids.reshape(1, points),
                scale_index.reshape(1, points),
                cotangent,
            )
        ]
    )
    def gather(array, group):
        masks = masks_of(group)[1:]
        return [array] + swaps([array] * len(masks), masks, devices)

    def join(arrays, *widths):
        height = sum(a.shape[0] for a in arrays)
        return small_kernel(
            "join",
            functools.partial(join_kernel, len(arrays)),
            [shape_of(height, width, BF16) for width in widths],
            *arrays[::-1],
        )

    if tuned:
        weight, code_weight = join(gather(held, groups[0]), lanes, half)
        weight, code_weight, x, x_t, cotangent = lax.optimization_barrier(
            (weight, code_weight, x, x_t, cotangent)
        )
        steps = [[bit] for group in groups[1:-1] for bit in group[::-1]]
        code_order = order_of(groups[:1] + steps)
        for group in groups[1:-1]:
            weights, code_weights = gather(weight, group), gather(code_weight, steps[0])
            (weight,) = join(weights, lanes)
            (code_weight,) = join(code_weights, half)
        weights = gather(weight, groups[-1])
        code_weights = gather(code_weight, steps[1])
        orders = [[m ^ r for r in order_of(groups[:-1])] for m in masks_of(groups[-1])]
        code_orders = [[m ^ r for r in code_order] for m in masks_of(groups[-1])]
        parts = orders
    else:
        held = lax.all_gather(held, AXES, axis=0, tiled=True)
        weights, code_weights, orders, code_orders, parts = [held[:, :lanes]], [held[:, lanes:]], None, None, [[0]]

    output, grad_hidden, *grads = pl.pallas_call(
        functools.partial(layer_kernel, hid, shapes, layer_tile, orders, parts),
        out_shape=[pltpu.HBM((points, width), F32), pltpu.HBM((points, hid), F32)]
        + [shape_of(2 * shapes + width // len(parts), half, BF16)] * len(parts),
        in_specs=vmem(len(weights) + 3),
        out_specs=[pl.BlockSpec(memory_space=pltpu.HBM)] * 2 + vmem(len(parts)),
        scratch_shapes=[
            VMEM((width, lanes), BF16),
            VMEM((width, half), F32),
            VMEM((points, width), F32),
            VMEM((points, hid), F32),
            VMEM((points, width), BF16),
            VMEM((2, layer_tile, width), F32),
            pltpu.SemaphoreType.DMA((2, points // layer_tile)),
        ],
        compiler_params=pltpu.CompilerParams(vmem_limit_bytes=20 * MIB),
        cost_estimate=pl.CostEstimate(
            flops=6 * points * width * cols,
            bytes_accessed=8 * points * (width + half),
            transcendentals=points * width,
        ),
        name="layer",
    )(*weights, x, x_t, cotangent)

    if tuned:
        *grads, code_weight = lax.optimization_barrier((*grads, code_weights[1]))
        (code_weight,) = join([code_weights[0], code_weight], half)
        code_weights = gather(code_weight, groups[-1])
        for r, group in enumerate(groups[::-1]):
            masks = masks_of(group)
            grads = [grads[0]] + swaps(grads[1:], masks[1:], devices)
            if r == len(groups) - 1:
                break
            n_out = len(masks_of(groups[-2 - r]))
            left = (grads[0].shape[0] - 2 * shapes) // n_out
            grads = small_kernel(
                "add",
                functools.partial(add_kernel, shapes, len(grads)),
                [shape_of(2 * shapes + left, half, BF16)] * n_out,
                *grads[::-1],
            )
    else:
        sums = lax.psum(grads[0][: 2 * shapes].astype(F32), AXES)
        high = sums.astype(BF16)
        own = lax.psum_scatter(grads[0][2 * shapes :].astype(F32), AXES, scatter_dimension=0, tiled=True)
        low = jnp.zeros((2 * shapes + rows, half), BF16).at[: 2 * shapes].set((sums - high).astype(BF16))
        grads = [jnp.concatenate([high, own.astype(BF16)], axis=0), low]
    grad_codes, grad_direction, grad_gain, grad_bias = small_kernel(
        "last",
        functools.partial(last_kernel, hid, shapes, code_orders, len(grads)),
        [
            shape_of(shapes, half, F32),
            shape_of(rows, cols, F32),
            shape_of(1, rows, F32),
            shape_of(1, rows, F32),
        ],
        *grads[::-1],
        direction,
        gain_row,
        codes,
        *code_weights,
        scratch=[VMEM((width, half), BF16)],
    )

    total = float(points * devices)
    batch_mean = jnp.mean(codes, axis=0)
    batch_square = jnp.mean(codes * codes, axis=0)
    batch_var = (batch_square - batch_mean * batch_mean) * (total / (total - 1.0))
    new_mean = 0.9 * running_mean + 0.1 * batch_mean
    new_var = 0.9 * running_var + 0.1 * batch_var
    return (
        output,
        grad_hidden,
        grad_codes,
        grad_direction,
        grad_gain.reshape(rows),
        grad_bias.reshape(rows),
        new_mean,
        new_var,
    )


def solution(mesh):
    return jax.shard_map(
        per_device,
        mesh=mesh,
        in_specs=(
            P(("dp", "inner"), None),
            P(),
            P(("dp", "inner"), None),
            P(("dp", "inner")),
            P(("dp", "inner")),
            P(("dp", "inner"), None),
            P(("dp", "inner")),
            P(("dp", "inner")),
            P(("dp", "inner"), None),
            P(),
            P(),
        ),
        out_specs=(
            P(("dp", "inner"), None),
            P(("dp", "inner"), None),
            P(),
            P(("dp", "inner"), None),
            P(("dp", "inner")),
            P(("dp", "inner")),
            P(),
            P(),
        ),
        check_vma=False,
    )
```

```python
import functools

import jax
import jax.numpy as jnp
from jax import lax
from jax.experimental import pallas as pl
from jax.experimental.pallas import tpu as pltpu
from jax.sharding import PartitionSpec as P

AXES = ("dp", "inner")
LANES = 128
MIB = 1024 * 1024
F32 = jnp.float32
BF16 = jnp.bfloat16
VMEM = pltpu.VMEM
NT = (((1,), (1,)), ((), ()))


def dot(a, b, dims=(((1,), (0,)), ((), ()))):
    return lax.dot_general(a, b, dims, preferred_element_type=F32)


def vmem(n):
    return [pl.BlockSpec(memory_space=VMEM)] * n


def small_kernel(name, body, out_shape, *args, scratch=(), space=VMEM, limit=8):
    many = isinstance(out_shape, list)
    return pl.pallas_call(
        body,
        out_shape=out_shape,
        in_specs=[pl.BlockSpec(memory_space=space)] * len(args),
        out_specs=vmem(len(out_shape)) if many else vmem(1)[0],
        scratch_shapes=list(scratch),
        compiler_params=pltpu.CompilerParams(vmem_limit_bytes=limit * MIB),
        cost_estimate=pl.CostEstimate(
            flops=4000 * MIB, bytes_accessed=8 * MIB, transcendentals=4 * MIB
        ),
        name=name,
    )(*args)


def diagonal(n):
    return lax.broadcasted_iota(jnp.int32, (n, n), 0) == lax.broadcasted_iota(jnp.int32, (n, n), 1)


def to_column(row):
    n = row.shape[1]
    return jnp.sum(jnp.where(diagonal(n), row, 0.0), axis=1, keepdims=True)


def to_row(column):
    n = column.shape[0]
    return jnp.sum(jnp.where(diagonal(n), column, 0.0), axis=0, keepdims=True)


def stacked_codes(codes_ref, count):
    codes = codes_ref[...].astype(BF16)
    parts = [codes, codes]
    if count > 2 * codes.shape[0]:
        parts.append(jnp.zeros((count - 2 * codes.shape[0], codes.shape[1]), BF16))
    return jnp.concatenate(parts, axis=0)


def split(x):
    high = x.astype(BF16).astype(F32)
    return high, x - high


def prep_kernel(hid, *refs):
    piece_ref, direction_ref, gain_ref, bias_ref, codes_ref, sems = refs[4:]
    copies = [
        pltpu.make_async_copy(source, target, sems.at[k])
        for k, (source, target) in enumerate(zip(refs[:4], refs[5:9]))
    ]
    for copy in copies:
        copy.start()
    for copy in copies:
        copy.wait()
    d = direction_ref[...]
    shapes = codes_ref.shape[0]
    rows, cols = d.shape
    half = cols // 2
    extra_lanes = piece_ref.shape[1] - cols
    inverse = lax.rsqrt(jnp.sum(d * d, axis=1, keepdims=True))
    w = to_column(gain_ref[...]) * (d * inverse)
    lane = lax.broadcasted_iota(jnp.int32, (rows, half), 1)
    first = jnp.where(lane < hid, w[:, :half], w[:, half:])
    code = pltpu.roll(w, half - hid, 1)[:, half:].astype(BF16)
    bias = to_column(bias_ref[...]).astype(BF16).astype(F32)
    high, low = split(dot(code, stacked_codes(codes_ref, extra_lanes), NT) + bias)
    own = first[:, half - LANES :]
    if extra_lanes > LANES:
        own = jnp.concatenate([jnp.zeros((rows, extra_lanes - LANES), F32), own], axis=1)
    lane = lax.broadcasted_iota(jnp.int32, (rows, extra_lanes), 1)
    table = jnp.where(lane < shapes, high, jnp.where(lane < 2 * shapes, low, 0.0))
    table = jnp.where(lane >= extra_lanes - (half - hid), own, table)
    piece_ref[:, :half] = first.astype(BF16)
    piece_ref[:, half : half + extra_lanes] = table.astype(BF16)
    piece_ref[:, half + extra_lanes :] = code


def join_kernel(n, *refs):
    rows = refs[0].shape[0]
    for k, ref in enumerate(refs[n - 1 :: -1]):
        lane = 0
        for out_ref in refs[n:]:
            lanes = out_ref.shape[1]
            out_ref[k * rows : (k + 1) * rows, :] = ref[:, lane : lane + lanes]
            lane += lanes


def place(refs, orders, me, out_ref):
    if orders is None:
        out_ref[...] = refs[0][...]
        return
    rows = refs[0].shape[0] // len(orders[0])
    for ref, order in zip(refs, orders):
        for k, mask in enumerate(order):
            at = pl.multiple_of((me ^ mask) * rows, rows)
            out_ref[pl.ds(at, rows), :] = ref[k * rows : (k + 1) * rows, :]


def inputs_kernel(hid, tile, *refs):
    x_ref, x_t_ref, cot_ref, hidden_ref, offsets_ref, ids_ref, scale_ref, sems = refs[5:]
    points = x_ref.shape[0]
    half = (hid + LANES - 1) // LANES * LANES
    shapes = x_t_ref.shape[0] - half
    extra_lanes = x_ref.shape[1] - half
    steps = points // tile
    small = [
        pltpu.make_async_copy(source, target, sems.at[steps + k])
        for k, (source, target) in enumerate(zip(refs[1:4], (offsets_ref, ids_ref, scale_ref)))
    ]
    large = [
        pltpu.make_async_copy(
            refs[0].at[pl.ds(k * tile, tile), :], hidden_ref.at[pl.ds(k * tile, tile), :], sems.at[k]
        )
        for k in range(steps)
    ]
    cotangent = pltpu.make_async_copy(refs[4], cot_ref, sems.at[steps + 3])
    for copy in small + large + [cotangent]:
        copy.start()
    for copy in small:
        copy.wait()
    for step, copy in enumerate(large):
        here = slice(step * tile, (step + 1) * tile)
        scale = scale_ref[:, here]
        jitter = jnp.where(scale == 0, 1.0, jnp.where(scale == 1, 0.5, 0.25))
        xyz = offsets_ref[:, here] * jitter
        row = lax.broadcasted_iota(jnp.int32, (16, tile), 0)
        last = jnp.zeros((16, tile), F32)
        for k in range(half - hid):
            last = jnp.where(row == 16 - (half - hid) + k, xyz[k : k + 1], last)
        last = last.astype(BF16)
        row = lax.broadcasted_iota(jnp.int32, (extra_lanes - 16, tile), 0)
        ids = ids_ref[:, here]
        member = jnp.where((row == ids) | (row == ids + shapes), 1.0, 0.0).astype(BF16)
        x_ref[here, half:] = jnp.concatenate([member, last], axis=0).T
        x_t_ref[half:, here] = member[:shapes]
        copy.wait()
        x_ref[here, half - LANES : half] = jnp.zeros((tile, LANES), BF16)
        x_ref[here, :hid] = hidden_ref[here, :].astype(BF16)
        hidden = x_ref[here, :half].T
        x_t_ref[: half - 16, here] = hidden[: half - 16]
        x_t_ref[half - 16 : half, here] = hidden[half - 16 :] + last
    cotangent.wait()


def layer_kernel(hid, shapes, tile, orders, parts, *refs):
    n = 1 if orders is None else len(orders)
    pieces = refs[:n]
    x_ref, x_t_ref, cot_ref, out_hbm, grad_hidden_hbm = refs[n : n + 5]
    grad_refs = refs[n + 5 : -6]
    w_ref, turned_ref, out_ref, grad_hidden_ref, grad_pre_ref, pre_ref, sems = refs[-7:]
    points, width = cot_ref.shape
    half = width // 2
    steps = points // tile
    me = lax.axis_index(AXES)
    place(pieces, orders, me, w_ref)
    copies = []

    def rows_of(step):
        return slice(step * tile, (step + 1) * tile)

    def forward(step):
        pre_ref[step % 2] = dot(x_ref[rows_of(step), :], w_ref[...], NT)

    def middle(step):
        here = rows_of(step)
        pre = pre_ref[step % 2]
        sigma = 0.5 * jnp.tanh(0.5 * pre) + 0.5
        out = pre * sigma
        out_ref[here, :] = out
        grad_pre_ref[here, :] = (cot_ref[here, :] * (sigma * (1.0 + (pre - out)))).astype(BF16)

    def backward(step):
        here = rows_of(step)
        grad_hidden_ref[here, :] = dot(grad_pre_ref[here, :], w_ref[:, :half])[:, :hid]

    def store(step, k, source, target):
        here = pl.ds(step * tile, tile)
        copy = pltpu.make_async_copy(source.at[here, :], target.at[here, :], sems.at[k, step])
        copy.start()
        copies.append(copy)

    forward(0)
    for step in range(steps):
        if step + 1 < steps:
            forward(step + 1)
        middle(step)
        if step > 0:
            backward(step - 1)
            store(step - 1, 1, grad_hidden_ref, grad_hidden_hbm)
        store(step, 0, out_ref, out_hbm)
    backward(steps - 1)
    store(steps - 1, 1, grad_hidden_ref, grad_hidden_hbm)
    grad = dot(x_t_ref[...], grad_pre_ref[...])
    sums = grad[half:].astype(BF16)
    for at in range(0, width, half):
        turned_ref[at : at + half, :] = grad[:half, at : at + half].T
    for ref, order in zip(grad_refs, parts):
        ref[:shapes, :] = sums[:, :half]
        ref[shapes : 2 * shapes, :] = sums[:, half:]
        if orders is None:
            ref[2 * shapes :, :] = turned_ref[...].astype(BF16)
            continue
        rows = (ref.shape[0] - 2 * shapes) // len(order)
        for k, mask in enumerate(order):
            at = pl.multiple_of((me ^ mask) * rows, rows)
            to = 2 * shapes + k * rows
            ref[to : to + rows, :] = turned_ref[pl.ds(at, rows), :].astype(BF16)

    for copy in copies:
        copy.wait()


def sum_of(refs):
    terms = [ref[...].astype(F32) for ref in refs]
    while len(terms) > 1:
        terms = [a + b for a, b in zip(terms[::2], terms[1::2])]
    return terms[0]


def add_kernel(shapes, n, *refs):
    total = sum_of(refs[:n]).astype(BF16)
    for k, ref in enumerate(refs[n:]):
        rows = ref.shape[0] - 2 * shapes
        at = 2 * shapes + k * rows
        ref[: 2 * shapes, :] = total[: 2 * shapes]
        ref[2 * shapes :, :] = total[at : at + rows]


def last_kernel(hid, shapes, orders, n, *refs):
    direction_ref, gain_ref, codes_ref = refs[n : n + 3]
    pieces = refs[n + 3 : -5]
    grad_codes_ref, grad_direction_ref, grad_gain_ref, grad_bias_ref, code_scratch = refs[-5:]
    d = direction_ref[...]
    rows, cols = d.shape
    half = cols // 2
    me = lax.axis_index(AXES)
    place(pieces, orders, me, code_scratch)
    total = sum_of(refs[:n])
    sums = jnp.concatenate([total[:shapes], total[shapes : 2 * shapes]], axis=1)
    sums = jnp.concatenate(split(sums), axis=0).astype(BF16)
    terms = dot(sums, code_scratch[...])
    grad_codes_ref[...] = terms[:shapes] + terms[shapes:]
    width = sums.shape[1]
    mine = lax.broadcasted_iota(jnp.int32, (rows, width), 0) + me * rows
    mine = jnp.where(mine == lax.broadcasted_iota(jnp.int32, (rows, width), 1), 1.0, 0.0).astype(BF16)
    own = dot(mine, sums, NT)
    grad_bias_ref[...] = to_row(jnp.sum(own, axis=1, keepdims=True))
    code = dot(own.astype(BF16), stacked_codes(codes_ref, 2 * shapes))
    packed = jnp.concatenate([total[2 * shapes :], code], axis=1)
    lane = lax.broadcasted_iota(jnp.int32, (rows, cols), 1)
    grad_weight = jnp.where(
        lane < hid,
        packed,
        jnp.where(lane < hid + half, pltpu.roll(packed, cols - (half - hid), 1), pltpu.roll(packed, half, 1)),
    )
    inverse = lax.rsqrt(jnp.sum(d * d, axis=1, keepdims=True))
    unit = d * inverse
    grad_gain = jnp.sum(grad_weight * unit, axis=1, keepdims=True)
    grad_gain_ref[...] = to_row(grad_gain)
    grad_direction_ref[...] = (to_column(gain_ref[...]) * inverse) * (grad_weight - grad_gain * unit)


def masks_of(group):
    masks = [0]
    for bit in group:
        masks = masks + [m ^ bit for m in masks]
    return masks


def order_of(groups):
    order = [0]
    for group in groups:
        order = [m ^ r for m in masks_of(group) for r in order]
    return order


def swaps(arrays, masks, devices):
    moved = [
        lax.ppermute(x, AXES, [(i, i ^ mask) for i in range(devices)])
        for x, mask in list(zip(arrays, masks))[::-1]
    ]
    return moved[::-1]


def per_device(
    hidden,
    codes,
    offsets,
    shape_ids,
    scale_index,
    direction,
    gain,
    bias,
    cotangent,
    running_mean,
    running_var,
):
    points, hid = hidden.shape
    shapes = codes.shape[0]
    rows, cols = direction.shape
    width = cotangent.shape[1]
    half = cols // 2
    devices = lax.axis_size("dp") * lax.axis_size("inner")
    tuned = rows % 16 == 0
    bits = [1 << k | 1 for k in range(devices.bit_length() - 1)]
    groups = [bits[k - 2 : k] for k in range(len(bits), 1, -2)]
    groups = groups + [bits[:1]] * (len(bits) % 2)
    tuned = rows % 16 == 0
    extra_lanes = -(-(2 * shapes + 16) // LANES) * LANES
    lanes = half + extra_lanes
    gain_row = gain.reshape(1, rows)

    def shape_of(rows, lanes, dtype):
        return jax.ShapeDtypeStruct((rows, lanes), dtype)

    held = small_kernel(
        "prep",
        functools.partial(prep_kernel, hid),
        shape_of(rows, lanes + half, BF16),
        *[
            pltpu.with_memory_space_constraint(x, pltpu.HBM)
            for x in (direction, gain_row, bias.reshape(1, rows), codes)
        ],
        scratch=[
            VMEM((rows, cols), F32),
            VMEM((1, rows), F32),
            VMEM((1, rows), F32),
            VMEM((shapes, half), F32),
            pltpu.SemaphoreType.DMA((4,)),
        ],
        space=pl.ANY,
    )
    tile, layer_tile = min(512, points), min(256, points)
    x, x_t, cotangent = pl.pallas_call(
        functools.partial(inputs_kernel, hid, tile),
        out_shape=[
            shape_of(points, lanes, BF16),
            shape_of(half + shapes, points, BF16),
            pltpu.VMEM((points, width), F32),
        ],
        in_specs=[pl.BlockSpec(memory_space=pl.ANY)] * 5,
        out_specs=vmem(3),
        scratch_shapes=[
            VMEM((points, hid), F32),
            VMEM((half - hid, points), F32),
            VMEM((1, points), jnp.int32),
            VMEM((1, points), jnp.int32),
            pltpu.SemaphoreType.DMA((points // tile + 4,)),
        ],
        compiler_params=pltpu.CompilerParams(vmem_limit_bytes=12 * MIB),
        cost_estimate=pl.CostEstimate(
            flops=4000 * MIB, bytes_accessed=8 * points * half, transcendentals=0
        ),
        name="inputs",
    )(
        *[
            pltpu.with_memory_space_constraint(a, pltpu.HBM)
            for a in (
                hidden,
                offsets.T,
                shape_ids.reshape(1, points),
                scale_index.reshape(1, points),
                cotangent,
            )
        ]
    )
    def gather(array, group):
        masks = masks_of(group)[1:]
        return [array] + swaps([array] * len(masks), masks, devices)

    def join(arrays, *widths):
        height = sum(a.shape[0] for a in arrays)
        return small_kernel(
            "join",
            functools.partial(join_kernel, len(arrays)),
            [shape_of(height, width, BF16) for width in widths],
            *arrays[::-1],
        )

    if tuned:
        weight, code_weight = join(gather(held, groups[0]), lanes, half)
        weight, code_weight, x, x_t, cotangent = lax.optimization_barrier(
            (weight, code_weight, x, x_t, cotangent)
        )
        steps = [[bit] for group in groups[1:-1] for bit in group[::-1]]
        code_order = order_of(groups[:1] + steps)
        for group in groups[1:-1]:
            weights, code_weights = gather(weight, group), gather(code_weight, steps[0])
            (weight,) = join(weights, lanes)
            (code_weight,) = join(code_weights, half)
        weights = gather(weight, groups[-1])
        code_weights = gather(code_weight, steps[1])
        orders = [[m ^ r for r in order_of(groups[:-1])] for m in masks_of(groups[-1])]
        code_orders = [[m ^ r for r in code_order] for m in masks_of(groups[-1])]
        parts = orders
    else:
        held = lax.all_gather(held, AXES, axis=0, tiled=True)
        weights, code_weights, orders, code_orders, parts = [held[:, :lanes]], [held[:, lanes:]], None, None, [[0]]

    output, grad_hidden, *grads = pl.pallas_call(
        functools.partial(layer_kernel, hid, shapes, layer_tile, orders, parts),
        out_shape=[pltpu.HBM((points, width), F32), pltpu.HBM((points, hid), F32)]
        + [shape_of(2 * shapes + width // len(parts), half, BF16)] * len(parts),
        in_specs=vmem(len(weights) + 3),
        out_specs=[pl.BlockSpec(memory_space=pltpu.HBM)] * 2 + vmem(len(parts)),
        scratch_shapes=[
            VMEM((width, lanes), BF16),
            VMEM((width, half), F32),
            VMEM((points, width), F32),
            VMEM((points, hid), F32),
            VMEM((points, width), BF16),
            VMEM((2, layer_tile, width), F32),
            pltpu.SemaphoreType.DMA((2, points // layer_tile)),
        ],
        compiler_params=pltpu.CompilerParams(vmem_limit_bytes=20 * MIB),
        cost_estimate=pl.CostEstimate(
            flops=6 * points * width * cols,
            bytes_accessed=8 * points * (width + half),
            transcendentals=points * width,
        ),
        name="layer",
    )(*weights, x, x_t, cotangent)

    if tuned:
        *grads, code_weight = lax.optimization_barrier((*grads, code_weights[1]))
        (code_weight,) = join([code_weights[0], code_weight], half)
        code_weights = gather(code_weight, groups[-1])
        for r, group in enumerate(groups[::-1]):
            masks = masks_of(group)
            grads = [grads[0]] + swaps(grads[1:], masks[1:], devices)
            if r == len(groups) - 1:
                break
            n_out = len(masks_of(groups[-2 - r]))
            left = (grads[0].shape[0] - 2 * shapes) // n_out
            grads = small_kernel(
                "add",
                functools.partial(add_kernel, shapes, len(grads)),
                [shape_of(2 * shapes + left, half, BF16)] * n_out,
                *grads[::-1],
            )
    else:
        sums = lax.psum(grads[0][: 2 * shapes].astype(F32), AXES)
        high = sums.astype(BF16)
        own = lax.psum_scatter(grads[0][2 * shapes :].astype(F32), AXES, scatter_dimension=0, tiled=True)
        low = jnp.zeros((2 * shapes + rows, half), BF16).at[: 2 * shapes].set((sums - high).astype(BF16))
        grads = [jnp.concatenate([high, own.astype(BF16)], axis=0), low]
    grad_codes, grad_direction, grad_gain, grad_bias = small_kernel(
        "last",
        functools.partial(last_kernel, hid, shapes, code_orders, len(grads)),
        [
            shape_of(shapes, half, F32),
            shape_of(rows, cols, F32),
            shape_of(1, rows, F32),
            shape_of(1, rows, F32),
        ],
        *grads[::-1],
        direction,
        gain_row,
        codes,
        *code_weights,
        scratch=[VMEM((width, half), BF16)],
    )

    total = float(points * devices)
    batch_mean = jnp.mean(codes, axis=0)
    batch_square = jnp.mean(codes * codes, axis=0)
    batch_var = (batch_square - batch_mean * batch_mean) * (total / (total - 1.0))
    new_mean = 0.9 * running_mean + 0.1 * batch_mean
    new_var = 0.9 * running_var + 0.1 * batch_var
    return (
        output,
        grad_hidden,
        grad_codes,
        grad_direction,
        grad_gain.reshape(rows),
        grad_bias.reshape(rows),
        new_mean,
        new_var,
    )


def solution(mesh):
    return jax.shard_map(
        per_device,
        mesh=mesh,
        in_specs=(
            P(("dp", "inner"), None),
            P(),
            P(("dp", "inner"), None),
            P(("dp", "inner")),
            P(("dp", "inner")),
            P(("dp", "inner"), None),
            P(("dp", "inner")),
            P(("dp", "inner")),
            P(("dp", "inner"), None),
            P(),
            P(),
        ),
        out_specs=(
            P(("dp", "inner"), None),
            P(("dp", "inner"), None),
            P(),
            P(("dp", "inner"), None),
            P(("dp", "inner")),
            P(("dp", "inner")),
            P(),
            P(),
        ),
        check_vma=False,
    )
```

```python
import functools

import jax
import jax.numpy as jnp
from jax import lax
from jax.experimental import pallas as pl
from jax.experimental.pallas import tpu as pltpu
from jax.sharding import PartitionSpec as P

AXES = ("dp", "inner")
LANES = 128
MIB = 1024 * 1024
F32 = jnp.float32
BF16 = jnp.bfloat16
VMEM = pltpu.VMEM
NT = (((1,), (1,)), ((), ()))


def dot(a, b, dims=(((1,), (0,)), ((), ()))):
    return lax.dot_general(a, b, dims, preferred_element_type=F32)


def vmem(n):
    return [pl.BlockSpec(memory_space=VMEM)] * n


def small_kernel(name, body, out_shape, *args, scratch=(), space=VMEM, limit=8):
    many = isinstance(out_shape, list)
    return pl.pallas_call(
        body,
        out_shape=out_shape,
        in_specs=[pl.BlockSpec(memory_space=space)] * len(args),
        out_specs=vmem(len(out_shape)) if many else vmem(1)[0],
        scratch_shapes=list(scratch),
        compiler_params=pltpu.CompilerParams(vmem_limit_bytes=limit * MIB),
        cost_estimate=pl.CostEstimate(
            flops=4000 * MIB, bytes_accessed=8 * MIB, transcendentals=4 * MIB
        ),
        name=name,
    )(*args)


def diagonal(n):
    return lax.broadcasted_iota(jnp.int32, (n, n), 0) == lax.broadcasted_iota(jnp.int32, (n, n), 1)


def to_column(row):
    n = row.shape[1]
    return jnp.sum(jnp.where(diagonal(n), row, 0.0), axis=1, keepdims=True)


def to_row(column):
    n = column.shape[0]
    return jnp.sum(jnp.where(diagonal(n), column, 0.0), axis=0, keepdims=True)


def stacked_codes(codes_ref, count):
    codes = codes_ref[...].astype(BF16)
    parts = [codes, codes]
    if count > 2 * codes.shape[0]:
        parts.append(jnp.zeros((count - 2 * codes.shape[0], codes.shape[1]), BF16))
    return jnp.concatenate(parts, axis=0)


def split(x):
    high = x.astype(BF16).astype(F32)
    return high, x - high


def prep_kernel(hid, *refs):
    piece_ref, direction_ref, gain_ref, bias_ref, codes_ref, sems = refs[4:]
    copies = [
        pltpu.make_async_copy(source, target, sems.at[k])
        for k, (source, target) in enumerate(zip(refs[:4], refs[5:9]))
    ]
    for copy in copies:
        copy.start()
    for copy in copies:
        copy.wait()
    d = direction_ref[...]
    shapes = codes_ref.shape[0]
    rows, cols = d.shape
    half = cols // 2
    extra_lanes = piece_ref.shape[1] - cols
    inverse = lax.rsqrt(jnp.sum(d * d, axis=1, keepdims=True))
    w = to_column(gain_ref[...]) * (d * inverse)
    lane = lax.broadcasted_iota(jnp.int32, (rows, half), 1)
    first = jnp.where(lane < hid, w[:, :half], w[:, half:])
    code = pltpu.roll(w, half - hid, 1)[:, half:].astype(BF16)
    bias = to_column(bias_ref[...]).astype(BF16).astype(F32)
    high, low = split(dot(code, stacked_codes(codes_ref, extra_lanes), NT) + bias)
    own = first[:, half - LANES :]
    if extra_lanes > LANES:
        own = jnp.concatenate([jnp.zeros((rows, extra_lanes - LANES), F32), own], axis=1)
    lane = lax.broadcasted_iota(jnp.int32, (rows, extra_lanes), 1)
    table = jnp.where(lane < shapes, high, jnp.where(lane < 2 * shapes, low, 0.0))
    table = jnp.where(lane >= extra_lanes - (half - hid), own, table)
    piece_ref[:, :half] = first.astype(BF16)
    piece_ref[:, half : half + extra_lanes] = table.astype(BF16)
    piece_ref[:, half + extra_lanes :] = code


def join_kernel(n, *refs):
    rows = refs[0].shape[0]
    for k, ref in enumerate(refs[n - 1 :: -1]):
        lane = 0
        for out_ref in refs[n:]:
            lanes = out_ref.shape[1]
            out_ref[k * rows : (k + 1) * rows, :] = ref[:, lane : lane + lanes]
            lane += lanes


def place(refs, orders, me, out_ref):
    if orders is None:
        out_ref[...] = refs[0][...]
        return
    rows = refs[0].shape[0] // len(orders[0])
    for ref, order in zip(refs, orders):
        for k, mask in enumerate(order):
            at = pl.multiple_of((me ^ mask) * rows, rows)
            out_ref[pl.ds(at, rows), :] = ref[k * rows : (k + 1) * rows, :]


def inputs_kernel(hid, tile, *refs):
    x_ref, x_t_ref, cot_ref, hidden_ref, offsets_ref, ids_ref, scale_ref, sems = refs[5:]
    points = x_ref.shape[0]
    half = (hid + LANES - 1) // LANES * LANES
    shapes = x_t_ref.shape[0] - half
    extra_lanes = x_ref.shape[1] - half
    steps = points // tile
    small = [
        pltpu.make_async_copy(source, target, sems.at[steps + k])
        for k, (source, target) in enumerate(zip(refs[1:4], (offsets_ref, ids_ref, scale_ref)))
    ]
    large = [
        pltpu.make_async_copy(
            refs[0].at[pl.ds(k * tile, tile), :], hidden_ref.at[pl.ds(k * tile, tile), :], sems.at[k]
        )
        for k in range(steps)
    ]
    cotangent = pltpu.make_async_copy(refs[4], cot_ref, sems.at[steps + 3])
    for copy in small + large + [cotangent]:
        copy.start()
    for copy in small:
        copy.wait()
    for step, copy in enumerate(large):
        here = slice(step * tile, (step + 1) * tile)
        scale = scale_ref[:, here]
        jitter = jnp.where(scale == 0, 1.0, jnp.where(scale == 1, 0.5, 0.25))
        xyz = offsets_ref[:, here] * jitter
        row = lax.broadcasted_iota(jnp.int32, (16, tile), 0)
        last = jnp.zeros((16, tile), F32)
        for k in range(half - hid):
            last = jnp.where(row == 16 - (half - hid) + k, xyz[k : k + 1], last)
        last = last.astype(BF16)
        row = lax.broadcasted_iota(jnp.int32, (extra_lanes - 16, tile), 0)
        ids = ids_ref[:, here]
        member = jnp.where((row == ids) | (row == ids + shapes), 1.0, 0.0).astype(BF16)
        x_ref[here, half:] = jnp.concatenate([member, last], axis=0).T
        x_t_ref[half:, here] = member[:shapes]
        copy.wait()
        x_ref[here, half - LANES : half] = jnp.zeros((tile, LANES), BF16)
        x_ref[here, :hid] = hidden_ref[here, :].astype(BF16)
        hidden = x_ref[here, :half].T
        x_t_ref[: half - 16, here] = hidden[: half - 16]
        x_t_ref[half - 16 : half, here] = hidden[half - 16 :] + last
    cotangent.wait()


def layer_kernel(hid, shapes, tile, orders, parts, *refs):
    n = 1 if orders is None else len(orders)
    pieces = refs[:n]
    x_ref, x_t_ref, cot_ref, out_hbm, grad_hidden_ref = refs[n : n + 5]
    grad_refs = refs[n + 5 : -6]
    w_ref, turned_ref, out_ref, grad_pre_ref, pre_ref, sems = refs[-6:]
    points, width = cot_ref.shape
    half = width // 2
    steps = points // tile
    me = lax.axis_index(AXES)
    place(pieces, orders, me, w_ref)
    copies = []

    def rows_of(step):
        return slice(step * tile, (step + 1) * tile)

    def forward(step):
        pre_ref[step % 2] = dot(x_ref[rows_of(step), :], w_ref[...], NT)

    def middle(step):
        here = rows_of(step)
        pre = pre_ref[step % 2]
        sigma = 0.5 * jnp.tanh(0.5 * pre) + 0.5
        out = pre * sigma
        out_ref[here, :] = out
        grad_pre_ref[here, :] = (cot_ref[here, :] * (sigma * (1.0 + (pre - out)))).astype(BF16)

    def backward(step):
        here = rows_of(step)
        grad_hidden_ref[here, :] = dot(grad_pre_ref[here, :], w_ref[:, :half])[:, :hid]

    def store(step):
        here = pl.ds(step * tile, tile)
        copy = pltpu.make_async_copy(out_ref.at[here, :], out_hbm.at[here, :], sems.at[step])
        copy.start()
        copies.append(copy)

    forward(0)
    for step in range(steps):
        if step + 1 < steps:
            forward(step + 1)
        middle(step)
        if step > 0:
            backward(step - 1)
        store(step)
    backward(steps - 1)
    grad = dot(x_t_ref[...], grad_pre_ref[...])
    sums = grad[half:].astype(BF16)
    for at in range(0, width, half):
        turned_ref[at : at + half, :] = grad[:half, at : at + half].T
    for ref, order in zip(grad_refs, parts):
        ref[:shapes, :] = sums[:, :half]
        ref[shapes : 2 * shapes, :] = sums[:, half:]
        if orders is None:
            ref[2 * shapes :, :] = turned_ref[...].astype(BF16)
            continue
        rows = (ref.shape[0] - 2 * shapes) // len(order)
        for k, mask in enumerate(order):
            at = pl.multiple_of((me ^ mask) * rows, rows)
            to = 2 * shapes + k * rows
            ref[to : to + rows, :] = turned_ref[pl.ds(at, rows), :].astype(BF16)

    for copy in copies:
        copy.wait()


def store_kernel(source_ref, target_ref, sem):
    copy = pltpu.make_async_copy(source_ref, target_ref, sem)
    copy.start()
    copy.wait()


def sum_of(refs):
    terms = [ref[...].astype(F32) for ref in refs]
    while len(terms) > 1:
        terms = [a + b for a, b in zip(terms[::2], terms[1::2])]
    return terms[0]


def add_kernel(shapes, n, *refs):
    total = sum_of(refs[:n]).astype(BF16)
    for k, ref in enumerate(refs[n:]):
        rows = ref.shape[0] - 2 * shapes
        at = 2 * shapes + k * rows
        ref[: 2 * shapes, :] = total[: 2 * shapes]
        ref[2 * shapes :, :] = total[at : at + rows]


def last_kernel(hid, shapes, orders, n, *refs):
    direction_ref, gain_ref, codes_ref = refs[n : n + 3]
    pieces = refs[n + 3 : -5]
    grad_codes_ref, grad_direction_ref, grad_gain_ref, grad_bias_ref, code_scratch = refs[-5:]
    d = direction_ref[...]
    rows, cols = d.shape
    half = cols // 2
    me = lax.axis_index(AXES)
    place(pieces, orders, me, code_scratch)
    total = sum_of(refs[:n])
    sums = jnp.concatenate([total[:shapes], total[shapes : 2 * shapes]], axis=1)
    sums = jnp.concatenate(split(sums), axis=0).astype(BF16)
    terms = dot(sums, code_scratch[...])
    grad_codes_ref[...] = terms[:shapes] + terms[shapes:]
    width = sums.shape[1]
    mine = lax.broadcasted_iota(jnp.int32, (rows, width), 0) + me * rows
    mine = jnp.where(mine == lax.broadcasted_iota(jnp.int32, (rows, width), 1), 1.0, 0.0).astype(BF16)
    own = dot(mine, sums, NT)
    grad_bias_ref[...] = to_row(jnp.sum(own, axis=1, keepdims=True))
    code = dot(own.astype(BF16), stacked_codes(codes_ref, 2 * shapes))
    packed = jnp.concatenate([total[2 * shapes :], code], axis=1)
    lane = lax.broadcasted_iota(jnp.int32, (rows, cols), 1)
    grad_weight = jnp.where(
        lane < hid,
        packed,
        jnp.where(lane < hid + half, pltpu.roll(packed, cols - (half - hid), 1), pltpu.roll(packed, half, 1)),
    )
    inverse = lax.rsqrt(jnp.sum(d * d, axis=1, keepdims=True))
    unit = d * inverse
    grad_gain = jnp.sum(grad_weight * unit, axis=1, keepdims=True)
    grad_gain_ref[...] = to_row(grad_gain)
    grad_direction_ref[...] = (to_column(gain_ref[...]) * inverse) * (grad_weight - grad_gain * unit)


def masks_of(group):
    masks = [0]
    for bit in group:
        masks = masks + [m ^ bit for m in masks]
    return masks


def order_of(groups):
    order = [0]
    for group in groups:
        order = [m ^ r for m in masks_of(group) for r in order]
    return order


def swaps(arrays, masks, devices):
    moved = [
        lax.ppermute(x, AXES, [(i, i ^ mask) for i in range(devices)])
        for x, mask in list(zip(arrays, masks))[::-1]
    ]
    return moved[::-1]


def per_device(
    hidden,
    codes,
    offsets,
    shape_ids,
    scale_index,
    direction,
    gain,
    bias,
    cotangent,
    running_mean,
    running_var,
):
    points, hid = hidden.shape
    shapes = codes.shape[0]
    rows, cols = direction.shape
    width = cotangent.shape[1]
    half = cols // 2
    devices = lax.axis_size("dp") * lax.axis_size("inner")
    tuned = rows % 16 == 0
    bits = [1 << k | 1 for k in range(devices.bit_length() - 1)]
    groups = [bits[k - 2 : k] for k in range(len(bits), 1, -2)]
    groups = groups + [bits[:1]] * (len(bits) % 2)
    tuned = rows % 16 == 0
    extra_lanes = -(-(2 * shapes + 16) // LANES) * LANES
    lanes = half + extra_lanes
    gain_row = gain.reshape(1, rows)

    def shape_of(rows, lanes, dtype):
        return jax.ShapeDtypeStruct((rows, lanes), dtype)

    held = small_kernel(
        "prep",
        functools.partial(prep_kernel, hid),
        shape_of(rows, lanes + half, BF16),
        *[
            pltpu.with_memory_space_constraint(x, pltpu.HBM)
            for x in (direction, gain_row, bias.reshape(1, rows), codes)
        ],
        scratch=[
            VMEM((rows, cols), F32),
            VMEM((1, rows), F32),
            VMEM((1, rows), F32),
            VMEM((shapes, half), F32),
            pltpu.SemaphoreType.DMA((4,)),
        ],
        space=pl.ANY,
    )
    tile, layer_tile = min(512, points), min(256, points)
    x, x_t, cotangent = pl.pallas_call(
        functools.partial(inputs_kernel, hid, tile),
        out_shape=[
            shape_of(points, lanes, BF16),
            shape_of(half + shapes, points, BF16),
            pltpu.VMEM((points, width), F32),
        ],
        in_specs=[pl.BlockSpec(memory_space=pl.ANY)] * 5,
        out_specs=vmem(3),
        scratch_shapes=[
            VMEM((points, hid), F32),
            VMEM((half - hid, points), F32),
            VMEM((1, points), jnp.int32),
            VMEM((1, points), jnp.int32),
            pltpu.SemaphoreType.DMA((points // tile + 4,)),
        ],
        compiler_params=pltpu.CompilerParams(vmem_limit_bytes=12 * MIB),
        cost_estimate=pl.CostEstimate(
            flops=4000 * MIB, bytes_accessed=8 * points * half, transcendentals=0
        ),
        name="inputs",
    )(
        *[
            pltpu.with_memory_space_constraint(a, pltpu.HBM)
            for a in (
                hidden,
                offsets.T,
                shape_ids.reshape(1, points),
                scale_index.reshape(1, points),
                cotangent,
            )
        ]
    )
    def gather(array, group):
        masks = masks_of(group)[1:]
        return [array] + swaps([array] * len(masks), masks, devices)

    def join(arrays, *widths):
        height = sum(a.shape[0] for a in arrays)
        return small_kernel(
            "join",
            functools.partial(join_kernel, len(arrays)),
            [shape_of(height, width, BF16) for width in widths],
            *arrays[::-1],
        )

    if tuned:
        weight, code_weight = join(gather(held, groups[0]), lanes, half)
        weight, code_weight, x, x_t, cotangent = lax.optimization_barrier(
            (weight, code_weight, x, x_t, cotangent)
        )
        steps = [[bit] for group in groups[1:-1] for bit in group[::-1]]
        code_order = order_of(groups[:1] + steps)
        for group in groups[1:-1]:
            weights, code_weights = gather(weight, group), gather(code_weight, steps[0])
            (weight,) = join(weights, lanes)
            (code_weight,) = join(code_weights, half)
        weights = gather(weight, groups[-1])
        code_weights = gather(code_weight, steps[1])
        orders = [[m ^ r for r in order_of(groups[:-1])] for m in masks_of(groups[-1])]
        code_orders = [[m ^ r for r in code_order] for m in masks_of(groups[-1])]
        parts = orders
    else:
        held = lax.all_gather(held, AXES, axis=0, tiled=True)
        weights, code_weights, orders, code_orders, parts = [held[:, :lanes]], [held[:, lanes:]], None, None, [[0]]

    output, grad_hidden, *grads = pl.pallas_call(
        functools.partial(layer_kernel, hid, shapes, layer_tile, orders, parts),
        out_shape=[pltpu.HBM((points, width), F32), pltpu.VMEM((points, hid), F32)]
        + [shape_of(2 * shapes + width // len(parts), half, BF16)] * len(parts),
        in_specs=vmem(len(weights) + 3),
        out_specs=[pl.BlockSpec(memory_space=pltpu.HBM)] + vmem(1 + len(parts)),
        scratch_shapes=[
            VMEM((width, lanes), BF16),
            VMEM((width, half), F32),
            VMEM((points, width), F32),
            VMEM((points, width), BF16),
            VMEM((2, layer_tile, width), F32),
            pltpu.SemaphoreType.DMA((points // layer_tile,)),
        ],
        compiler_params=pltpu.CompilerParams(vmem_limit_bytes=20 * MIB),
        cost_estimate=pl.CostEstimate(
            flops=6 * points * width * cols,
            bytes_accessed=8 * points * (width + half),
            transcendentals=points * width,
        ),
        name="layer",
    )(*weights, x, x_t, cotangent)

    grad_hidden = pl.pallas_call(
        store_kernel,
        out_shape=pltpu.HBM((points, hid), F32),
        in_specs=vmem(1),
        out_specs=pl.BlockSpec(memory_space=pltpu.HBM),
        scratch_shapes=[pltpu.SemaphoreType.DMA(())],
        compiler_params=pltpu.CompilerParams(vmem_limit_bytes=8 * MIB),
        cost_estimate=pl.CostEstimate(
            flops=4000 * MIB, bytes_accessed=8 * points * hid, transcendentals=0
        ),
        name="store",
    )(grad_hidden)

    if tuned:
        *grads, code_weight = lax.optimization_barrier((*grads, code_weights[1]))
        (code_weight,) = join([code_weights[0], code_weight], half)
        code_weights = gather(code_weight, groups[-1])
        for r, group in enumerate(groups[::-1]):
            masks = masks_of(group)
            grads = [grads[0]] + swaps(grads[1:], masks[1:], devices)
            if r == len(groups) - 1:
                break
            n_out = len(masks_of(groups[-2 - r]))
            left = (grads[0].shape[0] - 2 * shapes) // n_out
            grads = small_kernel(
                "add",
                functools.partial(add_kernel, shapes, len(grads)),
                [shape_of(2 * shapes + left, half, BF16)] * n_out,
                *grads[::-1],
            )
            if r == len(groups) - 2:
                *grads, grad_hidden = lax.optimization_barrier((*grads, grad_hidden))
    else:
        sums = lax.psum(grads[0][: 2 * shapes].astype(F32), AXES)
        high = sums.astype(BF16)
        own = lax.psum_scatter(grads[0][2 * shapes :].astype(F32), AXES, scatter_dimension=0, tiled=True)
        low = jnp.zeros((2 * shapes + rows, half), BF16).at[: 2 * shapes].set((sums - high).astype(BF16))
        grads = [jnp.concatenate([high, own.astype(BF16)], axis=0), low]
    grad_codes, grad_direction, grad_gain, grad_bias = small_kernel(
        "last",
        functools.partial(last_kernel, hid, shapes, code_orders, len(grads)),
        [
            shape_of(shapes, half, F32),
            shape_of(rows, cols, F32),
            shape_of(1, rows, F32),
            shape_of(1, rows, F32),
        ],
        *grads[::-1],
        direction,
        gain_row,
        codes,
        *code_weights,
        scratch=[VMEM((width, half), BF16)],
    )

    total = float(points * devices)
    batch_mean = jnp.mean(codes, axis=0)
    batch_square = jnp.mean(codes * codes, axis=0)
    batch_var = (batch_square - batch_mean * batch_mean) * (total / (total - 1.0))
    new_mean = 0.9 * running_mean + 0.1 * batch_mean
    new_var = 0.9 * running_var + 0.1 * batch_var
    return (
        output,
        grad_hidden,
        grad_codes,
        grad_direction,
        grad_gain.reshape(rows),
        grad_bias.reshape(rows),
        new_mean,
        new_var,
    )


def solution(mesh):
    return jax.shard_map(
        per_device,
        mesh=mesh,
        in_specs=(
            P(("dp", "inner"), None),
            P(),
            P(("dp", "inner"), None),
            P(("dp", "inner")),
            P(("dp", "inner")),
            P(("dp", "inner"), None),
            P(("dp", "inner")),
            P(("dp", "inner")),
            P(("dp", "inner"), None),
            P(),
            P(),
        ),
        out_specs=(
            P(("dp", "inner"), None),
            P(("dp", "inner"), None),
            P(),
            P(("dp", "inner"), None),
            P(("dp", "inner")),
            P(("dp", "inner")),
            P(),
            P(),
        ),
        check_vma=False,
    )
```

```python
import functools

import jax
import jax.numpy as jnp
from jax import lax
from jax.experimental import pallas as pl
from jax.experimental.pallas import tpu as pltpu
from jax.sharding import PartitionSpec as P

AXES = ("dp", "inner")
LANES = 128
MIB = 1024 * 1024
F32 = jnp.float32
BF16 = jnp.bfloat16
VMEM = pltpu.VMEM
NT = (((1,), (1,)), ((), ()))


def dot(a, b, dims=(((1,), (0,)), ((), ()))):
    return lax.dot_general(a, b, dims, preferred_element_type=F32)


def vmem(n):
    return [pl.BlockSpec(memory_space=VMEM)] * n


def small_kernel(name, body, out_shape, *args, scratch=(), space=VMEM, limit=8):
    many = isinstance(out_shape, list)
    return pl.pallas_call(
        body,
        out_shape=out_shape,
        in_specs=[pl.BlockSpec(memory_space=space)] * len(args),
        out_specs=vmem(len(out_shape)) if many else vmem(1)[0],
        scratch_shapes=list(scratch),
        compiler_params=pltpu.CompilerParams(vmem_limit_bytes=limit * MIB),
        cost_estimate=pl.CostEstimate(
            flops=4000 * MIB, bytes_accessed=8 * MIB, transcendentals=4 * MIB
        ),
        name=name,
    )(*args)


def diagonal(n):
    return lax.broadcasted_iota(jnp.int32, (n, n), 0) == lax.broadcasted_iota(jnp.int32, (n, n), 1)


def to_column(row):
    n = row.shape[1]
    return jnp.sum(jnp.where(diagonal(n), row, 0.0), axis=1, keepdims=True)


def to_row(column):
    n = column.shape[0]
    return jnp.sum(jnp.where(diagonal(n), column, 0.0), axis=0, keepdims=True)


def stacked_codes(codes_ref, count):
    codes = codes_ref[...].astype(BF16)
    parts = [codes, codes]
    if count > 2 * codes.shape[0]:
        parts.append(jnp.zeros((count - 2 * codes.shape[0], codes.shape[1]), BF16))
    return jnp.concatenate(parts, axis=0)


def split(x):
    high = x.astype(BF16).astype(F32)
    return high, x - high


def prep_kernel(hid, *refs):
    piece_ref, direction_ref, gain_ref, bias_ref, codes_ref, sems = refs[4:]
    copies = [
        pltpu.make_async_copy(source, target, sems.at[k])
        for k, (source, target) in enumerate(zip(refs[:4], refs[5:9]))
    ]
    for copy in copies:
        copy.start()
    for copy in copies:
        copy.wait()
    d = direction_ref[...]
    shapes = codes_ref.shape[0]
    rows, cols = d.shape
    half = cols // 2
    extra_lanes = piece_ref.shape[1] - cols
    inverse = lax.rsqrt(jnp.sum(d * d, axis=1, keepdims=True))
    w = to_column(gain_ref[...]) * (d * inverse)
    lane = lax.broadcasted_iota(jnp.int32, (rows, half), 1)
    first = jnp.where(lane < hid, w[:, :half], w[:, half:])
    code = pltpu.roll(w, half - hid, 1)[:, half:].astype(BF16)
    bias = to_column(bias_ref[...]).astype(BF16).astype(F32)
    high, low = split(dot(code, stacked_codes(codes_ref, extra_lanes), NT) + bias)
    own = first[:, half - LANES :]
    if extra_lanes > LANES:
        own = jnp.concatenate([jnp.zeros((rows, extra_lanes - LANES), F32), own], axis=1)
    lane = lax.broadcasted_iota(jnp.int32, (rows, extra_lanes), 1)
    table = jnp.where(lane < shapes, high, jnp.where(lane < 2 * shapes, low, 0.0))
    table = jnp.where(lane >= extra_lanes - (half - hid), own, table)
    piece_ref[:, :half] = first.astype(BF16)
    piece_ref[:, half : half + extra_lanes] = table.astype(BF16)
    piece_ref[:, half + extra_lanes :] = code


def join_kernel(n, n_early, *refs):
    rows = refs[0].shape[0]
    for k, ref in enumerate(refs[n - 1 :: -1]):
        lane = 0
        for out_ref in refs[n + n_early :]:
            lanes = out_ref.shape[1]
            out_ref[k * rows : (k + 1) * rows, :] = ref[:, lane : lane + lanes]
            lane += lanes


def place(refs, orders, me, out_ref):
    if orders is None:
        out_ref[...] = refs[0][...]
        return
    rows = refs[0].shape[0] // len(orders[0])
    for ref, order in zip(refs, orders):
        for k, mask in enumerate(order):
            at = pl.multiple_of((me ^ mask) * rows, rows)
            out_ref[pl.ds(at, rows), :] = ref[k * rows : (k + 1) * rows, :]


def inputs_kernel(hid, tile, *refs):
    x_ref, x_t_ref, hidden_ref, offsets_ref, ids_ref, scale_ref, sems = refs[4:]
    points = x_ref.shape[0]
    half = (hid + LANES - 1) // LANES * LANES
    shapes = x_t_ref.shape[0] - half
    extra_lanes = x_ref.shape[1] - half
    steps = points // tile
    small = [
        pltpu.make_async_copy(source, target, sems.at[steps + k])
        for k, (source, target) in enumerate(zip(refs[1:4], (offsets_ref, ids_ref, scale_ref)))
    ]
    large = [
        pltpu.make_async_copy(
            refs[0].at[pl.ds(k * tile, tile), :], hidden_ref.at[pl.ds(k * tile, tile), :], sems.at[k]
        )
        for k in range(steps)
    ]
    for copy in small + large:
        copy.start()
    for copy in small:
        copy.wait()
    for step, copy in enumerate(large):
        here = slice(step * tile, (step + 1) * tile)
        scale = scale_ref[:, here]
        jitter = jnp.where(scale == 0, 1.0, jnp.where(scale == 1, 0.5, 0.25))
        xyz = offsets_ref[:, here] * jitter
        row = lax.broadcasted_iota(jnp.int32, (16, tile), 0)
        last = jnp.zeros((16, tile), F32)
        for k in range(half - hid):
            last = jnp.where(row == 16 - (half - hid) + k, xyz[k : k + 1], last)
        last = last.astype(BF16)
        row = lax.broadcasted_iota(jnp.int32, (extra_lanes - 16, tile), 0)
        ids = ids_ref[:, here]
        member = jnp.where((row == ids) | (row == ids + shapes), 1.0, 0.0).astype(BF16)
        x_ref[here, half:] = jnp.concatenate([member, last], axis=0).T
        x_t_ref[half:, here] = member[:shapes]
        copy.wait()
        x_ref[here, half - LANES : half] = jnp.zeros((tile, LANES), BF16)
        x_ref[here, :hid] = hidden_ref[here, :].astype(BF16)
        hidden = x_ref[here, :half].T
        x_t_ref[: half - 16, here] = hidden[: half - 16]
        x_t_ref[half - 16 : half, here] = hidden[half - 16 :] + last


def layer_kernel(hid, shapes, tile, orders, parts, *refs):
    n = 1 if orders is None else len(orders)
    pieces = refs[:n]
    x_ref, x_t_ref, cot_ref, out_hbm, grad_hidden_ref = refs[n : n + 5]
    grad_refs = refs[n + 5 : -6]
    w_ref, turned_ref, out_ref, grad_pre_ref, pre_ref, sems = refs[-6:]
    points, width = cot_ref.shape
    half = width // 2
    steps = points // tile
    me = lax.axis_index(AXES)
    place(pieces, orders, me, w_ref)
    copies = []

    def rows_of(step):
        return slice(step * tile, (step + 1) * tile)

    def forward(step):
        pre_ref[step % 2] = dot(x_ref[rows_of(step), :], w_ref[...], NT)

    def middle(step):
        here = rows_of(step)
        pre = pre_ref[step % 2]
        sigma = 0.5 * jnp.tanh(0.5 * pre) + 0.5
        out = pre * sigma
        out_ref[here, :] = out
        grad_pre_ref[here, :] = (cot_ref[here, :] * (sigma * (1.0 + (pre - out)))).astype(BF16)

    def backward(step):
        here = rows_of(step)
        grad_hidden_ref[here, :] = dot(grad_pre_ref[here, :], w_ref[:, :half])[:, :hid]

    def store(step):
        here = pl.ds(step * tile, tile)
        copy = pltpu.make_async_copy(out_ref.at[here, :], out_hbm.at[here, :], sems.at[step])
        copy.start()
        copies.append(copy)

    forward(0)
    for step in range(steps):
        if step + 1 < steps:
            forward(step + 1)
        middle(step)
        if step > 0:
            backward(step - 1)
        store(step)
    backward(steps - 1)
    grad = dot(x_t_ref[...], grad_pre_ref[...])
    sums = grad[half:].astype(BF16)
    for at in range(0, width, half):
        turned_ref[at : at + half, :] = grad[:half, at : at + half].T
    for ref, order in zip(grad_refs, parts):
        ref[:shapes, :] = sums[:, :half]
        ref[shapes : 2 * shapes, :] = sums[:, half:]
        if orders is None:
            ref[2 * shapes :, :] = turned_ref[...].astype(BF16)
            continue
        rows = (ref.shape[0] - 2 * shapes) // len(order)
        for k, mask in enumerate(order):
            at = pl.multiple_of((me ^ mask) * rows, rows)
            to = 2 * shapes + k * rows
            ref[to : to + rows, :] = turned_ref[pl.ds(at, rows), :].astype(BF16)

    for copy in copies:
        copy.wait()


def store_kernel(source_ref, target_ref, sem):
    copy = pltpu.make_async_copy(source_ref, target_ref, sem)
    copy.start()
    copy.wait()


def sum_of(refs):
    terms = [ref[...].astype(F32) for ref in refs]
    while len(terms) > 1:
        terms = [a + b for a, b in zip(terms[::2], terms[1::2])]
    return terms[0]


def add_kernel(shapes, n, *refs):
    total = sum_of(refs[:n]).astype(BF16)
    for k, ref in enumerate(refs[n:]):
        rows = ref.shape[0] - 2 * shapes
        at = 2 * shapes + k * rows
        ref[: 2 * shapes, :] = total[: 2 * shapes]
        ref[2 * shapes :, :] = total[at : at + rows]


def last_kernel(hid, shapes, orders, n, *refs):
    direction_ref, gain_ref, codes_ref = refs[n : n + 3]
    pieces = refs[n + 3 : -5]
    grad_codes_ref, grad_direction_ref, grad_gain_ref, grad_bias_ref, code_scratch = refs[-5:]
    d = direction_ref[...]
    rows, cols = d.shape
    half = cols // 2
    me = lax.axis_index(AXES)
    place(pieces, orders, me, code_scratch)
    total = sum_of(refs[:n])
    sums = jnp.concatenate([total[:shapes], total[shapes : 2 * shapes]], axis=1)
    sums = jnp.concatenate(split(sums), axis=0).astype(BF16)
    terms = dot(sums, code_scratch[...])
    grad_codes_ref[...] = terms[:shapes] + terms[shapes:]
    width = sums.shape[1]
    mine = lax.broadcasted_iota(jnp.int32, (rows, width), 0) + me * rows
    mine = jnp.where(mine == lax.broadcasted_iota(jnp.int32, (rows, width), 1), 1.0, 0.0).astype(BF16)
    own = dot(mine, sums, NT)
    grad_bias_ref[...] = to_row(jnp.sum(own, axis=1, keepdims=True))
    code = dot(own.astype(BF16), stacked_codes(codes_ref, 2 * shapes))
    packed = jnp.concatenate([total[2 * shapes :], code], axis=1)
    lane = lax.broadcasted_iota(jnp.int32, (rows, cols), 1)
    grad_weight = jnp.where(
        lane < hid,
        packed,
        jnp.where(lane < hid + half, pltpu.roll(packed, cols - (half - hid), 1), pltpu.roll(packed, half, 1)),
    )
    inverse = lax.rsqrt(jnp.sum(d * d, axis=1, keepdims=True))
    unit = d * inverse
    grad_gain = jnp.sum(grad_weight * unit, axis=1, keepdims=True)
    grad_gain_ref[...] = to_row(grad_gain)
    grad_direction_ref[...] = (to_column(gain_ref[...]) * inverse) * (grad_weight - grad_gain * unit)


def masks_of(group):
    masks = [0]
    for bit in group:
        masks = masks + [m ^ bit for m in masks]
    return masks


def order_of(groups):
    order = [0]
    for group in groups:
        order = [m ^ r for m in masks_of(group) for r in order]
    return order


def swaps(arrays, masks, devices):
    moved = [
        lax.ppermute(x, AXES, [(i, i ^ mask) for i in range(devices)])
        for x, mask in list(zip(arrays, masks))[::-1]
    ]
    return moved[::-1]


def per_device(
    hidden,
    codes,
    offsets,
    shape_ids,
    scale_index,
    direction,
    gain,
    bias,
    cotangent,
    running_mean,
    running_var,
):
    points, hid = hidden.shape
    shapes = codes.shape[0]
    rows, cols = direction.shape
    width = cotangent.shape[1]
    half = cols // 2
    devices = lax.axis_size("dp") * lax.axis_size("inner")
    tuned = rows % 16 == 0
    bits = [1 << k | 1 for k in range(devices.bit_length() - 1)]
    groups = [bits[k - 2 : k] for k in range(len(bits), 1, -2)]
    groups = groups + [bits[:1]] * (len(bits) % 2)
    tuned = rows % 16 == 0
    extra_lanes = -(-(2 * shapes + 16) // LANES) * LANES
    lanes = half + extra_lanes
    gain_row = gain.reshape(1, rows)

    def shape_of(rows, lanes, dtype):
        return jax.ShapeDtypeStruct((rows, lanes), dtype)

    held = small_kernel(
        "prep",
        functools.partial(prep_kernel, hid),
        shape_of(rows, lanes + half, BF16),
        *[
            pltpu.with_memory_space_constraint(x, pltpu.HBM)
            for x in (direction, gain_row, bias.reshape(1, rows), codes)
        ],
        scratch=[
            VMEM((rows, cols), F32),
            VMEM((1, rows), F32),
            VMEM((1, rows), F32),
            VMEM((shapes, half), F32),
            pltpu.SemaphoreType.DMA((4,)),
        ],
        space=pl.ANY,
    )
    tile, layer_tile = min(512, points), min(256, points)
    x, x_t = pl.pallas_call(
        functools.partial(inputs_kernel, hid, tile),
        out_shape=[
            shape_of(points, lanes, BF16),
            shape_of(half + shapes, points, BF16),
        ],
        in_specs=[pl.BlockSpec(memory_space=pl.ANY)] * 4,
        out_specs=vmem(2),
        scratch_shapes=[
            VMEM((points, hid), F32),
            VMEM((half - hid, points), F32),
            VMEM((1, points), jnp.int32),
            VMEM((1, points), jnp.int32),
            pltpu.SemaphoreType.DMA((points // tile + 3,)),
        ],
        compiler_params=pltpu.CompilerParams(vmem_limit_bytes=12 * MIB),
        cost_estimate=pl.CostEstimate(
            flops=4000 * MIB, bytes_accessed=8 * points * half, transcendentals=0
        ),
        name="inputs",
    )(
        *[
            pltpu.with_memory_space_constraint(a, pltpu.HBM)
            for a in (
                hidden,
                offsets.T,
                shape_ids.reshape(1, points),
                scale_index.reshape(1, points),
            )
        ]
    )
    def gather(array, group):
        masks = masks_of(group)[1:]
        return [array] + swaps([array] * len(masks), masks, devices)

    def join(arrays, *widths, early=()):
        height = sum(a.shape[0] for a in arrays)
        return small_kernel(
            "join",
            functools.partial(join_kernel, len(arrays), len(early)),
            [shape_of(height, width, BF16) for width in widths],
            *arrays[::-1],
            *early,
        )

    if tuned:
        weight, code_weight = join(gather(held, groups[0]), lanes, half)
        weight, code_weight, x, x_t = lax.optimization_barrier((weight, code_weight, x, x_t))
        steps = [[bit] for group in groups[1:-1] for bit in group[::-1]]
        code_order = order_of(groups[:1] + steps)
        for group in groups[1:-1]:
            weights, code_weights = gather(weight, group), gather(code_weight, steps[0])
            (weight,) = join(weights, lanes, early=(cotangent,))
            (code_weight,) = join(code_weights, half)
        weights = gather(weight, groups[-1])
        code_weights = gather(code_weight, steps[1])
        orders = [[m ^ r for r in order_of(groups[:-1])] for m in masks_of(groups[-1])]
        code_orders = [[m ^ r for r in code_order] for m in masks_of(groups[-1])]
        parts = orders
    else:
        held = lax.all_gather(held, AXES, axis=0, tiled=True)
        weights, code_weights, orders, code_orders, parts = [held[:, :lanes]], [held[:, lanes:]], None, None, [[0]]

    output, grad_hidden, *grads = pl.pallas_call(
        functools.partial(layer_kernel, hid, shapes, layer_tile, orders, parts),
        out_shape=[pltpu.HBM((points, width), F32), pltpu.VMEM((points, hid), F32)]
        + [shape_of(2 * shapes + width // len(parts), half, BF16)] * len(parts),
        in_specs=vmem(len(weights) + 3),
        out_specs=[pl.BlockSpec(memory_space=pltpu.HBM)] + vmem(1 + len(parts)),
        scratch_shapes=[
            VMEM((width, lanes), BF16),
            VMEM((width, half), F32),
            VMEM((points, width), F32),
            VMEM((points, width), BF16),
            VMEM((2, layer_tile, width), F32),
            pltpu.SemaphoreType.DMA((points // layer_tile,)),
        ],
        compiler_params=pltpu.CompilerParams(vmem_limit_bytes=20 * MIB),
        cost_estimate=pl.CostEstimate(
            flops=6 * points * width * cols,
            bytes_accessed=8 * points * (width + half),
            transcendentals=points * width,
        ),
        name="layer",
    )(*weights, x, x_t, cotangent)

    grad_hidden = pl.pallas_call(
        store_kernel,
        out_shape=pltpu.HBM((points, hid), F32),
        in_specs=vmem(1),
        out_specs=pl.BlockSpec(memory_space=pltpu.HBM),
        scratch_shapes=[pltpu.SemaphoreType.DMA(())],
        compiler_params=pltpu.CompilerParams(vmem_limit_bytes=8 * MIB),
        cost_estimate=pl.CostEstimate(
            flops=4000 * MIB, bytes_accessed=8 * points * hid, transcendentals=0
        ),
        name="store",
    )(grad_hidden)

    if tuned:
        *grads, code_weight = lax.optimization_barrier((*grads, code_weights[1]))
        (code_weight,) = join([code_weights[0], code_weight], half)
        code_weights = gather(code_weight, groups[-1])
        for r, group in enumerate(groups[::-1]):
            masks = masks_of(group)
            grads = [grads[0]] + swaps(grads[1:], masks[1:], devices)
            if r == len(groups) - 1:
                break
            n_out = len(masks_of(groups[-2 - r]))
            left = (grads[0].shape[0] - 2 * shapes) // n_out
            grads = small_kernel(
                "add",
                functools.partial(add_kernel, shapes, len(grads)),
                [shape_of(2 * shapes + left, half, BF16)] * n_out,
                *grads[::-1],
            )
            if r == len(groups) - 2:
                *grads, grad_hidden = lax.optimization_barrier((*grads, grad_hidden))
    else:
        sums = lax.psum(grads[0][: 2 * shapes].astype(F32), AXES)
        high = sums.astype(BF16)
        own = lax.psum_scatter(grads[0][2 * shapes :].astype(F32), AXES, scatter_dimension=0, tiled=True)
        low = jnp.zeros((2 * shapes + rows, half), BF16).at[: 2 * shapes].set((sums - high).astype(BF16))
        grads = [jnp.concatenate([high, own.astype(BF16)], axis=0), low]
    grad_codes, grad_direction, grad_gain, grad_bias = small_kernel(
        "last",
        functools.partial(last_kernel, hid, shapes, code_orders, len(grads)),
        [
            shape_of(shapes, half, F32),
            shape_of(rows, cols, F32),
            shape_of(1, rows, F32),
            shape_of(1, rows, F32),
        ],
        *grads[::-1],
        direction,
        gain_row,
        codes,
        *code_weights,
        scratch=[VMEM((width, half), BF16)],
    )

    total = float(points * devices)
    batch_mean = jnp.mean(codes, axis=0)
    batch_square = jnp.mean(codes * codes, axis=0)
    batch_var = (batch_square - batch_mean * batch_mean) * (total / (total - 1.0))
    new_mean = 0.9 * running_mean + 0.1 * batch_mean
    new_var = 0.9 * running_var + 0.1 * batch_var
    return (
        output,
        grad_hidden,
        grad_codes,
        grad_direction,
        grad_gain.reshape(rows),
        grad_bias.reshape(rows),
        new_mean,
        new_var,
    )


def solution(mesh):
    return jax.shard_map(
        per_device,
        mesh=mesh,
        in_specs=(
            P(("dp", "inner"), None),
            P(),
            P(("dp", "inner"), None),
            P(("dp", "inner")),
            P(("dp", "inner")),
            P(("dp", "inner"), None),
            P(("dp", "inner")),
            P(("dp", "inner")),
            P(("dp", "inner"), None),
            P(),
            P(),
        ),
        out_specs=(
            P(("dp", "inner"), None),
            P(("dp", "inner"), None),
            P(),
            P(("dp", "inner"), None),
            P(("dp", "inner")),
            P(("dp", "inner")),
            P(),
            P(),
        ),
        check_vma=False,
    )
```

```python
import functools

import jax
import jax.numpy as jnp
from jax import lax
from jax.experimental import pallas as pl
from jax.experimental.pallas import tpu as pltpu
from jax.sharding import PartitionSpec as P

AXES = ("dp", "inner")
LANES = 128
MIB = 1024 * 1024
F32 = jnp.float32
BF16 = jnp.bfloat16
VMEM = pltpu.VMEM
NT = (((1,), (1,)), ((), ()))


def dot(a, b, dims=(((1,), (0,)), ((), ()))):
    return lax.dot_general(a, b, dims, preferred_element_type=F32)


def vmem(n):
    return [pl.BlockSpec(memory_space=VMEM)] * n


def small_kernel(name, body, out_shape, *args, scratch=(), space=VMEM, limit=8):
    many = isinstance(out_shape, list)
    return pl.pallas_call(
        body,
        out_shape=out_shape,
        in_specs=[pl.BlockSpec(memory_space=space)] * len(args),
        out_specs=vmem(len(out_shape)) if many else vmem(1)[0],
        scratch_shapes=list(scratch),
        compiler_params=pltpu.CompilerParams(vmem_limit_bytes=limit * MIB),
        cost_estimate=pl.CostEstimate(
            flops=4000 * MIB, bytes_accessed=8 * MIB, transcendentals=4 * MIB
        ),
        name=name,
    )(*args)


def diagonal(n):
    return lax.broadcasted_iota(jnp.int32, (n, n), 0) == lax.broadcasted_iota(jnp.int32, (n, n), 1)


def to_column(row):
    n = row.shape[1]
    return jnp.sum(jnp.where(diagonal(n), row, 0.0), axis=1, keepdims=True)


def to_row(column):
    n = column.shape[0]
    return jnp.sum(jnp.where(diagonal(n), column, 0.0), axis=0, keepdims=True)


def stacked_codes(codes_ref, count):
    codes = codes_ref[...].astype(BF16)
    parts = [codes, codes]
    if count > 2 * codes.shape[0]:
        parts.append(jnp.zeros((count - 2 * codes.shape[0], codes.shape[1]), BF16))
    return jnp.concatenate(parts, axis=0)


def split(x):
    high = x.astype(BF16).astype(F32)
    return high, x - high


def prep_kernel(hid, *refs):
    piece_ref, direction_ref, gain_ref, bias_ref, codes_ref, sems = refs[4:]
    copies = [
        pltpu.make_async_copy(source, target, sems.at[k])
        for k, (source, target) in enumerate(zip(refs[:4], refs[5:9]))
    ]
    for copy in copies:
        copy.start()
    for copy in copies:
        copy.wait()
    d = direction_ref[...]
    shapes = codes_ref.shape[0]
    rows, cols = d.shape
    half = cols // 2
    extra_lanes = piece_ref.shape[1] - cols
    inverse = lax.rsqrt(jnp.sum(d * d, axis=1, keepdims=True))
    w = to_column(gain_ref[...]) * (d * inverse)
    lane = lax.broadcasted_iota(jnp.int32, (rows, half), 1)
    first = jnp.where(lane < hid, w[:, :half], w[:, half:])
    code = pltpu.roll(w, half - hid, 1)[:, half:].astype(BF16)
    bias = to_column(bias_ref[...]).astype(BF16).astype(F32)
    high, low = split(dot(code, stacked_codes(codes_ref, extra_lanes), NT) + bias)
    own = first[:, half - LANES :]
    if extra_lanes > LANES:
        own = jnp.concatenate([jnp.zeros((rows, extra_lanes - LANES), F32), own], axis=1)
    lane = lax.broadcasted_iota(jnp.int32, (rows, extra_lanes), 1)
    table = jnp.where(lane < shapes, high, jnp.where(lane < 2 * shapes, low, 0.0))
    table = jnp.where(lane >= extra_lanes - (half - hid), own, table)
    piece_ref[:, :half] = first.astype(BF16)
    piece_ref[:, half : half + extra_lanes] = table.astype(BF16)
    piece_ref[:, half + extra_lanes :] = code


def join_kernel(n, n_early, *refs):
    rows = refs[0].shape[0]
    for k, ref in enumerate(refs[n - 1 :: -1]):
        lane = 0
        for out_ref in refs[n + n_early :]:
            lanes = out_ref.shape[1]
            out_ref[k * rows : (k + 1) * rows, :] = ref[:, lane : lane + lanes]
            lane += lanes


def pack_kernel(shapes, *refs):
    weight_ref, code_ref = refs[-2:]
    count = len(refs) - 2
    rows, half = refs[0].shape[0], code_ref.shape[1]
    products = jnp.zeros((rows, LANES), F32)
    for k, ref in enumerate(refs[count - 1 :: -1]):
        for block in range(half // LANES):
            at = (block * count + k) * rows
            weight_ref[at : at + rows, :] = ref[:, block * LANES : (block + 1) * LANES]
        own = ref[:, half : half + LANES].astype(F32)
        own = jnp.where(lax.broadcasted_iota(jnp.int32, own.shape, 1) < 2 * shapes, own, 0.0)
        products = products + (pltpu.roll(own, 2 * shapes * k, 1) if k else own)
        code_ref[k * rows : (k + 1) * rows, :] = ref[:, half + LANES :]
    weight_ref[half // LANES * count * rows :, :] = products.astype(BF16)


def unpack(hid, shapes, refs, orders, me, w_ref):
    count = LANES // (2 * shapes)
    half = w_ref.shape[1] - LANES
    blocks = half // LANES
    for ref, order in zip(refs, orders):
        height = ref.shape[0] // (len(order) // count)
        rows = height // (blocks * count + 1)
        lane = lax.broadcasted_iota(jnp.int32, (rows, LANES), 1)
        for j, mask in enumerate(order):
            start, k = j // count * height, j % count
            at = pl.ds(pl.multiple_of((me ^ mask) * rows, rows), rows)
            for block in range(blocks):
                here = start + (block * count + k) * rows
                part = ref[here : here + rows, :]
                w_ref[at, block * LANES : (block + 1) * LANES] = part
            here = start + blocks * count * rows
            products = ref[here : here + rows, :].astype(F32)
            if k:
                products = pltpu.roll(products, LANES - 2 * shapes * k, 1)
            products = jnp.where(lane < 2 * shapes, products, 0.0)
            products = jnp.where(lane >= LANES - (half - hid), part.astype(F32), products)
            w_ref[at, half:] = products.astype(BF16)


def place(refs, orders, me, out_ref):
    if orders is None:
        out_ref[...] = refs[0][...]
        return
    rows = refs[0].shape[0] // len(orders[0])
    for ref, order in zip(refs, orders):
        for k, mask in enumerate(order):
            at = pl.multiple_of((me ^ mask) * rows, rows)
            out_ref[pl.ds(at, rows), :] = ref[k * rows : (k + 1) * rows, :]


def inputs_kernel(hid, tile, *refs):
    x_ref, x_t_ref, hidden_ref, offsets_ref, ids_ref, scale_ref, sems = refs[4:]
    points = x_ref.shape[0]
    half = (hid + LANES - 1) // LANES * LANES
    shapes = x_t_ref.shape[0] - half
    extra_lanes = x_ref.shape[1] - half
    steps = points // tile
    small = [
        pltpu.make_async_copy(source, target, sems.at[steps + k])
        for k, (source, target) in enumerate(zip(refs[1:4], (offsets_ref, ids_ref, scale_ref)))
    ]
    large = [
        pltpu.make_async_copy(
            refs[0].at[pl.ds(k * tile, tile), :], hidden_ref.at[pl.ds(k * tile, tile), :], sems.at[k]
        )
        for k in range(steps)
    ]
    for copy in small + large:
        copy.start()
    for copy in small:
        copy.wait()
    for step, copy in enumerate(large):
        here = slice(step * tile, (step + 1) * tile)
        scale = scale_ref[:, here]
        jitter = jnp.where(scale == 0, 1.0, jnp.where(scale == 1, 0.5, 0.25))
        xyz = offsets_ref[:, here] * jitter
        row = lax.broadcasted_iota(jnp.int32, (16, tile), 0)
        last = jnp.zeros((16, tile), F32)
        for k in range(half - hid):
            last = jnp.where(row == 16 - (half - hid) + k, xyz[k : k + 1], last)
        last = last.astype(BF16)
        row = lax.broadcasted_iota(jnp.int32, (extra_lanes - 16, tile), 0)
        ids = ids_ref[:, here]
        member = jnp.where((row == ids) | (row == ids + shapes), 1.0, 0.0).astype(BF16)
        x_ref[here, half:] = jnp.concatenate([member, last], axis=0).T
        x_t_ref[half:, here] = member[:shapes]
        copy.wait()
        x_ref[here, half - LANES : half] = jnp.zeros((tile, LANES), BF16)
        x_ref[here, :hid] = hidden_ref[here, :].astype(BF16)
        hidden = x_ref[here, :half].T
        x_t_ref[: half - 16, here] = hidden[: half - 16]
        x_t_ref[half - 16 : half, here] = hidden[half - 16 :] + last


def layer_kernel(hid, shapes, tile, orders, parts, *refs):
    n = 1 if orders is None else len(orders)
    pieces = refs[:n]
    x_ref, x_t_ref, cot_ref, out_hbm, grad_hidden_ref = refs[n : n + 5]
    grad_refs = refs[n + 5 : -6]
    w_ref, turned_ref, out_ref, grad_pre_ref, pre_ref, sems = refs[-6:]
    points, width = cot_ref.shape
    half = width // 2
    steps = points // tile
    me = lax.axis_index(AXES)
    if orders is None:
        place(pieces, orders, me, w_ref)
    else:
        unpack(hid, shapes, pieces, orders, me, w_ref)
    copies = []

    def rows_of(step):
        return slice(step * tile, (step + 1) * tile)

    def forward(step):
        pre_ref[step % 2] = dot(x_ref[rows_of(step), :], w_ref[...], NT)

    def middle(step):
        here = rows_of(step)
        pre = pre_ref[step % 2]
        sigma = 0.5 * jnp.tanh(0.5 * pre) + 0.5
        out = pre * sigma
        out_ref[here, :] = out
        grad_pre_ref[here, :] = (cot_ref[here, :] * (sigma * (1.0 + (pre - out)))).astype(BF16)

    def backward(step):
        here = rows_of(step)
        grad_hidden_ref[here, :] = dot(grad_pre_ref[here, :], w_ref[:, :half])[:, :hid]

    def store(step):
        here = pl.ds(step * tile, tile)
        copy = pltpu.make_async_copy(out_ref.at[here, :], out_hbm.at[here, :], sems.at[step])
        copy.start()
        copies.append(copy)

    forward(0)
    for step in range(steps):
        if step + 1 < steps:
            forward(step + 1)
        middle(step)
        if step > 0:
            backward(step - 1)
        store(step)
    backward(steps - 1)
    grad = dot(x_t_ref[...], grad_pre_ref[...])
    sums = grad[half:].astype(BF16)
    for at in range(0, width, half):
        turned_ref[at : at + half, :] = grad[:half, at : at + half].T
    for ref, order in zip(grad_refs, parts):
        ref[:shapes, :] = sums[:, :half]
        ref[shapes : 2 * shapes, :] = sums[:, half:]
        if orders is None:
            ref[2 * shapes :, :] = turned_ref[...].astype(BF16)
            continue
        rows = (ref.shape[0] - 2 * shapes) // len(order)
        for k, mask in enumerate(order):
            at = pl.multiple_of((me ^ mask) * rows, rows)
            to = 2 * shapes + k * rows
            ref[to : to + rows, :] = turned_ref[pl.ds(at, rows), :].astype(BF16)

    for copy in copies:
        copy.wait()


def store_kernel(source_ref, target_ref, sem):
    copy = pltpu.make_async_copy(source_ref, target_ref, sem)
    copy.start()
    copy.wait()


def sum_of(refs):
    terms = [ref[...].astype(F32) for ref in refs]
    while len(terms) > 1:
        terms = [a + b for a, b in zip(terms[::2], terms[1::2])]
    return terms[0]


def add_kernel(shapes, n, *refs):
    total = sum_of(refs[:n]).astype(BF16)
    for k, ref in enumerate(refs[n:]):
        rows = ref.shape[0] - 2 * shapes
        at = 2 * shapes + k * rows
        ref[: 2 * shapes, :] = total[: 2 * shapes]
        ref[2 * shapes :, :] = total[at : at + rows]


def last_kernel(hid, shapes, orders, n, *refs):
    direction_ref, gain_ref, codes_ref = refs[n : n + 3]
    pieces = refs[n + 3 : -5]
    grad_codes_ref, grad_direction_ref, grad_gain_ref, grad_bias_ref, code_scratch = refs[-5:]
    d = direction_ref[...]
    rows, cols = d.shape
    half = cols // 2
    me = lax.axis_index(AXES)
    place(pieces, orders, me, code_scratch)
    total = sum_of(refs[:n])
    sums = jnp.concatenate([total[:shapes], total[shapes : 2 * shapes]], axis=1)
    sums = jnp.concatenate(split(sums), axis=0).astype(BF16)
    terms = dot(sums, code_scratch[...])
    grad_codes_ref[...] = terms[:shapes] + terms[shapes:]
    width = sums.shape[1]
    mine = lax.broadcasted_iota(jnp.int32, (rows, width), 0) + me * rows
    mine = jnp.where(mine == lax.broadcasted_iota(jnp.int32, (rows, width), 1), 1.0, 0.0).astype(BF16)
    own = dot(mine, sums, NT)
    grad_bias_ref[...] = to_row(jnp.sum(own, axis=1, keepdims=True))
    code = dot(own.astype(BF16), stacked_codes(codes_ref, 2 * shapes))
    packed = jnp.concatenate([total[2 * shapes :], code], axis=1)
    lane = lax.broadcasted_iota(jnp.int32, (rows, cols), 1)
    grad_weight = jnp.where(
        lane < hid,
        packed,
        jnp.where(lane < hid + half, pltpu.roll(packed, cols - (half - hid), 1), pltpu.roll(packed, half, 1)),
    )
    inverse = lax.rsqrt(jnp.sum(d * d, axis=1, keepdims=True))
    unit = d * inverse
    grad_gain = jnp.sum(grad_weight * unit, axis=1, keepdims=True)
    grad_gain_ref[...] = to_row(grad_gain)
    grad_direction_ref[...] = (to_column(gain_ref[...]) * inverse) * (grad_weight - grad_gain * unit)


def masks_of(group):
    masks = [0]
    for bit in group:
        masks = masks + [m ^ bit for m in masks]
    return masks


def order_of(groups):
    order = [0]
    for group in groups:
        order = [m ^ r for m in masks_of(group) for r in order]
    return order


def swaps(arrays, masks, devices):
    moved = [
        lax.ppermute(x, AXES, [(i, i ^ mask) for i in range(devices)])
        for x, mask in list(zip(arrays, masks))[::-1]
    ]
    return moved[::-1]


def per_device(
    hidden,
    codes,
    offsets,
    shape_ids,
    scale_index,
    direction,
    gain,
    bias,
    cotangent,
    running_mean,
    running_var,
):
    points, hid = hidden.shape
    shapes = codes.shape[0]
    rows, cols = direction.shape
    width = cotangent.shape[1]
    half = cols // 2
    devices = lax.axis_size("dp") * lax.axis_size("inner")
    bits = [1 << k | 1 for k in range(devices.bit_length() - 1)]
    groups = [bits[k - 2 : k] for k in range(len(bits), 1, -2)]
    groups = groups + [bits[:1]] * (len(bits) % 2)
    extra_lanes = -(-(2 * shapes + 16) // LANES) * LANES
    tuned = rows % 16 == 0 and 2 * shapes * len(masks_of(groups[0])) == LANES
    lanes = half + extra_lanes
    gain_row = gain.reshape(1, rows)

    def shape_of(rows, lanes, dtype):
        return jax.ShapeDtypeStruct((rows, lanes), dtype)

    held = small_kernel(
        "prep",
        functools.partial(prep_kernel, hid),
        shape_of(rows, lanes + half, BF16),
        *[
            pltpu.with_memory_space_constraint(x, pltpu.HBM)
            for x in (direction, gain_row, bias.reshape(1, rows), codes)
        ],
        scratch=[
            VMEM((rows, cols), F32),
            VMEM((1, rows), F32),
            VMEM((1, rows), F32),
            VMEM((shapes, half), F32),
            pltpu.SemaphoreType.DMA((4,)),
        ],
        space=pl.ANY,
    )
    tile, layer_tile = min(512, points), min(256, points)
    x, x_t = pl.pallas_call(
        functools.partial(inputs_kernel, hid, tile),
        out_shape=[
            shape_of(points, lanes, BF16),
            shape_of(half + shapes, points, BF16),
        ],
        in_specs=[pl.BlockSpec(memory_space=pl.ANY)] * 4,
        out_specs=vmem(2),
        scratch_shapes=[
            VMEM((points, hid), F32),
            VMEM((half - hid, points), F32),
            VMEM((1, points), jnp.int32),
            VMEM((1, points), jnp.int32),
            pltpu.SemaphoreType.DMA((points // tile + 3,)),
        ],
        compiler_params=pltpu.CompilerParams(vmem_limit_bytes=12 * MIB),
        cost_estimate=pl.CostEstimate(
            flops=4000 * MIB, bytes_accessed=8 * points * half, transcendentals=0
        ),
        name="inputs",
    )(
        *[
            pltpu.with_memory_space_constraint(a, pltpu.HBM)
            for a in (
                hidden,
                offsets.T,
                shape_ids.reshape(1, points),
                scale_index.reshape(1, points),
            )
        ]
    )
    def gather(array, group):
        masks = masks_of(group)[1:]
        return [array] + swaps([array] * len(masks), masks, devices)

    def join(arrays, *widths, early=()):
        height = sum(a.shape[0] for a in arrays)
        return small_kernel(
            "join",
            functools.partial(join_kernel, len(arrays), len(early)),
            [shape_of(height, width, BF16) for width in widths],
            *arrays[::-1],
            *early,
        )

    if tuned:
        arrays = gather(held, groups[0])
        weight, code_weight = small_kernel(
            "pack",
            functools.partial(pack_kernel, shapes),
            [
                shape_of((half // LANES * len(arrays) + 1) * rows, LANES, BF16),
                shape_of(len(arrays) * rows, half, BF16),
            ],
            *arrays[::-1],
        )
        weight, code_weight, x, x_t = lax.optimization_barrier((weight, code_weight, x, x_t))
        steps = [[bit] for group in groups[1:-1] for bit in group[::-1]]
        code_order = order_of(groups[:1] + steps)
        for group in groups[1:-1]:
            weights, code_weights = gather(weight, group), gather(code_weight, steps[0])
            (weight,) = join(weights, LANES, early=(cotangent,))
            (code_weight,) = join(code_weights, half)
        weights = gather(weight, groups[-1])
        code_weights = gather(code_weight, steps[1])
        orders = [[m ^ r for r in order_of(groups[:-1])] for m in masks_of(groups[-1])]
        code_orders = [[m ^ r for r in code_order] for m in masks_of(groups[-1])]
        parts = orders
    else:
        held = lax.all_gather(held, AXES, axis=0, tiled=True)
        weights, code_weights, orders, code_orders, parts = [held[:, :lanes]], [held[:, lanes:]], None, None, [[0]]

    output, grad_hidden, *grads = pl.pallas_call(
        functools.partial(layer_kernel, hid, shapes, layer_tile, orders, parts),
        out_shape=[pltpu.HBM((points, width), F32), pltpu.VMEM((points, hid), F32)]
        + [shape_of(2 * shapes + width // len(parts), half, BF16)] * len(parts),
        in_specs=vmem(len(weights) + 3),
        out_specs=[pl.BlockSpec(memory_space=pltpu.HBM)] + vmem(1 + len(parts)),
        scratch_shapes=[
            VMEM((width, lanes), BF16),
            VMEM((width, half), F32),
            VMEM((points, width), F32),
            VMEM((points, width), BF16),
            VMEM((2, layer_tile, width), F32),
            pltpu.SemaphoreType.DMA((points // layer_tile,)),
        ],
        compiler_params=pltpu.CompilerParams(vmem_limit_bytes=20 * MIB),
        cost_estimate=pl.CostEstimate(
            flops=6 * points * width * cols,
            bytes_accessed=8 * points * (width + half),
            transcendentals=points * width,
        ),
        name="layer",
    )(*weights, x, x_t, cotangent)

    grad_hidden = pl.pallas_call(
        store_kernel,
        out_shape=pltpu.HBM((points, hid), F32),
        in_specs=vmem(1),
        out_specs=pl.BlockSpec(memory_space=pltpu.HBM),
        scratch_shapes=[pltpu.SemaphoreType.DMA(())],
        compiler_params=pltpu.CompilerParams(vmem_limit_bytes=8 * MIB),
        cost_estimate=pl.CostEstimate(
            flops=4000 * MIB, bytes_accessed=8 * points * hid, transcendentals=0
        ),
        name="store",
    )(grad_hidden)

    if tuned:
        *grads, code_weight = lax.optimization_barrier((*grads, code_weights[1]))
        (code_weight,) = join([code_weights[0], code_weight], half)
        code_weights = gather(code_weight, groups[-1])
        for r, group in enumerate(groups[::-1]):
            masks = masks_of(group)
            grads = [grads[0]] + swaps(grads[1:], masks[1:], devices)
            if r == len(groups) - 1:
                break
            n_out = len(masks_of(groups[-2 - r]))
            left = (grads[0].shape[0] - 2 * shapes) // n_out
            grads = small_kernel(
                "add",
                functools.partial(add_kernel, shapes, len(grads)),
                [shape_of(2 * shapes + left, half, BF16)] * n_out,
                *grads[::-1],
            )
            if r == len(groups) - 2:
                *grads, grad_hidden = lax.optimization_barrier((*grads, grad_hidden))
    else:
        sums = lax.psum(grads[0][: 2 * shapes].astype(F32), AXES)
        high = sums.astype(BF16)
        own = lax.psum_scatter(grads[0][2 * shapes :].astype(F32), AXES, scatter_dimension=0, tiled=True)
        low = jnp.zeros((2 * shapes + rows, half), BF16).at[: 2 * shapes].set((sums - high).astype(BF16))
        grads = [jnp.concatenate([high, own.astype(BF16)], axis=0), low]
    grad_codes, grad_direction, grad_gain, grad_bias = small_kernel(
        "last",
        functools.partial(last_kernel, hid, shapes, code_orders, len(grads)),
        [
            shape_of(shapes, half, F32),
            shape_of(rows, cols, F32),
            shape_of(1, rows, F32),
            shape_of(1, rows, F32),
        ],
        *grads[::-1],
        direction,
        gain_row,
        codes,
        *code_weights,
        scratch=[VMEM((width, half), BF16)],
    )

    total = float(points * devices)
    batch_mean = jnp.mean(codes, axis=0)
    batch_square = jnp.mean(codes * codes, axis=0)
    batch_var = (batch_square - batch_mean * batch_mean) * (total / (total - 1.0))
    new_mean = 0.9 * running_mean + 0.1 * batch_mean
    new_var = 0.9 * running_var + 0.1 * batch_var
    return (
        output,
        grad_hidden,
        grad_codes,
        grad_direction,
        grad_gain.reshape(rows),
        grad_bias.reshape(rows),
        new_mean,
        new_var,
    )


def solution(mesh):
    return jax.shard_map(
        per_device,
        mesh=mesh,
        in_specs=(
            P(("dp", "inner"), None),
            P(),
            P(("dp", "inner"), None),
            P(("dp", "inner")),
            P(("dp", "inner")),
            P(("dp", "inner"), None),
            P(("dp", "inner")),
            P(("dp", "inner")),
            P(("dp", "inner"), None),
            P(),
            P(),
        ),
        out_specs=(
            P(("dp", "inner"), None),
            P(("dp", "inner"), None),
            P(),
            P(("dp", "inner"), None),
            P(("dp", "inner")),
            P(("dp", "inner")),
            P(),
            P(),
        ),
        check_vma=False,
    )
```

```python
import functools

import jax
import jax.numpy as jnp
from jax import lax
from jax.experimental import pallas as pl
from jax.experimental.pallas import tpu as pltpu
from jax.sharding import PartitionSpec as P

AXES = ("dp", "inner")
LANES = 128
MIB = 1024 * 1024
FIRST = (2, 3, 1, 0)
F32 = jnp.float32
BF16 = jnp.bfloat16
VMEM = pltpu.VMEM
NT = (((1,), (1,)), ((), ()))


def dot(a, b, dims=(((1,), (0,)), ((), ()))):
    return lax.dot_general(a, b, dims, preferred_element_type=F32)


def vmem(n):
    return [pl.BlockSpec(memory_space=VMEM)] * n


def small_kernel(name, body, out_shape, *args, scratch=(), space=VMEM, limit=8):
    many = isinstance(out_shape, list)
    return pl.pallas_call(
        body,
        out_shape=out_shape,
        in_specs=[pl.BlockSpec(memory_space=space)] * len(args),
        out_specs=vmem(len(out_shape)) if many else vmem(1)[0],
        scratch_shapes=list(scratch),
        compiler_params=pltpu.CompilerParams(vmem_limit_bytes=limit * MIB),
        cost_estimate=pl.CostEstimate(
            flops=4000 * MIB, bytes_accessed=8 * MIB, transcendentals=4 * MIB
        ),
        name=name,
    )(*args)


def diagonal(n):
    return lax.broadcasted_iota(jnp.int32, (n, n), 0) == lax.broadcasted_iota(jnp.int32, (n, n), 1)


def to_column(row):
    n = row.shape[1]
    return jnp.sum(jnp.where(diagonal(n), row, 0.0), axis=1, keepdims=True)


def to_row(column):
    n = column.shape[0]
    return jnp.sum(jnp.where(diagonal(n), column, 0.0), axis=0, keepdims=True)


def stacked_codes(codes_ref, count):
    codes = codes_ref[...].astype(BF16)
    parts = [codes, codes]
    if count > 2 * codes.shape[0]:
        parts.append(jnp.zeros((count - 2 * codes.shape[0], codes.shape[1]), BF16))
    return jnp.concatenate(parts, axis=0)


def split(x):
    high = x.astype(BF16).astype(F32)
    return high, x - high


def prep_kernel(hid, *refs):
    piece_ref, direction_ref, gain_ref, bias_ref, codes_ref, sems = refs[4:]
    copies = [
        pltpu.make_async_copy(source, target, sems.at[k])
        for k, (source, target) in enumerate(zip(refs[:4], refs[5:9]))
    ]
    for copy in copies:
        copy.start()
    for copy in copies:
        copy.wait()
    d = direction_ref[...]
    shapes = codes_ref.shape[0]
    rows, cols = d.shape
    half = cols // 2
    extra_lanes = piece_ref.shape[1] - cols
    inverse = lax.rsqrt(jnp.sum(d * d, axis=1, keepdims=True))
    w = to_column(gain_ref[...]) * (d * inverse)
    lane = lax.broadcasted_iota(jnp.int32, (rows, half), 1)
    first = jnp.where(lane < hid, w[:, :half], w[:, half:])
    code = pltpu.roll(w, half - hid, 1)[:, half:].astype(BF16)
    bias = to_column(bias_ref[...]).astype(BF16).astype(F32)
    high, low = split(dot(code, stacked_codes(codes_ref, extra_lanes), NT) + bias)
    own = first[:, half - LANES :]
    if extra_lanes > LANES:
        own = jnp.concatenate([jnp.zeros((rows, extra_lanes - LANES), F32), own], axis=1)
    lane = lax.broadcasted_iota(jnp.int32, (rows, extra_lanes), 1)
    table = jnp.where(lane < shapes, high, jnp.where(lane < 2 * shapes, low, 0.0))
    table = jnp.where(lane >= extra_lanes - (half - hid), own, table)
    piece_ref[:, :half] = first.astype(BF16)
    piece_ref[:, half : half + extra_lanes] = table.astype(BF16)
    piece_ref[:, half + extra_lanes :] = code


def join_kernel(n, n_early, *refs):
    rows = refs[0].shape[0]
    for k, ref in enumerate(refs[n - 1 :: -1]):
        lane = 0
        for out_ref in refs[n + n_early :]:
            lanes = out_ref.shape[1]
            out_ref[k * rows : (k + 1) * rows, :] = ref[:, lane : lane + lanes]
            lane += lanes


def pack_kernel(shapes, *refs):
    weight_ref, code_ref = refs[-2:]
    count = len(refs) - 2
    rows, half = refs[0].shape[0], code_ref.shape[1]
    products = jnp.zeros((rows, LANES), F32)
    for k, ref in zip(FIRST, refs):
        for block in range(half // LANES):
            at = (block * count + k) * rows
            weight_ref[at : at + rows, :] = ref[:, block * LANES : (block + 1) * LANES]
        own = ref[:, half : half + LANES].astype(F32)
        own = jnp.where(lax.broadcasted_iota(jnp.int32, own.shape, 1) < 2 * shapes, own, 0.0)
        products = products + (pltpu.roll(own, 2 * shapes * k, 1) if k else own)
        code_ref[k * rows : (k + 1) * rows, :] = ref[:, half + LANES :]
    weight_ref[half // LANES * count * rows :, :] = products.astype(BF16)


def unpack(hid, shapes, refs, orders, me, w_ref):
    count = LANES // (2 * shapes)
    half = w_ref.shape[1] - LANES
    blocks = half // LANES
    for ref, order in zip(refs, orders):
        height = ref.shape[0] // (len(order) // count)
        rows = height // (blocks * count + 1)
        lane = lax.broadcasted_iota(jnp.int32, (rows, LANES), 1)
        for j, mask in enumerate(order):
            start, k = j // count * height, j % count
            at = pl.ds(pl.multiple_of((me ^ mask) * rows, rows), rows)
            for block in range(blocks):
                here = start + (block * count + k) * rows
                part = ref[here : here + rows, :]
                w_ref[at, block * LANES : (block + 1) * LANES] = part
            here = start + blocks * count * rows
            products = ref[here : here + rows, :].astype(F32)
            if k:
                products = pltpu.roll(products, LANES - 2 * shapes * k, 1)
            products = jnp.where(lane < 2 * shapes, products, 0.0)
            products = jnp.where(lane >= LANES - (half - hid), part.astype(F32), products)
            w_ref[at, half:] = products.astype(BF16)


def place(refs, orders, me, out_ref):
    if orders is None:
        out_ref[...] = refs[0][...]
        return
    rows = refs[0].shape[0] // len(orders[0])
    for ref, order in zip(refs, orders):
        for k, mask in enumerate(order):
            at = pl.multiple_of((me ^ mask) * rows, rows)
            out_ref[pl.ds(at, rows), :] = ref[k * rows : (k + 1) * rows, :]


def inputs_kernel(hid, tile, *refs):
    x_ref, x_t_ref, hidden_ref, offsets_ref, ids_ref, scale_ref, sems = refs[4:]
    points = x_ref.shape[0]
    half = (hid + LANES - 1) // LANES * LANES
    shapes = x_t_ref.shape[0] - half
    extra_lanes = x_ref.shape[1] - half
    steps = points // tile
    small = [
        pltpu.make_async_copy(source, target, sems.at[steps + k])
        for k, (source, target) in enumerate(zip(refs[1:4], (offsets_ref, ids_ref, scale_ref)))
    ]
    large = [
        pltpu.make_async_copy(
            refs[0].at[pl.ds(k * tile, tile), :], hidden_ref.at[pl.ds(k * tile, tile), :], sems.at[k]
        )
        for k in range(steps)
    ]
    for copy in small + large:
        copy.start()
    for copy in small:
        copy.wait()
    for step, copy in enumerate(large):
        here = slice(step * tile, (step + 1) * tile)
        scale = scale_ref[:, here]
        jitter = jnp.where(scale == 0, 1.0, jnp.where(scale == 1, 0.5, 0.25))
        xyz = offsets_ref[:, here] * jitter
        row = lax.broadcasted_iota(jnp.int32, (16, tile), 0)
        last = jnp.zeros((16, tile), F32)
        for k in range(half - hid):
            last = jnp.where(row == 16 - (half - hid) + k, xyz[k : k + 1], last)
        last = last.astype(BF16)
        row = lax.broadcasted_iota(jnp.int32, (extra_lanes - 16, tile), 0)
        ids = ids_ref[:, here]
        member = jnp.where((row == ids) | (row == ids + shapes), 1.0, 0.0).astype(BF16)
        x_ref[here, half:] = jnp.concatenate([member, last], axis=0).T
        x_t_ref[half:, here] = member[:shapes]
        copy.wait()
        x_ref[here, half - LANES : half] = jnp.zeros((tile, LANES), BF16)
        x_ref[here, :hid] = hidden_ref[here, :].astype(BF16)
        hidden = x_ref[here, :half].T
        x_t_ref[: half - 16, here] = hidden[: half - 16]
        x_t_ref[half - 16 : half, here] = hidden[half - 16 :] + last


def layer_kernel(hid, shapes, tile, orders, parts, *refs):
    n = 1 if orders is None else len(orders)
    pieces = refs[:n]
    x_ref, x_t_ref, cot_ref, out_hbm, grad_hidden_ref = refs[n : n + 5]
    grad_refs = refs[n + 5 : -6]
    w_ref, turned_ref, out_ref, grad_pre_ref, pre_ref, sems = refs[-6:]
    points, width = cot_ref.shape
    half = width // 2
    steps = points // tile
    me = lax.axis_index(AXES)
    if orders is None:
        place(pieces, orders, me, w_ref)
    else:
        unpack(hid, shapes, pieces, orders, me, w_ref)
    copies = []

    def rows_of(step):
        return slice(step * tile, (step + 1) * tile)

    def forward(step):
        pre_ref[step % 2] = dot(x_ref[rows_of(step), :], w_ref[...], NT)

    def middle(step):
        here = rows_of(step)
        pre = pre_ref[step % 2]
        sigma = 0.5 * jnp.tanh(0.5 * pre) + 0.5
        out = pre * sigma
        out_ref[here, :] = out
        grad_pre_ref[here, :] = (cot_ref[here, :] * (sigma * (1.0 + (pre - out)))).astype(BF16)

    def backward(step):
        here = rows_of(step)
        grad_hidden_ref[here, :] = dot(grad_pre_ref[here, :], w_ref[:, :half])[:, :hid]

    def store(step):
        here = pl.ds(step * tile, tile)
        copy = pltpu.make_async_copy(out_ref.at[here, :], out_hbm.at[here, :], sems.at[step])
        copy.start()
        copies.append(copy)

    forward(0)
    for step in range(steps):
        if step + 1 < steps:
            forward(step + 1)
        middle(step)
        if step > 0:
            backward(step - 1)
        store(step)
    backward(steps - 1)
    grad = dot(x_t_ref[...], grad_pre_ref[...])
    sums = grad[half:].astype(BF16)
    for at in range(0, width, half):
        turned_ref[at : at + half, :] = grad[:half, at : at + half].T
    for ref, order in zip(grad_refs, parts):
        ref[:shapes, :] = sums[:, :half]
        ref[shapes : 2 * shapes, :] = sums[:, half:]
        if orders is None:
            ref[2 * shapes :, :] = turned_ref[...].astype(BF16)
            continue
        rows = (ref.shape[0] - 2 * shapes) // len(order)
        for k, mask in enumerate(order):
            at = pl.multiple_of((me ^ mask) * rows, rows)
            to = 2 * shapes + k * rows
            ref[to : to + rows, :] = turned_ref[pl.ds(at, rows), :].astype(BF16)

    for copy in copies:
        copy.wait()


def store_kernel(source_ref, target_ref, sem):
    copy = pltpu.make_async_copy(source_ref, target_ref, sem)
    copy.start()
    copy.wait()


def sum_of(refs):
    terms = [ref[...].astype(F32) for ref in refs]
    while len(terms) > 1:
        terms = [a + b for a, b in zip(terms[::2], terms[1::2])]
    return terms[0]


def add_kernel(shapes, n, *refs):
    total = sum_of(refs[:n]).astype(BF16)
    for k, ref in enumerate(refs[n:]):
        rows = ref.shape[0] - 2 * shapes
        at = 2 * shapes + k * rows
        ref[: 2 * shapes, :] = total[: 2 * shapes]
        ref[2 * shapes :, :] = total[at : at + rows]


def last_kernel(hid, shapes, orders, n, *refs):
    direction_ref, gain_ref, codes_ref = refs[n : n + 3]
    pieces = refs[n + 3 : -5]
    grad_codes_ref, grad_direction_ref, grad_gain_ref, grad_bias_ref, code_scratch = refs[-5:]
    d = direction_ref[...]
    rows, cols = d.shape
    half = cols // 2
    me = lax.axis_index(AXES)
    place(pieces, orders, me, code_scratch)
    total = sum_of(refs[:n])
    sums = jnp.concatenate([total[:shapes], total[shapes : 2 * shapes]], axis=1)
    sums = jnp.concatenate(split(sums), axis=0).astype(BF16)
    terms = dot(sums, code_scratch[...])
    grad_codes_ref[...] = terms[:shapes] + terms[shapes:]
    width = sums.shape[1]
    mine = lax.broadcasted_iota(jnp.int32, (rows, width), 0) + me * rows
    mine = jnp.where(mine == lax.broadcasted_iota(jnp.int32, (rows, width), 1), 1.0, 0.0).astype(BF16)
    own = dot(mine, sums, NT)
    grad_bias_ref[...] = to_row(jnp.sum(own, axis=1, keepdims=True))
    code = dot(own.astype(BF16), stacked_codes(codes_ref, 2 * shapes))
    packed = jnp.concatenate([total[2 * shapes :], code], axis=1)
    lane = lax.broadcasted_iota(jnp.int32, (rows, cols), 1)
    grad_weight = jnp.where(
        lane < hid,
        packed,
        jnp.where(lane < hid + half, pltpu.roll(packed, cols - (half - hid), 1), pltpu.roll(packed, half, 1)),
    )
    inverse = lax.rsqrt(jnp.sum(d * d, axis=1, keepdims=True))
    unit = d * inverse
    grad_gain = jnp.sum(grad_weight * unit, axis=1, keepdims=True)
    grad_gain_ref[...] = to_row(grad_gain)
    grad_direction_ref[...] = (to_column(gain_ref[...]) * inverse) * (grad_weight - grad_gain * unit)


def masks_of(group):
    masks = [0]
    for bit in group:
        masks = masks + [m ^ bit for m in masks]
    return masks


def order_of(groups):
    order = [0]
    for group in groups:
        order = [m ^ r for m in masks_of(group) for r in order]
    return order


def swaps(arrays, masks, devices):
    moved = [
        lax.ppermute(x, AXES, [(i, i ^ mask) for i in range(devices)])
        for x, mask in list(zip(arrays, masks))[::-1]
    ]
    return moved[::-1]


def per_device(
    hidden,
    codes,
    offsets,
    shape_ids,
    scale_index,
    direction,
    gain,
    bias,
    cotangent,
    running_mean,
    running_var,
):
    points, hid = hidden.shape
    shapes = codes.shape[0]
    rows, cols = direction.shape
    width = cotangent.shape[1]
    half = cols // 2
    devices = lax.axis_size("dp") * lax.axis_size("inner")
    bits = [1 << k | 1 for k in range(devices.bit_length() - 1)]
    groups = [bits[k - 2 : k] for k in range(len(bits), 1, -2)]
    groups = groups + [bits[:1]] * (len(bits) % 2)
    extra_lanes = -(-(2 * shapes + 16) // LANES) * LANES
    tuned = rows % 16 == 0 and 2 * shapes * len(masks_of(groups[0])) == LANES
    lanes = half + extra_lanes
    gain_row = gain.reshape(1, rows)

    def shape_of(rows, lanes, dtype):
        return jax.ShapeDtypeStruct((rows, lanes), dtype)

    held = small_kernel(
        "prep",
        functools.partial(prep_kernel, hid),
        shape_of(rows, lanes + half, BF16),
        *[
            pltpu.with_memory_space_constraint(x, pltpu.HBM)
            for x in (direction, gain_row, bias.reshape(1, rows), codes)
        ],
        scratch=[
            VMEM((rows, cols), F32),
            VMEM((1, rows), F32),
            VMEM((1, rows), F32),
            VMEM((shapes, half), F32),
            pltpu.SemaphoreType.DMA((4,)),
        ],
        space=pl.ANY,
    )
    tile, layer_tile = min(512, points), min(256, points)
    x, x_t = pl.pallas_call(
        functools.partial(inputs_kernel, hid, tile),
        out_shape=[
            shape_of(points, lanes, BF16),
            shape_of(half + shapes, points, BF16),
        ],
        in_specs=[pl.BlockSpec(memory_space=pl.ANY)] * 4,
        out_specs=vmem(2),
        scratch_shapes=[
            VMEM((points, hid), F32),
            VMEM((half - hid, points), F32),
            VMEM((1, points), jnp.int32),
            VMEM((1, points), jnp.int32),
            pltpu.SemaphoreType.DMA((points // tile + 3,)),
        ],
        compiler_params=pltpu.CompilerParams(vmem_limit_bytes=12 * MIB),
        cost_estimate=pl.CostEstimate(
            flops=4000 * MIB, bytes_accessed=8 * points * half, transcendentals=0
        ),
        name="inputs",
    )(
        *[
            pltpu.with_memory_space_constraint(a, pltpu.HBM)
            for a in (
                hidden,
                offsets.T,
                shape_ids.reshape(1, points),
                scale_index.reshape(1, points),
            )
        ]
    )
    def gather(array, group):
        masks = masks_of(group)[1:]
        return [array] + swaps([array] * len(masks), masks, devices)

    def join(arrays, *widths, early=()):
        height = sum(a.shape[0] for a in arrays)
        return small_kernel(
            "join",
            functools.partial(join_kernel, len(arrays), len(early)),
            [shape_of(height, width, BF16) for width in widths],
            *arrays[::-1],
            *early,
        )

    if tuned:
        arrays = gather(held, groups[0])
        weight, code_weight = small_kernel(
            "pack",
            functools.partial(pack_kernel, shapes),
            [
                shape_of((half // LANES * len(arrays) + 1) * rows, LANES, BF16),
                shape_of(len(arrays) * rows, half, BF16),
            ],
            *[arrays[k] for k in FIRST],
        )
        weight, code_weight, x, x_t = lax.optimization_barrier((weight, code_weight, x, x_t))
        steps = [[bit] for group in groups[1:-1] for bit in group[::-1]]
        code_order = order_of(groups[:1] + steps)
        for group in groups[1:-1]:
            weights, code_weights = gather(weight, group), gather(code_weight, steps[0])
            (weight,) = join(weights, LANES, early=(cotangent,))
            (code_weight,) = join(code_weights, half)
        weights = gather(weight, groups[-1])
        code_weights = gather(code_weight, steps[1])
        orders = [[m ^ r for r in order_of(groups[:-1])] for m in masks_of(groups[-1])]
        code_orders = [[m ^ r for r in code_order] for m in masks_of(groups[-1])]
        parts = orders
    else:
        held = lax.all_gather(held, AXES, axis=0, tiled=True)
        weights, code_weights, orders, code_orders, parts = [held[:, :lanes]], [held[:, lanes:]], None, None, [[0]]

    output, grad_hidden, *grads = pl.pallas_call(
        functools.partial(layer_kernel, hid, shapes, layer_tile, orders, parts),
        out_shape=[pltpu.HBM((points, width), F32), pltpu.VMEM((points, hid), F32)]
        + [shape_of(2 * shapes + width // len(parts), half, BF16)] * len(parts),
        in_specs=vmem(len(weights) + 3),
        out_specs=[pl.BlockSpec(memory_space=pltpu.HBM)] + vmem(1 + len(parts)),
        scratch_shapes=[
            VMEM((width, lanes), BF16),
            VMEM((width, half), F32),
            VMEM((points, width), F32),
            VMEM((points, width), BF16),
            VMEM((2, layer_tile, width), F32),
            pltpu.SemaphoreType.DMA((points // layer_tile,)),
        ],
        compiler_params=pltpu.CompilerParams(vmem_limit_bytes=20 * MIB),
        cost_estimate=pl.CostEstimate(
            flops=6 * points * width * cols,
            bytes_accessed=8 * points * (width + half),
            transcendentals=points * width,
        ),
        name="layer",
    )(*weights, x, x_t, cotangent)

    grad_hidden = pl.pallas_call(
        store_kernel,
        out_shape=pltpu.HBM((points, hid), F32),
        in_specs=vmem(1),
        out_specs=pl.BlockSpec(memory_space=pltpu.HBM),
        scratch_shapes=[pltpu.SemaphoreType.DMA(())],
        compiler_params=pltpu.CompilerParams(vmem_limit_bytes=8 * MIB),
        cost_estimate=pl.CostEstimate(
            flops=4000 * MIB, bytes_accessed=8 * points * hid, transcendentals=0
        ),
        name="store",
    )(grad_hidden)

    if tuned:
        *grads, code_weight = lax.optimization_barrier((*grads, code_weights[1]))
        (code_weight,) = join([code_weights[0], code_weight], half)
        code_weights = gather(code_weight, groups[-1])
        for r, group in enumerate(groups[::-1]):
            masks = masks_of(group)
            grads = [grads[0]] + swaps(grads[1:], masks[1:], devices)
            if r == len(groups) - 1:
                break
            n_out = len(masks_of(groups[-2 - r]))
            left = (grads[0].shape[0] - 2 * shapes) // n_out
            grads = small_kernel(
                "add",
                functools.partial(add_kernel, shapes, len(grads)),
                [shape_of(2 * shapes + left, half, BF16)] * n_out,
                *grads[::-1],
            )
            if r == len(groups) - 2:
                *grads, grad_hidden = lax.optimization_barrier((*grads, grad_hidden))
    else:
        sums = lax.psum(grads[0][: 2 * shapes].astype(F32), AXES)
        high = sums.astype(BF16)
        own = lax.psum_scatter(grads[0][2 * shapes :].astype(F32), AXES, scatter_dimension=0, tiled=True)
        low = jnp.zeros((2 * shapes + rows, half), BF16).at[: 2 * shapes].set((sums - high).astype(BF16))
        grads = [jnp.concatenate([high, own.astype(BF16)], axis=0), low]
    grad_codes, grad_direction, grad_gain, grad_bias = small_kernel(
        "last",
        functools.partial(last_kernel, hid, shapes, code_orders, len(grads)),
        [
            shape_of(shapes, half, F32),
            shape_of(rows, cols, F32),
            shape_of(1, rows, F32),
            shape_of(1, rows, F32),
        ],
        *grads[::-1],
        direction,
        gain_row,
        codes,
        *code_weights,
        scratch=[VMEM((width, half), BF16)],
    )

    total = float(points * devices)
    batch_mean = jnp.mean(codes, axis=0)
    batch_square = jnp.mean(codes * codes, axis=0)
    batch_var = (batch_square - batch_mean * batch_mean) * (total / (total - 1.0))
    new_mean = 0.9 * running_mean + 0.1 * batch_mean
    new_var = 0.9 * running_var + 0.1 * batch_var
    return (
        output,
        grad_hidden,
        grad_codes,
        grad_direction,
        grad_gain.reshape(rows),
        grad_bias.reshape(rows),
        new_mean,
        new_var,
    )


def solution(mesh):
    return jax.shard_map(
        per_device,
        mesh=mesh,
        in_specs=(
            P(("dp", "inner"), None),
            P(),
            P(("dp", "inner"), None),
            P(("dp", "inner")),
            P(("dp", "inner")),
            P(("dp", "inner"), None),
            P(("dp", "inner")),
            P(("dp", "inner")),
            P(("dp", "inner"), None),
            P(),
            P(),
        ),
        out_specs=(
            P(("dp", "inner"), None),
            P(("dp", "inner"), None),
            P(),
            P(("dp", "inner"), None),
            P(("dp", "inner")),
            P(("dp", "inner")),
            P(),
            P(),
        ),
        check_vma=False,
    )
```

```python
import functools

import jax
import jax.numpy as jnp
from jax import lax
from jax.experimental import pallas as pl
from jax.experimental.pallas import tpu as pltpu
from jax.sharding import PartitionSpec as P

AXES = ("dp", "inner")
LANES = 128
MIB = 1024 * 1024
FIRST = (2, 3, 1, 0)
SUMS = (1, 3, 2, 0)
F32 = jnp.float32
BF16 = jnp.bfloat16
VMEM = pltpu.VMEM
NT = (((1,), (1,)), ((), ()))


def dot(a, b, dims=(((1,), (0,)), ((), ()))):
    return lax.dot_general(a, b, dims, preferred_element_type=F32)


def vmem(n):
    return [pl.BlockSpec(memory_space=VMEM)] * n


def small_kernel(name, body, out_shape, *args, scratch=(), space=VMEM, limit=8):
    many = isinstance(out_shape, list)
    return pl.pallas_call(
        body,
        out_shape=out_shape,
        in_specs=[pl.BlockSpec(memory_space=space)] * len(args),
        out_specs=vmem(len(out_shape)) if many else vmem(1)[0],
        scratch_shapes=list(scratch),
        compiler_params=pltpu.CompilerParams(vmem_limit_bytes=limit * MIB),
        cost_estimate=pl.CostEstimate(
            flops=4000 * MIB, bytes_accessed=8 * MIB, transcendentals=4 * MIB
        ),
        name=name,
    )(*args)


def diagonal(n):
    return lax.broadcasted_iota(jnp.int32, (n, n), 0) == lax.broadcasted_iota(jnp.int32, (n, n), 1)


def to_column(row):
    n = row.shape[1]
    return jnp.sum(jnp.where(diagonal(n), row, 0.0), axis=1, keepdims=True)


def to_row(column):
    n = column.shape[0]
    return jnp.sum(jnp.where(diagonal(n), column, 0.0), axis=0, keepdims=True)


def stacked_codes(codes_ref, count):
    codes = codes_ref[...].astype(BF16)
    parts = [codes, codes]
    if count > 2 * codes.shape[0]:
        parts.append(jnp.zeros((count - 2 * codes.shape[0], codes.shape[1]), BF16))
    return jnp.concatenate(parts, axis=0)


def split(x):
    high = x.astype(BF16).astype(F32)
    return high, x - high


def prep_kernel(hid, *refs):
    piece_ref, direction_ref, gain_ref, bias_ref, codes_ref, sems = refs[4:]
    copies = [
        pltpu.make_async_copy(source, target, sems.at[k])
        for k, (source, target) in enumerate(zip(refs[:4], refs[5:9]))
    ]
    for copy in copies:
        copy.start()
    for copy in copies:
        copy.wait()
    d = direction_ref[...]
    shapes = codes_ref.shape[0]
    rows, cols = d.shape
    half = cols // 2
    extra_lanes = piece_ref.shape[1] - cols
    inverse = lax.rsqrt(jnp.sum(d * d, axis=1, keepdims=True))
    w = to_column(gain_ref[...]) * (d * inverse)
    lane = lax.broadcasted_iota(jnp.int32, (rows, half), 1)
    first = jnp.where(lane < hid, w[:, :half], w[:, half:])
    code = pltpu.roll(w, half - hid, 1)[:, half:].astype(BF16)
    bias = to_column(bias_ref[...]).astype(BF16).astype(F32)
    high, low = split(dot(code, stacked_codes(codes_ref, extra_lanes), NT) + bias)
    own = first[:, half - LANES :]
    if extra_lanes > LANES:
        own = jnp.concatenate([jnp.zeros((rows, extra_lanes - LANES), F32), own], axis=1)
    lane = lax.broadcasted_iota(jnp.int32, (rows, extra_lanes), 1)
    table = jnp.where(lane < shapes, high, jnp.where(lane < 2 * shapes, low, 0.0))
    table = jnp.where(lane >= extra_lanes - (half - hid), own, table)
    piece_ref[:, :half] = first.astype(BF16)
    piece_ref[:, half : half + extra_lanes] = table.astype(BF16)
    piece_ref[:, half + extra_lanes :] = code


def join_kernel(n, n_early, *refs):
    rows = refs[0].shape[0]
    for k, ref in enumerate(refs[n - 1 :: -1]):
        lane = 0
        for out_ref in refs[n + n_early :]:
            lanes = out_ref.shape[1]
            out_ref[k * rows : (k + 1) * rows, :] = ref[:, lane : lane + lanes]
            lane += lanes


def pack_kernel(shapes, *refs):
    weight_ref, code_ref = refs[-2:]
    count = len(refs) - 2
    rows, half = refs[0].shape[0], code_ref.shape[1]
    products = jnp.zeros((rows, LANES), F32)
    for k, ref in zip(FIRST, refs):
        for block in range(half // LANES):
            at = (block * count + k) * rows
            weight_ref[at : at + rows, :] = ref[:, block * LANES : (block + 1) * LANES]
        own = ref[:, half : half + LANES].astype(F32)
        own = jnp.where(lax.broadcasted_iota(jnp.int32, own.shape, 1) < 2 * shapes, own, 0.0)
        products = products + (pltpu.roll(own, 2 * shapes * k, 1) if k else own)
        code_ref[k * rows : (k + 1) * rows, :] = ref[:, half + LANES :]
    weight_ref[half // LANES * count * rows :, :] = products.astype(BF16)


def unpack(hid, shapes, refs, orders, me, w_ref):
    count = LANES // (2 * shapes)
    half = w_ref.shape[1] - LANES
    blocks = half // LANES
    for ref, order in zip(refs, orders):
        height = ref.shape[0] // (len(order) // count)
        rows = height // (blocks * count + 1)
        lane = lax.broadcasted_iota(jnp.int32, (rows, LANES), 1)
        for j, mask in enumerate(order):
            start, k = j // count * height, j % count
            at = pl.ds(pl.multiple_of((me ^ mask) * rows, rows), rows)
            for block in range(blocks):
                here = start + (block * count + k) * rows
                part = ref[here : here + rows, :]
                w_ref[at, block * LANES : (block + 1) * LANES] = part
            here = start + blocks * count * rows
            products = ref[here : here + rows, :].astype(F32)
            if k:
                products = pltpu.roll(products, LANES - 2 * shapes * k, 1)
            products = jnp.where(lane < 2 * shapes, products, 0.0)
            products = jnp.where(lane >= LANES - (half - hid), part.astype(F32), products)
            w_ref[at, half:] = products.astype(BF16)


def place(refs, orders, me, out_ref):
    if orders is None:
        out_ref[...] = refs[0][...]
        return
    rows = refs[0].shape[0] // len(orders[0])
    for ref, order in zip(refs, orders):
        for k, mask in enumerate(order):
            at = pl.multiple_of((me ^ mask) * rows, rows)
            out_ref[pl.ds(at, rows), :] = ref[k * rows : (k + 1) * rows, :]


def inputs_kernel(hid, tile, *refs):
    x_ref, x_t_ref, hidden_ref, offsets_ref, ids_ref, scale_ref, sems = refs[4:]
    points = x_ref.shape[0]
    half = (hid + LANES - 1) // LANES * LANES
    shapes = x_t_ref.shape[0] - half
    extra_lanes = x_ref.shape[1] - half
    steps = points // tile
    small = [
        pltpu.make_async_copy(source, target, sems.at[steps + k])
        for k, (source, target) in enumerate(zip(refs[1:4], (offsets_ref, ids_ref, scale_ref)))
    ]
    large = [
        pltpu.make_async_copy(
            refs[0].at[pl.ds(k * tile, tile), :], hidden_ref.at[pl.ds(k * tile, tile), :], sems.at[k]
        )
        for k in range(steps)
    ]
    for copy in small + large:
        copy.start()
    for copy in small:
        copy.wait()
    for step, copy in enumerate(large):
        here = slice(step * tile, (step + 1) * tile)
        scale = scale_ref[:, here]
        jitter = jnp.where(scale == 0, 1.0, jnp.where(scale == 1, 0.5, 0.25))
        xyz = offsets_ref[:, here] * jitter
        row = lax.broadcasted_iota(jnp.int32, (16, tile), 0)
        last = jnp.zeros((16, tile), F32)
        for k in range(half - hid):
            last = jnp.where(row == 16 - (half - hid) + k, xyz[k : k + 1], last)
        last = last.astype(BF16)
        row = lax.broadcasted_iota(jnp.int32, (extra_lanes - 16, tile), 0)
        ids = ids_ref[:, here]
        member = jnp.where((row == ids) | (row == ids + shapes), 1.0, 0.0).astype(BF16)
        x_ref[here, half:] = jnp.concatenate([member, last], axis=0).T
        x_t_ref[half:, here] = member[:shapes]
        copy.wait()
        x_ref[here, half - LANES : half] = jnp.zeros((tile, LANES), BF16)
        x_ref[here, :hid] = hidden_ref[here, :].astype(BF16)
        hidden = x_ref[here, :half].T
        x_t_ref[: half - 16, here] = hidden[: half - 16]
        x_t_ref[half - 16 : half, here] = hidden[half - 16 :] + last


def layer_kernel(hid, shapes, tile, orders, parts, *refs):
    n = 1 if orders is None else len(orders)
    pieces = refs[:n]
    x_ref, x_t_ref, cot_ref, out_hbm, grad_hidden_ref = refs[n : n + 5]
    grad_refs = refs[n + 5 : -6]
    w_ref, turned_ref, out_ref, grad_pre_ref, pre_ref, sems = refs[-6:]
    points, width = cot_ref.shape
    half = width // 2
    steps = points // tile
    me = lax.axis_index(AXES)
    if orders is None:
        place(pieces, orders, me, w_ref)
    else:
        unpack(hid, shapes, pieces, orders, me, w_ref)
    copies = []

    def rows_of(step):
        return slice(step * tile, (step + 1) * tile)

    def forward(step):
        pre_ref[step % 2] = dot(x_ref[rows_of(step), :], w_ref[...], NT)

    def middle(step):
        here = rows_of(step)
        pre = pre_ref[step % 2]
        sigma = 0.5 * jnp.tanh(0.5 * pre) + 0.5
        out = pre * sigma
        out_ref[here, :] = out
        grad_pre_ref[here, :] = (cot_ref[here, :] * (sigma * (1.0 + (pre - out)))).astype(BF16)

    def backward(step):
        here = rows_of(step)
        grad_hidden_ref[here, :] = dot(grad_pre_ref[here, :], w_ref[:, :half])[:, :hid]

    def store(step):
        here = pl.ds(step * tile, tile)
        copy = pltpu.make_async_copy(out_ref.at[here, :], out_hbm.at[here, :], sems.at[step])
        copy.start()
        copies.append(copy)

    forward(0)
    for step in range(steps):
        if step + 1 < steps:
            forward(step + 1)
        middle(step)
        if step > 0:
            backward(step - 1)
        store(step)
    backward(steps - 1)
    grad = dot(x_t_ref[...], grad_pre_ref[...])
    sums = grad[half:].astype(BF16)
    for at in range(0, width, half):
        turned_ref[at : at + half, :] = grad[:half, at : at + half].T
    for ref, order in zip(grad_refs, parts):
        ref[:shapes, :] = sums[:, :half]
        ref[shapes : 2 * shapes, :] = sums[:, half:]
        if orders is None:
            ref[2 * shapes :, :] = turned_ref[...].astype(BF16)
            continue
        rows = (ref.shape[0] - 2 * shapes) // len(order)
        for k, mask in enumerate(order):
            at = pl.multiple_of((me ^ mask) * rows, rows)
            to = 2 * shapes + k * rows
            ref[to : to + rows, :] = turned_ref[pl.ds(at, rows), :].astype(BF16)

    for copy in copies:
        copy.wait()


def store_kernel(source_ref, target_ref, sem):
    copy = pltpu.make_async_copy(source_ref, target_ref, sem)
    copy.start()
    copy.wait()


def sum_of(refs):
    terms = [ref[...].astype(F32) for ref in refs]
    while len(terms) > 1:
        terms = [a + b for a, b in zip(terms[::2], terms[1::2])]
    return terms[0]


def add_kernel(shapes, n, *refs):
    total = sum_of(refs[:n]).astype(BF16)
    for k, ref in enumerate(refs[n:]):
        rows = ref.shape[0] - 2 * shapes
        at = 2 * shapes + k * rows
        ref[: 2 * shapes, :] = total[: 2 * shapes]
        ref[2 * shapes :, :] = total[at : at + rows]


def last_kernel(hid, shapes, orders, n, *refs):
    direction_ref, gain_ref, codes_ref = refs[n : n + 3]
    pieces = refs[n + 3 : -5]
    grad_codes_ref, grad_direction_ref, grad_gain_ref, grad_bias_ref, code_scratch = refs[-5:]
    d = direction_ref[...]
    rows, cols = d.shape
    half = cols // 2
    me = lax.axis_index(AXES)
    place(pieces, orders, me, code_scratch)
    total = sum_of(refs[:n])
    sums = jnp.concatenate([total[:shapes], total[shapes : 2 * shapes]], axis=1)
    sums = jnp.concatenate(split(sums), axis=0).astype(BF16)
    terms = dot(sums, code_scratch[...])
    grad_codes_ref[...] = terms[:shapes] + terms[shapes:]
    width = sums.shape[1]
    mine = lax.broadcasted_iota(jnp.int32, (rows, width), 0) + me * rows
    mine = jnp.where(mine == lax.broadcasted_iota(jnp.int32, (rows, width), 1), 1.0, 0.0).astype(BF16)
    own = dot(mine, sums, NT)
    grad_bias_ref[...] = to_row(jnp.sum(own, axis=1, keepdims=True))
    code = dot(own.astype(BF16), stacked_codes(codes_ref, 2 * shapes))
    packed = jnp.concatenate([total[2 * shapes :], code], axis=1)
    lane = lax.broadcasted_iota(jnp.int32, (rows, cols), 1)
    grad_weight = jnp.where(
        lane < hid,
        packed,
        jnp.where(lane < hid + half, pltpu.roll(packed, cols - (half - hid), 1), pltpu.roll(packed, half, 1)),
    )
    inverse = lax.rsqrt(jnp.sum(d * d, axis=1, keepdims=True))
    unit = d * inverse
    grad_gain = jnp.sum(grad_weight * unit, axis=1, keepdims=True)
    grad_gain_ref[...] = to_row(grad_gain)
    grad_direction_ref[...] = (to_column(gain_ref[...]) * inverse) * (grad_weight - grad_gain * unit)


def masks_of(group):
    masks = [0]
    for bit in group:
        masks = masks + [m ^ bit for m in masks]
    return masks


def order_of(groups):
    order = [0]
    for group in groups:
        order = [m ^ r for m in masks_of(group) for r in order]
    return order


def swaps(arrays, masks, devices):
    moved = [
        lax.ppermute(x, AXES, [(i, i ^ mask) for i in range(devices)])
        for x, mask in list(zip(arrays, masks))[::-1]
    ]
    return moved[::-1]


def per_device(
    hidden,
    codes,
    offsets,
    shape_ids,
    scale_index,
    direction,
    gain,
    bias,
    cotangent,
    running_mean,
    running_var,
):
    points, hid = hidden.shape
    shapes = codes.shape[0]
    rows, cols = direction.shape
    width = cotangent.shape[1]
    half = cols // 2
    devices = lax.axis_size("dp") * lax.axis_size("inner")
    bits = [1 << k | 1 for k in range(devices.bit_length() - 1)]
    groups = [bits[k - 2 : k] for k in range(len(bits), 1, -2)]
    groups = groups + [bits[:1]] * (len(bits) % 2)
    extra_lanes = -(-(2 * shapes + 16) // LANES) * LANES
    tuned = rows % 16 == 0 and 2 * shapes * len(masks_of(groups[0])) == LANES
    lanes = half + extra_lanes
    gain_row = gain.reshape(1, rows)

    def shape_of(rows, lanes, dtype):
        return jax.ShapeDtypeStruct((rows, lanes), dtype)

    held = small_kernel(
        "prep",
        functools.partial(prep_kernel, hid),
        shape_of(rows, lanes + half, BF16),
        *[
            pltpu.with_memory_space_constraint(x, pltpu.HBM)
            for x in (direction, gain_row, bias.reshape(1, rows), codes)
        ],
        scratch=[
            VMEM((rows, cols), F32),
            VMEM((1, rows), F32),
            VMEM((1, rows), F32),
            VMEM((shapes, half), F32),
            pltpu.SemaphoreType.DMA((4,)),
        ],
        space=pl.ANY,
    )
    tile, layer_tile = min(512, points), min(256, points)
    x, x_t = pl.pallas_call(
        functools.partial(inputs_kernel, hid, tile),
        out_shape=[
            shape_of(points, lanes, BF16),
            shape_of(half + shapes, points, BF16),
        ],
        in_specs=[pl.BlockSpec(memory_space=pl.ANY)] * 4,
        out_specs=vmem(2),
        scratch_shapes=[
            VMEM((points, hid), F32),
            VMEM((half - hid, points), F32),
            VMEM((1, points), jnp.int32),
            VMEM((1, points), jnp.int32),
            pltpu.SemaphoreType.DMA((points // tile + 3,)),
        ],
        compiler_params=pltpu.CompilerParams(vmem_limit_bytes=12 * MIB),
        cost_estimate=pl.CostEstimate(
            flops=4000 * MIB, bytes_accessed=8 * points * half, transcendentals=0
        ),
        name="inputs",
    )(
        *[
            pltpu.with_memory_space_constraint(a, pltpu.HBM)
            for a in (
                hidden,
                offsets.T,
                shape_ids.reshape(1, points),
                scale_index.reshape(1, points),
            )
        ]
    )
    def gather(array, group):
        masks = masks_of(group)[1:]
        return [array] + swaps([array] * len(masks), masks, devices)

    def join(arrays, *widths, early=()):
        height = sum(a.shape[0] for a in arrays)
        return small_kernel(
            "join",
            functools.partial(join_kernel, len(arrays), len(early)),
            [shape_of(height, width, BF16) for width in widths],
            *arrays[::-1],
            *early,
        )

    if tuned:
        arrays = gather(held, groups[0])
        weight, code_weight = small_kernel(
            "pack",
            functools.partial(pack_kernel, shapes),
            [
                shape_of((half // LANES * len(arrays) + 1) * rows, LANES, BF16),
                shape_of(len(arrays) * rows, half, BF16),
            ],
            *[arrays[k] for k in FIRST],
        )
        weight, code_weight, x, x_t = lax.optimization_barrier((weight, code_weight, x, x_t))
        (weights,) = [gather(weight, group) for group in groups[1:-1]]
        along, across = [[bit] for bit in groups[1][::-1]]
        code_weights = gather(code_weight, along)
        (weight,) = join(weights, LANES, early=(cotangent,))
        weights = gather(weight, groups[-1])
        (code_weight,) = join(code_weights, half)
        *weights, code_weight = lax.optimization_barrier((*weights, code_weight))
        code_order = order_of([groups[0], along, across])
        orders = [[m ^ r for r in order_of(groups[:-1])] for m in masks_of(groups[-1])]
        code_orders = [[m ^ r for r in code_order] for m in masks_of(groups[-1])]
        parts = orders
    else:
        held = lax.all_gather(held, AXES, axis=0, tiled=True)
        weights, code_weights, orders, code_orders, parts = [held[:, :lanes]], [held[:, lanes:]], None, None, [[0]]

    output, grad_hidden, *grads = pl.pallas_call(
        functools.partial(layer_kernel, hid, shapes, layer_tile, orders, parts),
        out_shape=[pltpu.HBM((points, width), F32), pltpu.VMEM((points, hid), F32)]
        + [shape_of(2 * shapes + width // len(parts), half, BF16)] * len(parts),
        in_specs=vmem(len(weights) + 3),
        out_specs=[pl.BlockSpec(memory_space=pltpu.HBM)] + vmem(1 + len(parts)),
        scratch_shapes=[
            VMEM((width, lanes), BF16),
            VMEM((width, half), F32),
            VMEM((points, width), F32),
            VMEM((points, width), BF16),
            VMEM((2, layer_tile, width), F32),
            pltpu.SemaphoreType.DMA((points // layer_tile,)),
        ],
        compiler_params=pltpu.CompilerParams(vmem_limit_bytes=20 * MIB),
        cost_estimate=pl.CostEstimate(
            flops=6 * points * width * cols,
            bytes_accessed=8 * points * (width + half),
            transcendentals=points * width,
        ),
        name="layer",
    )(*weights, x, x_t, cotangent)

    stored = pl.pallas_call(
        store_kernel,
        out_shape=pltpu.HBM((points, hid), F32),
        in_specs=vmem(1),
        out_specs=pl.BlockSpec(memory_space=pltpu.HBM),
        scratch_shapes=[pltpu.SemaphoreType.DMA(())],
        compiler_params=pltpu.CompilerParams(vmem_limit_bytes=8 * MIB),
        cost_estimate=pl.CostEstimate(
            flops=4000 * MIB, bytes_accessed=8 * points * hid, transcendentals=0
        ),
        name="store",
    )

    if tuned:
        for r, group in enumerate(groups[::-1]):
            masks = masks_of(group)
            grads = [grads[0]] + swaps(grads[1:], masks[1:], devices)
            if r == len(groups) - 1:
                break
            n_out = len(masks_of(groups[-2 - r]))
            left = (grads[0].shape[0] - 2 * shapes) // n_out
            grads = small_kernel(
                "add",
                functools.partial(add_kernel, shapes, len(grads)),
                [shape_of(2 * shapes + left, half, BF16)] * n_out,
                *(grads[::-1] if r == 0 else [grads[k] for k in SUMS]),
            )
            if r == 0:
                *grads, grad_hidden = lax.optimization_barrier((*grads, grad_hidden))
                grad_hidden = stored(grad_hidden)
                grad_hidden, code_weight = lax.optimization_barrier((grad_hidden, code_weight))
                code_weights = gather(code_weight, across)
            if r == len(groups) - 2:
                *grads, grad_hidden = lax.optimization_barrier((*grads, grad_hidden))
        (code_weight,) = join(code_weights, half)
        code_weights = gather(code_weight, groups[-1])
    else:
        grad_hidden = stored(grad_hidden)
        sums = lax.psum(grads[0][: 2 * shapes].astype(F32), AXES)
        high = sums.astype(BF16)
        own = lax.psum_scatter(grads[0][2 * shapes :].astype(F32), AXES, scatter_dimension=0, tiled=True)
        low = jnp.zeros((2 * shapes + rows, half), BF16).at[: 2 * shapes].set((sums - high).astype(BF16))
        grads = [jnp.concatenate([high, own.astype(BF16)], axis=0), low]
    grad_codes, grad_direction, grad_gain, grad_bias = small_kernel(
        "last",
        functools.partial(last_kernel, hid, shapes, code_orders, len(grads)),
        [
            shape_of(shapes, half, F32),
            shape_of(rows, cols, F32),
            shape_of(1, rows, F32),
            shape_of(1, rows, F32),
        ],
        *grads[::-1],
        direction,
        gain_row,
        codes,
        *code_weights,
        scratch=[VMEM((width, half), BF16)],
    )

    total = float(points * devices)
    batch_mean = jnp.mean(codes, axis=0)
    batch_square = jnp.mean(codes * codes, axis=0)
    batch_var = (batch_square - batch_mean * batch_mean) * (total / (total - 1.0))
    new_mean = 0.9 * running_mean + 0.1 * batch_mean
    new_var = 0.9 * running_var + 0.1 * batch_var
    return (
        output,
        grad_hidden,
        grad_codes,
        grad_direction,
        grad_gain.reshape(rows),
        grad_bias.reshape(rows),
        new_mean,
        new_var,
    )


def solution(mesh):
    return jax.shard_map(
        per_device,
        mesh=mesh,
        in_specs=(
            P(("dp", "inner"), None),
            P(),
            P(("dp", "inner"), None),
            P(("dp", "inner")),
            P(("dp", "inner")),
            P(("dp", "inner"), None),
            P(("dp", "inner")),
            P(("dp", "inner")),
            P(("dp", "inner"), None),
            P(),
            P(),
        ),
        out_specs=(
            P(("dp", "inner"), None),
            P(("dp", "inner"), None),
            P(),
            P(("dp", "inner"), None),
            P(("dp", "inner")),
            P(("dp", "inner")),
            P(),
            P(),
        ),
        check_vma=False,
    )
```

```python
import functools

import jax
import jax.numpy as jnp
from jax import lax
from jax.experimental import pallas as pl
from jax.experimental.pallas import tpu as pltpu
from jax.sharding import PartitionSpec as P

AXES = ("dp", "inner")
LANES = 128
MIB = 1024 * 1024
FIRST = (2, 3, 1, 0)
SUMS = (1, 3, 2, 0)
F32 = jnp.float32
BF16 = jnp.bfloat16
VMEM = pltpu.VMEM
NT = (((1,), (1,)), ((), ()))


def dot(a, b, dims=(((1,), (0,)), ((), ()))):
    return lax.dot_general(a, b, dims, preferred_element_type=F32)


def vmem(n):
    return [pl.BlockSpec(memory_space=VMEM)] * n


def small_kernel(name, body, out_shape, *args, scratch=(), space=VMEM, limit=8):
    many = isinstance(out_shape, list)
    return pl.pallas_call(
        body,
        out_shape=out_shape,
        in_specs=[pl.BlockSpec(memory_space=space)] * len(args),
        out_specs=vmem(len(out_shape)) if many else vmem(1)[0],
        scratch_shapes=list(scratch),
        compiler_params=pltpu.CompilerParams(vmem_limit_bytes=limit * MIB),
        cost_estimate=pl.CostEstimate(
            flops=4000 * MIB, bytes_accessed=8 * MIB, transcendentals=4 * MIB
        ),
        name=name,
    )(*args)


def diagonal(n):
    return lax.broadcasted_iota(jnp.int32, (n, n), 0) == lax.broadcasted_iota(jnp.int32, (n, n), 1)


def to_column(row):
    n = row.shape[1]
    return jnp.sum(jnp.where(diagonal(n), row, 0.0), axis=1, keepdims=True)


def to_row(column):
    n = column.shape[0]
    return jnp.sum(jnp.where(diagonal(n), column, 0.0), axis=0, keepdims=True)


def stacked_codes(codes_ref, count):
    codes = codes_ref[...].astype(BF16)
    parts = [codes, codes]
    if count > 2 * codes.shape[0]:
        parts.append(jnp.zeros((count - 2 * codes.shape[0], codes.shape[1]), BF16))
    return jnp.concatenate(parts, axis=0)


def split(x):
    high = x.astype(BF16).astype(F32)
    return high, x - high


def prep_kernel(hid, *refs):
    piece_ref, direction_ref, gain_ref, bias_ref, codes_ref, sems = refs[4:]
    copies = [
        pltpu.make_async_copy(source, target, sems.at[k])
        for k, (source, target) in enumerate(zip(refs[:4], refs[5:9]))
    ]
    for copy in copies:
        copy.start()
    for copy in copies:
        copy.wait()
    d = direction_ref[...]
    shapes = codes_ref.shape[0]
    rows, cols = d.shape
    half = cols // 2
    extra_lanes = piece_ref.shape[1] - cols
    inverse = lax.rsqrt(jnp.sum(d * d, axis=1, keepdims=True))
    w = to_column(gain_ref[...]) * (d * inverse)
    lane = lax.broadcasted_iota(jnp.int32, (rows, half), 1)
    first = jnp.where(lane < hid, w[:, :half], w[:, half:])
    code = pltpu.roll(w, half - hid, 1)[:, half:].astype(BF16)
    bias = to_column(bias_ref[...]).astype(BF16).astype(F32)
    high, low = split(dot(code, stacked_codes(codes_ref, extra_lanes), NT) + bias)
    own = first[:, half - LANES :]
    if extra_lanes > LANES:
        own = jnp.concatenate([jnp.zeros((rows, extra_lanes - LANES), F32), own], axis=1)
    lane = lax.broadcasted_iota(jnp.int32, (rows, extra_lanes), 1)
    table = jnp.where(lane < shapes, high, jnp.where(lane < 2 * shapes, low, 0.0))
    table = jnp.where(lane >= extra_lanes - (half - hid), own, table)
    piece_ref[:, :half] = first.astype(BF16)
    piece_ref[:, half : half + extra_lanes] = table.astype(BF16)
    piece_ref[:, half + extra_lanes :] = code


def join_kernel(n, n_early, *refs):
    rows = refs[0].shape[0]
    for k, ref in enumerate(refs[n - 1 :: -1]):
        lane = 0
        for out_ref in refs[n + n_early :]:
            lanes = out_ref.shape[1]
            out_ref[k * rows : (k + 1) * rows, :] = ref[:, lane : lane + lanes]
            lane += lanes


def pack_kernel(shapes, *refs):
    weight_ref, code_ref = refs[-2:]
    count = len(refs) - 2
    rows, half = refs[0].shape[0], code_ref.shape[1]
    products = jnp.zeros((rows, LANES), F32)
    for k, ref in zip(FIRST, refs):
        for block in range(half // LANES):
            at = (block * count + k) * rows
            weight_ref[at : at + rows, :] = ref[:, block * LANES : (block + 1) * LANES]
        own = ref[:, half : half + LANES].astype(F32)
        own = jnp.where(lax.broadcasted_iota(jnp.int32, own.shape, 1) < 2 * shapes, own, 0.0)
        products = products + (pltpu.roll(own, 2 * shapes * k, 1) if k else own)
        code_ref[k * rows : (k + 1) * rows, :] = ref[:, half + LANES :]
    weight_ref[half // LANES * count * rows :, :] = products.astype(BF16)


def unpack(hid, shapes, refs, orders, me, w_ref):
    count = LANES // (2 * shapes)
    half = w_ref.shape[1] - LANES
    blocks = half // LANES
    for ref, order in zip(refs, orders):
        height = ref.shape[0] // (len(order) // count)
        rows = height // (blocks * count + 1)
        lane = lax.broadcasted_iota(jnp.int32, (rows, LANES), 1)
        for j, mask in enumerate(order):
            start, k = j // count * height, j % count
            at = pl.ds(pl.multiple_of((me ^ mask) * rows, rows), rows)
            for block in range(blocks):
                here = start + (block * count + k) * rows
                part = ref[here : here + rows, :]
                w_ref[at, block * LANES : (block + 1) * LANES] = part
            here = start + blocks * count * rows
            products = ref[here : here + rows, :].astype(F32)
            if k:
                products = pltpu.roll(products, LANES - 2 * shapes * k, 1)
            products = jnp.where(lane < 2 * shapes, products, 0.0)
            products = jnp.where(lane >= LANES - (half - hid), part.astype(F32), products)
            w_ref[at, half:] = products.astype(BF16)


def place(refs, orders, me, out_ref):
    if orders is None:
        out_ref[...] = refs[0][...]
        return
    rows = refs[0].shape[0] // len(orders[0])
    for ref, order in zip(refs, orders):
        for k, mask in enumerate(order):
            at = pl.multiple_of((me ^ mask) * rows, rows)
            out_ref[pl.ds(at, rows), :] = ref[k * rows : (k + 1) * rows, :]


def inputs_kernel(hid, tile, *refs):
    x_ref, x_t_ref, hidden_ref, offsets_ref, ids_ref, scale_ref, sems = refs[4:]
    points = x_ref.shape[0]
    half = (hid + LANES - 1) // LANES * LANES
    shapes = x_t_ref.shape[0] - half
    extra_lanes = x_ref.shape[1] - half
    steps = points // tile
    small = [
        pltpu.make_async_copy(source, target, sems.at[steps + k])
        for k, (source, target) in enumerate(zip(refs[1:4], (offsets_ref, ids_ref, scale_ref)))
    ]
    large = [
        pltpu.make_async_copy(
            refs[0].at[pl.ds(k * tile, tile), :], hidden_ref.at[pl.ds(k * tile, tile), :], sems.at[k]
        )
        for k in range(steps)
    ]
    for copy in small + large:
        copy.start()
    for copy in small:
        copy.wait()
    for step, copy in enumerate(large):
        here = slice(step * tile, (step + 1) * tile)
        scale = scale_ref[:, here]
        jitter = jnp.where(scale == 0, 1.0, jnp.where(scale == 1, 0.5, 0.25))
        xyz = offsets_ref[:, here] * jitter
        row = lax.broadcasted_iota(jnp.int32, (16, tile), 0)
        last = jnp.zeros((16, tile), F32)
        for k in range(half - hid):
            last = jnp.where(row == 16 - (half - hid) + k, xyz[k : k + 1], last)
        last = last.astype(BF16)
        row = lax.broadcasted_iota(jnp.int32, (extra_lanes - 16, tile), 0)
        ids = ids_ref[:, here]
        member = jnp.where((row == ids) | (row == ids + shapes), 1.0, 0.0).astype(BF16)
        x_ref[here, half:] = jnp.concatenate([member, last], axis=0).T
        x_t_ref[half:, here] = member[:shapes]
        copy.wait()
        x_ref[here, half - LANES : half] = jnp.zeros((tile, LANES), BF16)
        x_ref[here, :hid] = hidden_ref[here, :].astype(BF16)
        hidden = x_ref[here, :half].T
        x_t_ref[: half - 16, here] = hidden[: half - 16]
        x_t_ref[half - 16 : half, here] = hidden[half - 16 :] + last


def layer_kernel(hid, shapes, tile, orders, parts, *refs):
    n = 1 if orders is None else len(orders)
    pieces = refs[:n]
    x_ref, x_t_ref, cot_ref, out_hbm, grad_hidden_ref = refs[n : n + 5]
    grad_refs = refs[n + 5 : -6]
    w_ref, turned_ref, out_ref, grad_pre_ref, pre_ref, sems = refs[-6:]
    points, width = cot_ref.shape
    half = width // 2
    steps = points // tile
    me = lax.axis_index(AXES)
    if orders is None:
        place(pieces, orders, me, w_ref)
    else:
        unpack(hid, shapes, pieces, orders, me, w_ref)
    copies = []

    def rows_of(step):
        return slice(step * tile, (step + 1) * tile)

    def forward(step):
        pre_ref[step % 2] = dot(x_ref[rows_of(step), :], w_ref[...], NT)

    def middle(step):
        here = rows_of(step)
        pre = pre_ref[step % 2]
        sigma = 0.5 * jnp.tanh(0.5 * pre) + 0.5
        out = pre * sigma
        out_ref[here, :] = out
        grad_pre_ref[here, :] = (cot_ref[here, :] * (sigma * (1.0 + (pre - out)))).astype(BF16)

    def backward(step):
        here = rows_of(step)
        grad_hidden_ref[here, :] = dot(grad_pre_ref[here, :], w_ref[:, :half])[:, :hid]

    def store(step):
        here = pl.ds(step * tile, tile)
        copy = pltpu.make_async_copy(out_ref.at[here, :], out_hbm.at[here, :], sems.at[step])
        copy.start()
        copies.append(copy)

    forward(0)
    for step in range(steps):
        if step + 1 < steps:
            forward(step + 1)
        middle(step)
        if step > 0:
            backward(step - 1)
        store(step)
    backward(steps - 1)
    grad = dot(x_t_ref[...], grad_pre_ref[...])
    sums = grad[half:].astype(BF16)
    for at in range(0, width, half):
        turned_ref[at : at + half, :] = grad[:half, at : at + half].T
    for ref, order in zip(grad_refs, parts):
        ref[:shapes, :] = sums[:, :half]
        ref[shapes : 2 * shapes, :] = sums[:, half:]
        if orders is None:
            ref[2 * shapes :, :] = turned_ref[...].astype(BF16)
            continue
        rows = (ref.shape[0] - 2 * shapes) // len(order)
        for k, mask in enumerate(order):
            at = pl.multiple_of((me ^ mask) * rows, rows)
            to = 2 * shapes + k * rows
            ref[to : to + rows, :] = turned_ref[pl.ds(at, rows), :].astype(BF16)

    for copy in copies:
        copy.wait()


def store_kernel(source_ref, target_ref, sem):
    copy = pltpu.make_async_copy(source_ref, target_ref, sem)
    copy.start()
    copy.wait()


def sum_of(refs):
    terms = [ref[...].astype(F32) for ref in refs]
    while len(terms) > 1:
        terms = [a + b for a, b in zip(terms[::2], terms[1::2])]
    return terms[0]


def add_kernel(shapes, n, *refs):
    total = sum_of(refs[:n]).astype(BF16)
    for k, ref in enumerate(refs[n:]):
        rows = ref.shape[0] - 2 * shapes
        at = 2 * shapes + k * rows
        ref[: 2 * shapes, :] = total[: 2 * shapes]
        ref[2 * shapes :, :] = total[at : at + rows]


def last_kernel(hid, shapes, orders, n, *refs):
    direction_ref, gain_ref, codes_ref = refs[n : n + 3]
    pieces = refs[n + 3 : -5]
    grad_codes_ref, grad_direction_ref, grad_gain_ref, grad_bias_ref, code_scratch = refs[-5:]
    d = direction_ref[...]
    rows, cols = d.shape
    half = cols // 2
    me = lax.axis_index(AXES)
    place(pieces, orders, me, code_scratch)
    total = sum_of(refs[:n])
    sums = jnp.concatenate([total[:shapes], total[shapes : 2 * shapes]], axis=1)
    sums = jnp.concatenate(split(sums), axis=0).astype(BF16)
    terms = dot(sums, code_scratch[...])
    grad_codes_ref[...] = terms[:shapes] + terms[shapes:]
    width = sums.shape[1]
    mine = lax.broadcasted_iota(jnp.int32, (rows, width), 0) + me * rows
    mine = jnp.where(mine == lax.broadcasted_iota(jnp.int32, (rows, width), 1), 1.0, 0.0).astype(BF16)
    own = dot(mine, sums, NT)
    grad_bias_ref[...] = to_row(jnp.sum(own, axis=1, keepdims=True))
    code = dot(own.astype(BF16), stacked_codes(codes_ref, 2 * shapes))
    packed = jnp.concatenate([total[2 * shapes :], code], axis=1)
    lane = lax.broadcasted_iota(jnp.int32, (rows, cols), 1)
    grad_weight = jnp.where(
        lane < hid,
        packed,
        jnp.where(lane < hid + half, pltpu.roll(packed, cols - (half - hid), 1), pltpu.roll(packed, half, 1)),
    )
    inverse = lax.rsqrt(jnp.sum(d * d, axis=1, keepdims=True))
    unit = d * inverse
    grad_gain = jnp.sum(grad_weight * unit, axis=1, keepdims=True)
    grad_gain_ref[...] = to_row(grad_gain)
    grad_direction_ref[...] = (to_column(gain_ref[...]) * inverse) * (grad_weight - grad_gain * unit)


def masks_of(group):
    masks = [0]
    for bit in group:
        masks = masks + [m ^ bit for m in masks]
    return masks


def order_of(groups):
    order = [0]
    for group in groups:
        order = [m ^ r for m in masks_of(group) for r in order]
    return order


def swaps(arrays, masks, devices):
    moved = [
        lax.ppermute(x, AXES, [(i, i ^ mask) for i in range(devices)])
        for x, mask in list(zip(arrays, masks))[::-1]
    ]
    return moved[::-1]


def per_device(
    hidden,
    codes,
    offsets,
    shape_ids,
    scale_index,
    direction,
    gain,
    bias,
    cotangent,
    running_mean,
    running_var,
):
    points, hid = hidden.shape
    shapes = codes.shape[0]
    rows, cols = direction.shape
    width = cotangent.shape[1]
    half = cols // 2
    devices = lax.axis_size("dp") * lax.axis_size("inner")
    bits = [1 << k | 1 for k in range(devices.bit_length() - 1)]
    groups = [bits[k - 2 : k] for k in range(len(bits), 1, -2)]
    groups = groups + [bits[:1]] * (len(bits) % 2)
    gathers = [[groups[0][0], groups[0][-1] ^ 1]] + groups[1:]
    extra_lanes = -(-(2 * shapes + 16) // LANES) * LANES
    tuned = rows % 16 == 0 and 2 * shapes * len(masks_of(groups[0])) == LANES
    lanes = half + extra_lanes
    gain_row = gain.reshape(1, rows)

    def shape_of(rows, lanes, dtype):
        return jax.ShapeDtypeStruct((rows, lanes), dtype)

    held = small_kernel(
        "prep",
        functools.partial(prep_kernel, hid),
        shape_of(rows, lanes + half, BF16),
        *[
            pltpu.with_memory_space_constraint(x, pltpu.HBM)
            for x in (direction, gain_row, bias.reshape(1, rows), codes)
        ],
        scratch=[
            VMEM((rows, cols), F32),
            VMEM((1, rows), F32),
            VMEM((1, rows), F32),
            VMEM((shapes, half), F32),
            pltpu.SemaphoreType.DMA((4,)),
        ],
        space=pl.ANY,
    )
    tile, layer_tile = min(512, points), min(256, points)
    x, x_t = pl.pallas_call(
        functools.partial(inputs_kernel, hid, tile),
        out_shape=[
            shape_of(points, lanes, BF16),
            shape_of(half + shapes, points, BF16),
        ],
        in_specs=[pl.BlockSpec(memory_space=pl.ANY)] * 4,
        out_specs=vmem(2),
        scratch_shapes=[
            VMEM((points, hid), F32),
            VMEM((half - hid, points), F32),
            VMEM((1, points), jnp.int32),
            VMEM((1, points), jnp.int32),
            pltpu.SemaphoreType.DMA((points // tile + 3,)),
        ],
        compiler_params=pltpu.CompilerParams(vmem_limit_bytes=12 * MIB),
        cost_estimate=pl.CostEstimate(
            flops=4000 * MIB, bytes_accessed=8 * points * half, transcendentals=0
        ),
        name="inputs",
    )(
        *[
            pltpu.with_memory_space_constraint(a, pltpu.HBM)
            for a in (
                hidden,
                offsets.T,
                shape_ids.reshape(1, points),
                scale_index.reshape(1, points),
            )
        ]
    )
    def gather(array, group):
        masks = masks_of(group)[1:]
        return [array] + swaps([array] * len(masks), masks, devices)

    def join(arrays, *widths, early=()):
        height = sum(a.shape[0] for a in arrays)
        return small_kernel(
            "join",
            functools.partial(join_kernel, len(arrays), len(early)),
            [shape_of(height, width, BF16) for width in widths],
            *arrays[::-1],
            *early,
        )

    if tuned:
        arrays = gather(held, gathers[0])
        weight, code_weight = small_kernel(
            "pack",
            functools.partial(pack_kernel, shapes),
            [
                shape_of((half // LANES * len(arrays) + 1) * rows, LANES, BF16),
                shape_of(len(arrays) * rows, half, BF16),
            ],
            *[arrays[k] for k in FIRST],
        )
        weight, code_weight, x, x_t = lax.optimization_barrier((weight, code_weight, x, x_t))
        (weights,) = [gather(weight, group) for group in gathers[1:-1]]
        along, across = [[bit] for bit in gathers[1][::-1]]
        code_weights = gather(code_weight, along)
        (weight,) = join(weights, LANES, early=(cotangent,))
        weights = gather(weight, gathers[-1])
        (code_weight,) = join(code_weights, half)
        *weights, code_weight = lax.optimization_barrier((*weights, code_weight))
        code_order = order_of([gathers[0], along, across])
        orders = [[m ^ r for r in order_of(gathers[:-1])] for m in masks_of(gathers[-1])]
        code_orders = [[m ^ r for r in code_order] for m in masks_of(gathers[-1])]
        parts = [[m ^ r for r in order_of(groups[:-1])] for m in masks_of(groups[-1])]
    else:
        held = lax.all_gather(held, AXES, axis=0, tiled=True)
        weights, code_weights, orders, code_orders, parts = [held[:, :lanes]], [held[:, lanes:]], None, None, [[0]]

    output, grad_hidden, *grads = pl.pallas_call(
        functools.partial(layer_kernel, hid, shapes, layer_tile, orders, parts),
        out_shape=[pltpu.HBM((points, width), F32), pltpu.VMEM((points, hid), F32)]
        + [shape_of(2 * shapes + width // len(parts), half, BF16)] * len(parts),
        in_specs=vmem(len(weights) + 3),
        out_specs=[pl.BlockSpec(memory_space=pltpu.HBM)] + vmem(1 + len(parts)),
        scratch_shapes=[
            VMEM((width, lanes), BF16),
            VMEM((width, half), F32),
            VMEM((points, width), F32),
            VMEM((points, width), BF16),
            VMEM((2, layer_tile, width), F32),
            pltpu.SemaphoreType.DMA((points // layer_tile,)),
        ],
        compiler_params=pltpu.CompilerParams(vmem_limit_bytes=20 * MIB),
        cost_estimate=pl.CostEstimate(
            flops=6 * points * width * cols,
            bytes_accessed=8 * points * (width + half),
            transcendentals=points * width,
        ),
        name="layer",
    )(*weights, x, x_t, cotangent)

    stored = pl.pallas_call(
        store_kernel,
        out_shape=pltpu.HBM((points, hid), F32),
        in_specs=vmem(1),
        out_specs=pl.BlockSpec(memory_space=pltpu.HBM),
        scratch_shapes=[pltpu.SemaphoreType.DMA(())],
        compiler_params=pltpu.CompilerParams(vmem_limit_bytes=8 * MIB),
        cost_estimate=pl.CostEstimate(
            flops=4000 * MIB, bytes_accessed=8 * points * hid, transcendentals=0
        ),
        name="store",
    )

    if tuned:
        for r, group in enumerate(groups[::-1]):
            masks = masks_of(group)
            grads = [grads[0]] + swaps(grads[1:], masks[1:], devices)
            if r == len(groups) - 1:
                break
            n_out = len(masks_of(groups[-2 - r]))
            left = (grads[0].shape[0] - 2 * shapes) // n_out
            grads = small_kernel(
                "add",
                functools.partial(add_kernel, shapes, len(grads)),
                [shape_of(2 * shapes + left, half, BF16)] * n_out,
                *(grads[::-1] if r == 0 else [grads[k] for k in SUMS]),
            )
            if r == 0:
                *grads, grad_hidden = lax.optimization_barrier((*grads, grad_hidden))
                grad_hidden = stored(grad_hidden)
                grad_hidden, code_weight = lax.optimization_barrier((grad_hidden, code_weight))
                code_weights = gather(code_weight, across)
            if r == len(groups) - 2:
                *grads, grad_hidden = lax.optimization_barrier((*grads, grad_hidden))
        (code_weight,) = join(code_weights, half)
        code_weights = gather(code_weight, groups[-1])
    else:
        grad_hidden = stored(grad_hidden)
        sums = lax.psum(grads[0][: 2 * shapes].astype(F32), AXES)
        high = sums.astype(BF16)
        own = lax.psum_scatter(grads[0][2 * shapes :].astype(F32), AXES, scatter_dimension=0, tiled=True)
        low = jnp.zeros((2 * shapes + rows, half), BF16).at[: 2 * shapes].set((sums - high).astype(BF16))
        grads = [jnp.concatenate([high, own.astype(BF16)], axis=0), low]
    grad_codes, grad_direction, grad_gain, grad_bias = small_kernel(
        "last",
        functools.partial(last_kernel, hid, shapes, code_orders, len(grads)),
        [
            shape_of(shapes, half, F32),
            shape_of(rows, cols, F32),
            shape_of(1, rows, F32),
            shape_of(1, rows, F32),
        ],
        *grads[::-1],
        direction,
        gain_row,
        codes,
        *code_weights,
        scratch=[VMEM((width, half), BF16)],
    )

    total = float(points * devices)
    batch_mean = jnp.mean(codes, axis=0)
    batch_square = jnp.mean(codes * codes, axis=0)
    batch_var = (batch_square - batch_mean * batch_mean) * (total / (total - 1.0))
    new_mean = 0.9 * running_mean + 0.1 * batch_mean
    new_var = 0.9 * running_var + 0.1 * batch_var
    return (
        output,
        grad_hidden,
        grad_codes,
        grad_direction,
        grad_gain.reshape(rows),
        grad_bias.reshape(rows),
        new_mean,
        new_var,
    )


def solution(mesh):
    return jax.shard_map(
        per_device,
        mesh=mesh,
        in_specs=(
            P(("dp", "inner"), None),
            P(),
            P(("dp", "inner"), None),
            P(("dp", "inner")),
            P(("dp", "inner")),
            P(("dp", "inner"), None),
            P(("dp", "inner")),
            P(("dp", "inner")),
            P(("dp", "inner"), None),
            P(),
            P(),
        ),
        out_specs=(
            P(("dp", "inner"), None),
            P(("dp", "inner"), None),
            P(),
            P(("dp", "inner"), None),
            P(("dp", "inner")),
            P(("dp", "inner")),
            P(),
            P(),
        ),
        check_vma=False,
    )
```

```python
import functools

import jax
import jax.numpy as jnp
from jax import lax
from jax.experimental import pallas as pl
from jax.experimental.pallas import tpu as pltpu
from jax.sharding import PartitionSpec as P

AXES = ("dp", "inner")
LANES = 128
MIB = 1024 * 1024
FIRST = (2, 3, 1, 0)
SUMS = (1, 3, 2, 0)
F32 = jnp.float32
BF16 = jnp.bfloat16
VMEM = pltpu.VMEM
NT = (((1,), (1,)), ((), ()))


def dot(a, b, dims=(((1,), (0,)), ((), ()))):
    return lax.dot_general(a, b, dims, preferred_element_type=F32)


def vmem(n):
    return [pl.BlockSpec(memory_space=VMEM)] * n


def small_kernel(name, body, out_shape, *args, scratch=(), space=VMEM, limit=8):
    many = isinstance(out_shape, list)
    return pl.pallas_call(
        body,
        out_shape=out_shape,
        in_specs=[pl.BlockSpec(memory_space=space)] * len(args),
        out_specs=vmem(len(out_shape)) if many else vmem(1)[0],
        scratch_shapes=list(scratch),
        compiler_params=pltpu.CompilerParams(vmem_limit_bytes=limit * MIB),
        cost_estimate=pl.CostEstimate(
            flops=4000 * MIB, bytes_accessed=8 * MIB, transcendentals=4 * MIB
        ),
        name=name,
    )(*args)


def diagonal(n):
    return lax.broadcasted_iota(jnp.int32, (n, n), 0) == lax.broadcasted_iota(jnp.int32, (n, n), 1)


def to_column(row):
    n = row.shape[1]
    return jnp.sum(jnp.where(diagonal(n), row, 0.0), axis=1, keepdims=True)


def to_row(column):
    n = column.shape[0]
    return jnp.sum(jnp.where(diagonal(n), column, 0.0), axis=0, keepdims=True)


def stacked_codes(codes_ref, count):
    codes = codes_ref[...].astype(BF16)
    parts = [codes, codes]
    if count > 2 * codes.shape[0]:
        parts.append(jnp.zeros((count - 2 * codes.shape[0], codes.shape[1]), BF16))
    return jnp.concatenate(parts, axis=0)


def split(x):
    high = x.astype(BF16).astype(F32)
    return high, x - high


def prep_kernel(hid, *refs):
    piece_ref, direction_ref, gain_ref, bias_ref, codes_ref, sems = refs[4:]
    copies = [
        pltpu.make_async_copy(source, target, sems.at[k])
        for k, (source, target) in enumerate(zip(refs[:4], refs[5:9]))
    ]
    for copy in copies:
        copy.start()
    for copy in copies:
        copy.wait()
    d = direction_ref[...]
    shapes = codes_ref.shape[0]
    rows, cols = d.shape
    half = cols // 2
    extra_lanes = piece_ref.shape[1] - cols
    inverse = lax.rsqrt(jnp.sum(d * d, axis=1, keepdims=True))
    w = to_column(gain_ref[...]) * (d * inverse)
    lane = lax.broadcasted_iota(jnp.int32, (rows, half), 1)
    first = jnp.where(lane < hid, w[:, :half], w[:, half:])
    code = pltpu.roll(w, half - hid, 1)[:, half:].astype(BF16)
    bias = to_column(bias_ref[...]).astype(BF16).astype(F32)
    high, low = split(dot(code, stacked_codes(codes_ref, extra_lanes), NT) + bias)
    own = first[:, half - LANES :]
    if extra_lanes > LANES:
        own = jnp.concatenate([jnp.zeros((rows, extra_lanes - LANES), F32), own], axis=1)
    lane = lax.broadcasted_iota(jnp.int32, (rows, extra_lanes), 1)
    table = jnp.where(lane < shapes, high, jnp.where(lane < 2 * shapes, low, 0.0))
    table = jnp.where(lane >= extra_lanes - (half - hid), own, table)
    piece_ref[:, :half] = first.astype(BF16)
    piece_ref[:, half : half + extra_lanes] = table.astype(BF16)
    piece_ref[:, half + extra_lanes :] = code


def join_kernel(n, n_early, *refs):
    rows = refs[0].shape[0]
    for k, ref in enumerate(refs[n - 1 :: -1]):
        lane = 0
        for out_ref in refs[n + n_early :]:
            lanes = out_ref.shape[1]
            out_ref[k * rows : (k + 1) * rows, :] = ref[:, lane : lane + lanes]
            lane += lanes


def pack_kernel(shapes, *refs):
    weight_ref, code_ref = refs[-2:]
    count = len(refs) - 2
    rows, half = refs[0].shape[0], code_ref.shape[1]
    products = jnp.zeros((rows, LANES), F32)
    for k, ref in zip(FIRST, refs):
        for block in range(half // LANES):
            at = (block * count + k) * rows
            weight_ref[at : at + rows, :] = ref[:, block * LANES : (block + 1) * LANES]
        own = ref[:, half : half + LANES].astype(F32)
        own = jnp.where(lax.broadcasted_iota(jnp.int32, own.shape, 1) < 2 * shapes, own, 0.0)
        products = products + (pltpu.roll(own, 2 * shapes * k, 1) if k else own)
        code_ref[k * rows : (k + 1) * rows, :] = ref[:, half + LANES :]
    weight_ref[half // LANES * count * rows :, :] = products.astype(BF16)


def unpack(hid, shapes, refs, orders, me, w_ref):
    count = LANES // (2 * shapes)
    half = w_ref.shape[1] - LANES
    blocks = half // LANES
    for ref, order in zip(refs, orders):
        height = ref.shape[0] // (len(order) // count)
        rows = height // (blocks * count + 1)
        lane = lax.broadcasted_iota(jnp.int32, (rows, LANES), 1)
        for j, mask in enumerate(order):
            start, k = j // count * height, j % count
            at = pl.ds(pl.multiple_of((me ^ mask) * rows, rows), rows)
            for block in range(blocks):
                here = start + (block * count + k) * rows
                part = ref[here : here + rows, :]
                w_ref[at, block * LANES : (block + 1) * LANES] = part
            here = start + blocks * count * rows
            products = ref[here : here + rows, :].astype(F32)
            if k:
                products = pltpu.roll(products, LANES - 2 * shapes * k, 1)
            products = jnp.where(lane < 2 * shapes, products, 0.0)
            products = jnp.where(lane >= LANES - (half - hid), part.astype(F32), products)
            w_ref[at, half:] = products.astype(BF16)


def place(refs, orders, me, out_ref):
    if orders is None:
        out_ref[...] = refs[0][...]
        return
    rows = refs[0].shape[0] // len(orders[0])
    for ref, order in zip(refs, orders):
        for k, mask in enumerate(order):
            at = pl.multiple_of((me ^ mask) * rows, rows)
            out_ref[pl.ds(at, rows), :] = ref[k * rows : (k + 1) * rows, :]


def inputs_kernel(hid, tile, *refs):
    x_ref, x_t_ref, hidden_ref, offsets_ref, ids_ref, scale_ref, sems = refs[4:]
    points = x_ref.shape[0]
    half = (hid + LANES - 1) // LANES * LANES
    shapes = x_t_ref.shape[0] - half
    extra_lanes = x_ref.shape[1] - half
    steps = points // tile
    small = [
        pltpu.make_async_copy(source, target, sems.at[steps + k])
        for k, (source, target) in enumerate(zip(refs[1:4], (offsets_ref, ids_ref, scale_ref)))
    ]
    large = [
        pltpu.make_async_copy(
            refs[0].at[pl.ds(k * tile, tile), :], hidden_ref.at[pl.ds(k * tile, tile), :], sems.at[k]
        )
        for k in range(steps)
    ]
    for copy in small + large:
        copy.start()
    for copy in small:
        copy.wait()
    for step, copy in enumerate(large):
        here = slice(step * tile, (step + 1) * tile)
        scale = scale_ref[:, here]
        jitter = jnp.where(scale == 0, 1.0, jnp.where(scale == 1, 0.5, 0.25))
        xyz = offsets_ref[:, here] * jitter
        row = lax.broadcasted_iota(jnp.int32, (16, tile), 0)
        last = jnp.zeros((16, tile), F32)
        for k in range(half - hid):
            last = jnp.where(row == 16 - (half - hid) + k, xyz[k : k + 1], last)
        last = last.astype(BF16)
        row = lax.broadcasted_iota(jnp.int32, (extra_lanes - 16, tile), 0)
        ids = ids_ref[:, here]
        member = jnp.where((row == ids) | (row == ids + shapes), 1.0, 0.0).astype(BF16)
        x_ref[here, half:] = jnp.concatenate([member, last], axis=0).T
        x_t_ref[half:, here] = member[:shapes]
        copy.wait()
        x_ref[here, half - LANES : half] = jnp.zeros((tile, LANES), BF16)
        x_ref[here, :hid] = hidden_ref[here, :].astype(BF16)
        hidden = x_ref[here, :half].T
        x_t_ref[: half - 16, here] = hidden[: half - 16]
        x_t_ref[half - 16 : half, here] = hidden[half - 16 :] + last


def layer_kernel(hid, shapes, tile, orders, parts, *refs):
    n = 1 if orders is None else len(orders)
    pieces = refs[:n]
    x_ref, x_t_ref, cot_ref, out_hbm, grad_hidden_ref = refs[n : n + 5]
    grad_refs = refs[n + 5 : -6]
    w_ref, w_t_ref, turned_ref, out_ref, grad_pre_ref, pre_ref, sems = refs[-7:]
    points, width = cot_ref.shape
    half = width // 2
    steps = points // tile
    me = lax.axis_index(AXES)
    if orders is None:
        place(pieces, orders, me, w_ref)
    else:
        unpack(hid, shapes, pieces, orders, me, w_ref)
    w_t_ref[...] = w_ref[...].T
    copies = []

    def rows_of(step):
        return slice(step * tile, (step + 1) * tile)

    def forward(step):
        pre_ref[step % 2] = dot(x_ref[rows_of(step), :], w_t_ref[...])

    def middle(step):
        here = rows_of(step)
        pre = pre_ref[step % 2]
        sigma = 0.5 * jnp.tanh(0.5 * pre) + 0.5
        out = pre * sigma
        out_ref[here, :] = out
        grad_pre_ref[here, :] = (cot_ref[here, :] * (sigma * (1.0 + (pre - out)))).astype(BF16)

    def backward(step):
        here = rows_of(step)
        grad_hidden_ref[here, :] = dot(grad_pre_ref[here, :], w_ref[:, :half])[:, :hid]

    def store(step):
        here = pl.ds(step * tile, tile)
        copy = pltpu.make_async_copy(out_ref.at[here, :], out_hbm.at[here, :], sems.at[step])
        copy.start()
        copies.append(copy)

    forward(0)
    for step in range(steps):
        if step + 1 < steps:
            forward(step + 1)
        middle(step)
        if step > 0:
            backward(step - 1)
        store(step)
    backward(steps - 1)
    grad = dot(x_t_ref[...], grad_pre_ref[...])
    sums = grad[half:].astype(BF16)
    for at in range(0, width, half):
        turned_ref[at : at + half, :] = grad[:half, at : at + half].T
    for ref, order in zip(grad_refs, parts):
        ref[:shapes, :] = sums[:, :half]
        ref[shapes : 2 * shapes, :] = sums[:, half:]
        if orders is None:
            ref[2 * shapes :, :] = turned_ref[...].astype(BF16)
            continue
        rows = (ref.shape[0] - 2 * shapes) // len(order)
        for k, mask in enumerate(order):
            at = pl.multiple_of((me ^ mask) * rows, rows)
            to = 2 * shapes + k * rows
            ref[to : to + rows, :] = turned_ref[pl.ds(at, rows), :].astype(BF16)

    for copy in copies:
        copy.wait()


def store_kernel(source_ref, target_ref, sem):
    copy = pltpu.make_async_copy(source_ref, target_ref, sem)
    copy.start()
    copy.wait()


def sum_of(refs):
    terms = [ref[...].astype(F32) for ref in refs]
    while len(terms) > 1:
        terms = [a + b for a, b in zip(terms[::2], terms[1::2])]
    return terms[0]


def add_kernel(shapes, n, *refs):
    total = sum_of(refs[:n]).astype(BF16)
    for k, ref in enumerate(refs[n:]):
        rows = ref.shape[0] - 2 * shapes
        at = 2 * shapes + k * rows
        ref[: 2 * shapes, :] = total[: 2 * shapes]
        ref[2 * shapes :, :] = total[at : at + rows]


def last_kernel(hid, shapes, orders, n, *refs):
    direction_ref, gain_ref, codes_ref = refs[n : n + 3]
    pieces = refs[n + 3 : -5]
    grad_codes_ref, grad_direction_ref, grad_gain_ref, grad_bias_ref, code_scratch = refs[-5:]
    d = direction_ref[...]
    rows, cols = d.shape
    half = cols // 2
    me = lax.axis_index(AXES)
    place(pieces, orders, me, code_scratch)
    total = sum_of(refs[:n])
    sums = jnp.concatenate([total[:shapes], total[shapes : 2 * shapes]], axis=1)
    sums = jnp.concatenate(split(sums), axis=0).astype(BF16)
    terms = dot(sums, code_scratch[...])
    grad_codes_ref[...] = terms[:shapes] + terms[shapes:]
    width = sums.shape[1]
    mine = lax.broadcasted_iota(jnp.int32, (rows, width), 0) + me * rows
    mine = jnp.where(mine == lax.broadcasted_iota(jnp.int32, (rows, width), 1), 1.0, 0.0).astype(BF16)
    own = dot(mine, sums, NT)
    grad_bias_ref[...] = to_row(jnp.sum(own, axis=1, keepdims=True))
    code = dot(own.astype(BF16), stacked_codes(codes_ref, 2 * shapes))
    packed = jnp.concatenate([total[2 * shapes :], code], axis=1)
    lane = lax.broadcasted_iota(jnp.int32, (rows, cols), 1)
    grad_weight = jnp.where(
        lane < hid,
        packed,
        jnp.where(lane < hid + half, pltpu.roll(packed, cols - (half - hid), 1), pltpu.roll(packed, half, 1)),
    )
    inverse = lax.rsqrt(jnp.sum(d * d, axis=1, keepdims=True))
    unit = d * inverse
    grad_gain = jnp.sum(grad_weight * unit, axis=1, keepdims=True)
    grad_gain_ref[...] = to_row(grad_gain)
    grad_direction_ref[...] = (to_column(gain_ref[...]) * inverse) * (grad_weight - grad_gain * unit)


def masks_of(group):
    masks = [0]
    for bit in group:
        masks = masks + [m ^ bit for m in masks]
    return masks


def order_of(groups):
    order = [0]
    for group in groups:
        order = [m ^ r for m in masks_of(group) for r in order]
    return order


def swaps(arrays, masks, devices):
    moved = [
        lax.ppermute(x, AXES, [(i, i ^ mask) for i in range(devices)])
        for x, mask in list(zip(arrays, masks))[::-1]
    ]
    return moved[::-1]


def per_device(
    hidden,
    codes,
    offsets,
    shape_ids,
    scale_index,
    direction,
    gain,
    bias,
    cotangent,
    running_mean,
    running_var,
):
    points, hid = hidden.shape
    shapes = codes.shape[0]
    rows, cols = direction.shape
    width = cotangent.shape[1]
    half = cols // 2
    devices = lax.axis_size("dp") * lax.axis_size("inner")
    bits = [1 << k | 1 for k in range(devices.bit_length() - 1)]
    groups = [bits[k - 2 : k] for k in range(len(bits), 1, -2)]
    groups = groups + [bits[:1]] * (len(bits) % 2)
    gathers = [[groups[0][0], groups[0][-1] ^ 1]] + groups[1:]
    extra_lanes = -(-(2 * shapes + 16) // LANES) * LANES
    tuned = rows % 16 == 0 and 2 * shapes * len(masks_of(groups[0])) == LANES
    lanes = half + extra_lanes
    gain_row = gain.reshape(1, rows)

    def shape_of(rows, lanes, dtype):
        return jax.ShapeDtypeStruct((rows, lanes), dtype)

    held = small_kernel(
        "prep",
        functools.partial(prep_kernel, hid),
        shape_of(rows, lanes + half, BF16),
        *[
            pltpu.with_memory_space_constraint(x, pltpu.HBM)
            for x in (direction, gain_row, bias.reshape(1, rows), codes)
        ],
        scratch=[
            VMEM((rows, cols), F32),
            VMEM((1, rows), F32),
            VMEM((1, rows), F32),
            VMEM((shapes, half), F32),
            pltpu.SemaphoreType.DMA((4,)),
        ],
        space=pl.ANY,
    )
    tile, layer_tile = min(512, points), min(256, points)
    x, x_t = pl.pallas_call(
        functools.partial(inputs_kernel, hid, tile),
        out_shape=[
            shape_of(points, lanes, BF16),
            shape_of(half + shapes, points, BF16),
        ],
        in_specs=[pl.BlockSpec(memory_space=pl.ANY)] * 4,
        out_specs=vmem(2),
        scratch_shapes=[
            VMEM((points, hid), F32),
            VMEM((half - hid, points), F32),
            VMEM((1, points), jnp.int32),
            VMEM((1, points), jnp.int32),
            pltpu.SemaphoreType.DMA((points // tile + 3,)),
        ],
        compiler_params=pltpu.CompilerParams(vmem_limit_bytes=12 * MIB),
        cost_estimate=pl.CostEstimate(
            flops=4000 * MIB, bytes_accessed=8 * points * half, transcendentals=0
        ),
        name="inputs",
    )(
        *[
            pltpu.with_memory_space_constraint(a, pltpu.HBM)
            for a in (
                hidden,
                offsets.T,
                shape_ids.reshape(1, points),
                scale_index.reshape(1, points),
            )
        ]
    )
    def gather(array, group):
        masks = masks_of(group)[1:]
        return [array] + swaps([array] * len(masks), masks, devices)

    def join(arrays, *widths, early=()):
        height = sum(a.shape[0] for a in arrays)
        return small_kernel(
            "join",
            functools.partial(join_kernel, len(arrays), len(early)),
            [shape_of(height, width, BF16) for width in widths],
            *arrays[::-1],
            *early,
        )

    if tuned:
        arrays = gather(held, gathers[0])
        weight, code_weight = small_kernel(
            "pack",
            functools.partial(pack_kernel, shapes),
            [
                shape_of((half // LANES * len(arrays) + 1) * rows, LANES, BF16),
                shape_of(len(arrays) * rows, half, BF16),
            ],
            *[arrays[k] for k in FIRST],
        )
        weight, code_weight, x, x_t = lax.optimization_barrier((weight, code_weight, x, x_t))
        (weights,) = [gather(weight, group) for group in gathers[1:-1]]
        along, across = [[bit] for bit in gathers[1][::-1]]
        code_weights = gather(code_weight, along)
        (weight,) = join(weights, LANES, early=(cotangent,))
        weights = gather(weight, gathers[-1])
        (code_weight,) = join(code_weights, half)
        *weights, code_weight = lax.optimization_barrier((*weights, code_weight))
        code_order = order_of([gathers[0], along, across])
        orders = [[m ^ r for r in order_of(gathers[:-1])] for m in masks_of(gathers[-1])]
        code_orders = [[m ^ r for r in code_order] for m in masks_of(gathers[-1])]
        parts = [[m ^ r for r in order_of(groups[:-1])] for m in masks_of(groups[-1])]
    else:
        held = lax.all_gather(held, AXES, axis=0, tiled=True)
        weights, code_weights, orders, code_orders, parts = [held[:, :lanes]], [held[:, lanes:]], None, None, [[0]]

    output, grad_hidden, *grads = pl.pallas_call(
        functools.partial(layer_kernel, hid, shapes, layer_tile, orders, parts),
        out_shape=[pltpu.HBM((points, width), F32), pltpu.VMEM((points, hid), F32)]
        + [shape_of(2 * shapes + width // len(parts), half, BF16)] * len(parts),
        in_specs=vmem(len(weights) + 3),
        out_specs=[pl.BlockSpec(memory_space=pltpu.HBM)] + vmem(1 + len(parts)),
        scratch_shapes=[
            VMEM((width, lanes), BF16),
            VMEM((lanes, width), BF16),
            VMEM((width, half), F32),
            VMEM((points, width), F32),
            VMEM((points, width), BF16),
            VMEM((2, layer_tile, width), F32),
            pltpu.SemaphoreType.DMA((points // layer_tile,)),
        ],
        compiler_params=pltpu.CompilerParams(vmem_limit_bytes=20 * MIB),
        cost_estimate=pl.CostEstimate(
            flops=6 * points * width * cols,
            bytes_accessed=8 * points * (width + half),
            transcendentals=points * width,
        ),
        name="layer",
    )(*weights, x, x_t, cotangent)

    stored = pl.pallas_call(
        store_kernel,
        out_shape=pltpu.HBM((points, hid), F32),
        in_specs=vmem(1),
        out_specs=pl.BlockSpec(memory_space=pltpu.HBM),
        scratch_shapes=[pltpu.SemaphoreType.DMA(())],
        compiler_params=pltpu.CompilerParams(vmem_limit_bytes=8 * MIB),
        cost_estimate=pl.CostEstimate(
            flops=4000 * MIB, bytes_accessed=8 * points * hid, transcendentals=0
        ),
        name="store",
    )

    if tuned:
        for r, group in enumerate(groups[::-1]):
            masks = masks_of(group)
            grads = [grads[0]] + swaps(grads[1:], masks[1:], devices)
            if r == len(groups) - 1:
                break
            n_out = len(masks_of(groups[-2 - r]))
            left = (grads[0].shape[0] - 2 * shapes) // n_out
            grads = small_kernel(
                "add",
                functools.partial(add_kernel, shapes, len(grads)),
                [shape_of(2 * shapes + left, half, BF16)] * n_out,
                *(grads[::-1] if r == 0 else [grads[k] for k in SUMS]),
            )
            if r == 0:
                *grads, grad_hidden = lax.optimization_barrier((*grads, grad_hidden))
                grad_hidden = stored(grad_hidden)
                grad_hidden, code_weight = lax.optimization_barrier((grad_hidden, code_weight))
                code_weights = gather(code_weight, across)
            if r == len(groups) - 2:
                *grads, grad_hidden = lax.optimization_barrier((*grads, grad_hidden))
        (code_weight,) = join(code_weights, half)
        code_weights = gather(code_weight, groups[-1])
    else:
        grad_hidden = stored(grad_hidden)
        sums = lax.psum(grads[0][: 2 * shapes].astype(F32), AXES)
        high = sums.astype(BF16)
        own = lax.psum_scatter(grads[0][2 * shapes :].astype(F32), AXES, scatter_dimension=0, tiled=True)
        low = jnp.zeros((2 * shapes + rows, half), BF16).at[: 2 * shapes].set((sums - high).astype(BF16))
        grads = [jnp.concatenate([high, own.astype(BF16)], axis=0), low]
    grad_codes, grad_direction, grad_gain, grad_bias = small_kernel(
        "last",
        functools.partial(last_kernel, hid, shapes, code_orders, len(grads)),
        [
            shape_of(shapes, half, F32),
            shape_of(rows, cols, F32),
            shape_of(1, rows, F32),
            shape_of(1, rows, F32),
        ],
        *grads[::-1],
        direction,
        gain_row,
        codes,
        *code_weights,
        scratch=[VMEM((width, half), BF16)],
    )

    total = float(points * devices)
    batch_mean = jnp.mean(codes, axis=0)
    batch_square = jnp.mean(codes * codes, axis=0)
    batch_var = (batch_square - batch_mean * batch_mean) * (total / (total - 1.0))
    new_mean = 0.9 * running_mean + 0.1 * batch_mean
    new_var = 0.9 * running_var + 0.1 * batch_var
    return (
        output,
        grad_hidden,
        grad_codes,
        grad_direction,
        grad_gain.reshape(rows),
        grad_bias.reshape(rows),
        new_mean,
        new_var,
    )


def solution(mesh):
    return jax.shard_map(
        per_device,
        mesh=mesh,
        in_specs=(
            P(("dp", "inner"), None),
            P(),
            P(("dp", "inner"), None),
            P(("dp", "inner")),
            P(("dp", "inner")),
            P(("dp", "inner"), None),
            P(("dp", "inner")),
            P(("dp", "inner")),
            P(("dp", "inner"), None),
            P(),
            P(),
        ),
        out_specs=(
            P(("dp", "inner"), None),
            P(("dp", "inner"), None),
            P(),
            P(("dp", "inner"), None),
            P(("dp", "inner")),
            P(("dp", "inner")),
            P(),
            P(),
        ),
        check_vma=False,
    )
```

```python
import functools

import jax
import jax.numpy as jnp
from jax import lax
from jax.experimental import pallas as pl
from jax.experimental.pallas import tpu as pltpu
from jax.sharding import PartitionSpec as P

AXES = ("dp", "inner")
LANES = 128
MIB = 1024 * 1024
FIRST = (2, 3, 1, 0)
SUMS = (1, 3, 2, 0)
F32 = jnp.float32
BF16 = jnp.bfloat16
VMEM = pltpu.VMEM
NT = (((1,), (1,)), ((), ()))


def dot(a, b, dims=(((1,), (0,)), ((), ()))):
    return lax.dot_general(a, b, dims, preferred_element_type=F32)


def vmem(n):
    return [pl.BlockSpec(memory_space=VMEM)] * n


def small_kernel(name, body, out_shape, *args, scratch=(), space=VMEM, limit=8):
    many = isinstance(out_shape, list)
    return pl.pallas_call(
        body,
        out_shape=out_shape,
        in_specs=[pl.BlockSpec(memory_space=space)] * len(args),
        out_specs=vmem(len(out_shape)) if many else vmem(1)[0],
        scratch_shapes=list(scratch),
        compiler_params=pltpu.CompilerParams(vmem_limit_bytes=limit * MIB),
        cost_estimate=pl.CostEstimate(
            flops=4000 * MIB, bytes_accessed=8 * MIB, transcendentals=4 * MIB
        ),
        name=name,
    )(*args)


def diagonal(n):
    return lax.broadcasted_iota(jnp.int32, (n, n), 0) == lax.broadcasted_iota(jnp.int32, (n, n), 1)


def to_column(row):
    n = row.shape[1]
    return jnp.sum(jnp.where(diagonal(n), row, 0.0), axis=1, keepdims=True)


def to_row(column):
    n = column.shape[0]
    return jnp.sum(jnp.where(diagonal(n), column, 0.0), axis=0, keepdims=True)


def stacked_codes(codes_ref, count):
    codes = codes_ref[...].astype(BF16)
    parts = [codes, codes]
    if count > 2 * codes.shape[0]:
        parts.append(jnp.zeros((count - 2 * codes.shape[0], codes.shape[1]), BF16))
    return jnp.concatenate(parts, axis=0)


def split(x):
    high = x.astype(BF16).astype(F32)
    return high, x - high


def prep_kernel(hid, *refs):
    piece_ref, direction_ref, gain_ref, bias_ref, codes_ref, sems = refs[4:]
    copies = [
        pltpu.make_async_copy(source, target, sems.at[k])
        for k, (source, target) in enumerate(zip(refs[:4], refs[5:9]))
    ]
    for copy in copies:
        copy.start()
    for copy in copies:
        copy.wait()
    d = direction_ref[...]
    shapes = codes_ref.shape[0]
    rows, cols = d.shape
    half = cols // 2
    extra_lanes = piece_ref.shape[1] - cols
    inverse = lax.rsqrt(jnp.sum(d * d, axis=1, keepdims=True))
    w = to_column(gain_ref[...]) * (d * inverse)
    lane = lax.broadcasted_iota(jnp.int32, (rows, half), 1)
    first = jnp.where(lane < hid, w[:, :half], w[:, half:])
    code = pltpu.roll(w, half - hid, 1)[:, half:].astype(BF16)
    bias = to_column(bias_ref[...]).astype(BF16).astype(F32)
    high, low = split(dot(code, stacked_codes(codes_ref, extra_lanes), NT) + bias)
    own = first[:, half - LANES :]
    if extra_lanes > LANES:
        own = jnp.concatenate([jnp.zeros((rows, extra_lanes - LANES), F32), own], axis=1)
    lane = lax.broadcasted_iota(jnp.int32, (rows, extra_lanes), 1)
    table = jnp.where(lane < shapes, high, jnp.where(lane < 2 * shapes, low, 0.0))
    table = jnp.where(lane >= extra_lanes - (half - hid), own, table)
    piece_ref[:, :half] = first.astype(BF16)
    piece_ref[:, half : half + extra_lanes] = table.astype(BF16)
    piece_ref[:, half + extra_lanes :] = code


def join_kernel(n, n_early, *refs):
    rows = refs[0].shape[0]
    for k, ref in enumerate(refs[n - 1 :: -1]):
        lane = 0
        for out_ref in refs[n + n_early :]:
            lanes = out_ref.shape[1]
            out_ref[k * rows : (k + 1) * rows, :] = ref[:, lane : lane + lanes]
            lane += lanes


def pack_kernel(shapes, *refs):
    weight_ref, code_ref = refs[-2:]
    count = len(refs) - 2
    rows, half = refs[0].shape[0], code_ref.shape[1]
    products = jnp.zeros((rows, LANES), F32)
    for k, ref in zip(FIRST, refs):
        for block in range(half // LANES):
            at = (block * count + k) * rows
            weight_ref[at : at + rows, :] = ref[:, block * LANES : (block + 1) * LANES]
        own = ref[:, half : half + LANES].astype(F32)
        own = jnp.where(lax.broadcasted_iota(jnp.int32, own.shape, 1) < 2 * shapes, own, 0.0)
        products = products + (pltpu.roll(own, 2 * shapes * k, 1) if k else own)
        code_ref[k * rows : (k + 1) * rows, :] = ref[:, half + LANES :]
    weight_ref[half // LANES * count * rows :, :] = products.astype(BF16)


def unpack(hid, shapes, refs, orders, me, w_ref):
    count = LANES // (2 * shapes)
    half = w_ref.shape[1] - LANES
    blocks = half // LANES
    for ref, order in zip(refs, orders):
        height = ref.shape[0] // (len(order) // count)
        rows = height // (blocks * count + 1)
        lane = lax.broadcasted_iota(jnp.int32, (rows, LANES), 1)
        for j, mask in enumerate(order):
            start, k = j // count * height, j % count
            at = pl.ds(pl.multiple_of((me ^ mask) * rows, rows), rows)
            for block in range(blocks):
                here = start + (block * count + k) * rows
                part = ref[here : here + rows, :]
                w_ref[at, block * LANES : (block + 1) * LANES] = part
            here = start + blocks * count * rows
            products = ref[here : here + rows, :].astype(F32)
            if k:
                products = pltpu.roll(products, LANES - 2 * shapes * k, 1)
            products = jnp.where(lane < 2 * shapes, products, 0.0)
            products = jnp.where(lane >= LANES - (half - hid), part.astype(F32), products)
            w_ref[at, half:] = products.astype(BF16)


def place(refs, orders, me, out_ref):
    if orders is None:
        out_ref[...] = refs[0][...]
        return
    rows = refs[0].shape[0] // len(orders[0])
    for ref, order in zip(refs, orders):
        for k, mask in enumerate(order):
            at = pl.multiple_of((me ^ mask) * rows, rows)
            out_ref[pl.ds(at, rows), :] = ref[k * rows : (k + 1) * rows, :]


def inputs_kernel(hid, tile, *refs):
    x_ref, x_t_ref, hidden_ref, offsets_ref, ids_ref, scale_ref, sems = refs[4:]
    points = x_ref.shape[0]
    half = (hid + LANES - 1) // LANES * LANES
    shapes = x_t_ref.shape[0] - half
    extra_lanes = x_ref.shape[1] - half
    steps = points // tile
    small = [
        pltpu.make_async_copy(source, target, sems.at[steps + k])
        for k, (source, target) in enumerate(zip(refs[1:4], (offsets_ref, ids_ref, scale_ref)))
    ]
    large = [
        pltpu.make_async_copy(
            refs[0].at[pl.ds(k * tile, tile), :], hidden_ref.at[pl.ds(k * tile, tile), :], sems.at[k]
        )
        for k in range(steps)
    ]
    for copy in small + large:
        copy.start()
    for copy in small:
        copy.wait()
    for step, copy in enumerate(large):
        here = slice(step * tile, (step + 1) * tile)
        scale = scale_ref[:, here]
        jitter = jnp.where(scale == 0, 1.0, jnp.where(scale == 1, 0.5, 0.25))
        xyz = offsets_ref[:, here] * jitter
        row = lax.broadcasted_iota(jnp.int32, (16, tile), 0)
        last = jnp.zeros((16, tile), F32)
        for k in range(half - hid):
            last = jnp.where(row == 16 - (half - hid) + k, xyz[k : k + 1], last)
        last = last.astype(BF16)
        row = lax.broadcasted_iota(jnp.int32, (extra_lanes - 16, tile), 0)
        ids = ids_ref[:, here]
        member = jnp.where((row == ids) | (row == ids + shapes), 1.0, 0.0).astype(BF16)
        x_ref[here, half:] = jnp.concatenate([member, last], axis=0).T
        x_t_ref[half:, here] = member[:shapes]
        copy.wait()
        x_ref[here, half - LANES : half] = jnp.zeros((tile, LANES), BF16)
        x_ref[here, :hid] = hidden_ref[here, :].astype(BF16)
        hidden = x_ref[here, :half].T
        x_t_ref[: half - 16, here] = hidden[: half - 16]
        x_t_ref[half - 16 : half, here] = hidden[half - 16 :] + last


def layer_kernel(hid, shapes, tile, orders, parts, *refs):
    n = 1 if orders is None else len(orders)
    pieces = refs[:n]
    x_ref, x_t_ref, cot_ref, out_hbm, tail_ref, grad_hidden_ref = refs[n : n + 6]
    grad_refs = refs[n + 6 : -6]
    w_ref, turned_ref, out_ref, grad_pre_ref, pre_ref, sems = refs[-6:]
    points, width = cot_ref.shape
    half = width // 2
    steps = points // tile
    head = out_ref.shape[0] // tile
    me = lax.axis_index(AXES)
    if orders is None:
        place(pieces, orders, me, w_ref)
    else:
        unpack(hid, shapes, pieces, orders, me, w_ref)
    copies = []

    def rows_of(step):
        return slice(step * tile, (step + 1) * tile)

    def forward(step):
        pre_ref[step % 2] = dot(x_ref[rows_of(step), :], w_ref[...], NT)

    def middle(step):
        here = rows_of(step)
        pre = pre_ref[step % 2]
        sigma = 0.5 * jnp.tanh(0.5 * pre) + 0.5
        out = pre * sigma
        if step < head:
            out_ref[here, :] = out
        else:
            tail_ref[rows_of(step - head), :] = out
        grad_pre_ref[here, :] = (cot_ref[here, :] * (sigma * (1.0 + (pre - out)))).astype(BF16)

    def backward(step):
        here = rows_of(step)
        grad_hidden_ref[here, :] = dot(grad_pre_ref[here, :], w_ref[:, :half])[:, :hid]

    def store(step):
        here = pl.ds(step * tile, tile)
        copy = pltpu.make_async_copy(out_ref.at[here, :], out_hbm.at[here, :], sems.at[step])
        copy.start()
        copies.append(copy)

    forward(0)
    for step in range(steps):
        if step + 1 < steps:
            forward(step + 1)
        middle(step)
        if step > 0:
            backward(step - 1)
        if step < head:
            store(step)
    backward(steps - 1)
    grad = dot(x_t_ref[...], grad_pre_ref[...])
    sums = grad[half:].astype(BF16)
    for at in range(0, width, half):
        turned_ref[at : at + half, :] = grad[:half, at : at + half].T
    for ref, order in zip(grad_refs, parts):
        ref[:shapes, :] = sums[:, :half]
        ref[shapes : 2 * shapes, :] = sums[:, half:]
        if orders is None:
            ref[2 * shapes :, :] = turned_ref[...].astype(BF16)
            continue
        rows = (ref.shape[0] - 2 * shapes) // len(order)
        for k, mask in enumerate(order):
            at = pl.multiple_of((me ^ mask) * rows, rows)
            to = 2 * shapes + k * rows
            ref[to : to + rows, :] = turned_ref[pl.ds(at, rows), :].astype(BF16)

    for copy in copies:
        copy.wait()


def store_kernel(source_ref, target_ref, sem):
    copy = pltpu.make_async_copy(source_ref, target_ref, sem)
    copy.start()
    copy.wait()


def tail_kernel(_, source_ref, target_ref, sem):
    points, rows = target_ref.shape[0], source_ref.shape[0]
    store_kernel(source_ref, target_ref.at[pl.ds(points - rows, rows), :], sem)


def sum_of(refs):
    terms = [ref[...].astype(F32) for ref in refs]
    while len(terms) > 1:
        terms = [a + b for a, b in zip(terms[::2], terms[1::2])]
    return terms[0]


def add_kernel(shapes, n, *refs):
    total = sum_of(refs[:n]).astype(BF16)
    for k, ref in enumerate(refs[n:]):
        rows = ref.shape[0] - 2 * shapes
        at = 2 * shapes + k * rows
        ref[: 2 * shapes, :] = total[: 2 * shapes]
        ref[2 * shapes :, :] = total[at : at + rows]


def last_kernel(hid, shapes, orders, n, *refs):
    direction_ref, gain_ref, codes_ref = refs[n : n + 3]
    pieces = refs[n + 3 : -5]
    grad_codes_ref, grad_direction_ref, grad_gain_ref, grad_bias_ref, code_scratch = refs[-5:]
    d = direction_ref[...]
    rows, cols = d.shape
    half = cols // 2
    me = lax.axis_index(AXES)
    place(pieces, orders, me, code_scratch)
    total = sum_of(refs[:n])
    sums = jnp.concatenate([total[:shapes], total[shapes : 2 * shapes]], axis=1)
    sums = jnp.concatenate(split(sums), axis=0).astype(BF16)
    terms = dot(sums, code_scratch[...])
    grad_codes_ref[...] = terms[:shapes] + terms[shapes:]
    width = sums.shape[1]
    mine = lax.broadcasted_iota(jnp.int32, (rows, width), 0) + me * rows
    mine = jnp.where(mine == lax.broadcasted_iota(jnp.int32, (rows, width), 1), 1.0, 0.0).astype(BF16)
    own = dot(mine, sums, NT)
    grad_bias_ref[...] = to_row(jnp.sum(own, axis=1, keepdims=True))
    code = dot(own.astype(BF16), stacked_codes(codes_ref, 2 * shapes))
    packed = jnp.concatenate([total[2 * shapes :], code], axis=1)
    lane = lax.broadcasted_iota(jnp.int32, (rows, cols), 1)
    grad_weight = jnp.where(
        lane < hid,
        packed,
        jnp.where(lane < hid + half, pltpu.roll(packed, cols - (half - hid), 1), pltpu.roll(packed, half, 1)),
    )
    inverse = lax.rsqrt(jnp.sum(d * d, axis=1, keepdims=True))
    unit = d * inverse
    grad_gain = jnp.sum(grad_weight * unit, axis=1, keepdims=True)
    grad_gain_ref[...] = to_row(grad_gain)
    grad_direction_ref[...] = (to_column(gain_ref[...]) * inverse) * (grad_weight - grad_gain * unit)


def masks_of(group):
    masks = [0]
    for bit in group:
        masks = masks + [m ^ bit for m in masks]
    return masks


def order_of(groups):
    order = [0]
    for group in groups:
        order = [m ^ r for m in masks_of(group) for r in order]
    return order


def swaps(arrays, masks, devices):
    moved = [
        lax.ppermute(x, AXES, [(i, i ^ mask) for i in range(devices)])
        for x, mask in list(zip(arrays, masks))[::-1]
    ]
    return moved[::-1]


def per_device(
    hidden,
    codes,
    offsets,
    shape_ids,
    scale_index,
    direction,
    gain,
    bias,
    cotangent,
    running_mean,
    running_var,
):
    points, hid = hidden.shape
    shapes = codes.shape[0]
    rows, cols = direction.shape
    width = cotangent.shape[1]
    half = cols // 2
    devices = lax.axis_size("dp") * lax.axis_size("inner")
    bits = [1 << k | 1 for k in range(devices.bit_length() - 1)]
    groups = [bits[k - 2 : k] for k in range(len(bits), 1, -2)]
    groups = groups + [bits[:1]] * (len(bits) % 2)
    gathers = [[groups[0][0], groups[0][-1] ^ 1]] + groups[1:]
    extra_lanes = -(-(2 * shapes + 16) // LANES) * LANES
    tuned = rows % 16 == 0 and 2 * shapes * len(masks_of(groups[0])) == LANES
    lanes = half + extra_lanes
    gain_row = gain.reshape(1, rows)

    def shape_of(rows, lanes, dtype):
        return jax.ShapeDtypeStruct((rows, lanes), dtype)

    held = small_kernel(
        "prep",
        functools.partial(prep_kernel, hid),
        shape_of(rows, lanes + half, BF16),
        *[
            pltpu.with_memory_space_constraint(x, pltpu.HBM)
            for x in (direction, gain_row, bias.reshape(1, rows), codes)
        ],
        scratch=[
            VMEM((rows, cols), F32),
            VMEM((1, rows), F32),
            VMEM((1, rows), F32),
            VMEM((shapes, half), F32),
            pltpu.SemaphoreType.DMA((4,)),
        ],
        space=pl.ANY,
    )
    tile, layer_tile = min(512, points), min(256, points)
    x, x_t = pl.pallas_call(
        functools.partial(inputs_kernel, hid, tile),
        out_shape=[
            shape_of(points, lanes, BF16),
            shape_of(half + shapes, points, BF16),
        ],
        in_specs=[pl.BlockSpec(memory_space=pl.ANY)] * 4,
        out_specs=vmem(2),
        scratch_shapes=[
            VMEM((points, hid), F32),
            VMEM((half - hid, points), F32),
            VMEM((1, points), jnp.int32),
            VMEM((1, points), jnp.int32),
            pltpu.SemaphoreType.DMA((points // tile + 3,)),
        ],
        compiler_params=pltpu.CompilerParams(vmem_limit_bytes=12 * MIB),
        cost_estimate=pl.CostEstimate(
            flops=4000 * MIB, bytes_accessed=8 * points * half, transcendentals=0
        ),
        name="inputs",
    )(
        *[
            pltpu.with_memory_space_constraint(a, pltpu.HBM)
            for a in (
                hidden,
                offsets.T,
                shape_ids.reshape(1, points),
                scale_index.reshape(1, points),
            )
        ]
    )
    def gather(array, group):
        masks = masks_of(group)[1:]
        return [array] + swaps([array] * len(masks), masks, devices)

    def join(arrays, *widths, early=()):
        height = sum(a.shape[0] for a in arrays)
        return small_kernel(
            "join",
            functools.partial(join_kernel, len(arrays), len(early)),
            [shape_of(height, width, BF16) for width in widths],
            *arrays[::-1],
            *early,
        )

    if tuned:
        arrays = gather(held, gathers[0])
        weight, code_weight = small_kernel(
            "pack",
            functools.partial(pack_kernel, shapes),
            [
                shape_of((half // LANES * len(arrays) + 1) * rows, LANES, BF16),
                shape_of(len(arrays) * rows, half, BF16),
            ],
            *[arrays[k] for k in FIRST],
        )
        weight, code_weight, x, x_t = lax.optimization_barrier((weight, code_weight, x, x_t))
        (weights,) = [gather(weight, group) for group in gathers[1:-1]]
        along, across = [[bit] for bit in gathers[1][::-1]]
        code_weights = gather(code_weight, along)
        (weight,) = join(weights, LANES, early=(cotangent,))
        weights = gather(weight, gathers[-1])
        (code_weight,) = join(code_weights, half)
        *weights, code_weight = lax.optimization_barrier((*weights, code_weight))
        code_order = order_of([gathers[0], along, across])
        orders = [[m ^ r for r in order_of(gathers[:-1])] for m in masks_of(gathers[-1])]
        code_orders = [[m ^ r for r in code_order] for m in masks_of(gathers[-1])]
        parts = [[m ^ r for r in order_of(groups[:-1])] for m in masks_of(groups[-1])]
    else:
        held = lax.all_gather(held, AXES, axis=0, tiled=True)
        weights, code_weights, orders, code_orders, parts = [held[:, :lanes]], [held[:, lanes:]], None, None, [[0]]

    head = points // layer_tile // 2 * layer_tile
    output, tail, grad_hidden, *grads = pl.pallas_call(
        functools.partial(layer_kernel, hid, shapes, layer_tile, orders, parts),
        out_shape=[
            pltpu.HBM((points, width), F32),
            pltpu.VMEM((points - head, width), F32),
            pltpu.VMEM((points, hid), F32),
        ]
        + [shape_of(2 * shapes + width // len(parts), half, BF16)] * len(parts),
        in_specs=vmem(len(weights) + 3),
        out_specs=[pl.BlockSpec(memory_space=pltpu.HBM)] + vmem(2 + len(parts)),
        scratch_shapes=[
            VMEM((width, lanes), BF16),
            VMEM((width, half), F32),
            VMEM((head, width), F32),
            VMEM((points, width), BF16),
            VMEM((2, layer_tile, width), F32),
            pltpu.SemaphoreType.DMA((head // layer_tile,)),
        ],
        compiler_params=pltpu.CompilerParams(vmem_limit_bytes=20 * MIB),
        cost_estimate=pl.CostEstimate(
            flops=6 * points * width * cols,
            bytes_accessed=8 * points * (width + half),
            transcendentals=points * width,
        ),
        name="layer",
    )(*weights, x, x_t, cotangent)

    def store(name, body, shape, *args, **options):
        return pl.pallas_call(
            body,
            out_shape=pltpu.HBM(shape, F32),
            in_specs=[pl.BlockSpec(memory_space=pltpu.HBM)] * (len(args) - 1) + vmem(1),
            out_specs=pl.BlockSpec(memory_space=pltpu.HBM),
            scratch_shapes=[pltpu.SemaphoreType.DMA(())],
            compiler_params=pltpu.CompilerParams(vmem_limit_bytes=8 * MIB),
            cost_estimate=pl.CostEstimate(
                flops=4000 * MIB, bytes_accessed=8 * points * hid, transcendentals=0
            ),
            name=name,
            **options,
        )(*args)

    def store_grad_hidden():
        return store("store", store_kernel, (points, hid), grad_hidden)

    def store_tail():
        return store(
            "tail", tail_kernel, (points, width), output, tail, input_output_aliases={0: 0}
        )

    if tuned:
        for r, group in enumerate(groups[::-1]):
            masks = masks_of(group)
            grads = [grads[0]] + swaps(grads[1:], masks[1:], devices)
            if r == len(groups) - 1:
                break
            n_out = len(masks_of(groups[-2 - r]))
            left = (grads[0].shape[0] - 2 * shapes) // n_out
            grads = small_kernel(
                "add",
                functools.partial(add_kernel, shapes, len(grads)),
                [shape_of(2 * shapes + left, half, BF16)] * n_out,
                *(grads[::-1] if r == 0 else [grads[k] for k in SUMS]),
            )
            if r == 0:
                *grads, grad_hidden = lax.optimization_barrier((*grads, grad_hidden))
                grad_hidden = store_grad_hidden()
                grad_hidden, code_weight = lax.optimization_barrier((grad_hidden, code_weight))
                code_weights = gather(code_weight, across)
            if r == len(groups) - 2:
                *grads, grad_hidden, tail = lax.optimization_barrier((*grads, grad_hidden, tail))
                output = store_tail()
        (code_weight,) = join(code_weights, half)
        code_weights = gather(code_weight, groups[-1])
    else:
        grad_hidden, output = store_grad_hidden(), store_tail()
        sums = lax.psum(grads[0][: 2 * shapes].astype(F32), AXES)
        high = sums.astype(BF16)
        own = lax.psum_scatter(grads[0][2 * shapes :].astype(F32), AXES, scatter_dimension=0, tiled=True)
        low = jnp.zeros((2 * shapes + rows, half), BF16).at[: 2 * shapes].set((sums - high).astype(BF16))
        grads = [jnp.concatenate([high, own.astype(BF16)], axis=0), low]
    grad_codes, grad_direction, grad_gain, grad_bias = small_kernel(
        "last",
        functools.partial(last_kernel, hid, shapes, code_orders, len(grads)),
        [
            shape_of(shapes, half, F32),
            shape_of(rows, cols, F32),
            shape_of(1, rows, F32),
            shape_of(1, rows, F32),
        ],
        *grads[::-1],
        direction,
        gain_row,
        codes,
        *code_weights,
        scratch=[VMEM((width, half), BF16)],
    )

    total = float(points * devices)
    batch_mean = jnp.mean(codes, axis=0)
    batch_square = jnp.mean(codes * codes, axis=0)
    batch_var = (batch_square - batch_mean * batch_mean) * (total / (total - 1.0))
    new_mean = 0.9 * running_mean + 0.1 * batch_mean
    new_var = 0.9 * running_var + 0.1 * batch_var
    return (
        output,
        grad_hidden,
        grad_codes,
        grad_direction,
        grad_gain.reshape(rows),
        grad_bias.reshape(rows),
        new_mean,
        new_var,
    )


def solution(mesh):
    return jax.shard_map(
        per_device,
        mesh=mesh,
        in_specs=(
            P(("dp", "inner"), None),
            P(),
            P(("dp", "inner"), None),
            P(("dp", "inner")),
            P(("dp", "inner")),
            P(("dp", "inner"), None),
            P(("dp", "inner")),
            P(("dp", "inner")),
            P(("dp", "inner"), None),
            P(),
            P(),
        ),
        out_specs=(
            P(("dp", "inner"), None),
            P(("dp", "inner"), None),
            P(),
            P(("dp", "inner"), None),
            P(("dp", "inner")),
            P(("dp", "inner")),
            P(),
            P(),
        ),
        check_vma=False,
    )
```

```python
import functools

import jax
import jax.numpy as jnp
from jax import lax
from jax.experimental import pallas as pl
from jax.experimental.pallas import tpu as pltpu
from jax.sharding import PartitionSpec as P

AXES = ("dp", "inner")
LANES = 128
MIB = 1024 * 1024
FIRST = (2, 3, 1, 0)
SUMS = (1, 3, 2, 0)
F32 = jnp.float32
BF16 = jnp.bfloat16
VMEM = pltpu.VMEM
NT = (((1,), (1,)), ((), ()))


def dot(a, b, dims=(((1,), (0,)), ((), ()))):
    return lax.dot_general(a, b, dims, preferred_element_type=F32)


def vmem(n):
    return [pl.BlockSpec(memory_space=VMEM)] * n


def small_kernel(name, body, out_shape, *args, scratch=(), space=VMEM, limit=8):
    many = isinstance(out_shape, list)
    return pl.pallas_call(
        body,
        out_shape=out_shape,
        in_specs=[pl.BlockSpec(memory_space=space)] * len(args),
        out_specs=vmem(len(out_shape)) if many else vmem(1)[0],
        scratch_shapes=list(scratch),
        compiler_params=pltpu.CompilerParams(vmem_limit_bytes=limit * MIB),
        cost_estimate=pl.CostEstimate(
            flops=4000 * MIB, bytes_accessed=8 * MIB, transcendentals=4 * MIB
        ),
        name=name,
    )(*args)


def diagonal(n):
    return lax.broadcasted_iota(jnp.int32, (n, n), 0) == lax.broadcasted_iota(jnp.int32, (n, n), 1)


def to_column(row):
    n = row.shape[1]
    return jnp.sum(jnp.where(diagonal(n), row, 0.0), axis=1, keepdims=True)


def to_row(column):
    n = column.shape[0]
    return jnp.sum(jnp.where(diagonal(n), column, 0.0), axis=0, keepdims=True)


def stacked_codes(codes_ref, count):
    codes = codes_ref[...].astype(BF16)
    parts = [codes, codes]
    if count > 2 * codes.shape[0]:
        parts.append(jnp.zeros((count - 2 * codes.shape[0], codes.shape[1]), BF16))
    return jnp.concatenate(parts, axis=0)


def split(x):
    high = x.astype(BF16).astype(F32)
    return high, x - high


def prep_kernel(hid, *refs):
    piece_ref, direction_ref, gain_ref, bias_ref, codes_ref, sems = refs[4:]
    copies = [
        pltpu.make_async_copy(source, target, sems.at[k])
        for k, (source, target) in enumerate(zip(refs[:4], refs[5:9]))
    ]
    for copy in copies:
        copy.start()
    for copy in copies:
        copy.wait()
    d = direction_ref[...]
    shapes = codes_ref.shape[0]
    rows, cols = d.shape
    half = cols // 2
    extra_lanes = piece_ref.shape[1] - cols
    inverse = lax.rsqrt(jnp.sum(d * d, axis=1, keepdims=True))
    w = to_column(gain_ref[...]) * (d * inverse)
    lane = lax.broadcasted_iota(jnp.int32, (rows, half), 1)
    first = jnp.where(lane < hid, w[:, :half], w[:, half:])
    code = pltpu.roll(w, half - hid, 1)[:, half:].astype(BF16)
    bias = to_column(bias_ref[...]).astype(BF16).astype(F32)
    high, low = split(dot(code, stacked_codes(codes_ref, extra_lanes), NT) + bias)
    own = first[:, half - LANES :]
    if extra_lanes > LANES:
        own = jnp.concatenate([jnp.zeros((rows, extra_lanes - LANES), F32), own], axis=1)
    lane = lax.broadcasted_iota(jnp.int32, (rows, extra_lanes), 1)
    table = jnp.where(lane < shapes, high, jnp.where(lane < 2 * shapes, low, 0.0))
    table = jnp.where(lane >= extra_lanes - (half - hid), own, table)
    piece_ref[:, :half] = first.astype(BF16)
    piece_ref[:, half : half + extra_lanes] = table.astype(BF16)
    piece_ref[:, half + extra_lanes :] = code


def join_kernel(n, n_early, *refs):
    rows = refs[0].shape[0]
    for k, ref in enumerate(refs[n - 1 :: -1]):
        lane = 0
        for out_ref in refs[n + n_early :]:
            lanes = out_ref.shape[1]
            out_ref[k * rows : (k + 1) * rows, :] = ref[:, lane : lane + lanes]
            lane += lanes


def pack_kernel(shapes, *refs):
    weight_ref, code_ref = refs[-2:]
    count = len(refs) - 2
    rows, half = refs[0].shape[0], code_ref.shape[1]
    products = jnp.zeros((rows, LANES), F32)
    for k, ref in zip(FIRST, refs):
        for block in range(half // LANES):
            at = (block * count + k) * rows
            weight_ref[at : at + rows, :] = ref[:, block * LANES : (block + 1) * LANES]
        own = ref[:, half : half + LANES].astype(F32)
        own = jnp.where(lax.broadcasted_iota(jnp.int32, own.shape, 1) < 2 * shapes, own, 0.0)
        products = products + (pltpu.roll(own, 2 * shapes * k, 1) if k else own)
        code_ref[k * rows : (k + 1) * rows, :] = ref[:, half + LANES :]
    weight_ref[half // LANES * count * rows :, :] = products.astype(BF16)


def unpack(hid, shapes, refs, orders, me, w_ref):
    count = LANES // (2 * shapes)
    half = w_ref.shape[1] - LANES
    blocks = half // LANES
    for ref, order in zip(refs, orders):
        height = ref.shape[0] // (len(order) // count)
        rows = height // (blocks * count + 1)
        lane = lax.broadcasted_iota(jnp.int32, (rows, LANES), 1)
        for j, mask in enumerate(order):
            start, k = j // count * height, j % count
            at = pl.ds(pl.multiple_of((me ^ mask) * rows, rows), rows)
            for block in range(blocks):
                here = start + (block * count + k) * rows
                part = ref[here : here + rows, :]
                w_ref[at, block * LANES : (block + 1) * LANES] = part
            here = start + blocks * count * rows
            products = ref[here : here + rows, :].astype(F32)
            if k:
                products = pltpu.roll(products, LANES - 2 * shapes * k, 1)
            products = jnp.where(lane < 2 * shapes, products, 0.0)
            products = jnp.where(lane >= LANES - (half - hid), part.astype(F32), products)
            w_ref[at, half:] = products.astype(BF16)


def place(refs, orders, me, out_ref):
    if orders is None:
        out_ref[...] = refs[0][...]
        return
    rows = refs[0].shape[0] // len(orders[0])
    for ref, order in zip(refs, orders):
        for k, mask in enumerate(order):
            at = pl.multiple_of((me ^ mask) * rows, rows)
            out_ref[pl.ds(at, rows), :] = ref[k * rows : (k + 1) * rows, :]


def inputs_kernel(hid, tile, *refs):
    x_ref, x_t_ref, hidden_ref, offsets_ref, ids_ref, scale_ref, sems = refs[4:]
    points = x_ref.shape[0]
    half = (hid + LANES - 1) // LANES * LANES
    shapes = x_t_ref.shape[0] - half
    extra_lanes = x_ref.shape[1] - half
    steps = points // tile
    small = [
        pltpu.make_async_copy(source, target, sems.at[steps + k])
        for k, (source, target) in enumerate(zip(refs[1:4], (offsets_ref, ids_ref, scale_ref)))
    ]
    large = [
        pltpu.make_async_copy(
            refs[0].at[pl.ds(k * tile, tile), :], hidden_ref.at[pl.ds(k * tile, tile), :], sems.at[k]
        )
        for k in range(steps)
    ]
    for copy in small + large:
        copy.start()
    for copy in small:
        copy.wait()
    for step, copy in enumerate(large):
        here = slice(step * tile, (step + 1) * tile)
        scale = scale_ref[:, here]
        jitter = jnp.where(scale == 0, 1.0, jnp.where(scale == 1, 0.5, 0.25))
        xyz = offsets_ref[:, here] * jitter
        row = lax.broadcasted_iota(jnp.int32, (16, tile), 0)
        last = jnp.zeros((16, tile), F32)
        for k in range(half - hid):
            last = jnp.where(row == 16 - (half - hid) + k, xyz[k : k + 1], last)
        last = last.astype(BF16)
        row = lax.broadcasted_iota(jnp.int32, (extra_lanes - 16, tile), 0)
        ids = ids_ref[:, here]
        member = jnp.where((row == ids) | (row == ids + shapes), 1.0, 0.0).astype(BF16)
        x_ref[here, half:] = jnp.concatenate([member, last], axis=0).T
        x_t_ref[half:, here] = member[:shapes]
        copy.wait()
        x_ref[here, half - LANES : half] = jnp.zeros((tile, LANES), BF16)
        x_ref[here, :hid] = hidden_ref[here, :].astype(BF16)
        hidden = x_ref[here, :half].T
        x_t_ref[: half - 16, here] = hidden[: half - 16]
        x_t_ref[half - 16 : half, here] = hidden[half - 16 :] + last


def layer_kernel(hid, shapes, tile, orders, parts, *refs):
    n = 1 if orders is None else len(orders)
    pieces = refs[:n]
    x_ref, x_t_ref, cot_ref, out_hbm, tail_ref, grad_hidden_ref = refs[n : n + 6]
    grad_refs = refs[n + 6 : -6]
    w_ref, turned_ref, out_ref, grad_pre_ref, pre_ref, sems = refs[-6:]
    points, width = cot_ref.shape
    half = width // 2
    steps = points // tile
    head = out_ref.shape[0] // tile
    me = lax.axis_index(AXES)
    if orders is None:
        place(pieces, orders, me, w_ref)
    else:
        unpack(hid, shapes, pieces, orders, me, w_ref)
    copies = []

    def rows_of(step):
        return slice(step * tile, (step + 1) * tile)

    def forward(step):
        pre_ref[step % 2] = dot(x_ref[rows_of(step), :], w_ref[...], NT)

    def middle(step):
        here = rows_of(step)
        pre = pre_ref[step % 2]
        sigma = 0.5 * jnp.tanh(0.5 * pre) + 0.5
        out = pre * sigma
        if step < head:
            out_ref[here, :] = out
        else:
            tail_ref[rows_of(step - head), :] = out
        grad_pre_ref[here, :] = (cot_ref[here, :] * (sigma * (1.0 + (pre - out)))).astype(BF16)

    def backward(step):
        here = rows_of(step)
        grad_hidden_ref[here, :] = dot(grad_pre_ref[here, :], w_ref[:, :half])[:, :hid]

    def store(step):
        here = pl.ds(step * tile, tile)
        copy = pltpu.make_async_copy(out_ref.at[here, :], out_hbm.at[here, :], sems.at[step])
        copy.start()
        copies.append(copy)

    forward(0)
    for step in range(steps):
        if step + 1 < steps:
            forward(step + 1)
        middle(step)
        if step > 0:
            backward(step - 1)
        if step < head:
            store(step)
    backward(steps - 1)
    grad = dot(x_t_ref[...], grad_pre_ref[...])
    sums = grad[half:].astype(BF16)
    for at in range(0, width, half):
        turned_ref[at : at + half, :] = grad[:half, at : at + half].T
    for ref, order in zip(grad_refs, parts):
        ref[:shapes, :] = sums[:, :half]
        ref[shapes : 2 * shapes, :] = sums[:, half:]
        if orders is None:
            ref[2 * shapes :, :] = turned_ref[...].astype(BF16)
            continue
        rows = (ref.shape[0] - 2 * shapes) // len(order)
        for k, mask in enumerate(order):
            at = pl.multiple_of((me ^ mask) * rows, rows)
            to = 2 * shapes + k * rows
            ref[to : to + rows, :] = turned_ref[pl.ds(at, rows), :].astype(BF16)

    for copy in copies:
        copy.wait()


def store_kernel(source_ref, target_ref, sem):
    copy = pltpu.make_async_copy(source_ref, target_ref, sem)
    copy.start()
    copy.wait()


def tail_kernel(_, source_ref, target_ref, sem):
    points, rows = target_ref.shape[0], source_ref.shape[0]
    store_kernel(source_ref, target_ref.at[pl.ds(points - rows, rows), :], sem)


def sum_of(refs):
    terms = [ref[...].astype(F32) for ref in refs]
    while len(terms) > 1:
        terms = [a + b for a, b in zip(terms[::2], terms[1::2])]
    return terms[0]


def add_kernel(shapes, n, *refs):
    total = sum_of(refs[:n]).astype(BF16)
    for k, ref in enumerate(refs[n:]):
        rows = ref.shape[0] - 2 * shapes
        at = 2 * shapes + k * rows
        ref[: 2 * shapes, :] = total[: 2 * shapes]
        ref[2 * shapes :, :] = total[at : at + rows]


def last_kernel(hid, shapes, orders, n, *refs):
    direction_ref, gain_ref, codes_ref = refs[n : n + 3]
    pieces = refs[n + 3 : -5]
    grad_codes_ref, grad_direction_ref, grad_gain_ref, grad_bias_ref, code_scratch = refs[-5:]
    d = direction_ref[...]
    rows, cols = d.shape
    half = cols // 2
    me = lax.axis_index(AXES)
    place(pieces, orders, me, code_scratch)
    total = sum_of(refs[:n])
    sums = jnp.concatenate([total[:shapes], total[shapes : 2 * shapes]], axis=1)
    sums = jnp.concatenate(split(sums), axis=0).astype(BF16)
    terms = dot(sums, code_scratch[...])
    grad_codes_ref[...] = terms[:shapes] + terms[shapes:]
    width = sums.shape[1]
    mine = lax.broadcasted_iota(jnp.int32, (rows, width), 0) + me * rows
    mine = jnp.where(mine == lax.broadcasted_iota(jnp.int32, (rows, width), 1), 1.0, 0.0).astype(BF16)
    own = dot(mine, sums, NT)
    grad_bias_ref[...] = to_row(jnp.sum(own, axis=1, keepdims=True))
    code = dot(own.astype(BF16), stacked_codes(codes_ref, 2 * shapes))
    packed = jnp.concatenate([total[2 * shapes :], code], axis=1)
    lane = lax.broadcasted_iota(jnp.int32, (rows, cols), 1)
    grad_weight = jnp.where(
        lane < hid,
        packed,
        jnp.where(lane < hid + half, pltpu.roll(packed, cols - (half - hid), 1), pltpu.roll(packed, half, 1)),
    )
    inverse = lax.rsqrt(jnp.sum(d * d, axis=1, keepdims=True))
    unit = d * inverse
    grad_gain = jnp.sum(grad_weight * unit, axis=1, keepdims=True)
    grad_gain_ref[...] = to_row(grad_gain)
    grad_direction_ref[...] = (to_column(gain_ref[...]) * inverse) * (grad_weight - grad_gain * unit)


def masks_of(group):
    masks = [0]
    for bit in group:
        masks = masks + [m ^ bit for m in masks]
    return masks


def order_of(groups):
    order = [0]
    for group in groups:
        order = [m ^ r for m in masks_of(group) for r in order]
    return order


def swaps(arrays, masks, devices):
    moved = [
        lax.ppermute(x, AXES, [(i, i ^ mask) for i in range(devices)])
        for x, mask in list(zip(arrays, masks))[::-1]
    ]
    return moved[::-1]


def per_device(
    hidden,
    codes,
    offsets,
    shape_ids,
    scale_index,
    direction,
    gain,
    bias,
    cotangent,
    running_mean,
    running_var,
):
    points, hid = hidden.shape
    shapes = codes.shape[0]
    rows, cols = direction.shape
    width = cotangent.shape[1]
    half = cols // 2
    devices = lax.axis_size("dp") * lax.axis_size("inner")
    bits = [1 << k | 1 for k in range(devices.bit_length() - 1)]
    groups = [bits[k - 2 : k] for k in range(len(bits), 1, -2)]
    groups = groups + [bits[:1]] * (len(bits) % 2)
    gathers = [[groups[0][0], groups[0][-1] ^ 1]] + groups[1:]
    extra_lanes = -(-(2 * shapes + 16) // LANES) * LANES
    tuned = rows % 16 == 0 and 2 * shapes * len(masks_of(groups[0])) == LANES
    lanes = half + extra_lanes
    gain_row = gain.reshape(1, rows)

    def shape_of(rows, lanes, dtype):
        return jax.ShapeDtypeStruct((rows, lanes), dtype)

    held = small_kernel(
        "prep",
        functools.partial(prep_kernel, hid),
        shape_of(rows, lanes + half, BF16),
        *[
            pltpu.with_memory_space_constraint(x, pltpu.HBM)
            for x in (direction, gain_row, bias.reshape(1, rows), codes)
        ],
        scratch=[
            VMEM((rows, cols), F32),
            VMEM((1, rows), F32),
            VMEM((1, rows), F32),
            VMEM((shapes, half), F32),
            pltpu.SemaphoreType.DMA((4,)),
        ],
        space=pl.ANY,
    )
    tile, layer_tile = min(512, points), min(256, points)
    x, x_t = pl.pallas_call(
        functools.partial(inputs_kernel, hid, tile),
        out_shape=[
            shape_of(points, lanes, BF16),
            shape_of(half + shapes, points, BF16),
        ],
        in_specs=[pl.BlockSpec(memory_space=pl.ANY)] * 4,
        out_specs=vmem(2),
        scratch_shapes=[
            VMEM((points, hid), F32),
            VMEM((half - hid, points), F32),
            VMEM((1, points), jnp.int32),
            VMEM((1, points), jnp.int32),
            pltpu.SemaphoreType.DMA((points // tile + 3,)),
        ],
        compiler_params=pltpu.CompilerParams(vmem_limit_bytes=12 * MIB),
        cost_estimate=pl.CostEstimate(
            flops=4000 * MIB, bytes_accessed=8 * points * half, transcendentals=0
        ),
        name="inputs",
    )(
        *[
            pltpu.with_memory_space_constraint(a, pltpu.HBM)
            for a in (
                hidden,
                offsets.T,
                shape_ids.reshape(1, points),
                scale_index.reshape(1, points),
            )
        ]
    )
    def gather(array, group):
        masks = masks_of(group)[1:]
        return [array] + swaps([array] * len(masks), masks, devices)

    def join(arrays, *widths, early=()):
        height = sum(a.shape[0] for a in arrays)
        return small_kernel(
            "join",
            functools.partial(join_kernel, len(arrays), len(early)),
            [shape_of(height, width, BF16) for width in widths],
            *arrays[::-1],
            *early,
        )

    if tuned:
        arrays = gather(held, gathers[0])
        weight, code_weight = small_kernel(
            "pack",
            functools.partial(pack_kernel, shapes),
            [
                shape_of((half // LANES * len(arrays) + 1) * rows, LANES, BF16),
                shape_of(len(arrays) * rows, half, BF16),
            ],
            *[arrays[k] for k in FIRST],
        )
        weight, code_weight, x, x_t = lax.optimization_barrier((weight, code_weight, x, x_t))
        (weights,) = [gather(weight, group) for group in gathers[1:-1]]
        along, across = [[bit] for bit in gathers[1][::-1]]
        (weight,) = join(weights, LANES, early=(cotangent,))
        weights = gather(weight, gathers[-1])
        code_weights = gather(code_weight, along)
        code_order = order_of([gathers[0], along, across])
        orders = [[m ^ r for r in order_of(gathers[:-1])] for m in masks_of(gathers[-1])]
        code_orders = [[m ^ r for r in code_order] for m in masks_of(gathers[-1])]
        parts = [[m ^ r for r in order_of(groups[:-1])] for m in masks_of(groups[-1])]
    else:
        held = lax.all_gather(held, AXES, axis=0, tiled=True)
        weights, code_weights, orders, code_orders, parts = [held[:, :lanes]], [held[:, lanes:]], None, None, [[0]]

    head = points // layer_tile // 2 * layer_tile
    output, tail, grad_hidden, *grads = pl.pallas_call(
        functools.partial(layer_kernel, hid, shapes, layer_tile, orders, parts),
        out_shape=[
            pltpu.HBM((points, width), F32),
            pltpu.VMEM((points - head, width), F32),
            pltpu.VMEM((points, hid), F32),
        ]
        + [shape_of(2 * shapes + width // len(parts), half, BF16)] * len(parts),
        in_specs=vmem(len(weights) + 3),
        out_specs=[pl.BlockSpec(memory_space=pltpu.HBM)] + vmem(2 + len(parts)),
        scratch_shapes=[
            VMEM((width, lanes), BF16),
            VMEM((width, half), F32),
            VMEM((head, width), F32),
            VMEM((points, width), BF16),
            VMEM((2, layer_tile, width), F32),
            pltpu.SemaphoreType.DMA((head // layer_tile,)),
        ],
        compiler_params=pltpu.CompilerParams(vmem_limit_bytes=20 * MIB),
        cost_estimate=pl.CostEstimate(
            flops=6 * points * width * cols,
            bytes_accessed=8 * points * (width + half),
            transcendentals=points * width,
        ),
        name="layer",
    )(*weights, x, x_t, cotangent)

    def store(name, body, shape, *args, **options):
        return pl.pallas_call(
            body,
            out_shape=pltpu.HBM(shape, F32),
            in_specs=[pl.BlockSpec(memory_space=pltpu.HBM)] * (len(args) - 1) + vmem(1),
            out_specs=pl.BlockSpec(memory_space=pltpu.HBM),
            scratch_shapes=[pltpu.SemaphoreType.DMA(())],
            compiler_params=pltpu.CompilerParams(vmem_limit_bytes=8 * MIB),
            cost_estimate=pl.CostEstimate(
                flops=4000 * MIB, bytes_accessed=8 * points * hid, transcendentals=0
            ),
            name=name,
            **options,
        )(*args)

    def store_grad_hidden():
        return store("store", store_kernel, (points, hid), grad_hidden)

    def store_tail():
        return store(
            "tail", tail_kernel, (points, width), output, tail, input_output_aliases={0: 0}
        )

    if tuned:
        *grads, code_along = lax.optimization_barrier((*grads, code_weights[1]))
        (code_weight,) = join([code_weights[0], code_along], half)
        for r, group in enumerate(groups[::-1]):
            masks = masks_of(group)
            grads = [grads[0]] + swaps(grads[1:], masks[1:], devices)
            if r == len(groups) - 1:
                break
            n_out = len(masks_of(groups[-2 - r]))
            left = (grads[0].shape[0] - 2 * shapes) // n_out
            grads = small_kernel(
                "add",
                functools.partial(add_kernel, shapes, len(grads)),
                [shape_of(2 * shapes + left, half, BF16)] * n_out,
                *(grads[::-1] if r == 0 else [grads[k] for k in SUMS]),
            )
            if r == 0:
                *grads, grad_hidden = lax.optimization_barrier((*grads, grad_hidden))
                grad_hidden = store_grad_hidden()
                grad_hidden, code_weight = lax.optimization_barrier((grad_hidden, code_weight))
                code_weights = gather(code_weight, across)
            if r == len(groups) - 2:
                *grads, grad_hidden, tail = lax.optimization_barrier((*grads, grad_hidden, tail))
                output = store_tail()
        (code_weight,) = join(code_weights, half)
        code_weights = gather(code_weight, groups[-1])
    else:
        grad_hidden, output = store_grad_hidden(), store_tail()
        sums = lax.psum(grads[0][: 2 * shapes].astype(F32), AXES)
        high = sums.astype(BF16)
        own = lax.psum_scatter(grads[0][2 * shapes :].astype(F32), AXES, scatter_dimension=0, tiled=True)
        low = jnp.zeros((2 * shapes + rows, half), BF16).at[: 2 * shapes].set((sums - high).astype(BF16))
        grads = [jnp.concatenate([high, own.astype(BF16)], axis=0), low]
    grad_codes, grad_direction, grad_gain, grad_bias = small_kernel(
        "last",
        functools.partial(last_kernel, hid, shapes, code_orders, len(grads)),
        [
            shape_of(shapes, half, F32),
            shape_of(rows, cols, F32),
            shape_of(1, rows, F32),
            shape_of(1, rows, F32),
        ],
        *grads[::-1],
        direction,
        gain_row,
        codes,
        *code_weights,
        scratch=[VMEM((width, half), BF16)],
    )

    total = float(points * devices)
    batch_mean = jnp.mean(codes, axis=0)
    batch_square = jnp.mean(codes * codes, axis=0)
    batch_var = (batch_square - batch_mean * batch_mean) * (total / (total - 1.0))
    new_mean = 0.9 * running_mean + 0.1 * batch_mean
    new_var = 0.9 * running_var + 0.1 * batch_var
    return (
        output,
        grad_hidden,
        grad_codes,
        grad_direction,
        grad_gain.reshape(rows),
        grad_bias.reshape(rows),
        new_mean,
        new_var,
    )


def solution(mesh):
    return jax.shard_map(
        per_device,
        mesh=mesh,
        in_specs=(
            P(("dp", "inner"), None),
            P(),
            P(("dp", "inner"), None),
            P(("dp", "inner")),
            P(("dp", "inner")),
            P(("dp", "inner"), None),
            P(("dp", "inner")),
            P(("dp", "inner")),
            P(("dp", "inner"), None),
            P(),
            P(),
        ),
        out_specs=(
            P(("dp", "inner"), None),
            P(("dp", "inner"), None),
            P(),
            P(("dp", "inner"), None),
            P(("dp", "inner")),
            P(("dp", "inner")),
            P(),
            P(),
        ),
        check_vma=False,
    )
```

```python
import functools

import jax
import jax.numpy as jnp
from jax import lax
from jax.experimental import pallas as pl
from jax.experimental.pallas import tpu as pltpu
from jax.sharding import PartitionSpec as P

AXES = ("dp", "inner")
LANES = 128
MIB = 1024 * 1024
FIRST = (2, 3, 1, 0)
SUMS = (1, 3, 2, 0)
F32 = jnp.float32
BF16 = jnp.bfloat16
VMEM = pltpu.VMEM
NT = (((1,), (1,)), ((), ()))


def dot(a, b, dims=(((1,), (0,)), ((), ()))):
    return lax.dot_general(a, b, dims, preferred_element_type=F32)


def vmem(n):
    return [pl.BlockSpec(memory_space=VMEM)] * n


def small_kernel(name, body, out_shape, *args, scratch=(), space=VMEM, limit=8):
    many = isinstance(out_shape, list)
    return pl.pallas_call(
        body,
        out_shape=out_shape,
        in_specs=[pl.BlockSpec(memory_space=space)] * len(args),
        out_specs=vmem(len(out_shape)) if many else vmem(1)[0],
        scratch_shapes=list(scratch),
        compiler_params=pltpu.CompilerParams(vmem_limit_bytes=limit * MIB),
        cost_estimate=pl.CostEstimate(
            flops=4000 * MIB, bytes_accessed=8 * MIB, transcendentals=4 * MIB
        ),
        name=name,
    )(*args)


def diagonal(n):
    return lax.broadcasted_iota(jnp.int32, (n, n), 0) == lax.broadcasted_iota(jnp.int32, (n, n), 1)


def to_column(row):
    n = row.shape[1]
    return jnp.sum(jnp.where(diagonal(n), row, 0.0), axis=1, keepdims=True)


def to_row(column):
    n = column.shape[0]
    return jnp.sum(jnp.where(diagonal(n), column, 0.0), axis=0, keepdims=True)


def stacked_codes(codes_ref, count):
    codes = codes_ref[...].astype(BF16)
    parts = [codes, codes]
    if count > 2 * codes.shape[0]:
        parts.append(jnp.zeros((count - 2 * codes.shape[0], codes.shape[1]), BF16))
    return jnp.concatenate(parts, axis=0)


def split(x):
    high = x.astype(BF16).astype(F32)
    return high, x - high


def prep_kernel(hid, *refs):
    piece_ref, direction_ref, gain_ref, bias_ref, codes_ref, sems = refs[4:]
    copies = [
        pltpu.make_async_copy(source, target, sems.at[k])
        for k, (source, target) in enumerate(zip(refs[:4], refs[5:9]))
    ]
    for copy in copies:
        copy.start()
    for copy in copies:
        copy.wait()
    d = direction_ref[...]
    shapes = codes_ref.shape[0]
    rows, cols = d.shape
    half = cols // 2
    extra_lanes = piece_ref.shape[1] - cols
    inverse = lax.rsqrt(jnp.sum(d * d, axis=1, keepdims=True))
    w = to_column(gain_ref[...]) * (d * inverse)
    lane = lax.broadcasted_iota(jnp.int32, (rows, half), 1)
    first = jnp.where(lane < hid, w[:, :half], w[:, half:])
    code = pltpu.roll(w, half - hid, 1)[:, half:].astype(BF16)
    bias = to_column(bias_ref[...]).astype(BF16).astype(F32)
    high, low = split(dot(code, stacked_codes(codes_ref, extra_lanes), NT) + bias)
    own = first[:, half - LANES :]
    if extra_lanes > LANES:
        own = jnp.concatenate([jnp.zeros((rows, extra_lanes - LANES), F32), own], axis=1)
    lane = lax.broadcasted_iota(jnp.int32, (rows, extra_lanes), 1)
    table = jnp.where(lane < shapes, high, jnp.where(lane < 2 * shapes, low, 0.0))
    table = jnp.where(lane >= extra_lanes - (half - hid), own, table)
    piece_ref[:, :half] = first.astype(BF16)
    piece_ref[:, half : half + extra_lanes] = table.astype(BF16)
    piece_ref[:, half + extra_lanes :] = code


def join_kernel(n, n_early, *refs):
    rows = refs[0].shape[0]
    for k, ref in enumerate(refs[n - 1 :: -1]):
        lane = 0
        for out_ref in refs[n + n_early :]:
            lanes = out_ref.shape[1]
            out_ref[k * rows : (k + 1) * rows, :] = ref[:, lane : lane + lanes]
            lane += lanes


def pack_kernel(shapes, *refs):
    weight_ref, code_ref = refs[-2:]
    count = len(refs) - 2
    rows, half = refs[0].shape[0], code_ref.shape[1]
    products = jnp.zeros((rows, LANES), F32)
    for k, ref in zip(FIRST, refs):
        for block in range(half // LANES):
            at = (block * count + k) * rows
            weight_ref[at : at + rows, :] = ref[:, block * LANES : (block + 1) * LANES]
        own = ref[:, half : half + LANES].astype(F32)
        own = jnp.where(lax.broadcasted_iota(jnp.int32, own.shape, 1) < 2 * shapes, own, 0.0)
        products = products + (pltpu.roll(own, 2 * shapes * k, 1) if k else own)
        code_ref[k * rows : (k + 1) * rows, :] = ref[:, half + LANES :]
    weight_ref[half // LANES * count * rows :, :] = products.astype(BF16)


def unpack(hid, shapes, refs, orders, me, w_ref):
    count = LANES // (2 * shapes)
    half = w_ref.shape[1] - LANES
    blocks = half // LANES
    for ref, order in zip(refs, orders):
        height = ref.shape[0] // (len(order) // count)
        rows = height // (blocks * count + 1)
        lane = lax.broadcasted_iota(jnp.int32, (rows, LANES), 1)
        for j, mask in enumerate(order):
            start, k = j // count * height, j % count
            at = pl.ds(pl.multiple_of((me ^ mask) * rows, rows), rows)
            for block in range(blocks):
                here = start + (block * count + k) * rows
                part = ref[here : here + rows, :]
                w_ref[at, block * LANES : (block + 1) * LANES] = part
            here = start + blocks * count * rows
            products = ref[here : here + rows, :].astype(F32)
            if k:
                products = pltpu.roll(products, LANES - 2 * shapes * k, 1)
            products = jnp.where(lane < 2 * shapes, products, 0.0)
            products = jnp.where(lane >= LANES - (half - hid), part.astype(F32), products)
            w_ref[at, half:] = products.astype(BF16)


def place(refs, orders, me, out_ref):
    if orders is None:
        out_ref[...] = refs[0][...]
        return
    rows = refs[0].shape[0] // len(orders[0])
    for ref, order in zip(refs, orders):
        for k, mask in enumerate(order):
            at = pl.multiple_of((me ^ mask) * rows, rows)
            out_ref[pl.ds(at, rows), :] = ref[k * rows : (k + 1) * rows, :]


def inputs_kernel(hid, tile, *refs):
    x_ref, x_t_ref, hidden_ref, offsets_ref, ids_ref, scale_ref, sems = refs[4:]
    points = x_ref.shape[0]
    half = (hid + LANES - 1) // LANES * LANES
    shapes = x_t_ref.shape[0] - half
    extra_lanes = x_ref.shape[1] - half
    steps = points // tile
    small = [
        pltpu.make_async_copy(source, target, sems.at[steps + k])
        for k, (source, target) in enumerate(zip(refs[1:4], (offsets_ref, ids_ref, scale_ref)))
    ]
    large = [
        pltpu.make_async_copy(
            refs[0].at[pl.ds(k * tile, tile), :], hidden_ref.at[pl.ds(k * tile, tile), :], sems.at[k]
        )
        for k in range(steps)
    ]
    for copy in small + large:
        copy.start()
    for copy in small:
        copy.wait()
    for step, copy in enumerate(large):
        here = slice(step * tile, (step + 1) * tile)
        scale = scale_ref[:, here]
        jitter = jnp.where(scale == 0, 1.0, jnp.where(scale == 1, 0.5, 0.25))
        xyz = offsets_ref[:, here] * jitter
        row = lax.broadcasted_iota(jnp.int32, (16, tile), 0)
        last = jnp.zeros((16, tile), F32)
        for k in range(half - hid):
            last = jnp.where(row == 16 - (half - hid) + k, xyz[k : k + 1], last)
        last = last.astype(BF16)
        row = lax.broadcasted_iota(jnp.int32, (extra_lanes - 16, tile), 0)
        ids = ids_ref[:, here]
        member = jnp.where((row == ids) | (row == ids + shapes), 1.0, 0.0).astype(BF16)
        x_ref[here, half:] = jnp.concatenate([member, last], axis=0).T
        x_t_ref[half:, here] = member[:shapes]
        copy.wait()
        x_ref[here, half - LANES : half] = jnp.zeros((tile, LANES), BF16)
        x_ref[here, :hid] = hidden_ref[here, :].astype(BF16)
        hidden = x_ref[here, :half].T
        x_t_ref[: half - 16, here] = hidden[: half - 16]
        x_t_ref[half - 16 : half, here] = hidden[half - 16 :] + last


def layer_kernel(hid, shapes, tile, orders, parts, *refs):
    n = 1 if orders is None else len(orders)
    pieces = refs[:n]
    x_ref, x_t_ref, cot_ref, out_hbm, tail_ref, grad_hidden_ref = refs[n : n + 6]
    grad_refs = refs[n + 6 : -6]
    w_ref, turned_ref, out_ref, grad_pre_ref, pre_ref, sems = refs[-6:]
    points, width = cot_ref.shape
    half = width // 2
    steps = points // tile
    head = out_ref.shape[0] // tile
    me = lax.axis_index(AXES)
    if orders is None:
        place(pieces, orders, me, w_ref)
    else:
        unpack(hid, shapes, pieces, orders, me, w_ref)
    copies = []

    def rows_of(step):
        return slice(step * tile, (step + 1) * tile)

    def forward(step):
        pre_ref[step % 2] = dot(x_ref[rows_of(step), :], w_ref[...], NT)

    def middle(step):
        here = rows_of(step)
        pre = pre_ref[step % 2]
        sigma = 0.5 * jnp.tanh(0.5 * pre) + 0.5
        out = pre * sigma
        if step < head:
            out_ref[here, :] = out
        else:
            tail_ref[rows_of(step - head), :] = out
        grad_pre_ref[here, :] = (cot_ref[here, :] * (sigma * (1.0 + (pre - out)))).astype(BF16)

    def backward(step):
        here = rows_of(step)
        grad_hidden_ref[here, :] = dot(grad_pre_ref[here, :], w_ref[:, :half])[:, :hid]

    def store(step):
        here = pl.ds(step * tile, tile)
        copy = pltpu.make_async_copy(out_ref.at[here, :], out_hbm.at[here, :], sems.at[step])
        copy.start()
        copies.append(copy)

    forward(0)
    for step in range(steps):
        if step + 1 < steps:
            forward(step + 1)
        middle(step)
        if step > 0:
            backward(step - 1)
        if step < head:
            store(step)
    backward(steps - 1)
    grad = dot(x_t_ref[...], grad_pre_ref[...])
    sums = grad[half:].astype(BF16)
    for at in range(0, width, half):
        turned_ref[at : at + half, :] = grad[:half, at : at + half].T
    for ref, order in zip(grad_refs, parts):
        ref[:shapes, :] = sums[:, :half]
        ref[shapes : 2 * shapes, :] = sums[:, half:]
        if orders is None:
            ref[2 * shapes :, :] = turned_ref[...].astype(BF16)
            continue
        rows = (ref.shape[0] - 2 * shapes) // len(order)
        for k, mask in enumerate(order):
            at = pl.multiple_of((me ^ mask) * rows, rows)
            to = 2 * shapes + k * rows
            ref[to : to + rows, :] = turned_ref[pl.ds(at, rows), :].astype(BF16)

    for copy in copies:
        copy.wait()


def store_kernel(source_ref, target_ref, sem):
    copy = pltpu.make_async_copy(source_ref, target_ref, sem)
    copy.start()
    copy.wait()


def tail_kernel(_, source_ref, target_ref, sem):
    points, rows = target_ref.shape[0], source_ref.shape[0]
    store_kernel(source_ref, target_ref.at[pl.ds(points - rows, rows), :], sem)


def sum_of(refs):
    terms = [ref[...].astype(F32) for ref in refs]
    while len(terms) > 1:
        terms = [a + b for a, b in zip(terms[::2], terms[1::2])]
    return terms[0]


def add_kernel(shapes, n, *refs):
    total = sum_of(refs[:n]).astype(BF16)
    for k, ref in enumerate(refs[n:]):
        rows = ref.shape[0] - 2 * shapes
        at = 2 * shapes + k * rows
        ref[: 2 * shapes, :] = total[: 2 * shapes]
        ref[2 * shapes :, :] = total[at : at + rows]


def last_kernel(hid, shapes, orders, n, *refs):
    direction_ref, gain_ref, codes_ref = refs[n : n + 3]
    pieces = refs[n + 3 : -5]
    grad_codes_ref, grad_direction_ref, grad_gain_ref, grad_bias_ref, code_scratch = refs[-5:]
    d = direction_ref[...]
    rows, cols = d.shape
    half = cols // 2
    me = lax.axis_index(AXES)
    place(pieces, orders, me, code_scratch)
    total = sum_of(refs[:n])
    sums = jnp.concatenate([total[:shapes], total[shapes : 2 * shapes]], axis=1)
    sums = jnp.concatenate(split(sums), axis=0).astype(BF16)
    terms = dot(sums, code_scratch[...])
    grad_codes_ref[...] = terms[:shapes] + terms[shapes:]
    width = sums.shape[1]
    mine = lax.broadcasted_iota(jnp.int32, (rows, width), 0) + me * rows
    mine = jnp.where(mine == lax.broadcasted_iota(jnp.int32, (rows, width), 1), 1.0, 0.0).astype(BF16)
    own = dot(mine, sums, NT)
    grad_bias_ref[...] = to_row(jnp.sum(own, axis=1, keepdims=True))
    code = dot(own.astype(BF16), stacked_codes(codes_ref, 2 * shapes))
    packed = jnp.concatenate([total[2 * shapes :], code], axis=1)
    lane = lax.broadcasted_iota(jnp.int32, (rows, cols), 1)
    grad_weight = jnp.where(
        lane < hid,
        packed,
        jnp.where(lane < hid + half, pltpu.roll(packed, cols - (half - hid), 1), pltpu.roll(packed, half, 1)),
    )
    inverse = lax.rsqrt(jnp.sum(d * d, axis=1, keepdims=True))
    unit = d * inverse
    grad_gain = jnp.sum(grad_weight * unit, axis=1, keepdims=True)
    grad_gain_ref[...] = to_row(grad_gain)
    grad_direction_ref[...] = (to_column(gain_ref[...]) * inverse) * (grad_weight - grad_gain * unit)


def masks_of(group):
    masks = [0]
    for bit in group:
        masks = masks + [m ^ bit for m in masks]
    return masks


def order_of(groups):
    order = [0]
    for group in groups:
        order = [m ^ r for m in masks_of(group) for r in order]
    return order


def swaps(arrays, masks, devices):
    moved = [
        lax.ppermute(x, AXES, [(i, i ^ mask) for i in range(devices)])
        for x, mask in list(zip(arrays, masks))[::-1]
    ]
    return moved[::-1]


def per_device(
    hidden,
    codes,
    offsets,
    shape_ids,
    scale_index,
    direction,
    gain,
    bias,
    cotangent,
    running_mean,
    running_var,
):
    points, hid = hidden.shape
    shapes = codes.shape[0]
    rows, cols = direction.shape
    width = cotangent.shape[1]
    half = cols // 2
    devices = lax.axis_size("dp") * lax.axis_size("inner")
    bits = [1 << k | 1 for k in range(devices.bit_length() - 1)]
    groups = [bits[k - 2 : k] for k in range(len(bits), 1, -2)]
    groups = groups + [bits[:1]] * (len(bits) % 2)
    gathers = [[groups[0][0], groups[0][-1] ^ 1]] + groups[1:]
    extra_lanes = -(-(2 * shapes + 16) // LANES) * LANES
    tuned = rows % 16 == 0 and 2 * shapes * len(masks_of(groups[0])) == LANES
    lanes = half + extra_lanes
    gain_row = gain.reshape(1, rows)

    def shape_of(rows, lanes, dtype):
        return jax.ShapeDtypeStruct((rows, lanes), dtype)

    held = small_kernel(
        "prep",
        functools.partial(prep_kernel, hid),
        shape_of(rows, lanes + half, BF16),
        *[
            pltpu.with_memory_space_constraint(x, pltpu.HBM)
            for x in (direction, gain_row, bias.reshape(1, rows), codes)
        ],
        scratch=[
            VMEM((rows, cols), F32),
            VMEM((1, rows), F32),
            VMEM((1, rows), F32),
            VMEM((shapes, half), F32),
            pltpu.SemaphoreType.DMA((4,)),
        ],
        space=pl.ANY,
    )
    tile, layer_tile = min(512, points), min(256, points)
    x, x_t = pl.pallas_call(
        functools.partial(inputs_kernel, hid, tile),
        out_shape=[
            shape_of(points, lanes, BF16),
            shape_of(half + shapes, points, BF16),
        ],
        in_specs=[pl.BlockSpec(memory_space=pl.ANY)] * 4,
        out_specs=vmem(2),
        scratch_shapes=[
            VMEM((points, hid), F32),
            VMEM((half - hid, points), F32),
            VMEM((1, points), jnp.int32),
            VMEM((1, points), jnp.int32),
            pltpu.SemaphoreType.DMA((points // tile + 3,)),
        ],
        compiler_params=pltpu.CompilerParams(vmem_limit_bytes=12 * MIB),
        cost_estimate=pl.CostEstimate(
            flops=4000 * MIB, bytes_accessed=8 * points * half, transcendentals=0
        ),
        name="inputs",
    )(
        *[
            pltpu.with_memory_space_constraint(a, pltpu.HBM)
            for a in (
                hidden,
                offsets.T,
                shape_ids.reshape(1, points),
                scale_index.reshape(1, points),
            )
        ]
    )
    def gather(array, group):
        masks = masks_of(group)[1:]
        return [array] + swaps([array] * len(masks), masks, devices)

    def join(arrays, *widths, early=()):
        height = sum(a.shape[0] for a in arrays)
        return small_kernel(
            "join",
            functools.partial(join_kernel, len(arrays), len(early)),
            [shape_of(height, width, BF16) for width in widths],
            *arrays[::-1],
            *early,
        )

    if tuned:
        arrays = gather(held, gathers[0])
        weight, code_weight = small_kernel(
            "pack",
            functools.partial(pack_kernel, shapes),
            [
                shape_of((half // LANES * len(arrays) + 1) * rows, LANES, BF16),
                shape_of(len(arrays) * rows, half, BF16),
            ],
            *[arrays[k] for k in FIRST],
        )
        weight, code_weight, x, x_t = lax.optimization_barrier((weight, code_weight, x, x_t))
        (weights,) = [gather(weight, group) for group in gathers[1:-1]]
        along, across = [[bit] for bit in gathers[1][::-1]]
        (weight,) = join(weights, LANES, early=(cotangent,))
        weights = gather(weight, gathers[-1])
        code_weights = gather(code_weight, along)
        code_order = order_of([gathers[0], along, across])
        orders = [[m ^ r for r in order_of(gathers[:-1])] for m in masks_of(gathers[-1])]
        code_orders = [[m ^ r for r in code_order] for m in masks_of(gathers[-1])]
        parts = [[m ^ r for r in order_of(groups[:-1])] for m in masks_of(groups[-1])]
    else:
        held = lax.all_gather(held, AXES, axis=0, tiled=True)
        weights, code_weights, orders, code_orders, parts = [held[:, :lanes]], [held[:, lanes:]], None, None, [[0]]

    head = points // layer_tile // 2 * layer_tile
    output, tail, grad_hidden, *grads = pl.pallas_call(
        functools.partial(layer_kernel, hid, shapes, layer_tile, orders, parts),
        out_shape=[
            pltpu.HBM((points, width), F32),
            pltpu.VMEM((points - head, width), F32),
            pltpu.VMEM((points, hid), F32),
        ]
        + [shape_of(2 * shapes + width // len(parts), half, BF16)] * len(parts),
        in_specs=vmem(len(weights) + 3),
        out_specs=[pl.BlockSpec(memory_space=pltpu.HBM)] + vmem(2 + len(parts)),
        scratch_shapes=[
            VMEM((width, lanes), BF16),
            VMEM((width, half), F32),
            VMEM((head, width), F32),
            VMEM((points, width), BF16),
            VMEM((2, layer_tile, width), F32),
            pltpu.SemaphoreType.DMA((head // layer_tile,)),
        ],
        compiler_params=pltpu.CompilerParams(vmem_limit_bytes=20 * MIB),
        cost_estimate=pl.CostEstimate(
            flops=6 * points * width * cols,
            bytes_accessed=8 * points * (width + half),
            transcendentals=points * width,
        ),
        name="layer",
    )(*weights, x, x_t, cotangent)

    def store(name, body, shape, *args, **options):
        return pl.pallas_call(
            body,
            out_shape=pltpu.HBM(shape, F32),
            in_specs=[pl.BlockSpec(memory_space=pltpu.HBM)] * (len(args) - 1) + vmem(1),
            out_specs=pl.BlockSpec(memory_space=pltpu.HBM),
            scratch_shapes=[pltpu.SemaphoreType.DMA(())],
            compiler_params=pltpu.CompilerParams(vmem_limit_bytes=8 * MIB),
            cost_estimate=pl.CostEstimate(
                flops=4000 * MIB, bytes_accessed=8 * points * hid, transcendentals=0
            ),
            name=name,
            **options,
        )(*args)

    def store_grad_hidden():
        return store("store", store_kernel, (points, hid), grad_hidden)

    def store_tail():
        return store(
            "tail", tail_kernel, (points, width), output, tail, input_output_aliases={0: 0}
        )

    if tuned:
        *grads, code_along = lax.optimization_barrier((*grads, code_weights[1]))
        (code_weight,) = join([code_weights[0], code_along], half)
        for r, group in enumerate(groups[::-1]):
            masks = masks_of(group)
            grads = [grads[0]] + swaps(grads[1:], masks[1:], devices)
            if r == len(groups) - 1:
                break
            n_out = len(masks_of(groups[-2 - r]))
            left = (grads[0].shape[0] - 2 * shapes) // n_out
            grads = small_kernel(
                "add",
                functools.partial(add_kernel, shapes, len(grads)),
                [shape_of(2 * shapes + left, half, BF16)] * n_out,
                *(grads[::-1] if r == 0 else [grads[k] for k in SUMS]),
            )
            if r == 0:
                *grads, grad_hidden = lax.optimization_barrier((*grads, grad_hidden))
                grad_hidden = store_grad_hidden()
                grad_hidden, code_weight = lax.optimization_barrier((grad_hidden, code_weight))
                code_weights = gather(code_weight, across)
            if r == len(groups) - 2:
                *grads, grad_hidden, tail, running_mean, running_var = lax.optimization_barrier(
                    (*grads, grad_hidden, tail, running_mean, running_var)
                )
                output = store_tail()
        (code_weight,) = join(code_weights, half)
        code_weights = gather(code_weight, groups[-1])
    else:
        grad_hidden, output = store_grad_hidden(), store_tail()
        sums = lax.psum(grads[0][: 2 * shapes].astype(F32), AXES)
        high = sums.astype(BF16)
        own = lax.psum_scatter(grads[0][2 * shapes :].astype(F32), AXES, scatter_dimension=0, tiled=True)
        low = jnp.zeros((2 * shapes + rows, half), BF16).at[: 2 * shapes].set((sums - high).astype(BF16))
        grads = [jnp.concatenate([high, own.astype(BF16)], axis=0), low]
    grad_codes, grad_direction, grad_gain, grad_bias = small_kernel(
        "last",
        functools.partial(last_kernel, hid, shapes, code_orders, len(grads)),
        [
            shape_of(shapes, half, F32),
            shape_of(rows, cols, F32),
            shape_of(1, rows, F32),
            shape_of(1, rows, F32),
        ],
        *grads[::-1],
        direction,
        gain_row,
        codes,
        *code_weights,
        scratch=[VMEM((width, half), BF16)],
    )

    total = float(points * devices)
    batch_mean = jnp.mean(codes, axis=0)
    batch_square = jnp.mean(codes * codes, axis=0)
    batch_var = (batch_square - batch_mean * batch_mean) * (total / (total - 1.0))
    new_mean = 0.9 * running_mean + 0.1 * batch_mean
    new_var = 0.9 * running_var + 0.1 * batch_var
    return (
        output,
        grad_hidden,
        grad_codes,
        grad_direction,
        grad_gain.reshape(rows),
        grad_bias.reshape(rows),
        new_mean,
        new_var,
    )


def solution(mesh):
    return jax.shard_map(
        per_device,
        mesh=mesh,
        in_specs=(
            P(("dp", "inner"), None),
            P(),
            P(("dp", "inner"), None),
            P(("dp", "inner")),
            P(("dp", "inner")),
            P(("dp", "inner"), None),
            P(("dp", "inner")),
            P(("dp", "inner")),
            P(("dp", "inner"), None),
            P(),
            P(),
        ),
        out_specs=(
            P(("dp", "inner"), None),
            P(("dp", "inner"), None),
            P(),
            P(("dp", "inner"), None),
            P(("dp", "inner")),
            P(("dp", "inner")),
            P(),
            P(),
        ),
        check_vma=False,
    )
```

```python
import functools

import jax
import jax.numpy as jnp
from jax import lax
from jax.experimental import pallas as pl
from jax.experimental.pallas import tpu as pltpu
from jax.sharding import PartitionSpec as P

AXES = ("dp", "inner")
LANES = 128
MIB = 1024 * 1024
FIRST = (2, 3, 1, 0)
SUMS = (1, 3, 2, 0)
F32 = jnp.float32
BF16 = jnp.bfloat16
VMEM = pltpu.VMEM
NT = (((1,), (1,)), ((), ()))


def dot(a, b, dims=(((1,), (0,)), ((), ()))):
    return lax.dot_general(a, b, dims, preferred_element_type=F32)


def vmem(n):
    return [pl.BlockSpec(memory_space=VMEM)] * n


def small_kernel(name, body, out_shape, *args, scratch=(), space=VMEM, limit=8):
    many = isinstance(out_shape, list)
    return pl.pallas_call(
        body,
        out_shape=out_shape,
        in_specs=[pl.BlockSpec(memory_space=space)] * len(args),
        out_specs=vmem(len(out_shape)) if many else vmem(1)[0],
        scratch_shapes=list(scratch),
        compiler_params=pltpu.CompilerParams(vmem_limit_bytes=limit * MIB),
        cost_estimate=pl.CostEstimate(
            flops=4000 * MIB, bytes_accessed=8 * MIB, transcendentals=4 * MIB
        ),
        name=name,
    )(*args)


def diagonal(n):
    return lax.broadcasted_iota(jnp.int32, (n, n), 0) == lax.broadcasted_iota(jnp.int32, (n, n), 1)


def to_column(row):
    n = row.shape[1]
    return jnp.sum(jnp.where(diagonal(n), row, 0.0), axis=1, keepdims=True)


def to_row(column):
    n = column.shape[0]
    return jnp.sum(jnp.where(diagonal(n), column, 0.0), axis=0, keepdims=True)


def stacked_codes(codes_ref, count):
    codes = codes_ref[...].astype(BF16)
    parts = [codes, codes]
    if count > 2 * codes.shape[0]:
        parts.append(jnp.zeros((count - 2 * codes.shape[0], codes.shape[1]), BF16))
    return jnp.concatenate(parts, axis=0)


def split(x):
    high = x.astype(BF16).astype(F32)
    return high, x - high


def prep_kernel(hid, *refs):
    piece_ref, direction_ref, gain_ref, bias_ref, codes_ref, sems = refs[4:]
    copies = [
        pltpu.make_async_copy(source, target, sems.at[k])
        for k, (source, target) in enumerate(zip(refs[:4], refs[5:9]))
    ]
    for copy in copies:
        copy.start()
    for copy in copies:
        copy.wait()
    d = direction_ref[...]
    shapes = codes_ref.shape[0]
    rows, cols = d.shape
    half = cols // 2
    extra_lanes = piece_ref.shape[1] - cols
    inverse = lax.rsqrt(jnp.sum(d * d, axis=1, keepdims=True))
    w = to_column(gain_ref[...]) * (d * inverse)
    lane = lax.broadcasted_iota(jnp.int32, (rows, half), 1)
    first = jnp.where(lane < hid, w[:, :half], w[:, half:])
    code = pltpu.roll(w, half - hid, 1)[:, half:].astype(BF16)
    bias = to_column(bias_ref[...]).astype(BF16).astype(F32)
    high, low = split(dot(code, stacked_codes(codes_ref, extra_lanes), NT) + bias)
    own = first[:, half - LANES :]
    if extra_lanes > LANES:
        own = jnp.concatenate([jnp.zeros((rows, extra_lanes - LANES), F32), own], axis=1)
    lane = lax.broadcasted_iota(jnp.int32, (rows, extra_lanes), 1)
    table = jnp.where(lane < shapes, high, jnp.where(lane < 2 * shapes, low, 0.0))
    table = jnp.where(lane >= extra_lanes - (half - hid), own, table)
    piece_ref[:, :half] = first.astype(BF16)
    piece_ref[:, half : half + extra_lanes] = table.astype(BF16)
    piece_ref[:, half + extra_lanes :] = code


def join_kernel(n, n_early, *refs):
    rows = refs[0].shape[0]
    for k, ref in enumerate(refs[n - 1 :: -1]):
        lane = 0
        for out_ref in refs[n + n_early :]:
            lanes = out_ref.shape[1]
            out_ref[k * rows : (k + 1) * rows, :] = ref[:, lane : lane + lanes]
            lane += lanes


def pack_kernel(shapes, *refs):
    weight_ref, code_ref = refs[-2:]
    count = len(refs) - 2
    rows, half = refs[0].shape[0], code_ref.shape[1]
    products = jnp.zeros((rows, LANES), F32)
    for k, ref in zip(FIRST, refs):
        for block in range(half // LANES):
            at = (block * count + k) * rows
            weight_ref[at : at + rows, :] = ref[:, block * LANES : (block + 1) * LANES]
        own = ref[:, half : half + LANES].astype(F32)
        own = jnp.where(lax.broadcasted_iota(jnp.int32, own.shape, 1) < 2 * shapes, own, 0.0)
        products = products + (pltpu.roll(own, 2 * shapes * k, 1) if k else own)
        code_ref[k * rows : (k + 1) * rows, :] = ref[:, half + LANES :]
    weight_ref[half // LANES * count * rows :, :] = products.astype(BF16)


def unpack(hid, shapes, refs, orders, me, w_ref):
    count = LANES // (2 * shapes)
    half = w_ref.shape[1] - LANES
    blocks = half // LANES
    for ref, order in zip(refs, orders):
        height = ref.shape[0] // (len(order) // count)
        rows = height // (blocks * count + 1)
        lane = lax.broadcasted_iota(jnp.int32, (rows, LANES), 1)
        for j, mask in enumerate(order):
            start, k = j // count * height, j % count
            at = pl.ds(pl.multiple_of((me ^ mask) * rows, rows), rows)
            for block in range(blocks):
                here = start + (block * count + k) * rows
                part = ref[here : here + rows, :]
                w_ref[at, block * LANES : (block + 1) * LANES] = part
            here = start + blocks * count * rows
            products = ref[here : here + rows, :].astype(F32)
            if k:
                products = pltpu.roll(products, LANES - 2 * shapes * k, 1)
            products = jnp.where(lane < 2 * shapes, products, 0.0)
            products = jnp.where(lane >= LANES - (half - hid), part.astype(F32), products)
            w_ref[at, half:] = products.astype(BF16)


def place(refs, orders, me, out_ref):
    if orders is None:
        out_ref[...] = refs[0][...]
        return
    rows = refs[0].shape[0] // len(orders[0])
    for ref, order in zip(refs, orders):
        for k, mask in enumerate(order):
            at = pl.multiple_of((me ^ mask) * rows, rows)
            out_ref[pl.ds(at, rows), :] = ref[k * rows : (k + 1) * rows, :]


def inputs_kernel(hid, tile, *refs):
    x_ref, x_t_ref, hidden_ref, offsets_ref, ids_ref, scale_ref, sems = refs[4:]
    points = x_ref.shape[0]
    half = (hid + LANES - 1) // LANES * LANES
    shapes = x_t_ref.shape[0] - half
    extra_lanes = x_ref.shape[1] - half
    steps = points // tile
    small = [
        pltpu.make_async_copy(source, target, sems.at[steps + k])
        for k, (source, target) in enumerate(zip(refs[1:4], (offsets_ref, ids_ref, scale_ref)))
    ]
    large = [
        pltpu.make_async_copy(
            refs[0].at[pl.ds(k * tile, tile), :], hidden_ref.at[pl.ds(k * tile, tile), :], sems.at[k]
        )
        for k in range(steps)
    ]
    for copy in small + large:
        copy.start()
    for copy in small:
        copy.wait()
    for step, copy in enumerate(large):
        here = slice(step * tile, (step + 1) * tile)
        scale = scale_ref[:, here]
        jitter = jnp.where(scale == 0, 1.0, jnp.where(scale == 1, 0.5, 0.25))
        xyz = offsets_ref[:, here] * jitter
        row = lax.broadcasted_iota(jnp.int32, (16, tile), 0)
        last = jnp.zeros((16, tile), F32)
        for k in range(half - hid):
            last = jnp.where(row == 16 - (half - hid) + k, xyz[k : k + 1], last)
        last = last.astype(BF16)
        row = lax.broadcasted_iota(jnp.int32, (extra_lanes - 16, tile), 0)
        ids = ids_ref[:, here]
        member = jnp.where((row == ids) | (row == ids + shapes), 1.0, 0.0).astype(BF16)
        x_ref[here, half:] = jnp.concatenate([member, last], axis=0).T
        x_t_ref[half:, here] = member[:shapes]
        copy.wait()
        x_ref[here, half - LANES : half] = jnp.zeros((tile, LANES), BF16)
        x_ref[here, :hid] = hidden_ref[here, :].astype(BF16)
        hidden = x_ref[here, :half].T
        x_t_ref[: half - 16, here] = hidden[: half - 16]
        x_t_ref[half - 16 : half, here] = hidden[half - 16 :] + last


def layer_kernel(hid, shapes, tile, orders, parts, *refs):
    n = 1 if orders is None else len(orders)
    pieces = refs[:n]
    x_ref, x_t_ref, cot_ref, out_hbm, tail_ref, grad_hidden_ref = refs[n : n + 6]
    grad_refs = refs[n + 6 : -6]
    w_ref, turned_ref, out_ref, grad_pre_ref, pre_ref, sems = refs[-6:]
    points, width = cot_ref.shape
    half = width // 2
    steps = points // tile
    head = out_ref.shape[0] // tile
    me = lax.axis_index(AXES)
    if orders is None:
        place(pieces, orders, me, w_ref)
    else:
        unpack(hid, shapes, pieces, orders, me, w_ref)
    copies = []

    def rows_of(step):
        return slice(step * tile, (step + 1) * tile)

    def forward(step):
        pre_ref[step % 2] = dot(x_ref[rows_of(step), :], w_ref[...], NT)

    def middle(step):
        here = rows_of(step)
        pre = pre_ref[step % 2]
        sigma = 0.5 * jnp.tanh(0.5 * pre) + 0.5
        out = pre * sigma
        if step < head:
            out_ref[here, :] = out
        else:
            tail_ref[rows_of(step - head), :] = out
        grad_pre_ref[here, :] = (cot_ref[here, :] * (sigma * (1.0 + (pre - out)))).astype(BF16)

    def backward(step):
        here = rows_of(step)
        grad_hidden_ref[here, :] = dot(grad_pre_ref[here, :], w_ref[:, :half])[:, :hid]

    def store(step):
        here = pl.ds(step * tile, tile)
        copy = pltpu.make_async_copy(out_ref.at[here, :], out_hbm.at[here, :], sems.at[step])
        copy.start()
        copies.append(copy)

    forward(0)
    for step in range(steps):
        if step + 1 < steps:
            forward(step + 1)
        middle(step)
        if step > 0:
            backward(step - 1)
        if step < head:
            store(step)
    backward(steps - 1)
    grad = dot(x_t_ref[...], grad_pre_ref[...])
    sums = grad[half:].astype(BF16)
    for at in range(0, width, half):
        turned_ref[at : at + half, :] = grad[:half, at : at + half].T
    for ref, order in zip(grad_refs, parts):
        ref[:shapes, :] = sums[:, :half]
        ref[shapes : 2 * shapes, :] = sums[:, half:]
        if orders is None:
            ref[2 * shapes :, :] = turned_ref[...].astype(BF16)
            continue
        rows = (ref.shape[0] - 2 * shapes) // len(order)
        for k, mask in enumerate(order):
            at = pl.multiple_of((me ^ mask) * rows, rows)
            to = 2 * shapes + k * rows
            ref[to : to + rows, :] = turned_ref[pl.ds(at, rows), :].astype(BF16)

    for copy in copies:
        copy.wait()


def store_kernel(source_ref, target_ref, sem):
    copy = pltpu.make_async_copy(source_ref, target_ref, sem)
    copy.start()
    copy.wait()


def tail_kernel(_, source_ref, target_ref, sem):
    points, rows = target_ref.shape[0], source_ref.shape[0]
    store_kernel(source_ref, target_ref.at[pl.ds(points - rows, rows), :], sem)


def sum_of(refs):
    terms = [ref[...].astype(F32) for ref in refs]
    while len(terms) > 1:
        terms = [a + b for a, b in zip(terms[::2], terms[1::2])]
    return terms[0]


def add_kernel(shapes, n, *refs):
    total = sum_of(refs[:n]).astype(BF16)
    for k, ref in enumerate(refs[n:]):
        rows = ref.shape[0] - 2 * shapes
        at = 2 * shapes + k * rows
        ref[: 2 * shapes, :] = total[: 2 * shapes]
        ref[2 * shapes :, :] = total[at : at + rows]


def last_kernel(hid, shapes, orders, n, *refs):
    direction_ref, gain_ref, codes_ref = refs[n : n + 3]
    pieces = refs[n + 3 : -5]
    grad_codes_ref, grad_direction_ref, grad_gain_ref, grad_bias_ref, code_scratch = refs[-5:]
    d = direction_ref[...]
    rows, cols = d.shape
    half = cols // 2
    me = lax.axis_index(AXES)
    place(pieces, orders, me, code_scratch)
    total = sum_of(refs[:n])
    sums = jnp.concatenate([total[:shapes], total[shapes : 2 * shapes]], axis=1)
    sums = jnp.concatenate(split(sums), axis=0).astype(BF16)
    terms = dot(sums, code_scratch[...])
    grad_codes_ref[...] = terms[:shapes] + terms[shapes:]
    width = sums.shape[1]
    mine = lax.broadcasted_iota(jnp.int32, (rows, width), 0) + me * rows
    mine = jnp.where(mine == lax.broadcasted_iota(jnp.int32, (rows, width), 1), 1.0, 0.0).astype(BF16)
    own = dot(mine, sums, NT)
    grad_bias_ref[...] = to_row(jnp.sum(own, axis=1, keepdims=True))
    code = dot(own.astype(BF16), stacked_codes(codes_ref, 2 * shapes))
    packed = jnp.concatenate([total[2 * shapes :], code], axis=1)
    lane = lax.broadcasted_iota(jnp.int32, (rows, cols), 1)
    grad_weight = jnp.where(
        lane < hid,
        packed,
        jnp.where(lane < hid + half, pltpu.roll(packed, cols - (half - hid), 1), pltpu.roll(packed, half, 1)),
    )
    inverse = lax.rsqrt(jnp.sum(d * d, axis=1, keepdims=True))
    unit = d * inverse
    grad_gain = jnp.sum(grad_weight * unit, axis=1, keepdims=True)
    grad_gain_ref[...] = to_row(grad_gain)
    grad_direction_ref[...] = (to_column(gain_ref[...]) * inverse) * (grad_weight - grad_gain * unit)


def masks_of(group):
    masks = [0]
    for bit in group:
        masks = masks + [m ^ bit for m in masks]
    return masks


def order_of(groups):
    order = [0]
    for group in groups:
        order = [m ^ r for m in masks_of(group) for r in order]
    return order


def swaps(arrays, masks, devices):
    moved = [
        lax.ppermute(x, AXES, [(i, i ^ mask) for i in range(devices)])
        for x, mask in list(zip(arrays, masks))[::-1]
    ]
    return moved[::-1]


def per_device(
    hidden,
    codes,
    offsets,
    shape_ids,
    scale_index,
    direction,
    gain,
    bias,
    cotangent,
    running_mean,
    running_var,
):
    points, hid = hidden.shape
    shapes = codes.shape[0]
    rows, cols = direction.shape
    width = cotangent.shape[1]
    half = cols // 2
    devices = lax.axis_size("dp") * lax.axis_size("inner")
    bits = [1 << k | 1 for k in range(devices.bit_length() - 1)]
    groups = [bits[k - 2 : k] for k in range(len(bits), 1, -2)]
    groups = groups + [bits[:1]] * (len(bits) % 2)
    gathers = [[groups[0][0], groups[0][-1] ^ 1]] + groups[1:]
    extra_lanes = -(-(2 * shapes + 16) // LANES) * LANES
    tuned = rows % 16 == 0 and 2 * shapes * len(masks_of(groups[0])) == LANES
    lanes = half + extra_lanes
    gain_row = gain.reshape(1, rows)

    def shape_of(rows, lanes, dtype):
        return jax.ShapeDtypeStruct((rows, lanes), dtype)

    held = small_kernel(
        "prep",
        functools.partial(prep_kernel, hid),
        shape_of(rows, lanes + half, BF16),
        *[
            pltpu.with_memory_space_constraint(x, pltpu.HBM)
            for x in (direction, gain_row, bias.reshape(1, rows), codes)
        ],
        scratch=[
            VMEM((rows, cols), F32),
            VMEM((1, rows), F32),
            VMEM((1, rows), F32),
            VMEM((shapes, half), F32),
            pltpu.SemaphoreType.DMA((4,)),
        ],
        space=pl.ANY,
    )
    tile, layer_tile = min(512, points), min(256, points)
    x, x_t = pl.pallas_call(
        functools.partial(inputs_kernel, hid, tile),
        out_shape=[
            shape_of(points, lanes, BF16),
            shape_of(half + shapes, points, BF16),
        ],
        in_specs=[pl.BlockSpec(memory_space=pl.ANY)] * 4,
        out_specs=vmem(2),
        scratch_shapes=[
            VMEM((points, hid), F32),
            VMEM((half - hid, points), F32),
            VMEM((1, points), jnp.int32),
            VMEM((1, points), jnp.int32),
            pltpu.SemaphoreType.DMA((points // tile + 3,)),
        ],
        compiler_params=pltpu.CompilerParams(vmem_limit_bytes=12 * MIB),
        cost_estimate=pl.CostEstimate(
            flops=4000 * MIB, bytes_accessed=8 * points * half, transcendentals=0
        ),
        name="inputs",
    )(
        *[
            pltpu.with_memory_space_constraint(a, pltpu.HBM)
            for a in (
                hidden,
                offsets.T,
                shape_ids.reshape(1, points),
                scale_index.reshape(1, points),
            )
        ]
    )
    def gather(array, group):
        masks = masks_of(group)[1:]
        return [array] + swaps([array] * len(masks), masks, devices)

    def join(arrays, *widths, early=()):
        height = sum(a.shape[0] for a in arrays)
        return small_kernel(
            "join",
            functools.partial(join_kernel, len(arrays), len(early)),
            [shape_of(height, width, BF16) for width in widths],
            *arrays[::-1],
            *early,
        )

    if tuned:
        arrays = gather(held, gathers[0])
        weight, code_weight = small_kernel(
            "pack",
            functools.partial(pack_kernel, shapes),
            [
                shape_of((half // LANES * len(arrays) + 1) * rows, LANES, BF16),
                shape_of(len(arrays) * rows, half, BF16),
            ],
            *[arrays[k] for k in FIRST],
        )
        weight, code_weight, x, x_t = lax.optimization_barrier((weight, code_weight, x, x_t))
        (weights,) = [gather(weight, group) for group in gathers[1:-1]]
        along, across = [[bit] for bit in gathers[1][::-1]]
        (weight,) = join(weights, LANES, early=(cotangent,))
        weights = gather(weight, gathers[-1])
        code_weights = gather(code_weight, along)
        code_order = order_of([gathers[0], along, across])
        orders = [[m ^ r for r in order_of(gathers[:-1])] for m in masks_of(gathers[-1])]
        code_orders = [[m ^ r for r in code_order] for m in masks_of(gathers[-1])]
        parts = [[m ^ r for r in order_of(groups[:-1])] for m in masks_of(groups[-1])]
    else:
        held = lax.all_gather(held, AXES, axis=0, tiled=True)
        weights, code_weights, orders, code_orders, parts = [held[:, :lanes]], [held[:, lanes:]], None, None, [[0]]

    head = points // layer_tile // 2 * layer_tile
    output, tail, grad_hidden, *grads = pl.pallas_call(
        functools.partial(layer_kernel, hid, shapes, layer_tile, orders, parts),
        out_shape=[
            pltpu.HBM((points, width), F32),
            pltpu.VMEM((points - head, width), F32),
            pltpu.VMEM((points, hid), F32),
        ]
        + [shape_of(2 * shapes + width // len(parts), half, BF16)] * len(parts),
        in_specs=vmem(len(weights) + 3),
        out_specs=[pl.BlockSpec(memory_space=pltpu.HBM)] + vmem(2 + len(parts)),
        scratch_shapes=[
            VMEM((width, lanes), BF16),
            VMEM((width, half), F32),
            VMEM((head, width), F32),
            VMEM((points, width), BF16),
            VMEM((2, layer_tile, width), F32),
            pltpu.SemaphoreType.DMA((head // layer_tile,)),
        ],
        compiler_params=pltpu.CompilerParams(vmem_limit_bytes=20 * MIB),
        cost_estimate=pl.CostEstimate(
            flops=6 * points * width * cols,
            bytes_accessed=8 * points * (width + half),
            transcendentals=points * width,
        ),
        name="layer",
    )(*weights, x, x_t, cotangent)

    def store(name, body, shape, *args, **options):
        return pl.pallas_call(
            body,
            out_shape=pltpu.HBM(shape, F32),
            in_specs=[pl.BlockSpec(memory_space=pltpu.HBM)] * (len(args) - 1) + vmem(1),
            out_specs=pl.BlockSpec(memory_space=pltpu.HBM),
            scratch_shapes=[pltpu.SemaphoreType.DMA(())],
            compiler_params=pltpu.CompilerParams(vmem_limit_bytes=8 * MIB),
            cost_estimate=pl.CostEstimate(
                flops=4000 * MIB, bytes_accessed=8 * points * hid, transcendentals=0
            ),
            name=name,
            **options,
        )(*args)

    def store_grad_hidden():
        return store("store", store_kernel, (points, hid), grad_hidden)

    def store_tail():
        return store(
            "tail", tail_kernel, (points, width), output, tail, input_output_aliases={0: 0}
        )

    if tuned:
        *grads, code_along, running_mean, running_var = lax.optimization_barrier(
            (*grads, code_weights[1], running_mean, running_var)
        )
        (code_weight,) = join([code_weights[0], code_along], half)
        for r, group in enumerate(groups[::-1]):
            masks = masks_of(group)
            grads = [grads[0]] + swaps(grads[1:], masks[1:], devices)
            if r == len(groups) - 1:
                break
            n_out = len(masks_of(groups[-2 - r]))
            left = (grads[0].shape[0] - 2 * shapes) // n_out
            grads = small_kernel(
                "add",
                functools.partial(add_kernel, shapes, len(grads)),
                [shape_of(2 * shapes + left, half, BF16)] * n_out,
                *(grads[::-1] if r == 0 else [grads[k] for k in SUMS]),
            )
            if r == 0:
                *grads, grad_hidden = lax.optimization_barrier((*grads, grad_hidden))
                grad_hidden = store_grad_hidden()
                grad_hidden, code_weight = lax.optimization_barrier((grad_hidden, code_weight))
                code_weights = gather(code_weight, across)
            if r == len(groups) - 2:
                *grads, grad_hidden, tail = lax.optimization_barrier((*grads, grad_hidden, tail))
                output = store_tail()
        (code_weight,) = join(code_weights, half)
        code_weights = gather(code_weight, groups[-1])
    else:
        grad_hidden, output = store_grad_hidden(), store_tail()
        sums = lax.psum(grads[0][: 2 * shapes].astype(F32), AXES)
        high = sums.astype(BF16)
        own = lax.psum_scatter(grads[0][2 * shapes :].astype(F32), AXES, scatter_dimension=0, tiled=True)
        low = jnp.zeros((2 * shapes + rows, half), BF16).at[: 2 * shapes].set((sums - high).astype(BF16))
        grads = [jnp.concatenate([high, own.astype(BF16)], axis=0), low]
    grad_codes, grad_direction, grad_gain, grad_bias = small_kernel(
        "last",
        functools.partial(last_kernel, hid, shapes, code_orders, len(grads)),
        [
            shape_of(shapes, half, F32),
            shape_of(rows, cols, F32),
            shape_of(1, rows, F32),
            shape_of(1, rows, F32),
        ],
        *grads[::-1],
        direction,
        gain_row,
        codes,
        *code_weights,
        scratch=[VMEM((width, half), BF16)],
    )

    total = float(points * devices)
    batch_mean = jnp.mean(codes, axis=0)
    batch_square = jnp.mean(codes * codes, axis=0)
    batch_var = (batch_square - batch_mean * batch_mean) * (total / (total - 1.0))
    new_mean = 0.9 * running_mean + 0.1 * batch_mean
    new_var = 0.9 * running_var + 0.1 * batch_var
    return (
        output,
        grad_hidden,
        grad_codes,
        grad_direction,
        grad_gain.reshape(rows),
        grad_bias.reshape(rows),
        new_mean,
        new_var,
    )


def solution(mesh):
    return jax.shard_map(
        per_device,
        mesh=mesh,
        in_specs=(
            P(("dp", "inner"), None),
            P(),
            P(("dp", "inner"), None),
            P(("dp", "inner")),
            P(("dp", "inner")),
            P(("dp", "inner"), None),
            P(("dp", "inner")),
            P(("dp", "inner")),
            P(("dp", "inner"), None),
            P(),
            P(),
        ),
        out_specs=(
            P(("dp", "inner"), None),
            P(("dp", "inner"), None),
            P(),
            P(("dp", "inner"), None),
            P(("dp", "inner")),
            P(("dp", "inner")),
            P(),
            P(),
        ),
        check_vma=False,
    )
```

```python
import functools

import jax
import jax.numpy as jnp
from jax import lax
from jax.experimental import pallas as pl
from jax.experimental.pallas import tpu as pltpu
from jax.sharding import PartitionSpec as P

AXES = ("dp", "inner")
LANES = 128
MIB = 1024 * 1024
FIRST = (2, 3, 1, 0)
SUMS = (1, 3, 2, 0)
F32 = jnp.float32
BF16 = jnp.bfloat16
VMEM = pltpu.VMEM
NT = (((1,), (1,)), ((), ()))


def dot(a, b, dims=(((1,), (0,)), ((), ()))):
    return lax.dot_general(a, b, dims, preferred_element_type=F32)


def vmem(n):
    return [pl.BlockSpec(memory_space=VMEM)] * n


def small_kernel(name, body, out_shape, *args, scratch=(), space=VMEM, limit=8):
    many = isinstance(out_shape, list)
    return pl.pallas_call(
        body,
        out_shape=out_shape,
        in_specs=[pl.BlockSpec(memory_space=space)] * len(args),
        out_specs=vmem(len(out_shape)) if many else vmem(1)[0],
        scratch_shapes=list(scratch),
        compiler_params=pltpu.CompilerParams(vmem_limit_bytes=limit * MIB),
        cost_estimate=pl.CostEstimate(
            flops=4000 * MIB, bytes_accessed=8 * MIB, transcendentals=4 * MIB
        ),
        name=name,
    )(*args)


def diagonal(n):
    return lax.broadcasted_iota(jnp.int32, (n, n), 0) == lax.broadcasted_iota(jnp.int32, (n, n), 1)


def to_column(row):
    n = row.shape[1]
    return jnp.sum(jnp.where(diagonal(n), row, 0.0), axis=1, keepdims=True)


def to_row(column):
    n = column.shape[0]
    return jnp.sum(jnp.where(diagonal(n), column, 0.0), axis=0, keepdims=True)


def stacked_codes(codes_ref, count):
    codes = codes_ref[...].astype(BF16)
    parts = [codes, codes]
    if count > 2 * codes.shape[0]:
        parts.append(jnp.zeros((count - 2 * codes.shape[0], codes.shape[1]), BF16))
    return jnp.concatenate(parts, axis=0)


def split(x):
    high = x.astype(BF16).astype(F32)
    return high, x - high


def prep_kernel(hid, *refs):
    piece_ref, direction_ref, gain_ref, bias_ref, codes_ref, sems = refs[4:]
    copies = [
        pltpu.make_async_copy(source, target, sems.at[k])
        for k, (source, target) in enumerate(zip(refs[:4], refs[5:9]))
    ]
    for copy in copies:
        copy.start()
    for copy in copies:
        copy.wait()
    d = direction_ref[...]
    shapes = codes_ref.shape[0]
    rows, cols = d.shape
    half = cols // 2
    extra_lanes = piece_ref.shape[1] - cols
    inverse = lax.rsqrt(jnp.sum(d * d, axis=1, keepdims=True))
    w = to_column(gain_ref[...]) * (d * inverse)
    lane = lax.broadcasted_iota(jnp.int32, (rows, half), 1)
    first = jnp.where(lane < hid, w[:, :half], w[:, half:])
    code = pltpu.roll(w, half - hid, 1)[:, half:].astype(BF16)
    bias = to_column(bias_ref[...]).astype(BF16).astype(F32)
    high, low = split(dot(code, stacked_codes(codes_ref, extra_lanes), NT) + bias)
    own = first[:, half - LANES :]
    if extra_lanes > LANES:
        own = jnp.concatenate([jnp.zeros((rows, extra_lanes - LANES), F32), own], axis=1)
    lane = lax.broadcasted_iota(jnp.int32, (rows, extra_lanes), 1)
    table = jnp.where(lane < shapes, high, jnp.where(lane < 2 * shapes, low, 0.0))
    table = jnp.where(lane >= extra_lanes - (half - hid), own, table)
    piece_ref[:, :half] = first.astype(BF16)
    piece_ref[:, half : half + extra_lanes] = table.astype(BF16)
    piece_ref[:, half + extra_lanes :] = code


def join_kernel(n, n_early, *refs):
    rows = refs[0].shape[0]
    for k, ref in enumerate(refs[n - 1 :: -1]):
        lane = 0
        for out_ref in refs[n + n_early :]:
            lanes = out_ref.shape[1]
            out_ref[k * rows : (k + 1) * rows, :] = ref[:, lane : lane + lanes]
            lane += lanes


def pack_kernel(shapes, *refs):
    weight_ref, code_ref = refs[-2:]
    count = len(refs) - 2
    rows, half = refs[0].shape[0], code_ref.shape[1]
    products = jnp.zeros((rows, LANES), F32)
    for k, ref in zip(FIRST, refs):
        for block in range(half // LANES):
            at = (block * count + k) * rows
            weight_ref[at : at + rows, :] = ref[:, block * LANES : (block + 1) * LANES]
        own = ref[:, half : half + LANES].astype(F32)
        own = jnp.where(lax.broadcasted_iota(jnp.int32, own.shape, 1) < 2 * shapes, own, 0.0)
        products = products + (pltpu.roll(own, 2 * shapes * k, 1) if k else own)
        code_ref[k * rows : (k + 1) * rows, :] = ref[:, half + LANES :]
    weight_ref[half // LANES * count * rows :, :] = products.astype(BF16)


def unpack(hid, shapes, refs, orders, me, w_ref):
    count = LANES // (2 * shapes)
    half = w_ref.shape[1] - LANES
    blocks = half // LANES
    for ref, order in zip(refs, orders):
        height = ref.shape[0] // (len(order) // count)
        rows = height // (blocks * count + 1)
        lane = lax.broadcasted_iota(jnp.int32, (rows, LANES), 1)
        for j, mask in enumerate(order):
            start, k = j // count * height, j % count
            at = pl.ds(pl.multiple_of((me ^ mask) * rows, rows), rows)
            for block in range(blocks):
                here = start + (block * count + k) * rows
                part = ref[here : here + rows, :]
                w_ref[at, block * LANES : (block + 1) * LANES] = part
            here = start + blocks * count * rows
            products = ref[here : here + rows, :].astype(F32)
            if k:
                products = pltpu.roll(products, LANES - 2 * shapes * k, 1)
            products = jnp.where(lane < 2 * shapes, products, 0.0)
            products = jnp.where(lane >= LANES - (half - hid), part.astype(F32), products)
            w_ref[at, half:] = products.astype(BF16)


def place(refs, orders, me, out_ref):
    if orders is None:
        out_ref[...] = refs[0][...]
        return
    rows = refs[0].shape[0] // len(orders[0])
    for ref, order in zip(refs, orders):
        for k, mask in enumerate(order):
            at = pl.multiple_of((me ^ mask) * rows, rows)
            out_ref[pl.ds(at, rows), :] = ref[k * rows : (k + 1) * rows, :]


def inputs_kernel(hid, tile, *refs):
    x_ref, x_t_ref, hidden_ref, offsets_ref, ids_ref, scale_ref, sems = refs[4:]
    points = x_ref.shape[0]
    half = (hid + LANES - 1) // LANES * LANES
    shapes = x_t_ref.shape[0] - half
    extra_lanes = x_ref.shape[1] - half
    steps = points // tile
    small = [
        pltpu.make_async_copy(source, target, sems.at[steps + k])
        for k, (source, target) in enumerate(zip(refs[1:4], (offsets_ref, ids_ref, scale_ref)))
    ]
    large = [
        pltpu.make_async_copy(
            refs[0].at[pl.ds(k * tile, tile), :], hidden_ref.at[pl.ds(k * tile, tile), :], sems.at[k]
        )
        for k in range(steps)
    ]
    for copy in small + large:
        copy.start()
    for copy in small:
        copy.wait()
    for step, copy in enumerate(large):
        here = slice(step * tile, (step + 1) * tile)
        scale = scale_ref[:, here]
        jitter = jnp.where(scale == 0, 1.0, jnp.where(scale == 1, 0.5, 0.25))
        xyz = offsets_ref[:, here] * jitter
        row = lax.broadcasted_iota(jnp.int32, (16, tile), 0)
        last = jnp.zeros((16, tile), F32)
        for k in range(half - hid):
            last = jnp.where(row == 16 - (half - hid) + k, xyz[k : k + 1], last)
        last = last.astype(BF16)
        row = lax.broadcasted_iota(jnp.int32, (extra_lanes - 16, tile), 0)
        ids = ids_ref[:, here]
        member = jnp.where((row == ids) | (row == ids + shapes), 1.0, 0.0).astype(BF16)
        x_ref[here, half:] = jnp.concatenate([member, last], axis=0).T
        x_t_ref[half:, here] = member[:shapes]
        copy.wait()
        x_ref[here, half - LANES : half] = jnp.zeros((tile, LANES), BF16)
        x_ref[here, :hid] = hidden_ref[here, :].astype(BF16)
        hidden = x_ref[here, :half].T
        x_t_ref[: half - 16, here] = hidden[: half - 16]
        x_t_ref[half - 16 : half, here] = hidden[half - 16 :] + last


def layer_kernel(hid, shapes, tile, orders, parts, *refs):
    n = 1 if orders is None else len(orders)
    pieces = refs[:n]
    x_ref, x_t_ref, cot_ref, out_hbm, tail_ref, grad_hidden_ref = refs[n : n + 6]
    grad_refs = refs[n + 6 : -6]
    w_ref, turned_ref, out_ref, grad_pre_ref, pre_ref, sems = refs[-6:]
    points, width = cot_ref.shape
    half = width // 2
    steps = points // tile
    head = out_ref.shape[0] // tile
    me = lax.axis_index(AXES)
    if orders is None:
        place(pieces, orders, me, w_ref)
    else:
        unpack(hid, shapes, pieces, orders, me, w_ref)
    copies = []

    def rows_of(step):
        return slice(step * tile, (step + 1) * tile)

    def forward(step):
        pre_ref[step % 2] = dot(x_ref[rows_of(step), :], w_ref[...], NT)

    def middle(step):
        here = rows_of(step)
        pre = pre_ref[step % 2]
        sigma = 0.5 * jnp.tanh(0.5 * pre) + 0.5
        out = pre * sigma
        if step < head:
            out_ref[here, :] = out
        else:
            tail_ref[rows_of(step - head), :] = out
        grad_pre_ref[here, :] = (cot_ref[here, :] * (sigma * (1.0 + (pre - out)))).astype(BF16)

    def backward(step):
        here = rows_of(step)
        grad_hidden_ref[here, :] = dot(grad_pre_ref[here, :], w_ref[:, :half])[:, :hid]

    def store(step):
        here = pl.ds(step * tile, tile)
        copy = pltpu.make_async_copy(out_ref.at[here, :], out_hbm.at[here, :], sems.at[step])
        copy.start()
        copies.append(copy)

    forward(0)
    for step in range(steps):
        if step + 1 < steps:
            forward(step + 1)
        middle(step)
        if step > 0:
            backward(step - 1)
        if step < head:
            store(step)
    backward(steps - 1)
    grad = dot(x_t_ref[...], grad_pre_ref[...])
    sums = grad[half:].astype(BF16)
    for at in range(0, width, half):
        turned_ref[at : at + half, :] = grad[:half, at : at + half].T
    for ref, order in zip(grad_refs, parts):
        ref[:shapes, :] = sums[:, :half]
        ref[shapes : 2 * shapes, :] = sums[:, half:]
        if orders is None:
            ref[2 * shapes :, :] = turned_ref[...].astype(BF16)
            continue
        rows = (ref.shape[0] - 2 * shapes) // len(order)
        for k, mask in enumerate(order):
            at = pl.multiple_of((me ^ mask) * rows, rows)
            to = 2 * shapes + k * rows
            ref[to : to + rows, :] = turned_ref[pl.ds(at, rows), :].astype(BF16)

    for copy in copies:
        copy.wait()


def store_kernel(source_ref, target_ref, sem):
    copy = pltpu.make_async_copy(source_ref, target_ref, sem)
    copy.start()
    copy.wait()


def tail_kernel(_, source_ref, target_ref, sem):
    points, rows = target_ref.shape[0], source_ref.shape[0]
    store_kernel(source_ref, target_ref.at[pl.ds(points - rows, rows), :], sem)


def sum_of(refs):
    terms = [ref[...].astype(F32) for ref in refs]
    while len(terms) > 1:
        terms = [a + b for a, b in zip(terms[::2], terms[1::2])]
    return terms[0]


def add_kernel(shapes, n, *refs):
    total = sum_of(refs[:n]).astype(BF16)
    for k, ref in enumerate(refs[n:]):
        rows = ref.shape[0] - 2 * shapes
        at = 2 * shapes + k * rows
        ref[: 2 * shapes, :] = total[: 2 * shapes]
        ref[2 * shapes :, :] = total[at : at + rows]


def last_kernel(hid, shapes, orders, n, *refs):
    direction_ref, gain_ref, codes_ref = refs[n : n + 3]
    pieces = refs[n + 3 : -5]
    grad_codes_ref, grad_direction_ref, grad_gain_ref, grad_bias_ref, code_scratch = refs[-5:]
    d = direction_ref[...]
    rows, cols = d.shape
    half = cols // 2
    me = lax.axis_index(AXES)
    place(pieces, orders, me, code_scratch)
    total = sum_of(refs[:n])
    sums = jnp.concatenate([total[:shapes], total[shapes : 2 * shapes]], axis=1)
    sums = jnp.concatenate(split(sums), axis=0).astype(BF16)
    terms = dot(sums, code_scratch[...])
    grad_codes_ref[...] = terms[:shapes] + terms[shapes:]
    width = sums.shape[1]
    mine = lax.broadcasted_iota(jnp.int32, (rows, width), 0) + me * rows
    mine = jnp.where(mine == lax.broadcasted_iota(jnp.int32, (rows, width), 1), 1.0, 0.0).astype(BF16)
    own = dot(mine, sums, NT)
    grad_bias_ref[...] = to_row(jnp.sum(own, axis=1, keepdims=True))
    code = dot(own.astype(BF16), stacked_codes(codes_ref, 2 * shapes))
    packed = jnp.concatenate([total[2 * shapes :], code], axis=1)
    lane = lax.broadcasted_iota(jnp.int32, (rows, cols), 1)
    grad_weight = jnp.where(
        lane < hid,
        packed,
        jnp.where(lane < hid + half, pltpu.roll(packed, cols - (half - hid), 1), pltpu.roll(packed, half, 1)),
    )
    inverse = lax.rsqrt(jnp.sum(d * d, axis=1, keepdims=True))
    unit = d * inverse
    grad_gain = jnp.sum(grad_weight * unit, axis=1, keepdims=True)
    grad_gain_ref[...] = to_row(grad_gain)
    grad_direction_ref[...] = (to_column(gain_ref[...]) * inverse) * (grad_weight - grad_gain * unit)


def masks_of(group):
    masks = [0]
    for bit in group:
        masks = masks + [m ^ bit for m in masks]
    return masks


def order_of(groups):
    order = [0]
    for group in groups:
        order = [m ^ r for m in masks_of(group) for r in order]
    return order


def swaps(arrays, masks, devices):
    moved = [
        lax.ppermute(x, AXES, [(i, i ^ mask) for i in range(devices)])
        for x, mask in list(zip(arrays, masks))[::-1]
    ]
    return moved[::-1]


def per_device(
    hidden,
    codes,
    offsets,
    shape_ids,
    scale_index,
    direction,
    gain,
    bias,
    cotangent,
    running_mean,
    running_var,
):
    points, hid = hidden.shape
    shapes = codes.shape[0]
    rows, cols = direction.shape
    width = cotangent.shape[1]
    half = cols // 2
    devices = lax.axis_size("dp") * lax.axis_size("inner")
    bits = [1 << k | 1 for k in range(devices.bit_length() - 1)]
    groups = [bits[k - 2 : k] for k in range(len(bits), 1, -2)]
    groups = groups + [bits[:1]] * (len(bits) % 2)
    gathers = [[groups[0][0], groups[0][-1] ^ 1]] + groups[1:]
    extra_lanes = -(-(2 * shapes + 16) // LANES) * LANES
    tuned = rows % 16 == 0 and 2 * shapes * len(masks_of(groups[0])) == LANES
    lanes = half + extra_lanes
    gain_row = gain.reshape(1, rows)

    def shape_of(rows, lanes, dtype):
        return jax.ShapeDtypeStruct((rows, lanes), dtype)

    held = small_kernel(
        "prep",
        functools.partial(prep_kernel, hid),
        shape_of(rows, lanes + half, BF16),
        *[
            pltpu.with_memory_space_constraint(x, pltpu.HBM)
            for x in (direction, gain_row, bias.reshape(1, rows), codes)
        ],
        scratch=[
            VMEM((rows, cols), F32),
            VMEM((1, rows), F32),
            VMEM((1, rows), F32),
            VMEM((shapes, half), F32),
            pltpu.SemaphoreType.DMA((4,)),
        ],
        space=pl.ANY,
    )
    tile, layer_tile = min(512, points), min(512, points)
    x, x_t = pl.pallas_call(
        functools.partial(inputs_kernel, hid, tile),
        out_shape=[
            shape_of(points, lanes, BF16),
            shape_of(half + shapes, points, BF16),
        ],
        in_specs=[pl.BlockSpec(memory_space=pl.ANY)] * 4,
        out_specs=vmem(2),
        scratch_shapes=[
            VMEM((points, hid), F32),
            VMEM((half - hid, points), F32),
            VMEM((1, points), jnp.int32),
            VMEM((1, points), jnp.int32),
            pltpu.SemaphoreType.DMA((points // tile + 3,)),
        ],
        compiler_params=pltpu.CompilerParams(vmem_limit_bytes=12 * MIB),
        cost_estimate=pl.CostEstimate(
            flops=4000 * MIB, bytes_accessed=8 * points * half, transcendentals=0
        ),
        name="inputs",
    )(
        *[
            pltpu.with_memory_space_constraint(a, pltpu.HBM)
            for a in (
                hidden,
                offsets.T,
                shape_ids.reshape(1, points),
                scale_index.reshape(1, points),
            )
        ]
    )
    def gather(array, group):
        masks = masks_of(group)[1:]
        return [array] + swaps([array] * len(masks), masks, devices)

    def join(arrays, *widths, early=()):
        height = sum(a.shape[0] for a in arrays)
        return small_kernel(
            "join",
            functools.partial(join_kernel, len(arrays), len(early)),
            [shape_of(height, width, BF16) for width in widths],
            *arrays[::-1],
            *early,
        )

    if tuned:
        arrays = gather(held, gathers[0])
        weight, code_weight = small_kernel(
            "pack",
            functools.partial(pack_kernel, shapes),
            [
                shape_of((half // LANES * len(arrays) + 1) * rows, LANES, BF16),
                shape_of(len(arrays) * rows, half, BF16),
            ],
            *[arrays[k] for k in FIRST],
        )
        weight, code_weight, x, x_t = lax.optimization_barrier((weight, code_weight, x, x_t))
        (weights,) = [gather(weight, group) for group in gathers[1:-1]]
        along, across = [[bit] for bit in gathers[1][::-1]]
        (weight,) = join(weights, LANES, early=(cotangent,))
        weights = gather(weight, gathers[-1])
        code_weights = gather(code_weight, along)
        code_order = order_of([gathers[0], along, across])
        orders = [[m ^ r for r in order_of(gathers[:-1])] for m in masks_of(gathers[-1])]
        code_orders = [[m ^ r for r in code_order] for m in masks_of(gathers[-1])]
        parts = [[m ^ r for r in order_of(groups[:-1])] for m in masks_of(groups[-1])]
    else:
        held = lax.all_gather(held, AXES, axis=0, tiled=True)
        weights, code_weights, orders, code_orders, parts = [held[:, :lanes]], [held[:, lanes:]], None, None, [[0]]

    head = points // layer_tile // 2 * layer_tile
    output, tail, grad_hidden, *grads = pl.pallas_call(
        functools.partial(layer_kernel, hid, shapes, layer_tile, orders, parts),
        out_shape=[
            pltpu.HBM((points, width), F32),
            pltpu.VMEM((points - head, width), F32),
            pltpu.VMEM((points, hid), F32),
        ]
        + [shape_of(2 * shapes + width // len(parts), half, BF16)] * len(parts),
        in_specs=vmem(len(weights) + 3),
        out_specs=[pl.BlockSpec(memory_space=pltpu.HBM)] + vmem(2 + len(parts)),
        scratch_shapes=[
            VMEM((width, lanes), BF16),
            VMEM((width, half), F32),
            VMEM((head, width), F32),
            VMEM((points, width), BF16),
            VMEM((2, layer_tile, width), F32),
            pltpu.SemaphoreType.DMA((head // layer_tile,)),
        ],
        compiler_params=pltpu.CompilerParams(vmem_limit_bytes=20 * MIB),
        cost_estimate=pl.CostEstimate(
            flops=6 * points * width * cols,
            bytes_accessed=8 * points * (width + half),
            transcendentals=points * width,
        ),
        name="layer",
    )(*weights, x, x_t, cotangent)

    def store(name, body, shape, *args, **options):
        return pl.pallas_call(
            body,
            out_shape=pltpu.HBM(shape, F32),
            in_specs=[pl.BlockSpec(memory_space=pltpu.HBM)] * (len(args) - 1) + vmem(1),
            out_specs=pl.BlockSpec(memory_space=pltpu.HBM),
            scratch_shapes=[pltpu.SemaphoreType.DMA(())],
            compiler_params=pltpu.CompilerParams(vmem_limit_bytes=8 * MIB),
            cost_estimate=pl.CostEstimate(
                flops=4000 * MIB, bytes_accessed=8 * points * hid, transcendentals=0
            ),
            name=name,
            **options,
        )(*args)

    def store_grad_hidden():
        return store("store", store_kernel, (points, hid), grad_hidden)

    def store_tail():
        return store(
            "tail", tail_kernel, (points, width), output, tail, input_output_aliases={0: 0}
        )

    if tuned:
        *grads, code_along, running_mean, running_var = lax.optimization_barrier(
            (*grads, code_weights[1], running_mean, running_var)
        )
        (code_weight,) = join([code_weights[0], code_along], half)
        for r, group in enumerate(groups[::-1]):
            masks = masks_of(group)
            grads = [grads[0]] + swaps(grads[1:], masks[1:], devices)
            if r == len(groups) - 1:
                break
            n_out = len(masks_of(groups[-2 - r]))
            left = (grads[0].shape[0] - 2 * shapes) // n_out
            grads = small_kernel(
                "add",
                functools.partial(add_kernel, shapes, len(grads)),
                [shape_of(2 * shapes + left, half, BF16)] * n_out,
                *(grads[::-1] if r == 0 else [grads[k] for k in SUMS]),
            )
            if r == 0:
                *grads, grad_hidden = lax.optimization_barrier((*grads, grad_hidden))
                grad_hidden = store_grad_hidden()
                grad_hidden, code_weight = lax.optimization_barrier((grad_hidden, code_weight))
                code_weights = gather(code_weight, across)
            if r == len(groups) - 2:
                *grads, grad_hidden, tail = lax.optimization_barrier((*grads, grad_hidden, tail))
                output = store_tail()
        (code_weight,) = join(code_weights, half)
        code_weights = gather(code_weight, groups[-1])
    else:
        grad_hidden, output = store_grad_hidden(), store_tail()
        sums = lax.psum(grads[0][: 2 * shapes].astype(F32), AXES)
        high = sums.astype(BF16)
        own = lax.psum_scatter(grads[0][2 * shapes :].astype(F32), AXES, scatter_dimension=0, tiled=True)
        low = jnp.zeros((2 * shapes + rows, half), BF16).at[: 2 * shapes].set((sums - high).astype(BF16))
        grads = [jnp.concatenate([high, own.astype(BF16)], axis=0), low]
    grad_codes, grad_direction, grad_gain, grad_bias = small_kernel(
        "last",
        functools.partial(last_kernel, hid, shapes, code_orders, len(grads)),
        [
            shape_of(shapes, half, F32),
            shape_of(rows, cols, F32),
            shape_of(1, rows, F32),
            shape_of(1, rows, F32),
        ],
        *grads[::-1],
        direction,
        gain_row,
        codes,
        *code_weights,
        scratch=[VMEM((width, half), BF16)],
    )

    total = float(points * devices)
    batch_mean = jnp.mean(codes, axis=0)
    batch_square = jnp.mean(codes * codes, axis=0)
    batch_var = (batch_square - batch_mean * batch_mean) * (total / (total - 1.0))
    new_mean = 0.9 * running_mean + 0.1 * batch_mean
    new_var = 0.9 * running_var + 0.1 * batch_var
    return (
        output,
        grad_hidden,
        grad_codes,
        grad_direction,
        grad_gain.reshape(rows),
        grad_bias.reshape(rows),
        new_mean,
        new_var,
    )


def solution(mesh):
    return jax.shard_map(
        per_device,
        mesh=mesh,
        in_specs=(
            P(("dp", "inner"), None),
            P(),
            P(("dp", "inner"), None),
            P(("dp", "inner")),
            P(("dp", "inner")),
            P(("dp", "inner"), None),
            P(("dp", "inner")),
            P(("dp", "inner")),
            P(("dp", "inner"), None),
            P(),
            P(),
        ),
        out_specs=(
            P(("dp", "inner"), None),
            P(("dp", "inner"), None),
            P(),
            P(("dp", "inner"), None),
            P(("dp", "inner")),
            P(("dp", "inner")),
            P(),
            P(),
        ),
        check_vma=False,
    )
```

```python
import functools

import jax
import jax.numpy as jnp
from jax import lax
from jax.experimental import pallas as pl
from jax.experimental.pallas import tpu as pltpu
from jax.sharding import PartitionSpec as P

AXES = ("dp", "inner")
LANES = 128
MIB = 1024 * 1024
FIRST = (2, 3, 1, 0)
SUMS = (1, 3, 2, 0)
F32 = jnp.float32
BF16 = jnp.bfloat16
VMEM = pltpu.VMEM
NT = (((1,), (1,)), ((), ()))


def dot(a, b, dims=(((1,), (0,)), ((), ()))):
    return lax.dot_general(a, b, dims, preferred_element_type=F32)


def vmem(n):
    return [pl.BlockSpec(memory_space=VMEM)] * n


def small_kernel(name, body, out_shape, *args, scratch=(), space=VMEM, limit=8):
    many = isinstance(out_shape, list)
    return pl.pallas_call(
        body,
        out_shape=out_shape,
        in_specs=[pl.BlockSpec(memory_space=space)] * len(args),
        out_specs=vmem(len(out_shape)) if many else vmem(1)[0],
        scratch_shapes=list(scratch),
        compiler_params=pltpu.CompilerParams(vmem_limit_bytes=limit * MIB),
        cost_estimate=pl.CostEstimate(
            flops=4000 * MIB, bytes_accessed=8 * MIB, transcendentals=4 * MIB
        ),
        name=name,
    )(*args)


def diagonal(n):
    return lax.broadcasted_iota(jnp.int32, (n, n), 0) == lax.broadcasted_iota(jnp.int32, (n, n), 1)


def to_column(row):
    n = row.shape[1]
    return jnp.sum(jnp.where(diagonal(n), row, 0.0), axis=1, keepdims=True)


def to_row(column):
    n = column.shape[0]
    return jnp.sum(jnp.where(diagonal(n), column, 0.0), axis=0, keepdims=True)


def stacked_codes(codes_ref, count):
    codes = codes_ref[...].astype(BF16)
    parts = [codes, codes]
    if count > 2 * codes.shape[0]:
        parts.append(jnp.zeros((count - 2 * codes.shape[0], codes.shape[1]), BF16))
    return jnp.concatenate(parts, axis=0)


def split(x):
    high = x.astype(BF16).astype(F32)
    return high, x - high


def prep_kernel(hid, *refs):
    piece_ref, direction_ref, gain_ref, bias_ref, codes_ref, sems = refs[4:]
    copies = [
        pltpu.make_async_copy(source, target, sems.at[k])
        for k, (source, target) in enumerate(zip(refs[:4], refs[5:9]))
    ]
    for copy in copies:
        copy.start()
    for copy in copies:
        copy.wait()
    d = direction_ref[...]
    shapes = codes_ref.shape[0]
    rows, cols = d.shape
    half = cols // 2
    extra_lanes = piece_ref.shape[1] - cols
    inverse = lax.rsqrt(jnp.sum(d * d, axis=1, keepdims=True))
    w = to_column(gain_ref[...]) * (d * inverse)
    lane = lax.broadcasted_iota(jnp.int32, (rows, half), 1)
    first = jnp.where(lane < hid, w[:, :half], w[:, half:])
    code = pltpu.roll(w, half - hid, 1)[:, half:].astype(BF16)
    bias = to_column(bias_ref[...]).astype(BF16).astype(F32)
    high, low = split(dot(code, stacked_codes(codes_ref, extra_lanes), NT) + bias)
    own = first[:, half - LANES :]
    if extra_lanes > LANES:
        own = jnp.concatenate([jnp.zeros((rows, extra_lanes - LANES), F32), own], axis=1)
    lane = lax.broadcasted_iota(jnp.int32, (rows, extra_lanes), 1)
    table = jnp.where(lane < shapes, high, jnp.where(lane < 2 * shapes, low, 0.0))
    table = jnp.where(lane >= extra_lanes - (half - hid), own, table)
    piece_ref[:, :half] = first.astype(BF16)
    piece_ref[:, half : half + extra_lanes] = table.astype(BF16)
    piece_ref[:, half + extra_lanes :] = code


def join_kernel(n, n_early, *refs):
    rows = refs[0].shape[0]
    for k, ref in enumerate(refs[n - 1 :: -1]):
        lane = 0
        for out_ref in refs[n + n_early :]:
            lanes = out_ref.shape[1]
            out_ref[k * rows : (k + 1) * rows, :] = ref[:, lane : lane + lanes]
            lane += lanes


def pack_kernel(shapes, *refs):
    weight_ref, code_ref = refs[-2:]
    count = len(refs) - 2
    rows, half = refs[0].shape[0], code_ref.shape[1]
    products = jnp.zeros((rows, LANES), F32)
    for k, ref in zip(FIRST, refs):
        for block in range(half // LANES):
            at = (block * count + k) * rows
            weight_ref[at : at + rows, :] = ref[:, block * LANES : (block + 1) * LANES]
        own = ref[:, half : half + LANES].astype(F32)
        own = jnp.where(lax.broadcasted_iota(jnp.int32, own.shape, 1) < 2 * shapes, own, 0.0)
        products = products + (pltpu.roll(own, 2 * shapes * k, 1) if k else own)
        code_ref[k * rows : (k + 1) * rows, :] = ref[:, half + LANES :]
    weight_ref[half // LANES * count * rows :, :] = products.astype(BF16)


def unpack(hid, shapes, refs, orders, me, w_ref):
    count = LANES // (2 * shapes)
    half = w_ref.shape[1] - LANES
    blocks = half // LANES
    for ref, order in zip(refs, orders):
        height = ref.shape[0] // (len(order) // count)
        rows = height // (blocks * count + 1)
        lane = lax.broadcasted_iota(jnp.int32, (rows, LANES), 1)
        for j, mask in enumerate(order):
            start, k = j // count * height, j % count
            at = pl.ds(pl.multiple_of((me ^ mask) * rows, rows), rows)
            for block in range(blocks):
                here = start + (block * count + k) * rows
                part = ref[here : here + rows, :]
                w_ref[at, block * LANES : (block + 1) * LANES] = part
            here = start + blocks * count * rows
            products = ref[here : here + rows, :].astype(F32)
            if k:
                products = pltpu.roll(products, LANES - 2 * shapes * k, 1)
            products = jnp.where(lane < 2 * shapes, products, 0.0)
            products = jnp.where(lane >= LANES - (half - hid), part.astype(F32), products)
            w_ref[at, half:] = products.astype(BF16)


def place(refs, orders, me, out_ref):
    if orders is None:
        out_ref[...] = refs[0][...]
        return
    rows = refs[0].shape[0] // len(orders[0])
    for ref, order in zip(refs, orders):
        for k, mask in enumerate(order):
            at = pl.multiple_of((me ^ mask) * rows, rows)
            out_ref[pl.ds(at, rows), :] = ref[k * rows : (k + 1) * rows, :]


def inputs_kernel(hid, tile, *refs):
    x_ref, x_t_ref, hidden_ref, offsets_ref, ids_ref, scale_ref, sems = refs[4:]
    points = x_ref.shape[0]
    half = (hid + LANES - 1) // LANES * LANES
    shapes = x_t_ref.shape[0] - half
    extra_lanes = x_ref.shape[1] - half
    steps = points // tile
    small = [
        pltpu.make_async_copy(source, target, sems.at[steps + k])
        for k, (source, target) in enumerate(zip(refs[1:4], (offsets_ref, ids_ref, scale_ref)))
    ]
    large = [
        pltpu.make_async_copy(
            refs[0].at[pl.ds(k * tile, tile), :], hidden_ref.at[pl.ds(k * tile, tile), :], sems.at[k]
        )
        for k in range(steps)
    ]
    for copy in small + large:
        copy.start()
    for copy in small:
        copy.wait()
    for step, copy in enumerate(large):
        here = slice(step * tile, (step + 1) * tile)
        scale = scale_ref[:, here]
        jitter = jnp.where(scale == 0, 1.0, jnp.where(scale == 1, 0.5, 0.25))
        xyz = offsets_ref[:, here] * jitter
        row = lax.broadcasted_iota(jnp.int32, (16, tile), 0)
        last = jnp.zeros((16, tile), F32)
        for k in range(half - hid):
            last = jnp.where(row == 16 - (half - hid) + k, xyz[k : k + 1], last)
        last = last.astype(BF16)
        row = lax.broadcasted_iota(jnp.int32, (extra_lanes - 16, tile), 0)
        ids = ids_ref[:, here]
        member = jnp.where((row == ids) | (row == ids + shapes), 1.0, 0.0).astype(BF16)
        x_ref[here, half:] = jnp.concatenate([member, last], axis=0).T
        x_t_ref[half:, here] = member[:shapes]
        copy.wait()
        x_ref[here, half - LANES : half] = jnp.zeros((tile, LANES), BF16)
        x_ref[here, :hid] = hidden_ref[here, :].astype(BF16)
        hidden = x_ref[here, :half].T
        x_t_ref[: half - 16, here] = hidden[: half - 16]
        x_t_ref[half - 16 : half, here] = hidden[half - 16 :] + last


def layer_kernel(hid, shapes, tile, orders, parts, *refs):
    n = 1 if orders is None else len(orders)
    pieces = refs[:n]
    x_ref, x_t_ref, cot_ref, out_hbm, tail_ref, grad_hidden_ref = refs[n : n + 6]
    grad_refs = refs[n + 6 : -5]
    w_ref, turned_ref, out_ref, grad_pre_ref, sems = refs[-5:]
    points, width = cot_ref.shape
    half = width // 2
    steps = points // tile
    head = out_ref.shape[0] // tile
    me = lax.axis_index(AXES)
    if orders is None:
        place(pieces, orders, me, w_ref)
    else:
        unpack(hid, shapes, pieces, orders, me, w_ref)
    copies = []

    def rows_of(step):
        return slice(step * tile, (step + 1) * tile)

    def middle(step):
        here = rows_of(step)
        pre = dot(x_ref[here, :], w_ref[...], NT)
        sigma = 0.5 * jnp.tanh(0.5 * pre) + 0.5
        out = pre * sigma
        if step < head:
            out_ref[here, :] = out
        else:
            tail_ref[rows_of(step - head), :] = out
        grad_pre_ref[here, :] = (cot_ref[here, :] * (sigma * (1.0 + (pre - out)))).astype(BF16)

    def backward(step):
        here = rows_of(step)
        grad_hidden_ref[here, :] = dot(grad_pre_ref[here, :], w_ref[:, :half])[:, :hid]

    def store(step):
        here = pl.ds(step * tile, tile)
        copy = pltpu.make_async_copy(out_ref.at[here, :], out_hbm.at[here, :], sems.at[step])
        copy.start()
        copies.append(copy)

    for step in range(steps):
        middle(step)
        if step > 0:
            backward(step - 1)
        if step < head:
            store(step)
    backward(steps - 1)
    grad = dot(x_t_ref[...], grad_pre_ref[...])
    sums = grad[half:].astype(BF16)
    for at in range(0, width, half):
        turned_ref[at : at + half, :] = grad[:half, at : at + half].T
    for ref, order in zip(grad_refs, parts):
        ref[:shapes, :] = sums[:, :half]
        ref[shapes : 2 * shapes, :] = sums[:, half:]
        if orders is None:
            ref[2 * shapes :, :] = turned_ref[...].astype(BF16)
            continue
        rows = (ref.shape[0] - 2 * shapes) // len(order)
        for k, mask in enumerate(order):
            at = pl.multiple_of((me ^ mask) * rows, rows)
            to = 2 * shapes + k * rows
            ref[to : to + rows, :] = turned_ref[pl.ds(at, rows), :].astype(BF16)

    for copy in copies:
        copy.wait()


def store_kernel(source_ref, target_ref, sem):
    copy = pltpu.make_async_copy(source_ref, target_ref, sem)
    copy.start()
    copy.wait()


def tail_kernel(_, source_ref, target_ref, sem):
    points, rows = target_ref.shape[0], source_ref.shape[0]
    store_kernel(source_ref, target_ref.at[pl.ds(points - rows, rows), :], sem)


def sum_of(refs):
    terms = [ref[...].astype(F32) for ref in refs]
    while len(terms) > 1:
        terms = [a + b for a, b in zip(terms[::2], terms[1::2])]
    return terms[0]


def add_kernel(shapes, n, *refs):
    total = sum_of(refs[:n]).astype(BF16)
    for k, ref in enumerate(refs[n:]):
        rows = ref.shape[0] - 2 * shapes
        at = 2 * shapes + k * rows
        ref[: 2 * shapes, :] = total[: 2 * shapes]
        ref[2 * shapes :, :] = total[at : at + rows]


def last_kernel(hid, shapes, orders, n, *refs):
    direction_ref, gain_ref, codes_ref = refs[n : n + 3]
    pieces = refs[n + 3 : -5]
    grad_codes_ref, grad_direction_ref, grad_gain_ref, grad_bias_ref, code_scratch = refs[-5:]
    d = direction_ref[...]
    rows, cols = d.shape
    half = cols // 2
    me = lax.axis_index(AXES)
    place(pieces, orders, me, code_scratch)
    total = sum_of(refs[:n])
    sums = jnp.concatenate([total[:shapes], total[shapes : 2 * shapes]], axis=1)
    sums = jnp.concatenate(split(sums), axis=0).astype(BF16)
    terms = dot(sums, code_scratch[...])
    grad_codes_ref[...] = terms[:shapes] + terms[shapes:]
    width = sums.shape[1]
    mine = lax.broadcasted_iota(jnp.int32, (rows, width), 0) + me * rows
    mine = jnp.where(mine == lax.broadcasted_iota(jnp.int32, (rows, width), 1), 1.0, 0.0).astype(BF16)
    own = dot(mine, sums, NT)
    grad_bias_ref[...] = to_row(jnp.sum(own, axis=1, keepdims=True))
    code = dot(own.astype(BF16), stacked_codes(codes_ref, 2 * shapes))
    packed = jnp.concatenate([total[2 * shapes :], code], axis=1)
    lane = lax.broadcasted_iota(jnp.int32, (rows, cols), 1)
    grad_weight = jnp.where(
        lane < hid,
        packed,
        jnp.where(lane < hid + half, pltpu.roll(packed, cols - (half - hid), 1), pltpu.roll(packed, half, 1)),
    )
    inverse = lax.rsqrt(jnp.sum(d * d, axis=1, keepdims=True))
    unit = d * inverse
    grad_gain = jnp.sum(grad_weight * unit, axis=1, keepdims=True)
    grad_gain_ref[...] = to_row(grad_gain)
    grad_direction_ref[...] = (to_column(gain_ref[...]) * inverse) * (grad_weight - grad_gain * unit)


def masks_of(group):
    masks = [0]
    for bit in group:
        masks = masks + [m ^ bit for m in masks]
    return masks


def order_of(groups):
    order = [0]
    for group in groups:
        order = [m ^ r for m in masks_of(group) for r in order]
    return order


def swaps(arrays, masks, devices):
    moved = [
        lax.ppermute(x, AXES, [(i, i ^ mask) for i in range(devices)])
        for x, mask in list(zip(arrays, masks))[::-1]
    ]
    return moved[::-1]


def per_device(
    hidden,
    codes,
    offsets,
    shape_ids,
    scale_index,
    direction,
    gain,
    bias,
    cotangent,
    running_mean,
    running_var,
):
    points, hid = hidden.shape
    shapes = codes.shape[0]
    rows, cols = direction.shape
    width = cotangent.shape[1]
    half = cols // 2
    devices = lax.axis_size("dp") * lax.axis_size("inner")
    bits = [1 << k | 1 for k in range(devices.bit_length() - 1)]
    groups = [bits[k - 2 : k] for k in range(len(bits), 1, -2)]
    groups = groups + [bits[:1]] * (len(bits) % 2)
    gathers = [[groups[0][0], groups[0][-1] ^ 1]] + groups[1:]
    extra_lanes = -(-(2 * shapes + 16) // LANES) * LANES
    tuned = rows % 16 == 0 and 2 * shapes * len(masks_of(groups[0])) == LANES
    lanes = half + extra_lanes
    gain_row = gain.reshape(1, rows)

    def shape_of(rows, lanes, dtype):
        return jax.ShapeDtypeStruct((rows, lanes), dtype)

    held = small_kernel(
        "prep",
        functools.partial(prep_kernel, hid),
        shape_of(rows, lanes + half, BF16),
        *[
            pltpu.with_memory_space_constraint(x, pltpu.HBM)
            for x in (direction, gain_row, bias.reshape(1, rows), codes)
        ],
        scratch=[
            VMEM((rows, cols), F32),
            VMEM((1, rows), F32),
            VMEM((1, rows), F32),
            VMEM((shapes, half), F32),
            pltpu.SemaphoreType.DMA((4,)),
        ],
        space=pl.ANY,
    )
    tile, layer_tile = min(512, points), min(256, points)
    x, x_t = pl.pallas_call(
        functools.partial(inputs_kernel, hid, tile),
        out_shape=[
            shape_of(points, lanes, BF16),
            shape_of(half + shapes, points, BF16),
        ],
        in_specs=[pl.BlockSpec(memory_space=pl.ANY)] * 4,
        out_specs=vmem(2),
        scratch_shapes=[
            VMEM((points, hid), F32),
            VMEM((half - hid, points), F32),
            VMEM((1, points), jnp.int32),
            VMEM((1, points), jnp.int32),
            pltpu.SemaphoreType.DMA((points // tile + 3,)),
        ],
        compiler_params=pltpu.CompilerParams(vmem_limit_bytes=12 * MIB),
        cost_estimate=pl.CostEstimate(
            flops=4000 * MIB, bytes_accessed=8 * points * half, transcendentals=0
        ),
        name="inputs",
    )(
        *[
            pltpu.with_memory_space_constraint(a, pltpu.HBM)
            for a in (
                hidden,
                offsets.T,
                shape_ids.reshape(1, points),
                scale_index.reshape(1, points),
            )
        ]
    )
    def gather(array, group):
        masks = masks_of(group)[1:]
        return [array] + swaps([array] * len(masks), masks, devices)

    def join(arrays, *widths, early=()):
        height = sum(a.shape[0] for a in arrays)
        return small_kernel(
            "join",
            functools.partial(join_kernel, len(arrays), len(early)),
            [shape_of(height, width, BF16) for width in widths],
            *arrays[::-1],
            *early,
        )

    if tuned:
        arrays = gather(held, gathers[0])
        weight, code_weight = small_kernel(
            "pack",
            functools.partial(pack_kernel, shapes),
            [
                shape_of((half // LANES * len(arrays) + 1) * rows, LANES, BF16),
                shape_of(len(arrays) * rows, half, BF16),
            ],
            *[arrays[k] for k in FIRST],
        )
        weight, code_weight, x, x_t = lax.optimization_barrier((weight, code_weight, x, x_t))
        (weights,) = [gather(weight, group) for group in gathers[1:-1]]
        along, across = [[bit] for bit in gathers[1][::-1]]
        (weight,) = join(weights, LANES, early=(cotangent,))
        weights = gather(weight, gathers[-1])
        code_weights = gather(code_weight, along)
        code_order = order_of([gathers[0], along, across])
        orders = [[m ^ r for r in order_of(gathers[:-1])] for m in masks_of(gathers[-1])]
        code_orders = [[m ^ r for r in code_order] for m in masks_of(gathers[-1])]
        parts = [[m ^ r for r in order_of(groups[:-1])] for m in masks_of(groups[-1])]
    else:
        held = lax.all_gather(held, AXES, axis=0, tiled=True)
        weights, code_weights, orders, code_orders, parts = [held[:, :lanes]], [held[:, lanes:]], None, None, [[0]]

    head = points // layer_tile // 2 * layer_tile
    output, tail, grad_hidden, *grads = pl.pallas_call(
        functools.partial(layer_kernel, hid, shapes, layer_tile, orders, parts),
        out_shape=[
            pltpu.HBM((points, width), F32),
            pltpu.VMEM((points - head, width), F32),
            pltpu.VMEM((points, hid), F32),
        ]
        + [shape_of(2 * shapes + width // len(parts), half, BF16)] * len(parts),
        in_specs=vmem(len(weights) + 3),
        out_specs=[pl.BlockSpec(memory_space=pltpu.HBM)] + vmem(2 + len(parts)),
        scratch_shapes=[
            VMEM((width, lanes), BF16),
            VMEM((width, half), F32),
            VMEM((head, width), F32),
            VMEM((points, width), BF16),
            pltpu.SemaphoreType.DMA((head // layer_tile,)),
        ],
        compiler_params=pltpu.CompilerParams(vmem_limit_bytes=20 * MIB),
        cost_estimate=pl.CostEstimate(
            flops=6 * points * width * cols,
            bytes_accessed=8 * points * (width + half),
            transcendentals=points * width,
        ),
        name="layer",
    )(*weights, x, x_t, cotangent)

    def store(name, body, shape, *args, **options):
        return pl.pallas_call(
            body,
            out_shape=pltpu.HBM(shape, F32),
            in_specs=[pl.BlockSpec(memory_space=pltpu.HBM)] * (len(args) - 1) + vmem(1),
            out_specs=pl.BlockSpec(memory_space=pltpu.HBM),
            scratch_shapes=[pltpu.SemaphoreType.DMA(())],
            compiler_params=pltpu.CompilerParams(vmem_limit_bytes=8 * MIB),
            cost_estimate=pl.CostEstimate(
                flops=4000 * MIB, bytes_accessed=8 * points * hid, transcendentals=0
            ),
            name=name,
            **options,
        )(*args)

    def store_grad_hidden():
        return store("store", store_kernel, (points, hid), grad_hidden)

    def store_tail():
        return store(
            "tail", tail_kernel, (points, width), output, tail, input_output_aliases={0: 0}
        )

    if tuned:
        *grads, code_along, running_mean, running_var = lax.optimization_barrier(
            (*grads, code_weights[1], running_mean, running_var)
        )
        (code_weight,) = join([code_weights[0], code_along], half)
        for r, group in enumerate(groups[::-1]):
            masks = masks_of(group)
            grads = [grads[0]] + swaps(grads[1:], masks[1:], devices)
            if r == len(groups) - 1:
                break
            n_out = len(masks_of(groups[-2 - r]))
            left = (grads[0].shape[0] - 2 * shapes) // n_out
            grads = small_kernel(
                "add",
                functools.partial(add_kernel, shapes, len(grads)),
                [shape_of(2 * shapes + left, half, BF16)] * n_out,
                *(grads[::-1] if r == 0 else [grads[k] for k in SUMS]),
            )
            if r == 0:
                *grads, grad_hidden = lax.optimization_barrier((*grads, grad_hidden))
                grad_hidden = store_grad_hidden()
                grad_hidden, code_weight = lax.optimization_barrier((grad_hidden, code_weight))
                code_weights = gather(code_weight, across)
            if r == len(groups) - 2:
                *grads, grad_hidden, tail = lax.optimization_barrier((*grads, grad_hidden, tail))
                output = store_tail()
        (code_weight,) = join(code_weights, half)
        code_weights = gather(code_weight, groups[-1])
    else:
        grad_hidden, output = store_grad_hidden(), store_tail()
        sums = lax.psum(grads[0][: 2 * shapes].astype(F32), AXES)
        high = sums.astype(BF16)
        own = lax.psum_scatter(grads[0][2 * shapes :].astype(F32), AXES, scatter_dimension=0, tiled=True)
        low = jnp.zeros((2 * shapes + rows, half), BF16).at[: 2 * shapes].set((sums - high).astype(BF16))
        grads = [jnp.concatenate([high, own.astype(BF16)], axis=0), low]
    grad_codes, grad_direction, grad_gain, grad_bias = small_kernel(
        "last",
        functools.partial(last_kernel, hid, shapes, code_orders, len(grads)),
        [
            shape_of(shapes, half, F32),
            shape_of(rows, cols, F32),
            shape_of(1, rows, F32),
            shape_of(1, rows, F32),
        ],
        *grads[::-1],
        direction,
        gain_row,
        codes,
        *code_weights,
        scratch=[VMEM((width, half), BF16)],
    )

    total = float(points * devices)
    batch_mean = jnp.mean(codes, axis=0)
    batch_square = jnp.mean(codes * codes, axis=0)
    batch_var = (batch_square - batch_mean * batch_mean) * (total / (total - 1.0))
    new_mean = 0.9 * running_mean + 0.1 * batch_mean
    new_var = 0.9 * running_var + 0.1 * batch_var
    return (
        output,
        grad_hidden,
        grad_codes,
        grad_direction,
        grad_gain.reshape(rows),
        grad_bias.reshape(rows),
        new_mean,
        new_var,
    )


def solution(mesh):
    return jax.shard_map(
        per_device,
        mesh=mesh,
        in_specs=(
            P(("dp", "inner"), None),
            P(),
            P(("dp", "inner"), None),
            P(("dp", "inner")),
            P(("dp", "inner")),
            P(("dp", "inner"), None),
            P(("dp", "inner")),
            P(("dp", "inner")),
            P(("dp", "inner"), None),
            P(),
            P(),
        ),
        out_specs=(
            P(("dp", "inner"), None),
            P(("dp", "inner"), None),
            P(),
            P(("dp", "inner"), None),
            P(("dp", "inner")),
            P(("dp", "inner")),
            P(),
            P(),
        ),
        check_vma=False,
    )
```

```python
import functools

import jax
import jax.numpy as jnp
from jax import lax
from jax.experimental import pallas as pl
from jax.experimental.pallas import tpu as pltpu
from jax.sharding import PartitionSpec as P

AXES = ("dp", "inner")
LANES = 128
MIB = 1024 * 1024
FIRST = (2, 3, 1, 0)
SUMS = (1, 3, 2, 0)
F32 = jnp.float32
BF16 = jnp.bfloat16
VMEM = pltpu.VMEM
NT = (((1,), (1,)), ((), ()))


def dot(a, b, dims=(((1,), (0,)), ((), ()))):
    return lax.dot_general(a, b, dims, preferred_element_type=F32)


def vmem(n):
    return [pl.BlockSpec(memory_space=VMEM)] * n


def small_kernel(name, body, out_shape, *args, scratch=(), space=VMEM, limit=8):
    many = isinstance(out_shape, list)
    return pl.pallas_call(
        body,
        out_shape=out_shape,
        in_specs=[pl.BlockSpec(memory_space=space)] * len(args),
        out_specs=vmem(len(out_shape)) if many else vmem(1)[0],
        scratch_shapes=list(scratch),
        compiler_params=pltpu.CompilerParams(vmem_limit_bytes=limit * MIB),
        cost_estimate=pl.CostEstimate(
            flops=4000 * MIB, bytes_accessed=8 * MIB, transcendentals=4 * MIB
        ),
        name=name,
    )(*args)


def diagonal(n):
    return lax.broadcasted_iota(jnp.int32, (n, n), 0) == lax.broadcasted_iota(jnp.int32, (n, n), 1)


def to_column(row):
    n = row.shape[1]
    return jnp.sum(jnp.where(diagonal(n), row, 0.0), axis=1, keepdims=True)


def to_row(column):
    n = column.shape[0]
    return jnp.sum(jnp.where(diagonal(n), column, 0.0), axis=0, keepdims=True)


def stacked_codes(codes_ref, count):
    codes = codes_ref[...].astype(BF16)
    parts = [codes, codes]
    if count > 2 * codes.shape[0]:
        parts.append(jnp.zeros((count - 2 * codes.shape[0], codes.shape[1]), BF16))
    return jnp.concatenate(parts, axis=0)


def split(x):
    high = x.astype(BF16).astype(F32)
    return high, x - high


def prep_kernel(hid, *refs):
    piece_ref, direction_ref, gain_ref, bias_ref, codes_ref, sems = refs[4:]
    copies = [
        pltpu.make_async_copy(source, target, sems.at[k])
        for k, (source, target) in enumerate(zip(refs[:4], refs[5:9]))
    ]
    for copy in copies:
        copy.start()
    for copy in copies:
        copy.wait()
    d = direction_ref[...]
    shapes = codes_ref.shape[0]
    rows, cols = d.shape
    half = cols // 2
    extra_lanes = piece_ref.shape[1] - cols
    inverse = lax.rsqrt(jnp.sum(d * d, axis=1, keepdims=True))
    w = to_column(gain_ref[...]) * (d * inverse)
    lane = lax.broadcasted_iota(jnp.int32, (rows, half), 1)
    first = jnp.where(lane < hid, w[:, :half], w[:, half:])
    code = pltpu.roll(w, half - hid, 1)[:, half:].astype(BF16)
    bias = to_column(bias_ref[...]).astype(BF16).astype(F32)
    high, low = split(dot(code, stacked_codes(codes_ref, extra_lanes), NT) + bias)
    own = first[:, half - LANES :]
    if extra_lanes > LANES:
        own = jnp.concatenate([jnp.zeros((rows, extra_lanes - LANES), F32), own], axis=1)
    lane = lax.broadcasted_iota(jnp.int32, (rows, extra_lanes), 1)
    table = jnp.where(lane < shapes, high, jnp.where(lane < 2 * shapes, low, 0.0))
    table = jnp.where(lane >= extra_lanes - (half - hid), own, table)
    piece_ref[:, :half] = first.astype(BF16)
    piece_ref[:, half : half + extra_lanes] = table.astype(BF16)
    piece_ref[:, half + extra_lanes :] = code


def join_kernel(n, n_early, *refs):
    rows = refs[0].shape[0]
    for k, ref in enumerate(refs[n - 1 :: -1]):
        lane = 0
        for out_ref in refs[n + n_early :]:
            lanes = out_ref.shape[1]
            out_ref[k * rows : (k + 1) * rows, :] = ref[:, lane : lane + lanes]
            lane += lanes


def pack_kernel(shapes, *refs):
    weight_ref, code_ref = refs[-2:]
    count = len(refs) - 2
    rows, half = refs[0].shape[0], code_ref.shape[1]
    products = jnp.zeros((rows, LANES), F32)
    for k, ref in zip(FIRST, refs):
        for block in range(half // LANES):
            at = (block * count + k) * rows
            weight_ref[at : at + rows, :] = ref[:, block * LANES : (block + 1) * LANES]
        own = ref[:, half : half + LANES].astype(F32)
        own = jnp.where(lax.broadcasted_iota(jnp.int32, own.shape, 1) < 2 * shapes, own, 0.0)
        products = products + (pltpu.roll(own, 2 * shapes * k, 1) if k else own)
        code_ref[k * rows : (k + 1) * rows, :] = ref[:, half + LANES :]
    weight_ref[half // LANES * count * rows :, :] = products.astype(BF16)


def unpack(hid, shapes, refs, orders, me, w_ref):
    count = LANES // (2 * shapes)
    half = w_ref.shape[1] - LANES
    blocks = half // LANES
    for ref, order in zip(refs, orders):
        height = ref.shape[0] // (len(order) // count)
        rows = height // (blocks * count + 1)
        lane = lax.broadcasted_iota(jnp.int32, (rows, LANES), 1)
        for j, mask in enumerate(order):
            start, k = j // count * height, j % count
            at = pl.ds(pl.multiple_of((me ^ mask) * rows, rows), rows)
            for block in range(blocks):
                here = start + (block * count + k) * rows
                part = ref[here : here + rows, :]
                w_ref[at, block * LANES : (block + 1) * LANES] = part
            here = start + blocks * count * rows
            products = ref[here : here + rows, :].astype(F32)
            if k:
                products = pltpu.roll(products, LANES - 2 * shapes * k, 1)
            products = jnp.where(lane < 2 * shapes, products, 0.0)
            products = jnp.where(lane >= LANES - (half - hid), part.astype(F32), products)
            w_ref[at, half:] = products.astype(BF16)


def place(refs, orders, me, out_ref):
    if orders is None:
        out_ref[...] = refs[0][...]
        return
    rows = refs[0].shape[0] // len(orders[0])
    for ref, order in zip(refs, orders):
        for k, mask in enumerate(order):
            at = pl.multiple_of((me ^ mask) * rows, rows)
            out_ref[pl.ds(at, rows), :] = ref[k * rows : (k + 1) * rows, :]


def inputs_kernel(hid, tile, *refs):
    x_ref, x_t_ref, hidden_ref, offsets_ref, ids_ref, scale_ref, sems = refs[4:]
    points = x_ref.shape[0]
    half = (hid + LANES - 1) // LANES * LANES
    shapes = x_t_ref.shape[0] - half
    extra_lanes = x_ref.shape[1] - half
    steps = points // tile
    small = [
        pltpu.make_async_copy(source, target, sems.at[steps + k])
        for k, (source, target) in enumerate(zip(refs[1:4], (offsets_ref, ids_ref, scale_ref)))
    ]
    large = [
        pltpu.make_async_copy(
            refs[0].at[pl.ds(k * tile, tile), :], hidden_ref.at[pl.ds(k * tile, tile), :], sems.at[k]
        )
        for k in range(steps)
    ]
    for copy in small + large:
        copy.start()
    for copy in small:
        copy.wait()
    for step, copy in enumerate(large):
        here = slice(step * tile, (step + 1) * tile)
        scale = scale_ref[:, here]
        jitter = jnp.where(scale == 0, 1.0, jnp.where(scale == 1, 0.5, 0.25))
        xyz = offsets_ref[:, here] * jitter
        row = lax.broadcasted_iota(jnp.int32, (16, tile), 0)
        last = jnp.zeros((16, tile), F32)
        for k in range(half - hid):
            last = jnp.where(row == 16 - (half - hid) + k, xyz[k : k + 1], last)
        last = last.astype(BF16)
        row = lax.broadcasted_iota(jnp.int32, (extra_lanes - 16, tile), 0)
        ids = ids_ref[:, here]
        member = jnp.where((row == ids) | (row == ids + shapes), 1.0, 0.0).astype(BF16)
        x_ref[here, half:] = jnp.concatenate([member, last], axis=0).T
        x_t_ref[half:, here] = member[:shapes]
        copy.wait()
        x_ref[here, half - LANES : half] = jnp.zeros((tile, LANES), BF16)
        x_ref[here, :hid] = hidden_ref[here, :].astype(BF16)
        hidden = x_ref[here, :half].T
        x_t_ref[: half - 16, here] = hidden[: half - 16]
        x_t_ref[half - 16 : half, here] = hidden[half - 16 :] + last


def layer_kernel(hid, shapes, tile, orders, parts, *refs):
    n = 1 if orders is None else len(orders)
    pieces = refs[:n]
    x_ref, x_t_ref, cot_ref, out_hbm, tail_ref, grad_hidden_ref = refs[n : n + 6]
    grad_refs = refs[n + 6 : -6]
    w_ref, turned_ref, out_ref, grad_pre_ref, pre_ref, sems = refs[-6:]
    points, width = cot_ref.shape
    half = width // 2
    steps = points // tile
    head = out_ref.shape[0] // tile
    me = lax.axis_index(AXES)
    if orders is None:
        place(pieces, orders, me, w_ref)
    else:
        unpack(hid, shapes, pieces, orders, me, w_ref)
    copies = []

    def rows_of(step):
        return slice(step * tile, (step + 1) * tile)

    def forward(step):
        pre_ref[step % 2] = dot(x_ref[rows_of(step), :], w_ref[...], NT)

    def middle(step):
        here = rows_of(step)
        pre = pre_ref[step % 2]
        sigma = 0.5 * jnp.tanh(0.5 * pre) + 0.5
        out = pre * sigma
        if step < head:
            out_ref[here, :] = out
        else:
            tail_ref[rows_of(step - head), :] = out
        grad_pre_ref[here, :] = (cot_ref[here, :] * (sigma * (1.0 + (pre - out)))).astype(BF16)

    def backward(step):
        here = rows_of(step)
        grad_hidden_ref[here, :] = dot(grad_pre_ref[here, :], w_ref[:, :half])[:, :hid]

    def store(step):
        here = pl.ds(step * tile, tile)
        copy = pltpu.make_async_copy(out_ref.at[here, :], out_hbm.at[here, :], sems.at[step])
        copy.start()
        copies.append(copy)

    forward(0)
    for step in range(steps):
        if step + 1 < steps:
            forward(step + 1)
        middle(step)
        if step > 0:
            backward(step - 1)
        if step < head:
            store(step)
    backward(steps - 1)
    grad = dot(x_t_ref[...], grad_pre_ref[...])
    sums = grad[half:].astype(BF16)
    for at in range(0, width, half):
        turned_ref[at : at + half, :] = grad[:half, at : at + half].T
    for ref, order in zip(grad_refs, parts):
        ref[:shapes, :] = sums[:, :half]
        ref[shapes : 2 * shapes, :] = sums[:, half:]
        if orders is None:
            ref[2 * shapes :, :] = turned_ref[...].astype(BF16)
            continue
        rows = (ref.shape[0] - 2 * shapes) // len(order)
        for k, mask in enumerate(order):
            at = pl.multiple_of((me ^ mask) * rows, rows)
            to = 2 * shapes + k * rows
            ref[to : to + rows, :] = turned_ref[pl.ds(at, rows), :].astype(BF16)

    for copy in copies:
        copy.wait()


def store_kernel(source_ref, target_ref, sem):
    copy = pltpu.make_async_copy(source_ref, target_ref, sem)
    copy.start()
    copy.wait()


def tail_kernel(_, source_ref, target_ref, sem):
    points, rows = target_ref.shape[0], source_ref.shape[0]
    store_kernel(source_ref, target_ref.at[pl.ds(points - rows, rows), :], sem)


def sum_of(refs):
    terms = [ref[...].astype(F32) for ref in refs]
    while len(terms) > 1:
        terms = [a + b for a, b in zip(terms[::2], terms[1::2])]
    return terms[0]


def add_kernel(shapes, n, *refs):
    total = sum_of(refs[:n]).astype(BF16)
    for k, ref in enumerate(refs[n:]):
        rows = ref.shape[0] - 2 * shapes
        at = 2 * shapes + k * rows
        ref[: 2 * shapes, :] = total[: 2 * shapes]
        ref[2 * shapes :, :] = total[at : at + rows]


def last_kernel(hid, shapes, orders, n, *refs):
    direction_ref, gain_ref, codes_ref = refs[n : n + 3]
    pieces = refs[n + 3 : -5]
    grad_codes_ref, grad_direction_ref, grad_gain_ref, grad_bias_ref, code_scratch = refs[-5:]
    d = direction_ref[...]
    rows, cols = d.shape
    half = cols // 2
    me = lax.axis_index(AXES)
    place(pieces, orders, me, code_scratch)
    total = sum_of(refs[:n])
    sums = jnp.concatenate([total[:shapes], total[shapes : 2 * shapes]], axis=1)
    sums = jnp.concatenate(split(sums), axis=0).astype(BF16)
    terms = dot(sums, code_scratch[...])
    grad_codes_ref[...] = terms[:shapes] + terms[shapes:]
    width = sums.shape[1]
    mine = lax.broadcasted_iota(jnp.int32, (rows, width), 0) + me * rows
    mine = jnp.where(mine == lax.broadcasted_iota(jnp.int32, (rows, width), 1), 1.0, 0.0).astype(BF16)
    own = dot(mine, sums, NT)
    grad_bias_ref[...] = to_row(jnp.sum(own, axis=1, keepdims=True))
    code = dot(own.astype(BF16), stacked_codes(codes_ref, 2 * shapes))
    packed = jnp.concatenate([total[2 * shapes :], code], axis=1)
    lane = lax.broadcasted_iota(jnp.int32, (rows, cols), 1)
    grad_weight = jnp.where(
        lane < hid,
        packed,
        jnp.where(lane < hid + half, pltpu.roll(packed, cols - (half - hid), 1), pltpu.roll(packed, half, 1)),
    )
    inverse = lax.rsqrt(jnp.sum(d * d, axis=1, keepdims=True))
    unit = d * inverse
    grad_gain = jnp.sum(grad_weight * unit, axis=1, keepdims=True)
    grad_gain_ref[...] = to_row(grad_gain)
    grad_direction_ref[...] = (to_column(gain_ref[...]) * inverse) * (grad_weight - grad_gain * unit)


def masks_of(group):
    masks = [0]
    for bit in group:
        masks = masks + [m ^ bit for m in masks]
    return masks


def order_of(groups):
    order = [0]
    for group in groups:
        order = [m ^ r for m in masks_of(group) for r in order]
    return order


def swaps(arrays, masks, devices):
    moved = [
        lax.ppermute(x, AXES, [(i, i ^ mask) for i in range(devices)])
        for x, mask in list(zip(arrays, masks))[::-1]
    ]
    return moved[::-1]


def per_device(
    hidden,
    codes,
    offsets,
    shape_ids,
    scale_index,
    direction,
    gain,
    bias,
    cotangent,
    running_mean,
    running_var,
):
    points, hid = hidden.shape
    shapes = codes.shape[0]
    rows, cols = direction.shape
    width = cotangent.shape[1]
    half = cols // 2
    devices = lax.axis_size("dp") * lax.axis_size("inner")
    bits = [1 << k | 1 for k in range(devices.bit_length() - 1)]
    groups = [bits[k - 2 : k] for k in range(len(bits), 1, -2)]
    groups = groups + [bits[:1]] * (len(bits) % 2)
    groups[0] = [groups[0][0], groups[0][-1] ^ 1]
    extra_lanes = -(-(2 * shapes + 16) // LANES) * LANES
    tuned = len(groups) == 3 and rows % 16 == 0 and 2 * shapes * len(masks_of(groups[0])) == LANES
    lanes = half + extra_lanes
    gain_row = gain.reshape(1, rows)

    def shape_of(rows, lanes, dtype):
        return jax.ShapeDtypeStruct((rows, lanes), dtype)

    held = small_kernel(
        "prep",
        functools.partial(prep_kernel, hid),
        shape_of(rows, lanes + half, BF16),
        *[
            pltpu.with_memory_space_constraint(x, pltpu.HBM)
            for x in (direction, gain_row, bias.reshape(1, rows), codes)
        ],
        scratch=[
            VMEM((rows, cols), F32),
            VMEM((1, rows), F32),
            VMEM((1, rows), F32),
            VMEM((shapes, half), F32),
            pltpu.SemaphoreType.DMA((4,)),
        ],
        space=pl.ANY,
    )
    tile, layer_tile = min(512, points), min(512, points)
    x, x_t = pl.pallas_call(
        functools.partial(inputs_kernel, hid, tile),
        out_shape=[
            shape_of(points, lanes, BF16),
            shape_of(half + shapes, points, BF16),
        ],
        in_specs=[pl.BlockSpec(memory_space=pl.ANY)] * 4,
        out_specs=vmem(2),
        scratch_shapes=[
            VMEM((points, hid), F32),
            VMEM((half - hid, points), F32),
            VMEM((1, points), jnp.int32),
            VMEM((1, points), jnp.int32),
            pltpu.SemaphoreType.DMA((points // tile + 3,)),
        ],
        compiler_params=pltpu.CompilerParams(vmem_limit_bytes=12 * MIB),
        cost_estimate=pl.CostEstimate(
            flops=4000 * MIB, bytes_accessed=8 * points * half, transcendentals=0
        ),
        name="inputs",
    )(
        *[
            pltpu.with_memory_space_constraint(a, pltpu.HBM)
            for a in (
                hidden,
                offsets.T,
                shape_ids.reshape(1, points),
                scale_index.reshape(1, points),
            )
        ]
    )
    def gather(array, group):
        masks = masks_of(group)[1:]
        return [array] + swaps([array] * len(masks), masks, devices)

    def join(arrays, *widths, early=()):
        height = sum(a.shape[0] for a in arrays)
        return small_kernel(
            "join",
            functools.partial(join_kernel, len(arrays), len(early)),
            [shape_of(height, width, BF16) for width in widths],
            *arrays[::-1],
            *early,
        )

    if tuned:
        arrays = gather(held, groups[0])
        weight, code_weight = small_kernel(
            "pack",
            functools.partial(pack_kernel, shapes),
            [
                shape_of((half // LANES * len(arrays) + 1) * rows, LANES, BF16),
                shape_of(len(arrays) * rows, half, BF16),
            ],
            *[arrays[k] for k in FIRST],
        )
        weight, code_weight, x, x_t = lax.optimization_barrier((weight, code_weight, x, x_t))
        (weights,) = [gather(weight, group) for group in groups[1:-1]]
        along, across = [[bit] for bit in groups[1][::-1]]
        (weight,) = join(weights, LANES, early=(cotangent,))
        weights = gather(weight, groups[-1])
        code_weights = gather(code_weight, along)
        code_order = order_of([groups[0], along, across])
        orders = [[m ^ r for r in order_of(groups[:-1])] for m in masks_of(groups[-1])]
        code_orders = [[m ^ r for r in code_order] for m in masks_of(groups[-1])]
        parts = orders
    else:
        held = lax.all_gather(held, AXES, axis=0, tiled=True)
        weights, code_weights, orders, code_orders, parts = [held[:, :lanes]], [held[:, lanes:]], None, None, [[0]]

    head = points // layer_tile // 2 * layer_tile
    output, tail, grad_hidden, *grads = pl.pallas_call(
        functools.partial(layer_kernel, hid, shapes, layer_tile, orders, parts),
        out_shape=[
            pltpu.HBM((points, width), F32),
            pltpu.VMEM((points - head, width), F32),
            pltpu.VMEM((points, hid), F32),
        ]
        + [shape_of(2 * shapes + width // len(parts), half, BF16)] * len(parts),
        in_specs=vmem(len(weights) + 3),
        out_specs=[pl.BlockSpec(memory_space=pltpu.HBM)] + vmem(2 + len(parts)),
        scratch_shapes=[
            VMEM((width, lanes), BF16),
            VMEM((width, half), F32),
            VMEM((head, width), F32),
            VMEM((points, width), BF16),
            VMEM((2, layer_tile, width), F32),
            pltpu.SemaphoreType.DMA((head // layer_tile,)),
        ],
        compiler_params=pltpu.CompilerParams(vmem_limit_bytes=20 * MIB),
        cost_estimate=pl.CostEstimate(
            flops=6 * points * width * cols,
            bytes_accessed=8 * points * (width + half),
            transcendentals=points * width,
        ),
        name="layer",
    )(*weights, x, x_t, cotangent)

    def store(name, body, shape, *args, **options):
        return pl.pallas_call(
            body,
            out_shape=pltpu.HBM(shape, F32),
            in_specs=[pl.BlockSpec(memory_space=pltpu.HBM)] * (len(args) - 1) + vmem(1),
            out_specs=pl.BlockSpec(memory_space=pltpu.HBM),
            scratch_shapes=[pltpu.SemaphoreType.DMA(())],
            compiler_params=pltpu.CompilerParams(vmem_limit_bytes=8 * MIB),
            cost_estimate=pl.CostEstimate(
                flops=4000 * MIB, bytes_accessed=8 * points * hid, transcendentals=0
            ),
            name=name,
            **options,
        )(*args)

    def store_grad_hidden():
        return store("store", store_kernel, (points, hid), grad_hidden)

    def store_tail():
        return store(
            "tail", tail_kernel, (points, width), output, tail, input_output_aliases={0: 0}
        )

    if tuned:
        *grads, code_along, running_mean, running_var = lax.optimization_barrier(
            (*grads, code_weights[1], running_mean, running_var)
        )
        (code_weight,) = join([code_weights[0], code_along], half)
        for r, group in enumerate(groups[::-1]):
            masks = masks_of(group)
            grads = [grads[0]] + swaps(grads[1:], masks[1:], devices)
            if r == len(groups) - 1:
                break
            n_out = len(masks_of(groups[-2 - r]))
            left = (grads[0].shape[0] - 2 * shapes) // n_out
            grads = small_kernel(
                "add",
                functools.partial(add_kernel, shapes, len(grads)),
                [shape_of(2 * shapes + left, half, BF16)] * n_out,
                *(grads[::-1] if r == 0 else [grads[k] for k in SUMS]),
            )
            if r == 0:
                *grads, grad_hidden = lax.optimization_barrier((*grads, grad_hidden))
                grad_hidden = store_grad_hidden()
                grad_hidden, code_weight = lax.optimization_barrier((grad_hidden, code_weight))
                code_weights = gather(code_weight, across)
            if r == len(groups) - 2:
                *grads, grad_hidden, tail = lax.optimization_barrier((*grads, grad_hidden, tail))
                output = store_tail()
        (code_weight,) = join(code_weights, half)
        code_weights = gather(code_weight, groups[-1])
    else:
        grad_hidden, output = store_grad_hidden(), store_tail()
        sums = lax.psum(grads[0][: 2 * shapes].astype(F32), AXES)
        high = sums.astype(BF16)
        own = lax.psum_scatter(grads[0][2 * shapes :].astype(F32), AXES, scatter_dimension=0, tiled=True)
        low = jnp.zeros((2 * shapes + rows, half), BF16).at[: 2 * shapes].set((sums - high).astype(BF16))
        grads = [jnp.concatenate([high, own.astype(BF16)], axis=0), low]
    grad_codes, grad_direction, grad_gain, grad_bias = small_kernel(
        "last",
        functools.partial(last_kernel, hid, shapes, code_orders, len(grads)),
        [
            shape_of(shapes, half, F32),
            shape_of(rows, cols, F32),
            shape_of(1, rows, F32),
            shape_of(1, rows, F32),
        ],
        *([grads[k] for k in FIRST] if tuned else grads),
        direction,
        gain_row,
        codes,
        *code_weights,
        scratch=[VMEM((width, half), BF16)],
    )

    total = float(points * devices)
    batch_mean = jnp.mean(codes, axis=0)
    batch_square = jnp.mean(codes * codes, axis=0)
    batch_var = (batch_square - batch_mean * batch_mean) * (total / (total - 1.0))
    new_mean = 0.9 * running_mean + 0.1 * batch_mean
    new_var = 0.9 * running_var + 0.1 * batch_var
    return (
        output,
        grad_hidden,
        grad_codes,
        grad_direction,
        grad_gain.reshape(rows),
        grad_bias.reshape(rows),
        new_mean,
        new_var,
    )


def solution(mesh):
    return jax.shard_map(
        per_device,
        mesh=mesh,
        in_specs=(
            P(("dp", "inner"), None),
            P(),
            P(("dp", "inner"), None),
            P(("dp", "inner")),
            P(("dp", "inner")),
            P(("dp", "inner"), None),
            P(("dp", "inner")),
            P(("dp", "inner")),
            P(("dp", "inner"), None),
            P(),
            P(),
        ),
        out_specs=(
            P(("dp", "inner"), None),
            P(("dp", "inner"), None),
            P(),
            P(("dp", "inner"), None),
            P(("dp", "inner")),
            P(("dp", "inner")),
            P(),
            P(),
        ),
        check_vma=False,
    )
```

```python
import functools

import jax
import jax.numpy as jnp
from jax import lax
from jax.experimental import pallas as pl
from jax.experimental.pallas import tpu as pltpu
from jax.sharding import PartitionSpec as P

AXES = ("dp", "inner")
LANES = 128
MIB = 1024 * 1024
FIRST = (2, 3, 1, 0)
SUMS = (1, 3, 2, 0)
F32 = jnp.float32
BF16 = jnp.bfloat16
VMEM = pltpu.VMEM
NT = (((1,), (1,)), ((), ()))


def dot(a, b, dims=(((1,), (0,)), ((), ()))):
    return lax.dot_general(a, b, dims, preferred_element_type=F32)


def vmem(n):
    return [pl.BlockSpec(memory_space=VMEM)] * n


def small_kernel(name, body, out_shape, *args, scratch=(), space=VMEM, limit=8):
    many = isinstance(out_shape, list)
    return pl.pallas_call(
        body,
        out_shape=out_shape,
        in_specs=[pl.BlockSpec(memory_space=space)] * len(args),
        out_specs=vmem(len(out_shape)) if many else vmem(1)[0],
        scratch_shapes=list(scratch),
        compiler_params=pltpu.CompilerParams(vmem_limit_bytes=limit * MIB),
        cost_estimate=pl.CostEstimate(
            flops=4000 * MIB, bytes_accessed=8 * MIB, transcendentals=4 * MIB
        ),
        name=name,
    )(*args)


def diagonal(n):
    return lax.broadcasted_iota(jnp.int32, (n, n), 0) == lax.broadcasted_iota(jnp.int32, (n, n), 1)


def to_column(row):
    n = row.shape[1]
    return jnp.sum(jnp.where(diagonal(n), row, 0.0), axis=1, keepdims=True)


def to_row(column):
    n = column.shape[0]
    return jnp.sum(jnp.where(diagonal(n), column, 0.0), axis=0, keepdims=True)


def stacked_codes(codes_ref, count):
    codes = codes_ref[...].astype(BF16)
    parts = [codes, codes]
    if count > 2 * codes.shape[0]:
        parts.append(jnp.zeros((count - 2 * codes.shape[0], codes.shape[1]), BF16))
    return jnp.concatenate(parts, axis=0)


def split(x):
    high = x.astype(BF16).astype(F32)
    return high, x - high


def prep_kernel(hid, *refs):
    piece_ref, direction_ref, gain_ref, bias_ref, codes_ref, sems = refs[4:]
    copies = [
        pltpu.make_async_copy(source, target, sems.at[k])
        for k, (source, target) in enumerate(zip(refs[:4], refs[5:9]))
    ]
    for copy in copies:
        copy.start()
    for copy in copies:
        copy.wait()
    d = direction_ref[...]
    shapes = codes_ref.shape[0]
    rows, cols = d.shape
    half = cols // 2
    extra_lanes = piece_ref.shape[1] - cols
    inverse = lax.rsqrt(jnp.sum(d * d, axis=1, keepdims=True))
    w = to_column(gain_ref[...]) * (d * inverse)
    lane = lax.broadcasted_iota(jnp.int32, (rows, half), 1)
    first = jnp.where(lane < hid, w[:, :half], w[:, half:])
    code = pltpu.roll(w, half - hid, 1)[:, half:].astype(BF16)
    bias = to_column(bias_ref[...]).astype(BF16).astype(F32)
    high, low = split(dot(code, stacked_codes(codes_ref, extra_lanes), NT) + bias)
    own = first[:, half - LANES :]
    if extra_lanes > LANES:
        own = jnp.concatenate([jnp.zeros((rows, extra_lanes - LANES), F32), own], axis=1)
    lane = lax.broadcasted_iota(jnp.int32, (rows, extra_lanes), 1)
    table = jnp.where(lane < shapes, high, jnp.where(lane < 2 * shapes, low, 0.0))
    table = jnp.where(lane >= extra_lanes - (half - hid), own, table)
    piece_ref[:, :half] = first.astype(BF16)
    piece_ref[:, half : half + extra_lanes] = table.astype(BF16)
    piece_ref[:, half + extra_lanes :] = code


def join_kernel(n, n_early, *refs):
    rows = refs[0].shape[0]
    for k, ref in enumerate(refs[n - 1 :: -1]):
        lane = 0
        for out_ref in refs[n + n_early :]:
            lanes = out_ref.shape[1]
            out_ref[k * rows : (k + 1) * rows, :] = ref[:, lane : lane + lanes]
            lane += lanes


def pack_kernel(shapes, *refs):
    weight_ref, code_ref = refs[-2:]
    count = len(refs) - 2
    rows, half = refs[0].shape[0], code_ref.shape[1]
    products = jnp.zeros((rows, LANES), F32)
    for k, ref in zip(FIRST, refs):
        for block in range(half // LANES):
            at = (block * count + k) * rows
            weight_ref[at : at + rows, :] = ref[:, block * LANES : (block + 1) * LANES]
        own = ref[:, half : half + LANES].astype(F32)
        own = jnp.where(lax.broadcasted_iota(jnp.int32, own.shape, 1) < 2 * shapes, own, 0.0)
        products = products + (pltpu.roll(own, 2 * shapes * k, 1) if k else own)
        code_ref[k * rows : (k + 1) * rows, :] = ref[:, half + LANES :]
    weight_ref[half // LANES * count * rows :, :] = products.astype(BF16)


def unpack(hid, shapes, refs, orders, me, w_ref):
    count = LANES // (2 * shapes)
    half = w_ref.shape[1] - LANES
    blocks = half // LANES
    for ref, order in zip(refs, orders):
        height = ref.shape[0] // (len(order) // count)
        rows = height // (blocks * count + 1)
        lane = lax.broadcasted_iota(jnp.int32, (rows, LANES), 1)
        for j, mask in enumerate(order):
            start, k = j // count * height, j % count
            at = pl.ds(pl.multiple_of((me ^ mask) * rows, rows), rows)
            for block in range(blocks):
                here = start + (block * count + k) * rows
                part = ref[here : here + rows, :]
                w_ref[at, block * LANES : (block + 1) * LANES] = part
            here = start + blocks * count * rows
            products = ref[here : here + rows, :].astype(F32)
            if k:
                products = pltpu.roll(products, LANES - 2 * shapes * k, 1)
            products = jnp.where(lane < 2 * shapes, products, 0.0)
            products = jnp.where(lane >= LANES - (half - hid), part.astype(F32), products)
            w_ref[at, half:] = products.astype(BF16)


def place(refs, orders, me, out_ref):
    if orders is None:
        out_ref[...] = refs[0][...]
        return
    rows = refs[0].shape[0] // len(orders[0])
    for ref, order in zip(refs, orders):
        for k, mask in enumerate(order):
            at = pl.multiple_of((me ^ mask) * rows, rows)
            out_ref[pl.ds(at, rows), :] = ref[k * rows : (k + 1) * rows, :]


def inputs_kernel(hid, tile, *refs):
    x_ref, x_t_ref, hidden_ref, offsets_ref, ids_ref, scale_ref, sems = refs[4:]
    points = x_ref.shape[0]
    half = (hid + LANES - 1) // LANES * LANES
    shapes = x_t_ref.shape[0] - half
    extra_lanes = x_ref.shape[1] - half
    steps = points // tile
    small = [
        pltpu.make_async_copy(source, target, sems.at[steps + k])
        for k, (source, target) in enumerate(zip(refs[1:4], (offsets_ref, ids_ref, scale_ref)))
    ]
    large = [
        pltpu.make_async_copy(
            refs[0].at[pl.ds(k * tile, tile), :], hidden_ref.at[pl.ds(k * tile, tile), :], sems.at[k]
        )
        for k in range(steps)
    ]
    for copy in small + large:
        copy.start()
    for copy in small:
        copy.wait()
    for step, copy in enumerate(large):
        here = slice(step * tile, (step + 1) * tile)
        scale = scale_ref[:, here]
        jitter = jnp.where(scale == 0, 1.0, jnp.where(scale == 1, 0.5, 0.25))
        xyz = offsets_ref[:, here] * jitter
        row = lax.broadcasted_iota(jnp.int32, (16, tile), 0)
        last = jnp.zeros((16, tile), F32)
        for k in range(half - hid):
            last = jnp.where(row == 16 - (half - hid) + k, xyz[k : k + 1], last)
        last = last.astype(BF16)
        row = lax.broadcasted_iota(jnp.int32, (extra_lanes - 16, tile), 0)
        ids = ids_ref[:, here]
        member = jnp.where((row == ids) | (row == ids + shapes), 1.0, 0.0).astype(BF16)
        x_ref[here, half:] = jnp.concatenate([member, last], axis=0).T
        x_t_ref[half:, here] = member[:shapes]
        copy.wait()
        x_ref[here, half - LANES : half] = jnp.zeros((tile, LANES), BF16)
        x_ref[here, :hid] = hidden_ref[here, :].astype(BF16)
        hidden = x_ref[here, :half].T
        x_t_ref[: half - 16, here] = hidden[: half - 16]
        x_t_ref[half - 16 : half, here] = hidden[half - 16 :] + last


def layer_kernel(hid, shapes, tile, orders, parts, *refs):
    n = 1 if orders is None else len(orders)
    pieces = refs[:n]
    x_ref, x_t_ref, cot_ref, out_hbm, tail_ref, grad_hidden_ref = refs[n : n + 6]
    grad_refs = refs[n + 6 : -6]
    w_ref, turned_ref, out_ref, grad_pre_ref, pre_ref, sems = refs[-6:]
    points, width = cot_ref.shape
    half = width // 2
    steps = points // tile
    head = out_ref.shape[0] // tile
    me = lax.axis_index(AXES)
    if orders is None:
        place(pieces, orders, me, w_ref)
    else:
        unpack(hid, shapes, pieces, orders, me, w_ref)
    copies = []

    def rows_of(step):
        return slice(step * tile, (step + 1) * tile)

    def forward(step):
        pre_ref[step % 2] = dot(x_ref[rows_of(step), :], w_ref[...], NT)

    def middle(step):
        here = rows_of(step)
        pre = pre_ref[step % 2]
        sigma = 0.5 * jnp.tanh(0.5 * pre) + 0.5
        out = pre * sigma
        if step < head:
            out_ref[here, :] = out
        else:
            tail_ref[rows_of(step - head), :] = out
        grad_pre_ref[here, :] = (cot_ref[here, :] * (sigma * (1.0 + (pre - out)))).astype(BF16)

    def backward(step):
        here = rows_of(step)
        grad_hidden_ref[here, :] = dot(grad_pre_ref[here, :], w_ref[:, :half])[:, :hid]

    def store(step):
        here = pl.ds(step * tile, tile)
        copy = pltpu.make_async_copy(out_ref.at[here, :], out_hbm.at[here, :], sems.at[step])
        copy.start()
        copies.append(copy)

    forward(0)
    for step in range(steps):
        if step + 1 < steps:
            forward(step + 1)
        middle(step)
        if step > 0:
            backward(step - 1)
        if step < head:
            store(step)
    backward(steps - 1)
    grad = dot(x_t_ref[...], grad_pre_ref[...])
    sums = grad[half:].astype(BF16)
    for at in range(0, width, half):
        turned_ref[at : at + half, :] = grad[:half, at : at + half].T
    for ref, order in zip(grad_refs, parts):
        ref[:shapes, :] = sums[:, :half]
        ref[shapes : 2 * shapes, :] = sums[:, half:]
        if orders is None:
            ref[2 * shapes :, :] = turned_ref[...].astype(BF16)
            continue
        rows = (ref.shape[0] - 2 * shapes) // len(order)
        for k, mask in enumerate(order):
            at = pl.multiple_of((me ^ mask) * rows, rows)
            to = 2 * shapes + k * rows
            ref[to : to + rows, :] = turned_ref[pl.ds(at, rows), :].astype(BF16)

    for copy in copies:
        copy.wait()


def store_kernel(source_ref, target_ref, sem):
    copy = pltpu.make_async_copy(source_ref, target_ref, sem)
    copy.start()
    copy.wait()


def tail_kernel(_, source_ref, target_ref, sem):
    points, rows = target_ref.shape[0], source_ref.shape[0]
    store_kernel(source_ref, target_ref.at[pl.ds(points - rows, rows), :], sem)


def sum_of(refs):
    terms = [ref[...].astype(F32) for ref in refs]
    while len(terms) > 1:
        terms = [a + b for a, b in zip(terms[::2], terms[1::2])]
    return terms[0]


def add_kernel(shapes, n, *refs):
    total = sum_of(refs[:n]).astype(BF16)
    for k, ref in enumerate(refs[n:]):
        rows = ref.shape[0] - 2 * shapes
        at = 2 * shapes + k * rows
        ref[: 2 * shapes, :] = total[: 2 * shapes]
        ref[2 * shapes :, :] = total[at : at + rows]


def last_kernel(hid, shapes, orders, n, *refs):
    direction_ref, gain_ref, codes_ref = refs[n : n + 3]
    pieces = refs[n + 3 : -5]
    grad_codes_ref, grad_direction_ref, grad_gain_ref, grad_bias_ref, code_scratch = refs[-5:]
    d = direction_ref[...]
    rows, cols = d.shape
    half = cols // 2
    me = lax.axis_index(AXES)
    place(pieces, orders, me, code_scratch)
    total = sum_of(refs[:n])
    sums = jnp.concatenate([total[:shapes], total[shapes : 2 * shapes]], axis=1)
    sums = jnp.concatenate(split(sums), axis=0).astype(BF16)
    terms = dot(sums, code_scratch[...])
    grad_codes_ref[...] = terms[:shapes] + terms[shapes:]
    width = sums.shape[1]
    mine = lax.broadcasted_iota(jnp.int32, (rows, width), 0) + me * rows
    mine = jnp.where(mine == lax.broadcasted_iota(jnp.int32, (rows, width), 1), 1.0, 0.0).astype(BF16)
    own = dot(mine, sums, NT)
    grad_bias_ref[...] = to_row(jnp.sum(own, axis=1, keepdims=True))
    code = dot(own.astype(BF16), stacked_codes(codes_ref, 2 * shapes))
    packed = jnp.concatenate([total[2 * shapes :], code], axis=1)
    lane = lax.broadcasted_iota(jnp.int32, (rows, cols), 1)
    grad_weight = jnp.where(
        lane < hid,
        packed,
        jnp.where(lane < hid + half, pltpu.roll(packed, cols - (half - hid), 1), pltpu.roll(packed, half, 1)),
    )
    inverse = lax.rsqrt(jnp.sum(d * d, axis=1, keepdims=True))
    unit = d * inverse
    grad_gain = jnp.sum(grad_weight * unit, axis=1, keepdims=True)
    grad_gain_ref[...] = to_row(grad_gain)
    grad_direction_ref[...] = (to_column(gain_ref[...]) * inverse) * (grad_weight - grad_gain * unit)


def masks_of(group):
    masks = [0]
    for bit in group:
        masks = masks + [m ^ bit for m in masks]
    return masks


def order_of(groups):
    order = [0]
    for group in groups:
        order = [m ^ r for m in masks_of(group) for r in order]
    return order


def swaps(arrays, masks, devices):
    moved = [
        lax.ppermute(x, AXES, [(i, i ^ mask) for i in range(devices)])
        for x, mask in list(zip(arrays, masks))[::-1]
    ]
    return moved[::-1]


def per_device(
    hidden,
    codes,
    offsets,
    shape_ids,
    scale_index,
    direction,
    gain,
    bias,
    cotangent,
    running_mean,
    running_var,
):
    points, hid = hidden.shape
    shapes = codes.shape[0]
    rows, cols = direction.shape
    width = cotangent.shape[1]
    half = cols // 2
    devices = lax.axis_size("dp") * lax.axis_size("inner")
    bits = [1 << k | 1 for k in range(devices.bit_length() - 1)]
    groups = [bits[k - 2 : k] for k in range(len(bits), 1, -2)]
    groups = groups + [bits[:1]] * (len(bits) % 2)
    groups[0] = [groups[0][0], groups[0][-1] ^ 1]
    extra_lanes = -(-(2 * shapes + 16) // LANES) * LANES
    tuned = len(groups) == 3 and rows % 16 == 0 and 2 * shapes * len(masks_of(groups[0])) == LANES
    lanes = half + extra_lanes
    gain_row = gain.reshape(1, rows)

    def shape_of(rows, lanes, dtype):
        return jax.ShapeDtypeStruct((rows, lanes), dtype)

    held = small_kernel(
        "prep",
        functools.partial(prep_kernel, hid),
        shape_of(rows, lanes + half, BF16),
        *[
            pltpu.with_memory_space_constraint(x, pltpu.HBM)
            for x in (direction, gain_row, bias.reshape(1, rows), codes)
        ],
        scratch=[
            VMEM((rows, cols), F32),
            VMEM((1, rows), F32),
            VMEM((1, rows), F32),
            VMEM((shapes, half), F32),
            pltpu.SemaphoreType.DMA((4,)),
        ],
        space=pl.ANY,
    )
    tile, layer_tile = min(512, points), min(512, points)
    x, x_t = pl.pallas_call(
        functools.partial(inputs_kernel, hid, tile),
        out_shape=[
            shape_of(points, lanes, BF16),
            shape_of(half + shapes, points, BF16),
        ],
        in_specs=[pl.BlockSpec(memory_space=pl.ANY)] * 4,
        out_specs=vmem(2),
        scratch_shapes=[
            VMEM((points, hid), F32),
            VMEM((half - hid, points), F32),
            VMEM((1, points), jnp.int32),
            VMEM((1, points), jnp.int32),
            pltpu.SemaphoreType.DMA((points // tile + 3,)),
        ],
        compiler_params=pltpu.CompilerParams(vmem_limit_bytes=12 * MIB),
        cost_estimate=pl.CostEstimate(
            flops=4000 * MIB, bytes_accessed=8 * points * half, transcendentals=0
        ),
        name="inputs",
    )(
        *[
            pltpu.with_memory_space_constraint(a, pltpu.HBM)
            for a in (
                hidden,
                offsets.T,
                shape_ids.reshape(1, points),
                scale_index.reshape(1, points),
            )
        ]
    )
    def gather(array, group):
        masks = masks_of(group)[1:]
        return [array] + swaps([array] * len(masks), masks, devices)

    def join(arrays, *widths, early=()):
        height = sum(a.shape[0] for a in arrays)
        return small_kernel(
            "join",
            functools.partial(join_kernel, len(arrays), len(early)),
            [shape_of(height, width, BF16) for width in widths],
            *arrays[::-1],
            *early,
        )

    if tuned:
        arrays = gather(held, groups[0])
        weight, code_weight = small_kernel(
            "pack",
            functools.partial(pack_kernel, shapes),
            [
                shape_of((half // LANES * len(arrays) + 1) * rows, LANES, BF16),
                shape_of(len(arrays) * rows, half, BF16),
            ],
            *[arrays[k] for k in FIRST],
        )
        (weights,) = [gather(weight, group) for group in groups[1:-1]]
        along, across = [[bit] for bit in groups[1][::-1]]
        (weight,) = join(weights, LANES, early=(cotangent,))
        weight, x, x_t = lax.optimization_barrier((weight, x, x_t))
        weights = gather(weight, groups[-1])
        code_weights = gather(code_weight, along)
        code_order = order_of([groups[0], along, across])
        orders = [[m ^ r for r in order_of(groups[:-1])] for m in masks_of(groups[-1])]
        code_orders = [[m ^ r for r in code_order] for m in masks_of(groups[-1])]
        parts = orders
    else:
        held = lax.all_gather(held, AXES, axis=0, tiled=True)
        weights, code_weights, orders, code_orders, parts = [held[:, :lanes]], [held[:, lanes:]], None, None, [[0]]

    head = points // layer_tile // 2 * layer_tile
    output, tail, grad_hidden, *grads = pl.pallas_call(
        functools.partial(layer_kernel, hid, shapes, layer_tile, orders, parts),
        out_shape=[
            pltpu.HBM((points, width), F32),
            pltpu.VMEM((points - head, width), F32),
            pltpu.VMEM((points, hid), F32),
        ]
        + [shape_of(2 * shapes + width // len(parts), half, BF16)] * len(parts),
        in_specs=vmem(len(weights) + 3),
        out_specs=[pl.BlockSpec(memory_space=pltpu.HBM)] + vmem(2 + len(parts)),
        scratch_shapes=[
            VMEM((width, lanes), BF16),
            VMEM((width, half), F32),
            VMEM((head, width), F32),
            VMEM((points, width), BF16),
            VMEM((2, layer_tile, width), F32),
            pltpu.SemaphoreType.DMA((head // layer_tile,)),
        ],
        compiler_params=pltpu.CompilerParams(vmem_limit_bytes=20 * MIB),
        cost_estimate=pl.CostEstimate(
            flops=6 * points * width * cols,
            bytes_accessed=8 * points * (width + half),
            transcendentals=points * width,
        ),
        name="layer",
    )(*weights, x, x_t, cotangent)

    def store(name, body, shape, *args, **options):
        return pl.pallas_call(
            body,
            out_shape=pltpu.HBM(shape, F32),
            in_specs=[pl.BlockSpec(memory_space=pltpu.HBM)] * (len(args) - 1) + vmem(1),
            out_specs=pl.BlockSpec(memory_space=pltpu.HBM),
            scratch_shapes=[pltpu.SemaphoreType.DMA(())],
            compiler_params=pltpu.CompilerParams(vmem_limit_bytes=8 * MIB),
            cost_estimate=pl.CostEstimate(
                flops=4000 * MIB, bytes_accessed=8 * points * hid, transcendentals=0
            ),
            name=name,
            **options,
        )(*args)

    def store_grad_hidden():
        return store("store", store_kernel, (points, hid), grad_hidden)

    def store_tail():
        return store(
            "tail", tail_kernel, (points, width), output, tail, input_output_aliases={0: 0}
        )

    if tuned:
        *grads, code_along, running_mean, running_var = lax.optimization_barrier(
            (*grads, code_weights[1], running_mean, running_var)
        )
        (code_weight,) = join([code_weights[0], code_along], half)
        for r, group in enumerate(groups[::-1]):
            masks = masks_of(group)
            grads = [grads[0]] + swaps(grads[1:], masks[1:], devices)
            if r == len(groups) - 1:
                break
            n_out = len(masks_of(groups[-2 - r]))
            left = (grads[0].shape[0] - 2 * shapes) // n_out
            grads = small_kernel(
                "add",
                functools.partial(add_kernel, shapes, len(grads)),
                [shape_of(2 * shapes + left, half, BF16)] * n_out,
                *(grads[::-1] if r == 0 else [grads[k] for k in SUMS]),
            )
            if r == 0:
                *grads, grad_hidden = lax.optimization_barrier((*grads, grad_hidden))
                grad_hidden = store_grad_hidden()
                grad_hidden, code_weight = lax.optimization_barrier((grad_hidden, code_weight))
                code_weights = gather(code_weight, across)
            if r == len(groups) - 2:
                *grads, grad_hidden, tail = lax.optimization_barrier((*grads, grad_hidden, tail))
                output = store_tail()
        (code_weight,) = join(code_weights, half)
        code_weights = gather(code_weight, groups[-1])
    else:
        grad_hidden, output = store_grad_hidden(), store_tail()
        sums = lax.psum(grads[0][: 2 * shapes].astype(F32), AXES)
        high = sums.astype(BF16)
        own = lax.psum_scatter(grads[0][2 * shapes :].astype(F32), AXES, scatter_dimension=0, tiled=True)
        low = jnp.zeros((2 * shapes + rows, half), BF16).at[: 2 * shapes].set((sums - high).astype(BF16))
        grads = [jnp.concatenate([high, own.astype(BF16)], axis=0), low]
    grad_codes, grad_direction, grad_gain, grad_bias = small_kernel(
        "last",
        functools.partial(last_kernel, hid, shapes, code_orders, len(grads)),
        [
            shape_of(shapes, half, F32),
            shape_of(rows, cols, F32),
            shape_of(1, rows, F32),
            shape_of(1, rows, F32),
        ],
        *([grads[k] for k in FIRST] if tuned else grads),
        direction,
        gain_row,
        codes,
        *code_weights,
        scratch=[VMEM((width, half), BF16)],
    )

    total = float(points * devices)
    batch_mean = jnp.mean(codes, axis=0)
    batch_square = jnp.mean(codes * codes, axis=0)
    batch_var = (batch_square - batch_mean * batch_mean) * (total / (total - 1.0))
    new_mean = 0.9 * running_mean + 0.1 * batch_mean
    new_var = 0.9 * running_var + 0.1 * batch_var
    return (
        output,
        grad_hidden,
        grad_codes,
        grad_direction,
        grad_gain.reshape(rows),
        grad_bias.reshape(rows),
        new_mean,
        new_var,
    )


def solution(mesh):
    return jax.shard_map(
        per_device,
        mesh=mesh,
        in_specs=(
            P(("dp", "inner"), None),
            P(),
            P(("dp", "inner"), None),
            P(("dp", "inner")),
            P(("dp", "inner")),
            P(("dp", "inner"), None),
            P(("dp", "inner")),
            P(("dp", "inner")),
            P(("dp", "inner"), None),
            P(),
            P(),
        ),
        out_specs=(
            P(("dp", "inner"), None),
            P(("dp", "inner"), None),
            P(),
            P(("dp", "inner"), None),
            P(("dp", "inner")),
            P(("dp", "inner")),
            P(),
            P(),
        ),
        check_vma=False,
    )
```

```python
import functools

import jax
import jax.numpy as jnp
from jax import lax
from jax.experimental import pallas as pl
from jax.experimental.pallas import tpu as pltpu
from jax.sharding import PartitionSpec as P

AXES = ("dp", "inner")
LANES = 128
MIB = 1024 * 1024
FIRST = (2, 3, 1, 0)
SUMS = (1, 3, 2, 0)
F32 = jnp.float32
BF16 = jnp.bfloat16
VMEM = pltpu.VMEM
NT = (((1,), (1,)), ((), ()))


def dot(a, b, dims=(((1,), (0,)), ((), ()))):
    return lax.dot_general(a, b, dims, preferred_element_type=F32)


def vmem(n):
    return [pl.BlockSpec(memory_space=VMEM)] * n


def small_kernel(name, body, out_shape, *args, scratch=(), space=VMEM, limit=8):
    many = isinstance(out_shape, list)
    return pl.pallas_call(
        body,
        out_shape=out_shape,
        in_specs=[pl.BlockSpec(memory_space=space)] * len(args),
        out_specs=vmem(len(out_shape)) if many else vmem(1)[0],
        scratch_shapes=list(scratch),
        compiler_params=pltpu.CompilerParams(vmem_limit_bytes=limit * MIB),
        cost_estimate=pl.CostEstimate(
            flops=4000 * MIB, bytes_accessed=8 * MIB, transcendentals=4 * MIB
        ),
        name=name,
    )(*args)


def diagonal(n):
    return lax.broadcasted_iota(jnp.int32, (n, n), 0) == lax.broadcasted_iota(jnp.int32, (n, n), 1)


def to_column(row):
    n = row.shape[1]
    return jnp.sum(jnp.where(diagonal(n), row, 0.0), axis=1, keepdims=True)


def to_row(column):
    n = column.shape[0]
    return jnp.sum(jnp.where(diagonal(n), column, 0.0), axis=0, keepdims=True)


def stacked_codes(codes_ref, count):
    codes = codes_ref[...].astype(BF16)
    parts = [codes, codes]
    if count > 2 * codes.shape[0]:
        parts.append(jnp.zeros((count - 2 * codes.shape[0], codes.shape[1]), BF16))
    return jnp.concatenate(parts, axis=0)


def split(x):
    high = x.astype(BF16).astype(F32)
    return high, x - high


def prep_kernel(hid, *refs):
    piece_ref, direction_ref, gain_ref, bias_ref, codes_ref, sems = refs[4:]
    copies = [
        pltpu.make_async_copy(source, target, sems.at[k])
        for k, (source, target) in enumerate(zip(refs[:4], refs[5:9]))
    ]
    for copy in copies:
        copy.start()
    for copy in copies:
        copy.wait()
    d = direction_ref[...]
    shapes = codes_ref.shape[0]
    rows, cols = d.shape
    half = cols // 2
    extra_lanes = piece_ref.shape[1] - cols
    inverse = lax.rsqrt(jnp.sum(d * d, axis=1, keepdims=True))
    w = to_column(gain_ref[...]) * (d * inverse)
    lane = lax.broadcasted_iota(jnp.int32, (rows, half), 1)
    first = jnp.where(lane < hid, w[:, :half], w[:, half:])
    code = pltpu.roll(w, half - hid, 1)[:, half:].astype(BF16)
    bias = to_column(bias_ref[...]).astype(BF16).astype(F32)
    high, low = split(dot(code, stacked_codes(codes_ref, extra_lanes), NT) + bias)
    own = first[:, half - LANES :]
    if extra_lanes > LANES:
        own = jnp.concatenate([jnp.zeros((rows, extra_lanes - LANES), F32), own], axis=1)
    lane = lax.broadcasted_iota(jnp.int32, (rows, extra_lanes), 1)
    table = jnp.where(lane < shapes, high, jnp.where(lane < 2 * shapes, low, 0.0))
    table = jnp.where(lane >= extra_lanes - (half - hid), own, table)
    piece_ref[:, :half] = first.astype(BF16)
    piece_ref[:, half : half + extra_lanes] = table.astype(BF16)
    piece_ref[:, half + extra_lanes :] = code


def join_kernel(n, n_early, *refs):
    rows = refs[0].shape[0]
    for k, ref in enumerate(refs[n - 1 :: -1]):
        lane = 0
        for out_ref in refs[n + n_early :]:
            lanes = out_ref.shape[1]
            out_ref[k * rows : (k + 1) * rows, :] = ref[:, lane : lane + lanes]
            lane += lanes


def pack_kernel(shapes, *refs):
    weight_ref, code_ref = refs[-2:]
    count = len(refs) - 2
    rows, half = refs[0].shape[0], code_ref.shape[1]
    products = jnp.zeros((rows, LANES), F32)
    for k, ref in zip(FIRST, refs):
        for block in range(half // LANES):
            at = (block * count + k) * rows
            weight_ref[at : at + rows, :] = ref[:, block * LANES : (block + 1) * LANES]
        own = ref[:, half : half + LANES].astype(F32)
        own = jnp.where(lax.broadcasted_iota(jnp.int32, own.shape, 1) < 2 * shapes, own, 0.0)
        products = products + (pltpu.roll(own, 2 * shapes * k, 1) if k else own)
        code_ref[k * rows : (k + 1) * rows, :] = ref[:, half + LANES :]
    weight_ref[half // LANES * count * rows :, :] = products.astype(BF16)


def unpack(hid, shapes, refs, orders, me, w_ref):
    count = LANES // (2 * shapes)
    half = w_ref.shape[1] - LANES
    blocks = half // LANES
    for ref, order in zip(refs, orders):
        height = ref.shape[0] // (len(order) // count)
        rows = height // (blocks * count + 1)
        lane = lax.broadcasted_iota(jnp.int32, (rows, LANES), 1)
        for j, mask in enumerate(order):
            start, k = j // count * height, j % count
            at = pl.ds(pl.multiple_of((me ^ mask) * rows, rows), rows)
            for block in range(blocks):
                here = start + (block * count + k) * rows
                part = ref[here : here + rows, :]
                w_ref[at, block * LANES : (block + 1) * LANES] = part
            here = start + blocks * count * rows
            products = ref[here : here + rows, :].astype(F32)
            if k:
                products = pltpu.roll(products, LANES - 2 * shapes * k, 1)
            products = jnp.where(lane < 2 * shapes, products, 0.0)
            products = jnp.where(lane >= LANES - (half - hid), part.astype(F32), products)
            w_ref[at, half:] = products.astype(BF16)


def place(refs, orders, me, out_ref):
    if orders is None:
        out_ref[...] = refs[0][...]
        return
    rows = refs[0].shape[0] // len(orders[0])
    for ref, order in zip(refs, orders):
        for k, mask in enumerate(order):
            at = pl.multiple_of((me ^ mask) * rows, rows)
            out_ref[pl.ds(at, rows), :] = ref[k * rows : (k + 1) * rows, :]


def inputs_kernel(hid, tile, *refs):
    x_ref, x_t_ref, hidden_ref, offsets_ref, ids_ref, scale_ref, sems = refs[4:]
    points = x_ref.shape[0]
    half = (hid + LANES - 1) // LANES * LANES
    shapes = x_t_ref.shape[0] - half
    extra_lanes = x_ref.shape[1] - half
    steps = points // tile
    small = [
        pltpu.make_async_copy(source, target, sems.at[steps + k])
        for k, (source, target) in enumerate(zip(refs[1:4], (offsets_ref, ids_ref, scale_ref)))
    ]
    large = [
        pltpu.make_async_copy(
            refs[0].at[pl.ds(k * tile, tile), :], hidden_ref.at[pl.ds(k * tile, tile), :], sems.at[k]
        )
        for k in range(steps)
    ]
    for copy in small + large:
        copy.start()
    for copy in small:
        copy.wait()
    for step, copy in enumerate(large):
        here = slice(step * tile, (step + 1) * tile)
        scale = scale_ref[:, here]
        jitter = jnp.where(scale == 0, 1.0, jnp.where(scale == 1, 0.5, 0.25))
        xyz = offsets_ref[:, here] * jitter
        row = lax.broadcasted_iota(jnp.int32, (16, tile), 0)
        last = jnp.zeros((16, tile), F32)
        for k in range(half - hid):
            last = jnp.where(row == 16 - (half - hid) + k, xyz[k : k + 1], last)
        last = last.astype(BF16)
        row = lax.broadcasted_iota(jnp.int32, (extra_lanes - 16, tile), 0)
        ids = ids_ref[:, here]
        member = jnp.where((row == ids) | (row == ids + shapes), 1.0, 0.0).astype(BF16)
        x_ref[here, half:] = jnp.concatenate([member, last], axis=0).T
        x_t_ref[half:, here] = member[:shapes]
        copy.wait()
        x_ref[here, half - LANES : half] = jnp.zeros((tile, LANES), BF16)
        x_ref[here, :hid] = hidden_ref[here, :].astype(BF16)
        hidden = x_ref[here, :half].T
        x_t_ref[: half - 16, here] = hidden[: half - 16]
        x_t_ref[half - 16 : half, here] = hidden[half - 16 :] + last


def layer_kernel(hid, shapes, tile, orders, parts, *refs):
    n = 1 if orders is None else len(orders)
    pieces = refs[:n]
    x_ref, x_t_ref, cot_ref, out_hbm, tail_ref, grad_hidden_ref = refs[n : n + 6]
    grad_refs = refs[n + 6 : -6]
    w_ref, turned_ref, out_ref, grad_pre_ref, pre_ref, sems = refs[-6:]
    points, width = cot_ref.shape
    half = width // 2
    steps = points // tile
    head = out_ref.shape[0] // tile
    me = lax.axis_index(AXES)
    if orders is None:
        place(pieces, orders, me, w_ref)
    else:
        unpack(hid, shapes, pieces, orders, me, w_ref)
    copies = []

    def rows_of(step):
        return slice(step * tile, (step + 1) * tile)

    def forward(step):
        pre_ref[step % 2] = dot(x_ref[rows_of(step), :], w_ref[...], NT)

    def middle(step):
        here = rows_of(step)
        pre = pre_ref[step % 2]
        sigma = 0.5 * jnp.tanh(0.5 * pre) + 0.5
        out = pre * sigma
        if step < head:
            out_ref[here, :] = out
        else:
            tail_ref[rows_of(step - head), :] = out
        grad_pre_ref[here, :] = (cot_ref[here, :] * (sigma * (1.0 + (pre - out)))).astype(BF16)

    def backward(step):
        here = rows_of(step)
        grad_hidden_ref[here, :] = dot(grad_pre_ref[here, :], w_ref[:, :half])[:, :hid]

    def store(step):
        here = pl.ds(step * tile, tile)
        copy = pltpu.make_async_copy(out_ref.at[here, :], out_hbm.at[here, :], sems.at[step])
        copy.start()
        copies.append(copy)

    forward(0)
    for step in range(steps):
        if step + 1 < steps:
            forward(step + 1)
        middle(step)
        if step > 0:
            backward(step - 1)
        if step < head:
            store(step)
    backward(steps - 1)
    grad = dot(x_t_ref[...], grad_pre_ref[...])
    sums = grad[half:].astype(BF16)
    for at in range(0, width, half):
        turned_ref[at : at + half, :] = grad[:half, at : at + half].T
    for ref, order in zip(grad_refs, parts):
        ref[:shapes, :] = sums[:, :half]
        ref[shapes : 2 * shapes, :] = sums[:, half:]
        if orders is None:
            ref[2 * shapes :, :] = turned_ref[...].astype(BF16)
            continue
        rows = (ref.shape[0] - 2 * shapes) // len(order)
        for k, mask in enumerate(order):
            at = pl.multiple_of((me ^ mask) * rows, rows)
            to = 2 * shapes + k * rows
            ref[to : to + rows, :] = turned_ref[pl.ds(at, rows), :].astype(BF16)

    for copy in copies:
        copy.wait()


def store_kernel(source_ref, target_ref, sem):
    copy = pltpu.make_async_copy(source_ref, target_ref, sem)
    copy.start()
    copy.wait()


def tail_kernel(_, source_ref, target_ref, sem):
    points, rows = target_ref.shape[0], source_ref.shape[0]
    store_kernel(source_ref, target_ref.at[pl.ds(points - rows, rows), :], sem)


def sum_of(refs):
    terms = [ref[...].astype(F32) for ref in refs]
    while len(terms) > 1:
        terms = [a + b for a, b in zip(terms[::2], terms[1::2])]
    return terms[0]


def add_kernel(shapes, n, *refs):
    total = sum_of(refs[:n]).astype(BF16)
    for k, ref in enumerate(refs[n:]):
        rows = ref.shape[0] - 2 * shapes
        at = 2 * shapes + k * rows
        ref[: 2 * shapes, :] = total[: 2 * shapes]
        ref[2 * shapes :, :] = total[at : at + rows]


def last_kernel(hid, shapes, orders, n, *refs):
    direction_ref, gain_ref, codes_ref = refs[n : n + 3]
    pieces = refs[n + 3 : -5]
    grad_codes_ref, grad_direction_ref, grad_gain_ref, grad_bias_ref, code_scratch = refs[-5:]
    d = direction_ref[...]
    rows, cols = d.shape
    half = cols // 2
    me = lax.axis_index(AXES)
    place(pieces, orders, me, code_scratch)
    total = sum_of(refs[:n])
    sums = jnp.concatenate([total[:shapes], total[shapes : 2 * shapes]], axis=1)
    sums = jnp.concatenate(split(sums), axis=0).astype(BF16)
    terms = dot(sums, code_scratch[...])
    grad_codes_ref[...] = terms[:shapes] + terms[shapes:]
    width = sums.shape[1]
    mine = lax.broadcasted_iota(jnp.int32, (rows, width), 0) + me * rows
    mine = jnp.where(mine == lax.broadcasted_iota(jnp.int32, (rows, width), 1), 1.0, 0.0).astype(BF16)
    own = dot(mine, sums, NT)
    grad_bias_ref[...] = to_row(jnp.sum(own, axis=1, keepdims=True))
    code = dot(own.astype(BF16), stacked_codes(codes_ref, 2 * shapes))
    packed = jnp.concatenate([total[2 * shapes :], code], axis=1)
    lane = lax.broadcasted_iota(jnp.int32, (rows, cols), 1)
    grad_weight = jnp.where(
        lane < hid,
        packed,
        jnp.where(lane < hid + half, pltpu.roll(packed, cols - (half - hid), 1), pltpu.roll(packed, half, 1)),
    )
    inverse = lax.rsqrt(jnp.sum(d * d, axis=1, keepdims=True))
    unit = d * inverse
    grad_gain = jnp.sum(grad_weight * unit, axis=1, keepdims=True)
    grad_gain_ref[...] = to_row(grad_gain)
    grad_direction_ref[...] = (to_column(gain_ref[...]) * inverse) * (grad_weight - grad_gain * unit)


def masks_of(group):
    masks = [0]
    for bit in group:
        masks = masks + [m ^ bit for m in masks]
    return masks


def order_of(groups):
    order = [0]
    for group in groups:
        order = [m ^ r for m in masks_of(group) for r in order]
    return order


def swaps(arrays, masks, devices):
    moved = [
        lax.ppermute(x, AXES, [(i, i ^ mask) for i in range(devices)])
        for x, mask in list(zip(arrays, masks))[::-1]
    ]
    return moved[::-1]


def per_device(
    hidden,
    codes,
    offsets,
    shape_ids,
    scale_index,
    direction,
    gain,
    bias,
    cotangent,
    running_mean,
    running_var,
):
    points, hid = hidden.shape
    shapes = codes.shape[0]
    rows, cols = direction.shape
    width = cotangent.shape[1]
    half = cols // 2
    devices = lax.axis_size("dp") * lax.axis_size("inner")
    bits = [1 << k | 1 for k in range(devices.bit_length() - 1)]
    groups = [bits[k - 2 : k] for k in range(len(bits), 1, -2)]
    groups = groups + [bits[:1]] * (len(bits) % 2)
    groups[0] = [groups[0][0], groups[0][-1] ^ 1]
    gathers = [groups[0]] + [[group[0], group[-1] ^ 1] for group in groups[1:-1]] + groups[-1:]
    extra_lanes = -(-(2 * shapes + 16) // LANES) * LANES
    tuned = len(groups) == 3 and rows % 16 == 0 and 2 * shapes * len(masks_of(groups[0])) == LANES
    lanes = half + extra_lanes
    gain_row = gain.reshape(1, rows)

    def shape_of(rows, lanes, dtype):
        return jax.ShapeDtypeStruct((rows, lanes), dtype)

    held = small_kernel(
        "prep",
        functools.partial(prep_kernel, hid),
        shape_of(rows, lanes + half, BF16),
        *[
            pltpu.with_memory_space_constraint(x, pltpu.HBM)
            for x in (direction, gain_row, bias.reshape(1, rows), codes)
        ],
        scratch=[
            VMEM((rows, cols), F32),
            VMEM((1, rows), F32),
            VMEM((1, rows), F32),
            VMEM((shapes, half), F32),
            pltpu.SemaphoreType.DMA((4,)),
        ],
        space=pl.ANY,
    )
    tile, layer_tile = min(512, points), min(512, points)
    x, x_t = pl.pallas_call(
        functools.partial(inputs_kernel, hid, tile),
        out_shape=[
            shape_of(points, lanes, BF16),
            shape_of(half + shapes, points, BF16),
        ],
        in_specs=[pl.BlockSpec(memory_space=pl.ANY)] * 4,
        out_specs=vmem(2),
        scratch_shapes=[
            VMEM((points, hid), F32),
            VMEM((half - hid, points), F32),
            VMEM((1, points), jnp.int32),
            VMEM((1, points), jnp.int32),
            pltpu.SemaphoreType.DMA((points // tile + 3,)),
        ],
        compiler_params=pltpu.CompilerParams(vmem_limit_bytes=12 * MIB),
        cost_estimate=pl.CostEstimate(
            flops=4000 * MIB, bytes_accessed=8 * points * half, transcendentals=0
        ),
        name="inputs",
    )(
        *[
            pltpu.with_memory_space_constraint(a, pltpu.HBM)
            for a in (
                hidden,
                offsets.T,
                shape_ids.reshape(1, points),
                scale_index.reshape(1, points),
            )
        ]
    )
    def gather(array, group):
        masks = masks_of(group)[1:]
        return [array] + swaps([array] * len(masks), masks, devices)

    def join(arrays, *widths, early=()):
        height = sum(a.shape[0] for a in arrays)
        return small_kernel(
            "join",
            functools.partial(join_kernel, len(arrays), len(early)),
            [shape_of(height, width, BF16) for width in widths],
            *arrays[::-1],
            *early,
        )

    if tuned:
        arrays = gather(held, gathers[0])
        weight, code_weight = small_kernel(
            "pack",
            functools.partial(pack_kernel, shapes),
            [
                shape_of((half // LANES * len(arrays) + 1) * rows, LANES, BF16),
                shape_of(len(arrays) * rows, half, BF16),
            ],
            *[arrays[k] for k in FIRST],
        )
        weight, code_weight, x, x_t = lax.optimization_barrier((weight, code_weight, x, x_t))
        (weights,) = [gather(weight, group) for group in gathers[1:-1]]
        along, across = [[bit] for bit in gathers[1][::-1]]
        (weight,) = join(weights, LANES, early=(cotangent,))
        weights = gather(weight, gathers[-1])
        code_weights = gather(code_weight, along)
        code_order = order_of([gathers[0], along, across])
        orders = [[m ^ r for r in order_of(gathers[:-1])] for m in masks_of(gathers[-1])]
        code_orders = [[m ^ r for r in code_order] for m in masks_of(gathers[-1])]
        parts = [[m ^ r for r in order_of(groups[:-1])] for m in masks_of(groups[-1])]
    else:
        held = lax.all_gather(held, AXES, axis=0, tiled=True)
        weights, code_weights, orders, code_orders, parts = [held[:, :lanes]], [held[:, lanes:]], None, None, [[0]]

    head = points // layer_tile // 2 * layer_tile
    output, tail, grad_hidden, *grads = pl.pallas_call(
        functools.partial(layer_kernel, hid, shapes, layer_tile, orders, parts),
        out_shape=[
            pltpu.HBM((points, width), F32),
            pltpu.VMEM((points - head, width), F32),
            pltpu.VMEM((points, hid), F32),
        ]
        + [shape_of(2 * shapes + width // len(parts), half, BF16)] * len(parts),
        in_specs=vmem(len(weights) + 3),
        out_specs=[pl.BlockSpec(memory_space=pltpu.HBM)] + vmem(2 + len(parts)),
        scratch_shapes=[
            VMEM((width, lanes), BF16),
            VMEM((width, half), F32),
            VMEM((head, width), F32),
            VMEM((points, width), BF16),
            VMEM((2, layer_tile, width), F32),
            pltpu.SemaphoreType.DMA((head // layer_tile,)),
        ],
        compiler_params=pltpu.CompilerParams(vmem_limit_bytes=20 * MIB),
        cost_estimate=pl.CostEstimate(
            flops=6 * points * width * cols,
            bytes_accessed=8 * points * (width + half),
            transcendentals=points * width,
        ),
        name="layer",
    )(*weights, x, x_t, cotangent)

    def store(name, body, shape, *args, **options):
        return pl.pallas_call(
            body,
            out_shape=pltpu.HBM(shape, F32),
            in_specs=[pl.BlockSpec(memory_space=pltpu.HBM)] * (len(args) - 1) + vmem(1),
            out_specs=pl.BlockSpec(memory_space=pltpu.HBM),
            scratch_shapes=[pltpu.SemaphoreType.DMA(())],
            compiler_params=pltpu.CompilerParams(vmem_limit_bytes=8 * MIB),
            cost_estimate=pl.CostEstimate(
                flops=4000 * MIB, bytes_accessed=8 * points * hid, transcendentals=0
            ),
            name=name,
            **options,
        )(*args)

    def store_grad_hidden():
        return store("store", store_kernel, (points, hid), grad_hidden)

    def store_tail():
        return store(
            "tail", tail_kernel, (points, width), output, tail, input_output_aliases={0: 0}
        )

    if tuned:
        *grads, code_along, running_mean, running_var = lax.optimization_barrier(
            (*grads, code_weights[1], running_mean, running_var)
        )
        (code_weight,) = join([code_weights[0], code_along], half)
        for r, group in enumerate(groups[::-1]):
            masks = masks_of(group)
            grads = [grads[0]] + swaps(grads[1:], masks[1:], devices)
            if r == len(groups) - 1:
                break
            n_out = len(masks_of(groups[-2 - r]))
            left = (grads[0].shape[0] - 2 * shapes) // n_out
            grads = small_kernel(
                "add",
                functools.partial(add_kernel, shapes, len(grads)),
                [shape_of(2 * shapes + left, half, BF16)] * n_out,
                *(grads[::-1] if r == 0 else [grads[k] for k in SUMS]),
            )
            if r == 0:
                *grads, grad_hidden = lax.optimization_barrier((*grads, grad_hidden))
                grad_hidden = store_grad_hidden()
                grad_hidden, code_weight = lax.optimization_barrier((grad_hidden, code_weight))
                code_weights = gather(code_weight, across)
            if r == len(groups) - 2:
                *grads, grad_hidden, tail = lax.optimization_barrier((*grads, grad_hidden, tail))
                output = store_tail()
        (code_weight,) = join(code_weights, half)
        code_weights = gather(code_weight, groups[-1])
    else:
        grad_hidden, output = store_grad_hidden(), store_tail()
        sums = lax.psum(grads[0][: 2 * shapes].astype(F32), AXES)
        high = sums.astype(BF16)
        own = lax.psum_scatter(grads[0][2 * shapes :].astype(F32), AXES, scatter_dimension=0, tiled=True)
        low = jnp.zeros((2 * shapes + rows, half), BF16).at[: 2 * shapes].set((sums - high).astype(BF16))
        grads = [jnp.concatenate([high, own.astype(BF16)], axis=0), low]
    grad_codes, grad_direction, grad_gain, grad_bias = small_kernel(
        "last",
        functools.partial(last_kernel, hid, shapes, code_orders, len(grads)),
        [
            shape_of(shapes, half, F32),
            shape_of(rows, cols, F32),
            shape_of(1, rows, F32),
            shape_of(1, rows, F32),
        ],
        *([grads[k] for k in FIRST] if tuned else grads),
        direction,
        gain_row,
        codes,
        *code_weights,
        scratch=[VMEM((width, half), BF16)],
    )

    total = float(points * devices)
    batch_mean = jnp.mean(codes, axis=0)
    batch_square = jnp.mean(codes * codes, axis=0)
    batch_var = (batch_square - batch_mean * batch_mean) * (total / (total - 1.0))
    new_mean = 0.9 * running_mean + 0.1 * batch_mean
    new_var = 0.9 * running_var + 0.1 * batch_var
    return (
        output,
        grad_hidden,
        grad_codes,
        grad_direction,
        grad_gain.reshape(rows),
        grad_bias.reshape(rows),
        new_mean,
        new_var,
    )


def solution(mesh):
    return jax.shard_map(
        per_device,
        mesh=mesh,
        in_specs=(
            P(("dp", "inner"), None),
            P(),
            P(("dp", "inner"), None),
            P(("dp", "inner")),
            P(("dp", "inner")),
            P(("dp", "inner"), None),
            P(("dp", "inner")),
            P(("dp", "inner")),
            P(("dp", "inner"), None),
            P(),
            P(),
        ),
        out_specs=(
            P(("dp", "inner"), None),
            P(("dp", "inner"), None),
            P(),
            P(("dp", "inner"), None),
            P(("dp", "inner")),
            P(("dp", "inner")),
            P(),
            P(),
        ),
        check_vma=False,
    )
```

```python
import functools

import jax
import jax.numpy as jnp
from jax import lax
from jax.experimental import pallas as pl
from jax.experimental.pallas import tpu as pltpu
from jax.sharding import PartitionSpec as P

AXES = ("dp", "inner")
LANES = 128
MIB = 1024 * 1024
FIRST = (2, 3, 1, 0)
SUMS = (1, 3, 2, 0)
F32 = jnp.float32
BF16 = jnp.bfloat16
VMEM = pltpu.VMEM
NT = (((1,), (1,)), ((), ()))


def dot(a, b, dims=(((1,), (0,)), ((), ()))):
    return lax.dot_general(a, b, dims, preferred_element_type=F32)


def vmem(n):
    return [pl.BlockSpec(memory_space=VMEM)] * n


def small_kernel(name, body, out_shape, *args, scratch=(), space=VMEM, limit=8):
    many = isinstance(out_shape, list)
    return pl.pallas_call(
        body,
        out_shape=out_shape,
        in_specs=[pl.BlockSpec(memory_space=space)] * len(args),
        out_specs=vmem(len(out_shape)) if many else vmem(1)[0],
        scratch_shapes=list(scratch),
        compiler_params=pltpu.CompilerParams(vmem_limit_bytes=limit * MIB),
        cost_estimate=pl.CostEstimate(
            flops=4000 * MIB, bytes_accessed=8 * MIB, transcendentals=4 * MIB
        ),
        name=name,
    )(*args)


def diagonal(n):
    return lax.broadcasted_iota(jnp.int32, (n, n), 0) == lax.broadcasted_iota(jnp.int32, (n, n), 1)


def to_column(row):
    n = row.shape[1]
    return jnp.sum(jnp.where(diagonal(n), row, 0.0), axis=1, keepdims=True)


def to_row(column):
    n = column.shape[0]
    return jnp.sum(jnp.where(diagonal(n), column, 0.0), axis=0, keepdims=True)


def stacked_codes(codes_ref, count):
    codes = codes_ref[...].astype(BF16)
    parts = [codes, codes]
    if count > 2 * codes.shape[0]:
        parts.append(jnp.zeros((count - 2 * codes.shape[0], codes.shape[1]), BF16))
    return jnp.concatenate(parts, axis=0)


def split(x):
    high = x.astype(BF16).astype(F32)
    return high, x - high


def prep_kernel(hid, *refs):
    piece_ref, direction_ref, gain_ref, bias_ref, codes_ref, sems = refs[4:]
    copies = [
        pltpu.make_async_copy(source, target, sems.at[k])
        for k, (source, target) in enumerate(zip(refs[:4], refs[5:9]))
    ]
    for copy in copies:
        copy.start()
    for copy in copies:
        copy.wait()
    d = direction_ref[...]
    shapes = codes_ref.shape[0]
    rows, cols = d.shape
    half = cols // 2
    extra_lanes = piece_ref.shape[1] - cols
    inverse = lax.rsqrt(jnp.sum(d * d, axis=1, keepdims=True))
    w = to_column(gain_ref[...]) * (d * inverse)
    lane = lax.broadcasted_iota(jnp.int32, (rows, half), 1)
    first = jnp.where(lane < hid, w[:, :half], w[:, half:])
    code = pltpu.roll(w, half - hid, 1)[:, half:].astype(BF16)
    bias = to_column(bias_ref[...]).astype(BF16).astype(F32)
    high, low = split(dot(code, stacked_codes(codes_ref, extra_lanes), NT) + bias)
    own = first[:, half - LANES :]
    if extra_lanes > LANES:
        own = jnp.concatenate([jnp.zeros((rows, extra_lanes - LANES), F32), own], axis=1)
    lane = lax.broadcasted_iota(jnp.int32, (rows, extra_lanes), 1)
    table = jnp.where(lane < shapes, high, jnp.where(lane < 2 * shapes, low, 0.0))
    table = jnp.where(lane >= extra_lanes - (half - hid), own, table)
    piece_ref[:, :half] = first.astype(BF16)
    piece_ref[:, half : half + extra_lanes] = table.astype(BF16)
    piece_ref[:, half + extra_lanes :] = code


def join_kernel(n, n_early, *refs):
    rows = refs[0].shape[0]
    for k, ref in enumerate(refs[n - 1 :: -1]):
        lane = 0
        for out_ref in refs[n + n_early :]:
            lanes = out_ref.shape[1]
            out_ref[k * rows : (k + 1) * rows, :] = ref[:, lane : lane + lanes]
            lane += lanes


def pack_kernel(shapes, *refs):
    weight_ref, code_ref = refs[-2:]
    count = len(refs) - 2
    rows, half = refs[0].shape[0], code_ref.shape[1]
    products = jnp.zeros((rows, LANES), F32)
    for k, ref in zip(FIRST, refs):
        for block in range(half // LANES):
            at = (block * count + k) * rows
            weight_ref[at : at + rows, :] = ref[:, block * LANES : (block + 1) * LANES]
        own = ref[:, half : half + LANES].astype(F32)
        own = jnp.where(lax.broadcasted_iota(jnp.int32, own.shape, 1) < 2 * shapes, own, 0.0)
        products = products + (pltpu.roll(own, 2 * shapes * k, 1) if k else own)
        code_ref[k * rows : (k + 1) * rows, :] = ref[:, half + LANES :]
    weight_ref[half // LANES * count * rows :, :] = products.astype(BF16)


def unpack(hid, shapes, refs, orders, me, w_ref):
    count = LANES // (2 * shapes)
    half = w_ref.shape[1] - LANES
    blocks = half // LANES
    for ref, order in zip(refs, orders):
        height = ref.shape[0] // (len(order) // count)
        rows = height // (blocks * count + 1)
        lane = lax.broadcasted_iota(jnp.int32, (rows, LANES), 1)
        for j, mask in enumerate(order):
            start, k = j // count * height, j % count
            at = pl.ds(pl.multiple_of((me ^ mask) * rows, rows), rows)
            for block in range(blocks):
                here = start + (block * count + k) * rows
                part = ref[here : here + rows, :]
                w_ref[at, block * LANES : (block + 1) * LANES] = part
            here = start + blocks * count * rows
            products = ref[here : here + rows, :].astype(F32)
            if k:
                products = pltpu.roll(products, LANES - 2 * shapes * k, 1)
            products = jnp.where(lane < 2 * shapes, products, 0.0)
            products = jnp.where(lane >= LANES - (half - hid), part.astype(F32), products)
            w_ref[at, half:] = products.astype(BF16)


def place(refs, orders, me, out_ref):
    if orders is None:
        out_ref[...] = refs[0][...]
        return
    rows = refs[0].shape[0] // len(orders[0])
    for ref, order in zip(refs, orders):
        for k, mask in enumerate(order):
            at = pl.multiple_of((me ^ mask) * rows, rows)
            out_ref[pl.ds(at, rows), :] = ref[k * rows : (k + 1) * rows, :]


def inputs_kernel(hid, tile, *refs):
    x_ref, x_t_ref, hidden_ref, offsets_ref, ids_ref, scale_ref, sems = refs[4:]
    points = x_ref.shape[0]
    half = (hid + LANES - 1) // LANES * LANES
    shapes = x_t_ref.shape[0] - half
    extra_lanes = x_ref.shape[1] - half
    steps = points // tile
    small = [
        pltpu.make_async_copy(source, target, sems.at[steps + k])
        for k, (source, target) in enumerate(zip(refs[1:4], (offsets_ref, ids_ref, scale_ref)))
    ]
    large = [
        pltpu.make_async_copy(
            refs[0].at[pl.ds(k * tile, tile), :], hidden_ref.at[pl.ds(k * tile, tile), :], sems.at[k]
        )
        for k in range(steps)
    ]
    for copy in small + large:
        copy.start()
    for copy in small:
        copy.wait()
    for step, copy in enumerate(large):
        here = slice(step * tile, (step + 1) * tile)
        scale = scale_ref[:, here]
        jitter = jnp.where(scale == 0, 1.0, jnp.where(scale == 1, 0.5, 0.25))
        xyz = offsets_ref[:, here] * jitter
        row = lax.broadcasted_iota(jnp.int32, (16, tile), 0)
        last = jnp.zeros((16, tile), F32)
        for k in range(half - hid):
            last = jnp.where(row == 16 - (half - hid) + k, xyz[k : k + 1], last)
        last = last.astype(BF16)
        row = lax.broadcasted_iota(jnp.int32, (extra_lanes - 16, tile), 0)
        ids = ids_ref[:, here]
        member = jnp.where((row == ids) | (row == ids + shapes), 1.0, 0.0).astype(BF16)
        x_ref[here, half:] = jnp.concatenate([member, last], axis=0).T
        x_t_ref[half:, here] = member[:shapes]
        copy.wait()
        x_ref[here, half - LANES : half] = jnp.zeros((tile, LANES), BF16)
        x_ref[here, :hid] = hidden_ref[here, :].astype(BF16)
        hidden = x_ref[here, :half].T
        x_t_ref[: half - 16, here] = hidden[: half - 16]
        x_t_ref[half - 16 : half, here] = hidden[half - 16 :] + last


def layer_kernel(hid, shapes, tile, orders, parts, *refs):
    n = 1 if orders is None else len(orders)
    pieces = refs[:n]
    x_ref, x_t_ref, cot_ref, out_hbm, tail_ref, grad_hidden_ref = refs[n : n + 6]
    grad_refs = refs[n + 6 : -6]
    w_ref, turned_ref, out_ref, grad_pre_ref, pre_ref, sems = refs[-6:]
    points, width = cot_ref.shape
    half = width // 2
    steps = points // tile
    head = out_ref.shape[0] // tile
    me = lax.axis_index(AXES)
    if orders is None:
        place(pieces, orders, me, w_ref)
    else:
        unpack(hid, shapes, pieces, orders, me, w_ref)
    copies = []

    def rows_of(step):
        return slice(step * tile, (step + 1) * tile)

    def forward(step):
        pre_ref[step % 2] = dot(x_ref[rows_of(step), :], w_ref[...], NT)

    def middle(step):
        here = rows_of(step)
        pre = pre_ref[step % 2]
        sigma = 0.5 * jnp.tanh(0.5 * pre) + 0.5
        out = pre * sigma
        if step < head:
            out_ref[here, :] = out
        else:
            tail_ref[rows_of(step - head), :] = out
        grad_pre_ref[here, :] = (cot_ref[here, :] * (sigma * (1.0 + (pre - out)))).astype(BF16)

    def backward(step):
        here = rows_of(step)
        grad_hidden_ref[here, :] = dot(grad_pre_ref[here, :], w_ref[:, :half])[:, :hid]

    def store(step):
        here = pl.ds(step * tile, tile)
        copy = pltpu.make_async_copy(out_ref.at[here, :], out_hbm.at[here, :], sems.at[step])
        copy.start()
        copies.append(copy)

    forward(0)
    for step in range(steps):
        if step + 1 < steps:
            forward(step + 1)
        middle(step)
        if step > 0:
            backward(step - 1)
        if step < head:
            store(step)
    backward(steps - 1)
    grad = dot(x_t_ref[...], grad_pre_ref[...])
    sums = grad[half:].astype(BF16)
    for at in range(0, width, half):
        turned_ref[at : at + half, :] = grad[:half, at : at + half].T
    for ref, order in zip(grad_refs, parts):
        ref[:shapes, :] = sums[:, :half]
        ref[shapes : 2 * shapes, :] = sums[:, half:]
        if orders is None:
            ref[2 * shapes :, :] = turned_ref[...].astype(BF16)
            continue
        rows = (ref.shape[0] - 2 * shapes) // len(order)
        for k, mask in enumerate(order):
            at = pl.multiple_of((me ^ mask) * rows, rows)
            to = 2 * shapes + k * rows
            ref[to : to + rows, :] = turned_ref[pl.ds(at, rows), :].astype(BF16)

    for copy in copies:
        copy.wait()


def store_kernel(source_ref, target_ref, sem):
    copy = pltpu.make_async_copy(source_ref, target_ref, sem)
    copy.start()
    copy.wait()


def tail_kernel(_, source_ref, target_ref, sem):
    points, rows = target_ref.shape[0], source_ref.shape[0]
    store_kernel(source_ref, target_ref.at[pl.ds(points - rows, rows), :], sem)


def sum_of(refs):
    terms = [ref[...].astype(F32) for ref in refs]
    while len(terms) > 1:
        terms = [a + b for a, b in zip(terms[::2], terms[1::2])]
    return terms[0]


def add_kernel(shapes, n, *refs):
    total = sum_of(refs[:n]).astype(BF16)
    for k, ref in enumerate(refs[n:]):
        rows = ref.shape[0] - 2 * shapes
        at = 2 * shapes + k * rows
        ref[: 2 * shapes, :] = total[: 2 * shapes]
        ref[2 * shapes :, :] = total[at : at + rows]


def last_kernel(hid, shapes, orders, n, *refs):
    direction_ref, gain_ref, codes_ref = refs[n : n + 3]
    pieces = refs[n + 3 : -5]
    grad_codes_ref, grad_direction_ref, grad_gain_ref, grad_bias_ref, code_scratch = refs[-5:]
    d = direction_ref[...]
    rows, cols = d.shape
    half = cols // 2
    me = lax.axis_index(AXES)
    place(pieces, orders, me, code_scratch)
    total = sum_of(refs[:n])
    sums = jnp.concatenate([total[:shapes], total[shapes : 2 * shapes]], axis=1)
    sums = jnp.concatenate(split(sums), axis=0).astype(BF16)
    terms = dot(sums, code_scratch[...])
    grad_codes_ref[...] = terms[:shapes] + terms[shapes:]
    width = sums.shape[1]
    mine = lax.broadcasted_iota(jnp.int32, (rows, width), 0) + me * rows
    mine = jnp.where(mine == lax.broadcasted_iota(jnp.int32, (rows, width), 1), 1.0, 0.0).astype(BF16)
    own = dot(mine, sums, NT)
    grad_bias_ref[...] = to_row(jnp.sum(own, axis=1, keepdims=True))
    code = dot(own.astype(BF16), stacked_codes(codes_ref, 2 * shapes))
    packed = jnp.concatenate([total[2 * shapes :], code], axis=1)
    lane = lax.broadcasted_iota(jnp.int32, (rows, cols), 1)
    grad_weight = jnp.where(
        lane < hid,
        packed,
        jnp.where(lane < hid + half, pltpu.roll(packed, cols - (half - hid), 1), pltpu.roll(packed, half, 1)),
    )
    inverse = lax.rsqrt(jnp.sum(d * d, axis=1, keepdims=True))
    unit = d * inverse
    grad_gain = jnp.sum(grad_weight * unit, axis=1, keepdims=True)
    grad_gain_ref[...] = to_row(grad_gain)
    grad_direction_ref[...] = (to_column(gain_ref[...]) * inverse) * (grad_weight - grad_gain * unit)


def masks_of(group):
    masks = [0]
    for bit in group:
        masks = masks + [m ^ bit for m in masks]
    return masks


def order_of(groups):
    order = [0]
    for group in groups:
        order = [m ^ r for m in masks_of(group) for r in order]
    return order


def swaps(arrays, masks, devices):
    moved = [
        lax.ppermute(x, AXES, [(i, i ^ mask) for i in range(devices)])
        for x, mask in list(zip(arrays, masks))[::-1]
    ]
    return moved[::-1]


def per_device(
    hidden,
    codes,
    offsets,
    shape_ids,
    scale_index,
    direction,
    gain,
    bias,
    cotangent,
    running_mean,
    running_var,
):
    points, hid = hidden.shape
    shapes = codes.shape[0]
    rows, cols = direction.shape
    width = cotangent.shape[1]
    half = cols // 2
    devices = lax.axis_size("dp") * lax.axis_size("inner")
    bits = [1 << k | 1 for k in range(devices.bit_length() - 1)]
    groups = [bits[k - 2 : k] for k in range(len(bits), 1, -2)]
    groups = groups + [bits[:1]] * (len(bits) % 2)
    groups[0] = [groups[0][0], groups[0][-1] ^ 1]
    extra_lanes = -(-(2 * shapes + 16) // LANES) * LANES
    tuned = len(groups) == 3 and rows % 16 == 0 and 2 * shapes * len(masks_of(groups[0])) == LANES
    lanes = half + extra_lanes
    gain_row = gain.reshape(1, rows)

    def shape_of(rows, lanes, dtype):
        return jax.ShapeDtypeStruct((rows, lanes), dtype)

    held = small_kernel(
        "prep",
        functools.partial(prep_kernel, hid),
        shape_of(rows, lanes + half, BF16),
        *[
            pltpu.with_memory_space_constraint(x, pltpu.HBM)
            for x in (direction, gain_row, bias.reshape(1, rows), codes)
        ],
        scratch=[
            VMEM((rows, cols), F32),
            VMEM((1, rows), F32),
            VMEM((1, rows), F32),
            VMEM((shapes, half), F32),
            pltpu.SemaphoreType.DMA((4,)),
        ],
        space=pl.ANY,
    )
    tile, layer_tile = min(256, points), min(512, points)
    x, x_t = pl.pallas_call(
        functools.partial(inputs_kernel, hid, tile),
        out_shape=[
            shape_of(points, lanes, BF16),
            shape_of(half + shapes, points, BF16),
        ],
        in_specs=[pl.BlockSpec(memory_space=pl.ANY)] * 4,
        out_specs=vmem(2),
        scratch_shapes=[
            VMEM((points, hid), F32),
            VMEM((half - hid, points), F32),
            VMEM((1, points), jnp.int32),
            VMEM((1, points), jnp.int32),
            pltpu.SemaphoreType.DMA((points // tile + 3,)),
        ],
        compiler_params=pltpu.CompilerParams(vmem_limit_bytes=12 * MIB),
        cost_estimate=pl.CostEstimate(
            flops=4000 * MIB, bytes_accessed=8 * points * half, transcendentals=0
        ),
        name="inputs",
    )(
        *[
            pltpu.with_memory_space_constraint(a, pltpu.HBM)
            for a in (
                hidden,
                offsets.T,
                shape_ids.reshape(1, points),
                scale_index.reshape(1, points),
            )
        ]
    )
    def gather(array, group):
        masks = masks_of(group)[1:]
        return [array] + swaps([array] * len(masks), masks, devices)

    def join(arrays, *widths, early=()):
        height = sum(a.shape[0] for a in arrays)
        return small_kernel(
            "join",
            functools.partial(join_kernel, len(arrays), len(early)),
            [shape_of(height, width, BF16) for width in widths],
            *arrays[::-1],
            *early,
        )

    if tuned:
        arrays = gather(held, groups[0])
        weight, code_weight = small_kernel(
            "pack",
            functools.partial(pack_kernel, shapes),
            [
                shape_of((half // LANES * len(arrays) + 1) * rows, LANES, BF16),
                shape_of(len(arrays) * rows, half, BF16),
            ],
            *[arrays[k] for k in FIRST],
        )
        weight, code_weight, x, x_t = lax.optimization_barrier((weight, code_weight, x, x_t))
        (weights,) = [gather(weight, group) for group in groups[1:-1]]
        along, across = [[bit] for bit in groups[1][::-1]]
        (weight,) = join(weights, LANES, early=(cotangent,))
        weights = gather(weight, groups[-1])
        code_weights = gather(code_weight, along)
        code_order = order_of([groups[0], along, across])
        orders = [[m ^ r for r in order_of(groups[:-1])] for m in masks_of(groups[-1])]
        code_orders = [[m ^ r for r in code_order] for m in masks_of(groups[-1])]
        parts = orders
    else:
        held = lax.all_gather(held, AXES, axis=0, tiled=True)
        weights, code_weights, orders, code_orders, parts = [held[:, :lanes]], [held[:, lanes:]], None, None, [[0]]

    head = points // layer_tile // 2 * layer_tile
    output, tail, grad_hidden, *grads = pl.pallas_call(
        functools.partial(layer_kernel, hid, shapes, layer_tile, orders, parts),
        out_shape=[
            pltpu.HBM((points, width), F32),
            pltpu.VMEM((points - head, width), F32),
            pltpu.VMEM((points, hid), F32),
        ]
        + [shape_of(2 * shapes + width // len(parts), half, BF16)] * len(parts),
        in_specs=vmem(len(weights) + 3),
        out_specs=[pl.BlockSpec(memory_space=pltpu.HBM)] + vmem(2 + len(parts)),
        scratch_shapes=[
            VMEM((width, lanes), BF16),
            VMEM((width, half), F32),
            VMEM((head, width), F32),
            VMEM((points, width), BF16),
            VMEM((2, layer_tile, width), F32),
            pltpu.SemaphoreType.DMA((head // layer_tile,)),
        ],
        compiler_params=pltpu.CompilerParams(vmem_limit_bytes=20 * MIB),
        cost_estimate=pl.CostEstimate(
            flops=6 * points * width * cols,
            bytes_accessed=8 * points * (width + half),
            transcendentals=points * width,
        ),
        name="layer",
    )(*weights, x, x_t, cotangent)

    def store(name, body, shape, *args, **options):
        return pl.pallas_call(
            body,
            out_shape=pltpu.HBM(shape, F32),
            in_specs=[pl.BlockSpec(memory_space=pltpu.HBM)] * (len(args) - 1) + vmem(1),
            out_specs=pl.BlockSpec(memory_space=pltpu.HBM),
            scratch_shapes=[pltpu.SemaphoreType.DMA(())],
            compiler_params=pltpu.CompilerParams(vmem_limit_bytes=8 * MIB),
            cost_estimate=pl.CostEstimate(
                flops=4000 * MIB, bytes_accessed=8 * points * hid, transcendentals=0
            ),
            name=name,
            **options,
        )(*args)

    def store_grad_hidden():
        return store("store", store_kernel, (points, hid), grad_hidden)

    def store_tail():
        return store(
            "tail", tail_kernel, (points, width), output, tail, input_output_aliases={0: 0}
        )

    if tuned:
        *grads, code_along, running_mean, running_var = lax.optimization_barrier(
            (*grads, code_weights[1], running_mean, running_var)
        )
        (code_weight,) = join([code_weights[0], code_along], half)
        for r, group in enumerate(groups[::-1]):
            masks = masks_of(group)
            grads = [grads[0]] + swaps(grads[1:], masks[1:], devices)
            if r == len(groups) - 1:
                break
            n_out = len(masks_of(groups[-2 - r]))
            left = (grads[0].shape[0] - 2 * shapes) // n_out
            grads = small_kernel(
                "add",
                functools.partial(add_kernel, shapes, len(grads)),
                [shape_of(2 * shapes + left, half, BF16)] * n_out,
                *(grads[::-1] if r == 0 else [grads[k] for k in SUMS]),
            )
            if r == 0:
                *grads, grad_hidden = lax.optimization_barrier((*grads, grad_hidden))
                grad_hidden = store_grad_hidden()
                grad_hidden, code_weight = lax.optimization_barrier((grad_hidden, code_weight))
                code_weights = gather(code_weight, across)
            if r == len(groups) - 2:
                *grads, grad_hidden, tail = lax.optimization_barrier((*grads, grad_hidden, tail))
                output = store_tail()
        (code_weight,) = join(code_weights, half)
        code_weights = gather(code_weight, groups[-1])
    else:
        grad_hidden, output = store_grad_hidden(), store_tail()
        sums = lax.psum(grads[0][: 2 * shapes].astype(F32), AXES)
        high = sums.astype(BF16)
        own = lax.psum_scatter(grads[0][2 * shapes :].astype(F32), AXES, scatter_dimension=0, tiled=True)
        low = jnp.zeros((2 * shapes + rows, half), BF16).at[: 2 * shapes].set((sums - high).astype(BF16))
        grads = [jnp.concatenate([high, own.astype(BF16)], axis=0), low]
    grad_codes, grad_direction, grad_gain, grad_bias = small_kernel(
        "last",
        functools.partial(last_kernel, hid, shapes, code_orders, len(grads)),
        [
            shape_of(shapes, half, F32),
            shape_of(rows, cols, F32),
            shape_of(1, rows, F32),
            shape_of(1, rows, F32),
        ],
        *([grads[k] for k in FIRST] if tuned else grads),
        direction,
        gain_row,
        codes,
        *code_weights,
        scratch=[VMEM((width, half), BF16)],
    )

    total = float(points * devices)
    batch_mean = jnp.mean(codes, axis=0)
    batch_square = jnp.mean(codes * codes, axis=0)
    batch_var = (batch_square - batch_mean * batch_mean) * (total / (total - 1.0))
    new_mean = 0.9 * running_mean + 0.1 * batch_mean
    new_var = 0.9 * running_var + 0.1 * batch_var
    return (
        output,
        grad_hidden,
        grad_codes,
        grad_direction,
        grad_gain.reshape(rows),
        grad_bias.reshape(rows),
        new_mean,
        new_var,
    )


def solution(mesh):
    return jax.shard_map(
        per_device,
        mesh=mesh,
        in_specs=(
            P(("dp", "inner"), None),
            P(),
            P(("dp", "inner"), None),
            P(("dp", "inner")),
            P(("dp", "inner")),
            P(("dp", "inner"), None),
            P(("dp", "inner")),
            P(("dp", "inner")),
            P(("dp", "inner"), None),
            P(),
            P(),
        ),
        out_specs=(
            P(("dp", "inner"), None),
            P(("dp", "inner"), None),
            P(),
            P(("dp", "inner"), None),
            P(("dp", "inner")),
            P(("dp", "inner")),
            P(),
            P(),
        ),
        check_vma=False,
    )
```
